32 devices in a mesh: groups: 2 (over y), mesh: 4 (over z), mp: 2 (over x), batch: 2 (over core).
Axes of the slice: x: 2, y: 2, z: 4, core: 2. Of those that a mesh axis runs over, the one named last changes fastest.
Arguments:
- g_nodes: bfloat16 [4, 4096, 512], P(('groups', 'batch'), 'mesh', 'mp'), parts along dimension 0, may hold values from -6 to 6
- r_nodes: bfloat16 [4, 4096, 512], P(('groups', 'batch'), 'mesh', 'mp'), parts along dimension 0, may hold values from -6 to 6
- g_nbr: int32 [4096, 8], P('mesh'), may hold values from 0 to 2047, as said below
- g_count: int32 [4096], P('mesh'), may hold values from 1 to 8
- r_nbr: int32 [4096, 8], P('mesh'), may hold values from 0 to 2047, as said below
- r_count: int32 [4096], P('mesh'), may hold values from 1 to 8
- bnd_src: int32 [2048], P('mesh'), may hold values from 0 to 1023
- bnd_part: int32 [2048, 1], P('mesh'), may hold values from 0 to 3; in each aligned block of 512 rows (0 to 511, 512 to 1023, ...) at most 256 rows name the same one
- bnd_node: int32 [2048], P('mesh'), may hold values from 0 to 1023
- g_ws: bfloat16 [2, 512, 512], P(None, None, 'mp'), may hold values from -0.25 to 0.25
- g_wd: bfloat16 [2, 512, 512], P(None, None, 'mp'), may hold values from -0.25 to 0.25
- g_b1: bfloat16 [2, 512], P(None, 'mp'), may hold values from -4 to 4
- g_w2: bfloat16 [2, 512, 512], P(None, 'mp'), may hold values from -0.09375 to 0.09375
- r_ws: bfloat16 [2, 512, 512], P(None, None, 'mp'), may hold values from -0.25 to 0.25
- r_wd: bfloat16 [2, 512, 512], P(None, None, 'mp'), may hold values from -0.25 to 0.25
- r_b1: bfloat16 [2, 512], P(None, 'mp'), may hold values from -4 to 4
- r_w2: bfloat16 [2, 512, 512], P(None, 'mp'), may hold values from -0.09375 to 0.09375
Outputs:
- g_out: bfloat16 [4, 4096, 512], P(('groups', 'batch'), 'mesh', 'mp'), parts along dimension 0
- r_out: bfloat16 [4, 4096, 512], P(('groups', 'batch'), 'mesh', 'mp'), parts along dimension 0
The draws below stay inside these ranges and needn't reach their ends.
There are 2 independent parts, one for each index of `groups`. The reference program is written for one: setup_inputs(seed, part) draws one part's arguments, and reference() takes and returns one part's arrays. A program takes and returns all parts, laid end to end along the dimension named above; an argument that names none is the same for every part. Nothing has to cross between parts.
Inputs may be any that keep to these rules, and one draw needn't show every extreme that they name: `g_nbr`: row i of partition m points into the padded block of m at a row within 512 of its own row i + 512; both ends of the range are used. `r_nbr`: row i of partition m points into the padded block of m at a row within 512 of its own row i + 512; both ends of the range are used. `bnd_part`: among the boundary-zone rows of one partition, no regional partition is named by more than 256 rows, a bound that some block reaches.
All inputs are finite; a program needn't handle non-finite values.
Results may differ from the reference program's by a relative error of at most 0.015.
Values may be sent and summed in bfloat16 or wider, within the bound.
No kernel may reach another device: no remote copies, remote signals or barrier semaphores. Data moves between devices by JAX's collectives and lax.ppermute only.
A program may use at most 64 MiB of HBM per device.

```python
import math
import jax
import jax.numpy as jnp
import numpy as np
from jax import lax

D = 512
K = 8
LAYERS = 2
NG_DEV = 1024
NR_DEV = 1024
B_DEV = 512
HALO_G = 512
HALO_R = 512
CAP = 256
MB = 2
NG = 4096
NR = 4096
NB = 2048
N_MESH = 4
N_MP = 2


def local_links(key, total, rows, rim):
    own = jnp.arange(total, dtype=jnp.int32) % rows
    offset = jax.random.randint(key, (total, K), -rim, rim + 1, dtype=jnp.int32)
    links = own[:, None] + rim + offset
    links = links.at[0, 0].set(0)
    links = links.at[total - 1, K - 1].set(rows + 2 * rim - 1)
    return links


def draw_g_nbr(key, part):
    key = jax.random.fold_in(key, 11)
    return local_links(key, NG, NG_DEV, HALO_G)


def draw_r_nbr(key, part):
    key = jax.random.fold_in(key, 23)
    return local_links(key, NR, NR_DEV, HALO_R)


def place_ends(array, own_key, least, largest):
    dims = array.shape
    index_at = [jax.random.randint(jax.random.fold_in(own_key, axis), (), 0, dims[axis]) for axis in range(len(dims))]
    array = array.at[tuple(index_at)].set(least)
    longest = dims.index(max(dims))
    index_at[longest] = (index_at[longest] + 1) % dims[longest]
    return array.at[tuple(index_at)].set(largest)


def block_scale(key, extent, cuts, smallest, largest):
    def one(dim, shards_of):
        draws = jax.random.uniform(jax.random.fold_in(jax.random.fold_in(key, 6), dim), (shards_of,), jnp.float32, smallest / len(cuts), largest / len(cuts))
        return jnp.repeat(jnp.exp(draws), extent[dim] // shards_of).reshape((-1,) + (1,) * (len(extent) - dim - 1))

    level = one(*cuts[0])
    for cut in cuts[1:]:
        level = level * one(*cut)
    return level


def deal_out(rng, own, number, rows, number_of, top, limit, skew):
    order = jax.random.permutation(rng, number_of)
    packed, ordinary = portions_of(number_of, rows * top, limit, skew, True), portions_of(number_of, rows * top, limit, skew, False)
    places = jnp.arange(number_of)

    def named(sizes, turn):
        used = int((sizes > 0).sum())
        fixed = max(1, used // 4)
        shifted = fixed + (places - fixed + turn * (used - fixed)) % max(1, number_of - fixed)
        return jnp.zeros((number_of,), jnp.int32).at[order[jnp.where(places < fixed, places, shifted)]].set(jnp.asarray(sizes, jnp.int32))

    sizes = jnp.where(number % 4 == 0, named(packed, number // 4), named(ordinary, number - number // 4 - 1))
    mixed = jax.random.permutation(jax.random.fold_in(own, 3), number_of)
    source_of, sink = mixed[0:number_of // 2 * 2:2], mixed[1:number_of // 2 * 2:2]
    margin = jnp.minimum(sizes[source_of] - 1, limit - sizes[sink]) // 2
    margin = jnp.where((source_of == order[0]) | (sink == order[0]) | (sizes[sink] == 0), 0, jnp.maximum(margin, 0))
    shifted = jax.random.randint(jax.random.fold_in(own, 4), (number_of // 2,), 0, 1 << 20) % (margin + 1)
    sizes = sizes.at[source_of].add(-shifted).at[sink].add(shifted)
    labels = jnp.searchsorted(jnp.cumsum(sizes), jnp.arange(rows * top), side="right").astype(jnp.int32)
    grid = labels.reshape(top, rows).T
    grid = grid[jax.random.permutation(jax.random.fold_in(own, 1), rows)]
    turn = jax.random.randint(jax.random.fold_in(own, 2), (rows, 1), 0, top)
    return jnp.take_along_axis(grid, (jnp.arange(top)[None, :] + turn) % top, axis=1)


def portions_of(count, total, most, lean, full):
    portions = [(1 << 20) // math.isqrt(rank ** lean) + 1 for rank in range(1, count + 1)]
    largest = most if full else min(most, max(-(-total // count), total * portions[0] // sum(portions)))
    least = 1 if total - largest >= count - 1 else 0
    given, rest = [largest] + [least] * (count - 1), total - largest - least * (count - 1)
    while rest > 0:
        free = [i for i in range(1, count) if given[i] < largest] or [i for i in range(1, count) if given[i] < most]
        mass, remaining = sum([portions[i] for i in free]), rest
        for i in free:
            addition = min(most - given[i], max(1, remaining * portions[i] // mass), rest)
            given[i] = given[i] + addition
            rest = rest - addition
    return np.array(given)


def centred(own_key, dims, scale, reach, pieces=(), kind=jnp.bfloat16):
    result = scale * jax.random.normal(own_key, dims, jnp.float32)
    if pieces:
        result = result * block_scale(own_key, dims, pieces, -0.22, 0.18)
    return jnp.clip(result, -reach, reach).astype(kind)


def setup_inputs(seed: int = 0, part: int = 0) -> dict:
    key_of = jax.random.split(jax.random.key(seed), 18)
    part_keys = jax.random.split(jax.random.fold_in(key_of[17], part), 18)
    g_nodes = centred(part_keys[0], (MB, NG, D), 1.0, 6.0, ((0, 2), (1, 4), (2, 2)))
    r_nodes = centred(part_keys[1], (MB, NR, D), 1.0, 6.0, ((0, 2), (1, 4), (2, 2)))
    g_nbr = draw_g_nbr(jax.random.fold_in(key_of[17], 71), part)
    g_count = place_ends(jax.random.randint(key_of[3], (NG,), 1, K + 1), jax.random.fold_in(key_of[3], 1), 1, K).astype(jnp.int32)
    r_nbr = draw_r_nbr(jax.random.fold_in(key_of[17], 71), part)
    r_count = place_ends(jax.random.randint(key_of[5], (NR,), 1, K + 1), jax.random.fold_in(key_of[5], 1), 1, K).astype(jnp.int32)
    bnd_src = place_ends(jax.random.randint(key_of[6], (NB,), 0, NG_DEV), jax.random.fold_in(key_of[6], 1), 0, NG_DEV - 1).astype(jnp.int32)
    bnd_part_keys = jax.random.split(jax.random.fold_in(key_of[7], 1), NB // B_DEV)
    bnd_part_turns = jax.random.permutation(jax.random.fold_in(key_of[7], 3), NB // B_DEV)
    bnd_part = jax.vmap(lambda own, number: deal_out(jax.random.fold_in(key_of[7], 2), own, number, B_DEV, N_MESH, 1, CAP, 2))(bnd_part_keys, bnd_part_turns).reshape((NB, 1))
    bnd_node = place_ends(jax.random.randint(key_of[8], (NB,), 0, NR_DEV), jax.random.fold_in(key_of[8], 1), 0, NR_DEV - 1).astype(jnp.int32)
    g_ws = centred(key_of[9], (LAYERS, D, D), D ** -0.5, 0.25, ((2, 2),))
    g_wd = centred(key_of[10], (LAYERS, D, D), D ** -0.5, 0.25, ((2, 2),))
    g_b1 = centred(key_of[11], (LAYERS, D), 0.7, 4.0, ((1, 2),))
    g_w2 = centred(key_of[12], (LAYERS, D, D), (D * K) ** -0.5, 0.09375, ((1, 2),))
    r_ws = centred(key_of[13], (LAYERS, D, D), D ** -0.5, 0.25, ((2, 2),))
    r_wd = centred(key_of[14], (LAYERS, D, D), D ** -0.5, 0.25, ((2, 2),))
    r_b1 = centred(key_of[15], (LAYERS, D), 0.7, 4.0, ((1, 2),))
    r_w2 = centred(key_of[16], (LAYERS, D, D), (D * K) ** -0.5, 0.09375, ((1, 2),))
    return dict(g_nodes=g_nodes, r_nodes=r_nodes, g_nbr=g_nbr, g_count=g_count, r_nbr=r_nbr, r_count=r_count, bnd_src=bnd_src, bnd_part=bnd_part, bnd_node=bnd_node, g_ws=g_ws, g_wd=g_wd, g_b1=g_b1, g_w2=g_w2, r_ws=r_ws, r_wd=r_wd, r_b1=r_b1, r_w2=r_w2)


def pad_blocks(values, rows, rim, wrap):
    batch_rows, total, width = values.shape
    blocks = values.reshape(batch_rows, N_MESH, rows, width)
    before = jnp.roll(blocks[:, :, rows - rim:], 1, axis=1)
    after = jnp.roll(blocks[:, :, :rim], -1, axis=1)
    if not wrap:
        before = before.at[:, 0].set(0)
        after = after.at[:, -1].set(0)
    return jnp.concatenate([before, blocks, after], axis=2)


def graph_layer(latent, nbr, count, w_send, w_recv, bias, w_out, rows, rim, wrap):
    batch_rows = latent.shape[0]
    padded = pad_blocks(latent, rows, rim, wrap)
    proj = jnp.dot(padded, w_send, preferred_element_type=jnp.float32).astype(jnp.bfloat16)
    near = jnp.dot(latent, w_recv, preferred_element_type=jnp.float32) + bias.astype(jnp.float32)
    near = near.reshape(batch_rows, N_MESH, rows, D)
    block_nbr = nbr.reshape(N_MESH, rows, K)
    live = jnp.arange(K, dtype=jnp.int32)[None, None, :] < count.reshape(N_MESH, rows)[:, :, None]

    def one_block(items):
        proj_block, near_block, nbr_block, live_block = items
        pre = proj_block[:, nbr_block].astype(jnp.float32) + near_block[:, :, None]
        acts = jnp.where(live_block[None, :, :, None], jax.nn.silu(pre), 0.0)
        return jnp.sum(acts, axis=2).astype(jnp.bfloat16)

    summed = lax.map(one_block, (jnp.moveaxis(proj, 1, 0), jnp.moveaxis(near, 1, 0), block_nbr, live))
    summed = jnp.moveaxis(summed, 0, 1).reshape(batch_rows, N_MESH * rows, D)
    share = D // N_MP
    update = jnp.zeros((batch_rows, N_MESH * rows, D), jnp.float32)
    for group in range(N_MP):
        part_sum = jnp.dot(summed[:, :, group * share:(group + 1) * share],
                           w_out[group * share:(group + 1) * share],
                           preferred_element_type=jnp.float32).astype(jnp.bfloat16)
        update = update + lax.optimization_barrier(part_sum).astype(jnp.float32)
    return (latent.astype(jnp.float32) + update).astype(jnp.bfloat16)


def reference(g_nodes, r_nodes, g_nbr, g_count, r_nbr, r_count, bnd_src, bnd_part, bnd_node,
              g_ws, g_wd, g_b1, g_w2, r_ws, r_wd, r_b1, r_w2):
    source = (jnp.arange(B_DEV * N_MESH, dtype=jnp.int32) // B_DEV) * NG_DEV + bnd_src
    target = bnd_part[:, 0] * NR_DEV + bnd_node
    picked = g_nodes[:, source].astype(jnp.float32)
    force = jnp.zeros(r_nodes.shape, jnp.float32).at[:, target].add(picked)
    regional = (r_nodes.astype(jnp.float32) + force).astype(jnp.bfloat16)
    planet = g_nodes
    for layer in range(LAYERS):
        planet = graph_layer(planet, g_nbr, g_count, g_ws[layer], g_wd[layer], g_b1[layer], g_w2[layer],
                             NG_DEV, HALO_G, True)
    for layer in range(LAYERS):
        regional = graph_layer(regional, r_nbr, r_count, r_ws[layer], r_wd[layer], r_b1[layer], r_w2[layer],
                               NR_DEV, HALO_R, False)
    return planet, regional
```

```python
import functools

import jax
import jax.numpy as jnp
from jax import lax
from jax.experimental import pallas as pl
from jax.experimental.pallas import tpu as pltpu
from jax.sharding import PartitionSpec as P

LANES = 128
DEAD = -1e30


def padded_2(shard, sides, width, wrap):
    for axis, dim in sides:
        size, length = (lax.axis_size(axis), shard.shape[dim])
        up = [(i, (i + 1) % size) for i in range(size if wrap else size - 1)]
        down = [(j, i) for i, j in up]
        last = lax.slice_in_dim(shard, length - width, length, axis=dim)
        leading = lax.slice_in_dim(shard, 0, width, axis=dim)
        before = lax.ppermute(last, axis, up)
        after = lax.ppermute(leading, axis, down)
        shard = jnp.concatenate([before, shard, after], axis=dim)
    return shard


def edge_sums(proj, near, nbr, count):
    slots = nbr.shape[1]
    live = jnp.arange(slots, dtype=jnp.int32)[None, :] < count[:, None]
    pre = proj[:, nbr].astype(jnp.float32) + near[:, :, None]
    acts = jnp.where(live[None, :, :, None], jax.nn.silu(pre), 0.0)
    return jnp.sum(acts, axis=2).astype(jnp.bfloat16)


def graph_layer(latent, nbr, count, w_send, w_recv, bias, w_out, wrap):
    rim = latent.shape[1] // 2
    own_full = lax.all_gather(latent, "mp", axis=2, tiled=True)
    padded_full = padded_2(own_full, (("mesh", 1),), rim, wrap)
    proj = jnp.dot(padded_full, w_send, preferred_element_type=jnp.float32).astype(jnp.bfloat16)
    near = jnp.dot(own_full, w_recv, preferred_element_type=jnp.float32) + bias.astype(jnp.float32)
    summed = edge_sums(proj, near, nbr, count)
    partial_prod = jnp.dot(summed, w_out, preferred_element_type=jnp.float32)
    update = lax.psum_scatter(
        partial_prod.astype(jnp.bfloat16), "mp", scatter_dimension=2, tiled=True
    ).astype(jnp.float32)
    return (latent.astype(jnp.float32) + update).astype(jnp.bfloat16)


def by_features(
    g_nodes, r_nodes, g_nbr, g_count, r_nbr, r_count, bnd_src, bnd_part, bnd_node,
    g_ws, g_wd, g_b1, g_w2, r_ws, r_wd, r_b1, r_w2,
):
    batch_rows, reg_rows, feats = r_nodes.shape
    dest = bnd_part[:, 0]
    outgoing = jnp.moveaxis(g_nodes[:, bnd_src], 1, 0)
    init = jnp.zeros((reg_rows + 1, batch_rows, feats), jnp.float32)
    target = dest * reg_rows + bnd_node
    mine = lax.axis_index("mesh")
    piece_rows = lax.all_gather(outgoing, "mesh", axis=0, tiled=True)
    piece_target = lax.all_gather(target, "mesh", axis=0, tiled=True)
    local = jnp.where(piece_target // reg_rows == mine, piece_target % reg_rows + 1, 0)
    landed = init.at[local].add(piece_rows.astype(jnp.float32))
    force = jnp.moveaxis(landed[1:], 1, 0)
    regional = (r_nodes.astype(jnp.float32) + force).astype(jnp.bfloat16)
    planet = g_nodes
    for layer in range(g_ws.shape[0]):
        planet = graph_layer(
            planet, g_nbr, g_count, g_ws[layer], g_wd[layer], g_b1[layer], g_w2[layer], True
        )
    for layer in range(r_ws.shape[0]):
        regional = graph_layer(
            regional, r_nbr, r_count, r_ws[layer], r_wd[layer], r_b1[layer], r_w2[layer], False
        )
    return (planet, regional)


def one_hot(flags):
    return jnp.where(flags, 1.0, 0.0).astype(jnp.bfloat16)


def pick_kernel(parts, cap, me_ref, bnd_ref, g_ref, *out_refs):
    rows = g_ref.shape[0]
    total = bnd_ref.shape[1]
    me = me_ref[0]
    src, part, node = (bnd_ref[i:i + 1, :] for i in range(3))
    lines = -(-parts // 8) * 8
    target = lax.rem(lax.broadcasted_iota(jnp.int32, (lines, total), 0) + me, parts)
    named = part == target
    before = one_hot(
        lax.broadcasted_iota(jnp.int32, (total, total), 0) < lax.broadcasted_iota(jnp.int32, (total, total), 1)
    )
    rank = jnp.dot(one_hot(named), before, preferred_element_type=jnp.float32)
    rank = jnp.where(named, rank, -1.0)
    source = one_hot(lax.broadcasted_iota(jnp.int32, (rows, total), 0) == src)
    line = lax.broadcasted_iota(jnp.int32, (16, total), 0)
    high = lax.shift_right_logical(node, 7)
    facts = jnp.where(line == 0, high, jnp.where(line == 1, node - high * 128, jnp.where(line == 2, 1, 0)))
    facts = facts.astype(jnp.float32).astype(jnp.bfloat16)
    place = lax.broadcasted_iota(jnp.int32, (cap, total), 0).astype(jnp.float32)
    across = (((1,), (1,)), ((), ()))
    for k in range(parts):
        chosen = one_hot(place == rank[k:k + 1, :])
        pick = lax.dot_general(chosen, source, across, preferred_element_type=jnp.float32).astype(jnp.bfloat16)
        out_refs[k][:cap, :] = jnp.dot(pick, g_ref[...], preferred_element_type=jnp.float32).astype(jnp.bfloat16)
        told = lax.dot_general(facts, chosen, across, preferred_element_type=jnp.float32)
        out_refs[k][cap:, :] = told.astype(jnp.bfloat16)


def pick_rows(me, bnd, nodes, parts, cap):
    vmem = pl.BlockSpec(memory_space=pltpu.VMEM)
    rows, feats = nodes.shape
    total = bnd.shape[1]
    piece = jax.ShapeDtypeStruct((cap + 16, feats), jnp.bfloat16)
    return pl.pallas_call(
        functools.partial(pick_kernel, parts, cap),
        out_shape=(piece,) * parts,
        in_specs=[pl.BlockSpec(memory_space=pltpu.SMEM), vmem, vmem],
        out_specs=(vmem,) * parts,
        compiler_params=pltpu.CompilerParams(vmem_limit_bytes=32 << 20),
        cost_estimate=pl.CostEstimate(
            flops=2 * parts * cap * rows * (total + feats), bytes_accessed=4 * rows * feats, transcendentals=0
        ),
        name="pick_rows",
    )(me, bnd, nodes)


def force_kernel(cap, first_ref, r_ref, *refs):
    pieces, (same_ref, other_ref) = refs[:-2], refs[-2:]
    half = same_ref.shape[0]
    first = first_ref[0]
    for out_ref, start in ((same_ref, first * half), (other_ref, (1 - first) * half)):
        start = pl.multiple_of(start, 16)
        row = (lax.broadcasted_iota(jnp.int32, (half, cap), 0) + start).astype(jnp.float32)
        total = r_ref[pl.ds(start, half), :].astype(jnp.float32)
        for piece in pieces:
            facts = piece[cap:, :].astype(jnp.float32)
            node = jnp.where(facts[2:3, :] > 0.5, facts[0:1, :] * 128.0 + facts[1:2, :], -1.0)
            total += jnp.dot(one_hot(row == node), piece[:cap, :], preferred_element_type=jnp.float32)
        out_ref[...] = total.astype(jnp.bfloat16)


def add_force(first, nodes, pieces, cap):
    vmem = pl.BlockSpec(memory_space=pltpu.VMEM)
    rows, feats = nodes.shape
    block = jax.ShapeDtypeStruct((rows // 2, feats), jnp.bfloat16)
    return pl.pallas_call(
        functools.partial(force_kernel, cap),
        out_shape=(block, block),
        in_specs=[pl.BlockSpec(memory_space=pltpu.SMEM)] + [vmem] * (1 + len(pieces)),
        out_specs=(vmem, vmem),
        compiler_params=pltpu.CompilerParams(vmem_limit_bytes=32 << 20),
        cost_estimate=pl.CostEstimate(
            flops=2 * len(pieces) * cap * rows * feats, bytes_accessed=6 * rows * feats, transcendentals=0
        ),
        name="add_force",
    )(first, nodes, *pieces)


def layer_kernel(
    layer, slots, last, core_ref, idx_ref, own_hbm, sib_hbm, rim_hbm, ws_hbm, wd_hbm, w2_hbm, b_hbm, near_hbm, far_hbm,
    *refs,
):
    outs, refs = (refs[:2], refs[2:]) if last else (refs[:1], refs[1:])
    own, sib, rim, ws, wd, w2, bias, near_w, far_w, ws_x, wd_x, w2_x, proj, near, summed, sems = refs
    rows, width = own.shape
    share = width // 2
    chunks = width // LANES
    core = core_ref[0]
    pairs = (
        (own_hbm, own), (wd_hbm.at[layer], wd), (ws_hbm.at[layer], ws), (b_hbm, bias),
        (near_hbm, near_w), (far_hbm, far_w), (sib_hbm, sib), (rim_hbm, rim), (w2_hbm.at[layer], w2),
    )
    copies = [pltpu.make_async_copy(src, dst, sems.at[i]) for i, (src, dst) in enumerate(pairs)]
    for copy in copies:
        copy.start()
    window = 3 * rows
    proj[0:8, :] = jnp.full((8, LANES), DEAD, jnp.float32)
    proj[4 * window + 4:4 * window + 16, :] = jnp.full((12, LANES), DEAD, jnp.float32)

    def put(dst, base, first, values):
        for c in range(values.shape[1] // LANES):
            dst[pl.ds(base * chunks + first + c, rows, stride=chunks), :] = values[:, c * LANES:(c + 1) * LANES]

    for i in (0, 1, 2, 3):
        copies[i].wait()
    part = share // LANES
    b_own = bias[layer:layer + 1, :].astype(jnp.float32)
    put(near, 0, 0, (jnp.dot(own[...], wd[...], preferred_element_type=jnp.float32) + b_own) * 0.5)
    put(proj, 1, 0, jnp.dot(own[...], ws[...], preferred_element_type=jnp.float32) * 0.5)
    for i in (4, 5):
        copies[i].wait()
    here, there = pl.multiple_of(core * share, 16), pl.multiple_of((1 - core) * share, 16)
    for spot, piece in ((here, near_w), (there, far_w)):
        ws_x[pl.ds(spot, share), :] = piece[0:share, :]
        wd_x[pl.ds(spot, share), :] = piece[share:2 * share, :]

    @pl.when(core == 0)
    def _():
        w2_x[:, :share] = near_w[2 * share:3 * share, :]
        w2_x[:, share:] = far_w[2 * share:3 * share, :]

    @pl.when(core != 0)
    def _():
        w2_x[:, share:] = near_w[2 * share:3 * share, :]
        w2_x[:, :share] = far_w[2 * share:3 * share, :]

    b_other = near_w[3 * share:3 * share + 1, :].astype(jnp.float32)
    put(near, 0, part, (jnp.dot(own[...], wd_x[...], preferred_element_type=jnp.float32) + b_other) * 0.5)
    put(proj, 1, part, jnp.dot(own[...], ws_x[...], preferred_element_type=jnp.float32) * 0.5)
    for i, ref, base in ((6, sib, rows + 1), (7, rim, 2 * rows + 1)):
        copies[i].wait()
        put(proj, base, 0, jnp.dot(ref[...], ws[...], preferred_element_type=jnp.float32) * 0.5)
        put(proj, base, part, jnp.dot(ref[...], ws_x[...], preferred_element_type=jnp.float32) * 0.5)
    low = lax.broadcasted_iota(jnp.int32, (8, LANES), 0) < chunks

    def nodes(q, carry):
        spot = pl.ds(pl.multiple_of(8 * q, 8), 8)
        mine = near[spot, :]
        total = None
        for j in range(slots):
            upper = proj[pl.ds(pl.multiple_of(idx_ref[2 * q * slots + j], 4), 8), :]
            lower = proj[pl.ds(pl.multiple_of(idx_ref[(2 * q + 1) * slots + j], 4), 8), :]
            y = jnp.where(low, upper, lower) + mine
            act = y * jnp.tanh(y) + y
            total = act if total is None else total + act
        summed[spot, :] = total
        return carry

    lax.fori_loop(0, rows // 2, nodes, 0, unroll=8)
    copies[8].wait()
    update = None
    for c in range(chunks):
        values = summed[pl.ds(c, rows, stride=chunks), :].astype(jnp.bfloat16)
        if c < part:
            w_rows = w2[c * LANES:(c + 1) * LANES, :]
        else:
            w_rows = w2_x[(c - part) * LANES:(c - part + 1) * LANES, :]
        term = jnp.dot(values, w_rows, preferred_element_type=jnp.float32)
        update = term if update is None else update + term
    result = (own[...].astype(jnp.float32) + update).astype(jnp.bfloat16)
    if not last:
        outs[0][...] = result
    else:
        @pl.when(core == 0)
        def _():
            outs[0][...] = result[:, :share]
            outs[1][...] = result[:, share:]

        @pl.when(core != 0)
        def _():
            outs[0][...] = result[:, share:]
            outs[1][...] = result[:, :share]


def run_layer(layer, slots, last, core, idx, own, sib, rim, ws, wd, w2, bias, near_w, far_w):
    rows, width = own.shape
    share = width // 2
    chunks = width // LANES
    anywhere = pl.BlockSpec(memory_space=pl.ANY)
    smem = pl.BlockSpec(memory_space=pltpu.SMEM)
    vmem = pl.BlockSpec(memory_space=pltpu.VMEM)
    bf16, f32 = jnp.bfloat16, jnp.float32
    if last:
        out_shape = (jax.ShapeDtypeStruct((rows, share), bf16),) * 2
        out_specs = (vmem, vmem)
    else:
        out_shape, out_specs = jax.ShapeDtypeStruct((rows, width), bf16), vmem
    edges = rows * slots
    return pl.pallas_call(
        functools.partial(layer_kernel, layer, slots, last),
        out_shape=out_shape,
        in_specs=[smem, smem] + [anywhere] * 9,
        out_specs=out_specs,
        scratch_shapes=[
            pltpu.VMEM((rows, width), bf16),
            pltpu.VMEM((rows, width), bf16),
            pltpu.VMEM((rows, width), bf16),
            pltpu.VMEM((width, share), bf16),
            pltpu.VMEM((width, share), bf16),
            pltpu.VMEM((share, width), bf16),
            pltpu.VMEM(bias.shape, bf16),
            pltpu.VMEM(near_w.shape, bf16),
            pltpu.VMEM(far_w.shape, bf16),
            pltpu.VMEM((width, share), bf16),
            pltpu.VMEM((width, share), bf16),
            pltpu.VMEM((share, width), bf16),
            pltpu.VMEM((3 * rows * chunks + 96, LANES), f32),
            pltpu.VMEM((rows * chunks, LANES), f32),
            pltpu.VMEM((rows * chunks, LANES), f32),
            pltpu.SemaphoreType.DMA((9,)),
        ],
        compiler_params=pltpu.CompilerParams(vmem_limit_bytes=32 << 20),
        cost_estimate=pl.CostEstimate(
            flops=2 * 5 * rows * width * width, bytes_accessed=10 * rows * width, transcendentals=edges * width
        ),
        name="graph_layer",
    )(core, idx, own, sib, rim, ws, wd, w2, bias, near_w, far_w)


def edge_offsets(nbr, count, core):
    rows, slots = nbr.shape
    half = rows // 2
    nbr = lax.dynamic_slice(nbr, (core * half, 0), (half, slots)) - core * half
    count = lax.dynamic_slice(count, (core * half,), (half,))
    low = nbr + jnp.where(core == 0, 2 * half, half)
    high = nbr - jnp.where(core == 0, half, 0)
    place = jnp.where(nbr < half, low, jnp.where(nbr < 2 * half, nbr - half, high))
    live = jnp.arange(slots, dtype=jnp.int32)[None, :] < count[:, None]
    place = jnp.where(live, place, 3 * half)
    odd = jnp.arange(half, dtype=jnp.int32)[:, None] % 2
    return (4 * (place + 1 - odd)).reshape(half * slots)


def spread_rows(same, other):
    a = lax.ppermute(same, ("mp", "batch"), [(0, 0), (1, 2), (2, 1), (3, 3)])
    b = lax.ppermute(other, ("mp", "batch"), [(0, 1), (1, 3), (2, 0), (3, 2)])
    return a, b


def gather_rows(a, b):
    same = lax.ppermute(a, ("mp", "batch"), [(0, 0), (1, 2), (2, 1), (3, 3)])
    other = lax.ppermute(b, ("mp", "batch"), [(0, 2), (1, 0), (2, 3), (3, 1)])
    return same, other


def ordered(which, a, b, axis):
    return jnp.where(which == 0, jnp.concatenate([a, b], axis), jnp.concatenate([b, a], axis))


def swap(values, axis):
    return lax.ppermute(values, axis, [(0, 1), (1, 0)])


def rims(own, wrap):
    size = lax.axis_size("mesh")
    pairs = []
    for m in range(size):
        if wrap or m + 1 < size:
            pairs.append((2 * m + 1, 2 * ((m + 1) % size)))
        if wrap or m > 0:
            pairs.append((2 * m, 2 * ((m - 1) % size) + 1))
    return lax.ppermute(own, ("mesh", "batch"), pairs)


def other_weights(layer, core, ws, wd, w2, bias):
    share = ws.shape[2]
    picked = [
        lax.dynamic_slice(ws, (layer, core * share, 0), (1, share, share))[0],
        lax.dynamic_slice(wd, (layer, core * share, 0), (1, share, share))[0],
        lax.dynamic_slice(w2, (layer, 0, core * share), (1, share, share))[0],
        jnp.broadcast_to(bias[layer][None], (16, share)),
    ]
    near_w = swap(jnp.concatenate(picked, 0), "mp")
    return near_w, swap(near_w, "batch")


def by_rows(
    g_nodes, r_nodes, g_nbr, g_count, r_nbr, r_count, bnd_src, bnd_part, bnd_node,
    g_ws, g_wd, g_b1, g_w2, r_ws, r_wd, r_b1, r_w2,
):
    part = lax.axis_index("mp")
    core = lax.axis_index("batch")
    parts = lax.axis_size("mesh")
    slots = g_nbr.shape[1]
    layers = g_ws.shape[0]
    rows = g_nodes.shape[1]
    half = rows // 2
    cap = 2 * bnd_src.shape[0] // parts
    me = lax.axis_index("mesh").reshape(1)
    core1 = core.reshape(1)
    g_own, r_own = g_nodes[0], r_nodes[0]

    same = lax.dynamic_slice(g_own, (part * half, 0), (half, g_own.shape[1]))
    other = lax.dynamic_slice(g_own, ((1 - part) * half, 0), (half, g_own.shape[1]))
    g_a, g_b = spread_rows(same, other)
    bnd = jnp.stack([bnd_src, bnd_part[:, 0], bnd_node])
    pieces = pick_rows(me, bnd, g_own, parts, cap)
    landed = [pieces[0]]
    for k in range(1, parts):
        landed.append(lax.ppermute(pieces[k], "mesh", [(i, (i + k) % parts) for i in range(parts)]))
    g_idx = edge_offsets(g_nbr, g_count, core)
    r_idx = edge_offsets(r_nbr, r_count, core)
    r_a, r_b = spread_rows(*add_force(part.reshape(1), r_own, landed, cap))

    planet = ordered(core, g_a, g_b, 1)
    regional = ordered(core, r_a, r_b, 1)
    for layer in range(layers):
        last = layer == layers - 1
        g_w = other_weights(layer, core, g_ws, g_wd, g_w2, g_b1)
        planet = run_layer(
            layer, slots, last, core1, g_idx, planet, swap(planet, "batch"), rims(planet, True),
            g_ws, g_wd, g_w2, g_b1, *g_w,
        )
        r_w = other_weights(layer, core, r_ws, r_wd, r_w2, r_b1)
        regional = run_layer(
            layer, slots, last, core1, r_idx, regional, swap(regional, "batch"), rims(regional, False),
            r_ws, r_wd, r_w2, r_b1, *r_w,
        )
    g_out = ordered(part, *gather_rows(*planet), 0)
    r_out = ordered(part, *gather_rows(*regional), 0)
    return g_out[None], r_out[None]


def solution(mesh):
    in_specs = (
        P(("groups", "batch"), "mesh", "mp"),
        P(("groups", "batch"), "mesh", "mp"),
        P("mesh", None),
        P("mesh"),
        P("mesh", None),
        P("mesh"),
        P("mesh"),
        P("mesh", None),
        P("mesh"),
        P(None, None, "mp"),
        P(None, None, "mp"),
        P(None, "mp"),
        P(None, "mp", None),
        P(None, None, "mp"),
        P(None, None, "mp"),
        P(None, "mp"),
        P(None, "mp", None),
    )
    out_specs = (P(("groups", "batch"), "mesh", "mp"), P(("groups", "batch"), "mesh", "mp"))
    square = mesh.shape["mp"] == 2 and mesh.shape["batch"] == 2
    return jax.shard_map(
        by_rows if square else by_features, mesh=mesh, in_specs=in_specs, out_specs=out_specs, check_vma=False
    )
```

```python
import functools

import jax
import jax.numpy as jnp
from jax import lax
from jax.experimental import pallas as pl
from jax.experimental.pallas import tpu as pltpu
from jax.sharding import PartitionSpec as P

LANES = 128
DEAD = -1e30
SMALL = pl.CostEstimate(flops=1, bytes_accessed=1, transcendentals=0)


def padded_2(shard, sides, width, wrap):
    for axis, dim in sides:
        size, length = (lax.axis_size(axis), shard.shape[dim])
        up = [(i, (i + 1) % size) for i in range(size if wrap else size - 1)]
        down = [(j, i) for i, j in up]
        last = lax.slice_in_dim(shard, length - width, length, axis=dim)
        leading = lax.slice_in_dim(shard, 0, width, axis=dim)
        before = lax.ppermute(last, axis, up)
        after = lax.ppermute(leading, axis, down)
        shard = jnp.concatenate([before, shard, after], axis=dim)
    return shard


def edge_sums(proj, near, nbr, count):
    slots = nbr.shape[1]
    live = jnp.arange(slots, dtype=jnp.int32)[None, :] < count[:, None]
    pre = proj[:, nbr].astype(jnp.float32) + near[:, :, None]
    acts = jnp.where(live[None, :, :, None], jax.nn.silu(pre), 0.0)
    return jnp.sum(acts, axis=2).astype(jnp.bfloat16)


def graph_layer(latent, nbr, count, w_send, w_recv, bias, w_out, wrap):
    rim = latent.shape[1] // 2
    own_full = lax.all_gather(latent, "mp", axis=2, tiled=True)
    padded_full = padded_2(own_full, (("mesh", 1),), rim, wrap)
    proj = jnp.dot(padded_full, w_send, preferred_element_type=jnp.float32).astype(jnp.bfloat16)
    near = jnp.dot(own_full, w_recv, preferred_element_type=jnp.float32) + bias.astype(jnp.float32)
    summed = edge_sums(proj, near, nbr, count)
    partial_prod = jnp.dot(summed, w_out, preferred_element_type=jnp.float32)
    update = lax.psum_scatter(
        partial_prod.astype(jnp.bfloat16), "mp", scatter_dimension=2, tiled=True
    ).astype(jnp.float32)
    return (latent.astype(jnp.float32) + update).astype(jnp.bfloat16)


def by_features(
    g_nodes, r_nodes, g_nbr, g_count, r_nbr, r_count, bnd_src, bnd_part, bnd_node,
    g_ws, g_wd, g_b1, g_w2, r_ws, r_wd, r_b1, r_w2,
):
    batch_rows, reg_rows, feats = r_nodes.shape
    dest = bnd_part[:, 0]
    outgoing = jnp.moveaxis(g_nodes[:, bnd_src], 1, 0)
    init = jnp.zeros((reg_rows + 1, batch_rows, feats), jnp.float32)
    target = dest * reg_rows + bnd_node
    mine = lax.axis_index("mesh")
    piece_rows = lax.all_gather(outgoing, "mesh", axis=0, tiled=True)
    piece_target = lax.all_gather(target, "mesh", axis=0, tiled=True)
    local = jnp.where(piece_target // reg_rows == mine, piece_target % reg_rows + 1, 0)
    landed = init.at[local].add(piece_rows.astype(jnp.float32))
    force = jnp.moveaxis(landed[1:], 1, 0)
    regional = (r_nodes.astype(jnp.float32) + force).astype(jnp.bfloat16)
    planet = g_nodes
    for layer in range(g_ws.shape[0]):
        planet = graph_layer(
            planet, g_nbr, g_count, g_ws[layer], g_wd[layer], g_b1[layer], g_w2[layer], True
        )
    for layer in range(r_ws.shape[0]):
        regional = graph_layer(
            regional, r_nbr, r_count, r_ws[layer], r_wd[layer], r_b1[layer], r_w2[layer], False
        )
    return (planet, regional)


def one_hot(flags):
    return jnp.where(flags, 1.0, 0.0).astype(jnp.bfloat16)


def pick_kernel(parts, cap, me_ref, bnd_ref, g_ref, *out_refs):
    rows = g_ref.shape[0]
    total = bnd_ref.shape[1]
    me = me_ref[0]
    src, part, node = (bnd_ref[i:i + 1, :] for i in range(3))
    lines = -(-parts // 8) * 8
    target = lax.rem(lax.broadcasted_iota(jnp.int32, (lines, total), 0) + me, parts)
    named = part == target
    before = one_hot(
        lax.broadcasted_iota(jnp.int32, (total, total), 0) < lax.broadcasted_iota(jnp.int32, (total, total), 1)
    )
    rank = jnp.dot(one_hot(named), before, preferred_element_type=jnp.float32)
    rank = jnp.where(named, rank, -1.0)
    source = one_hot(lax.broadcasted_iota(jnp.int32, (rows, total), 0) == src)
    line = lax.broadcasted_iota(jnp.int32, (16, total), 0)
    high = lax.shift_right_logical(node, 7)
    facts = jnp.where(line == 0, high, jnp.where(line == 1, node - high * 128, jnp.where(line == 2, 1, 0)))
    facts = facts.astype(jnp.float32).astype(jnp.bfloat16)
    place = lax.broadcasted_iota(jnp.int32, (cap, total), 0).astype(jnp.float32)
    across = (((1,), (1,)), ((), ()))
    for k in range(parts):
        chosen = one_hot(place == rank[k:k + 1, :])
        pick = lax.dot_general(chosen, source, across, preferred_element_type=jnp.float32).astype(jnp.bfloat16)
        out_refs[k][:cap, :] = jnp.dot(pick, g_ref[...], preferred_element_type=jnp.float32).astype(jnp.bfloat16)
        told = lax.dot_general(facts, chosen, across, preferred_element_type=jnp.float32)
        out_refs[k][cap:, :] = told.astype(jnp.bfloat16)


def pick_rows(me, bnd, nodes, parts, cap):
    vmem = pl.BlockSpec(memory_space=pltpu.VMEM)
    rows, feats = nodes.shape
    total = bnd.shape[1]
    piece = jax.ShapeDtypeStruct((cap + 16, feats), jnp.bfloat16)
    return pl.pallas_call(
        functools.partial(pick_kernel, parts, cap),
        out_shape=(piece,) * parts,
        in_specs=[pl.BlockSpec(memory_space=pltpu.SMEM), vmem, vmem],
        out_specs=(vmem,) * parts,
        compiler_params=pltpu.CompilerParams(vmem_limit_bytes=32 << 20),
        cost_estimate=SMALL,
        name="pick_rows",
    )(me, bnd, nodes)


def force_kernel(cap, first_ref, r_ref, *refs):
    pieces, (same_ref, other_ref) = refs[:-2], refs[-2:]
    half = same_ref.shape[0]
    first = first_ref[0]
    for out_ref, start in ((same_ref, first * half), (other_ref, (1 - first) * half)):
        start = pl.multiple_of(start, 16)
        row = (lax.broadcasted_iota(jnp.int32, (half, cap), 0) + start).astype(jnp.float32)
        total = r_ref[pl.ds(start, half), :].astype(jnp.float32)
        for piece in pieces:
            facts = piece[cap:, :].astype(jnp.float32)
            node = jnp.where(facts[2:3, :] > 0.5, facts[0:1, :] * 128.0 + facts[1:2, :], -1.0)
            total += jnp.dot(one_hot(row == node), piece[:cap, :], preferred_element_type=jnp.float32)
        out_ref[...] = total.astype(jnp.bfloat16)


def add_force(first, nodes, pieces, cap):
    vmem = pl.BlockSpec(memory_space=pltpu.VMEM)
    rows, feats = nodes.shape
    block = jax.ShapeDtypeStruct((rows // 2, feats), jnp.bfloat16)
    return pl.pallas_call(
        functools.partial(force_kernel, cap),
        out_shape=(block, block),
        in_specs=[pl.BlockSpec(memory_space=pltpu.SMEM)] + [vmem] * (1 + len(pieces)),
        out_specs=(vmem, vmem),
        compiler_params=pltpu.CompilerParams(vmem_limit_bytes=32 << 20),
        cost_estimate=SMALL,
        name="add_force",
    )(first, nodes, *pieces)


def layer_kernel(
    layer, slots, last, spot, core_ref, idx_ref, own_hbm, sib_hbm, rim_hbm, ws_hbm, wd_hbm, w2_hbm, b_hbm, near_hbm, far_hbm,
    *refs,
):
    outs, refs = (refs[:2], refs[2:]) if last else (refs[:1], refs[1:])
    own, sib, rim, ws, wd, w2, bias, near_w, far_w, ws_x, wd_x, w2_x, proj, near, summed, sems = refs
    rows, width = own.shape
    share = width // 2
    chunks = width // LANES
    core = core_ref[0]
    pairs = (
        (own_hbm, own), (wd_hbm.at[layer], wd), (ws_hbm.at[layer], ws), (b_hbm, bias),
        (near_hbm.at[spot:spot + near_w.shape[0], :], near_w), (far_hbm.at[spot:spot + far_w.shape[0], :], far_w), (sib_hbm, sib), (rim_hbm, rim), (w2_hbm.at[layer], w2),
    )
    copies = [pltpu.make_async_copy(src, dst, sems.at[i]) for i, (src, dst) in enumerate(pairs)]
    for copy in copies:
        copy.start()
    window = 3 * rows
    proj[0:8, :] = jnp.full((8, LANES), DEAD, jnp.float32)
    proj[4 * window + 4:4 * window + 16, :] = jnp.full((12, LANES), DEAD, jnp.float32)

    def put(dst, base, first, values):
        for c in range(values.shape[1] // LANES):
            dst[pl.ds(base * chunks + first + c, rows, stride=chunks), :] = values[:, c * LANES:(c + 1) * LANES]

    for i in (0, 1, 2, 3):
        copies[i].wait()
    part = share // LANES
    b_own = bias[layer:layer + 1, :].astype(jnp.float32)
    put(near, 0, 0, (jnp.dot(own[...], wd[...], preferred_element_type=jnp.float32) + b_own) * 0.5)
    put(proj, 1, 0, jnp.dot(own[...], ws[...], preferred_element_type=jnp.float32) * 0.5)
    for i in (4, 5):
        copies[i].wait()
    here, there = pl.multiple_of(core * share, 16), pl.multiple_of((1 - core) * share, 16)
    for spot, piece in ((here, near_w), (there, far_w)):
        ws_x[pl.ds(spot, share), :] = piece[0:share, :]
        wd_x[pl.ds(spot, share), :] = piece[share:2 * share, :]

    @pl.when(core == 0)
    def _():
        w2_x[:, :share] = near_w[2 * share:3 * share, :]
        w2_x[:, share:] = far_w[2 * share:3 * share, :]

    @pl.when(core != 0)
    def _():
        w2_x[:, share:] = near_w[2 * share:3 * share, :]
        w2_x[:, :share] = far_w[2 * share:3 * share, :]

    b_other = near_w[3 * share:3 * share + 1, :].astype(jnp.float32)
    put(near, 0, part, (jnp.dot(own[...], wd_x[...], preferred_element_type=jnp.float32) + b_other) * 0.5)
    put(proj, 1, part, jnp.dot(own[...], ws_x[...], preferred_element_type=jnp.float32) * 0.5)
    for i, ref, base in ((6, sib, rows + 1), (7, rim, 2 * rows + 1)):
        copies[i].wait()
        put(proj, base, 0, jnp.dot(ref[...], ws[...], preferred_element_type=jnp.float32) * 0.5)
        put(proj, base, part, jnp.dot(ref[...], ws_x[...], preferred_element_type=jnp.float32) * 0.5)
    low = lax.broadcasted_iota(jnp.int32, (8, LANES), 0) < chunks

    def nodes(q, carry):
        spot = pl.ds(pl.multiple_of(8 * q, 8), 8)
        mine = near[spot, :]
        total = None
        for j in range(slots):
            upper = proj[pl.ds(pl.multiple_of(idx_ref[j * rows + 2 * q], 4), 8), :]
            lower = proj[pl.ds(pl.multiple_of(idx_ref[j * rows + 2 * q + 1], 4), 8), :]
            y = jnp.where(low, upper, lower) + mine
            act = y * jnp.tanh(y) + y
            total = act if total is None else total + act
        summed[spot, :] = total
        return carry

    lax.fori_loop(0, rows // 2, nodes, 0, unroll=8)
    copies[8].wait()
    update = None
    for c in range(chunks):
        values = summed[pl.ds(c, rows, stride=chunks), :].astype(jnp.bfloat16)
        if c < part:
            w_rows = w2[c * LANES:(c + 1) * LANES, :]
        else:
            w_rows = w2_x[(c - part) * LANES:(c - part + 1) * LANES, :]
        term = jnp.dot(values, w_rows, preferred_element_type=jnp.float32)
        update = term if update is None else update + term
    result = (own[...].astype(jnp.float32) + update).astype(jnp.bfloat16)
    if not last:
        outs[0][...] = result
    else:
        @pl.when(core == 0)
        def _():
            outs[0][...] = result[:, :share]
            outs[1][...] = result[:, share:]

        @pl.when(core != 0)
        def _():
            outs[0][...] = result[:, share:]
            outs[1][...] = result[:, :share]


def run_layer(layer, slots, last, core, idx, own, sib, rim, ws, wd, w2, bias, near_w, far_w, spot):
    rows, width = own.shape
    share = width // 2
    pack = 3 * share + 16
    chunks = width // LANES
    anywhere = pl.BlockSpec(memory_space=pl.ANY)
    smem = pl.BlockSpec(memory_space=pltpu.SMEM)
    vmem = pl.BlockSpec(memory_space=pltpu.VMEM)
    bf16, f32 = jnp.bfloat16, jnp.float32
    if last:
        out_shape = (jax.ShapeDtypeStruct((rows, share), bf16),) * 2
        out_specs = (vmem, vmem)
    else:
        out_shape, out_specs = jax.ShapeDtypeStruct((rows, width), bf16), vmem
    edges = rows * slots
    return pl.pallas_call(
        functools.partial(layer_kernel, layer, slots, last, spot * pack),
        out_shape=out_shape,
        in_specs=[smem, smem] + [anywhere] * 3 + [pl.BlockSpec(memory_space=pltpu.HBM)] * 3 + [anywhere] * 3,
        out_specs=out_specs,
        scratch_shapes=[
            pltpu.VMEM((rows, width), bf16),
            pltpu.VMEM((rows, width), bf16),
            pltpu.VMEM((rows, width), bf16),
            pltpu.VMEM((width, share), bf16),
            pltpu.VMEM((width, share), bf16),
            pltpu.VMEM((share, width), bf16),
            pltpu.VMEM(bias.shape, bf16),
            pltpu.VMEM((pack, share), bf16),
            pltpu.VMEM((pack, share), bf16),
            pltpu.VMEM((width, share), bf16),
            pltpu.VMEM((width, share), bf16),
            pltpu.VMEM((share, width), bf16),
            pltpu.VMEM((3 * rows * chunks + 96, LANES), f32),
            pltpu.VMEM((rows * chunks, LANES), f32),
            pltpu.VMEM((rows * chunks, LANES), f32),
            pltpu.SemaphoreType.DMA((9,)),
        ],
        compiler_params=pltpu.CompilerParams(vmem_limit_bytes=32 << 20),
        cost_estimate=pl.CostEstimate(flops=64 * rows * width * width, bytes_accessed=10 * rows * width, transcendentals=0),
        name="graph_layer",
    )(core, idx, own, sib, rim, ws, wd, w2, bias, near_w, far_w)


def edge_offsets(nbrs, counts, core):
    graphs, rows, slots = nbrs.shape
    half = rows // 2
    nbr = lax.dynamic_slice(nbrs.transpose(0, 2, 1), (0, 0, core * half), (graphs, slots, half)) - core * half
    count = lax.dynamic_slice(counts, (0, core * half), (graphs, half))
    low = nbr + jnp.where(core == 0, 2 * half, half)
    high = nbr - jnp.where(core == 0, half, 0)
    place = jnp.where(nbr < half, low, jnp.where(nbr < 2 * half, nbr - half, high))
    live = jnp.arange(slots, dtype=jnp.int32)[None, :, None] < count[:, None, :]
    place = jnp.where(live, place, 3 * half)
    odd = jnp.arange(half, dtype=jnp.int32) % 2
    return (4 * (place + 1 - odd)).reshape(graphs, slots * half)


def spread_rows(same, other):
    a = lax.ppermute(same, ("mp", "batch"), [(0, 0), (1, 2), (2, 1), (3, 3)])
    b = lax.ppermute(other, ("mp", "batch"), [(0, 1), (1, 3), (2, 0), (3, 2)])
    return a, b


def gather_rows(a, b):
    same = lax.ppermute(a, ("mp", "batch"), [(0, 0), (1, 2), (2, 1), (3, 3)])
    other = lax.ppermute(b, ("mp", "batch"), [(0, 2), (1, 0), (2, 3), (3, 1)])
    return same, other


def ordered(which, a, b, axis):
    return jnp.where(which == 0, jnp.concatenate([a, b], axis), jnp.concatenate([b, a], axis))


def swap(values, axis):
    return lax.ppermute(values, axis, [(0, 1), (1, 0)])


def rims(own, wrap):
    size = lax.axis_size("mesh")
    pairs = []
    for m in range(size):
        if wrap or m + 1 < size:
            pairs.append((2 * m + 1, 2 * ((m + 1) % size)))
        if wrap or m > 0:
            pairs.append((2 * m, 2 * ((m - 1) % size) + 1))
    return lax.ppermute(own, ("mesh", "batch"), pairs)


def pack_kernel(plan, core_ref, g_bias, r_bias, *refs):
    weights, refs = (refs[:3], refs[3:6]), refs[6:]
    outs, (lines, sems) = refs[:-2], refs[-2:]
    share = g_bias.shape[1]
    here = pl.multiple_of(core_ref[0] * share, share)
    count = 0
    copies = []
    for out, members in zip(outs, plan):
        for place, (graph, layer) in enumerate(members):
            base = place * (3 * share + 16)
            ws, wd, w2 = weights[graph]
            bias = (g_bias, r_bias)[graph][layer:layer + 1, :]
            lines[16 * count:16 * count + 16, :] = jnp.broadcast_to(bias, (16, share))
            sources = (
                (ws.at[layer, pl.ds(here, share), :], share),
                (wd.at[layer, pl.ds(here, share), :], share),
                (w2.at[layer, :, pl.ds(here, share)], share),
                (lines.at[16 * count:16 * count + 16, :], 16),
            )
            for i, (source, size) in enumerate(sources):
                copies.append(pltpu.make_async_copy(source, out.at[base:base + size, :], sems.at[4 * count + i]))
                copies[-1].start()
                base += size
            count += 1
    for copy in copies:
        copy.wait()


def pack_weights(plan, core, g_weights, g_bias, r_weights, r_bias):
    share = g_bias.shape[1]
    sizes = [len(members) for members in plan]
    hbm = pl.BlockSpec(memory_space=pltpu.HBM)
    vmem = pl.BlockSpec(memory_space=pltpu.VMEM)
    return pl.pallas_call(
        functools.partial(pack_kernel, plan),
        out_shape=tuple(jax.ShapeDtypeStruct((n * (3 * share + 16), share), jnp.bfloat16) for n in sizes),
        in_specs=[pl.BlockSpec(memory_space=pltpu.SMEM), vmem, vmem] + [hbm] * 6,
        out_specs=(hbm,) * len(plan),
        scratch_shapes=[pltpu.VMEM((16 * sum(sizes), share), jnp.bfloat16), pltpu.SemaphoreType.DMA((4 * sum(sizes),))],
        cost_estimate=SMALL,
        name="pack_weights",
    )(core, g_bias, r_bias, *g_weights, *r_weights)


def by_rows(
    g_nodes, r_nodes, g_nbr, g_count, r_nbr, r_count, bnd_src, bnd_part, bnd_node,
    g_ws, g_wd, g_b1, g_w2, r_ws, r_wd, r_b1, r_w2,
):
    part = lax.axis_index("mp")
    core = lax.axis_index("batch")
    parts = lax.axis_size("mesh")
    slots = g_nbr.shape[1]
    layers = g_ws.shape[0]
    rows = g_nodes.shape[1]
    half = rows // 2
    cap = 2 * bnd_src.shape[0] // parts
    me = lax.axis_index("mesh").reshape(1)
    core1 = core.reshape(1)
    g_own, r_own = g_nodes[0], r_nodes[0]
    g_weights, r_weights = (g_ws, g_wd, g_w2), (r_ws, r_wd, r_w2)
    after = lax.optimization_barrier

    same = lax.dynamic_slice(g_own, (part * half, 0), (half, g_own.shape[1]))
    other = lax.dynamic_slice(g_own, ((1 - part) * half, 0), (half, g_own.shape[1]))
    same, other, bnd_src = after((same, other, bnd_src))
    g_a, g_b = spread_rows(same, other)
    bnd = jnp.stack([bnd_src, bnd_part[:, 0], bnd_node])
    pieces = pick_rows(me, bnd, g_own, parts, cap)
    landed = [pieces[0]]
    for k in range(1, parts):
        landed.append(lax.ppermute(pieces[k], "mesh", [(i, (i + k) % parts) for i in range(parts)]))
    idx = edge_offsets(jnp.stack([g_nbr, r_nbr]), jnp.stack([g_count, r_count]), core)

    rest = tuple((graph, layer) for layer in range(1, layers) for graph in (0, 1))
    plan = (((0, 0),), ((1, 0),)) + ((rest,) if rest else ())
    g_a, g_b, g_idx, r_idx, core1, landed[0] = after((g_a, g_b, idx[0], idx[1], core1, landed[0]))
    packs = pack_weights(plan, core1, g_weights, g_b1, r_weights, r_b1)
    planet = ordered(core, g_a, g_b, 1)
    near_w = [swap(packs[0], "mp")]
    g_sib, g_rim = swap(planet, "batch"), rims(planet, True)
    g_sib, r_own = after((g_sib, r_own))
    r_a, r_b = spread_rows(*add_force(part.reshape(1), r_own, landed, cap))
    r_a, r_b, sent, g_rim = after((r_a, r_b, packs[1], g_rim))
    near_w.append(swap(sent, "mp"))
    regional = ordered(core, r_a, r_b, 1)
    r_sib, r_rim = swap(regional, "batch"), rims(regional, False)
    far_w = [swap(near_w[0], "batch")]
    for layer in range(layers):
        last = layer == layers - 1
        if layer:
            g_sib, g_rim = swap(planet, "batch"), rims(planet, True)
        spot = (0, 0) if layer == 0 else (2, 2 * layer - 2)
        planet = run_layer(
            layer, slots, last, core1, g_idx, planet, g_sib, g_rim,
            g_ws, g_wd, g_w2, g_b1, near_w[spot[0]], far_w[spot[0]], spot[1],
        )
        *planet, core1 = after((*(planet if last else (planet,)), core1))
        planet = planet if last else planet[0]
        if layer == 0:
            planet, near_w[1] = after((planet, near_w[1])) if rest else (planet, near_w[1])
            far_w.append(swap(near_w[1], "batch"))
            if rest:
                sent, near_w[1] = after((packs[2], near_w[1]))
                near_w.append(swap(sent, "mp"))
        else:
            r_sib, r_rim = swap(regional, "batch"), rims(regional, False)
        spot = (1, 0) if layer == 0 else (2, 2 * layer - 1)
        regional = run_layer(
            layer, slots, last, core1, r_idx, regional, r_sib, r_rim,
            r_ws, r_wd, r_w2, r_b1, near_w[spot[0]], far_w[spot[0]], spot[1],
        )
        if not last:
            regional, core1 = after((regional, core1))
            if layer == 0:
                regional, near_w[2] = after((regional, near_w[2]))
                far_w.append(swap(near_w[2], "batch"))
    g_out = ordered(part, *gather_rows(*planet), 0)
    r_out = ordered(part, *gather_rows(*regional), 0)
    return g_out[None], r_out[None]


def solution(mesh):
    in_specs = (
        P(("groups", "batch"), "mesh", "mp"),
        P(("groups", "batch"), "mesh", "mp"),
        P("mesh", None),
        P("mesh"),
        P("mesh", None),
        P("mesh"),
        P("mesh"),
        P("mesh", None),
        P("mesh"),
        P(None, None, "mp"),
        P(None, None, "mp"),
        P(None, "mp"),
        P(None, "mp", None),
        P(None, None, "mp"),
        P(None, None, "mp"),
        P(None, "mp"),
        P(None, "mp", None),
    )
    out_specs = (P(("groups", "batch"), "mesh", "mp"), P(("groups", "batch"), "mesh", "mp"))
    square = mesh.shape["mp"] == 2 and mesh.shape["batch"] == 2
    return jax.shard_map(
        by_rows if square else by_features, mesh=mesh, in_specs=in_specs, out_specs=out_specs, check_vma=False
    )
```

```python
import functools

import jax
import jax.numpy as jnp
from jax import lax
from jax.experimental import pallas as pl
from jax.experimental.pallas import tpu as pltpu
from jax.sharding import PartitionSpec as P

LANES = 128
DEAD = -1e30
SMALL = pl.CostEstimate(flops=1, bytes_accessed=1, transcendentals=0)


def padded_2(shard, sides, width, wrap):
    for axis, dim in sides:
        size, length = (lax.axis_size(axis), shard.shape[dim])
        up = [(i, (i + 1) % size) for i in range(size if wrap else size - 1)]
        down = [(j, i) for i, j in up]
        last = lax.slice_in_dim(shard, length - width, length, axis=dim)
        leading = lax.slice_in_dim(shard, 0, width, axis=dim)
        before = lax.ppermute(last, axis, up)
        after = lax.ppermute(leading, axis, down)
        shard = jnp.concatenate([before, shard, after], axis=dim)
    return shard


def edge_sums(proj, near, nbr, count):
    slots = nbr.shape[1]
    live = jnp.arange(slots, dtype=jnp.int32)[None, :] < count[:, None]
    pre = proj[:, nbr].astype(jnp.float32) + near[:, :, None]
    acts = jnp.where(live[None, :, :, None], jax.nn.silu(pre), 0.0)
    return jnp.sum(acts, axis=2).astype(jnp.bfloat16)


def graph_layer(latent, nbr, count, w_send, w_recv, bias, w_out, wrap):
    rim = latent.shape[1] // 2
    own_full = lax.all_gather(latent, "mp", axis=2, tiled=True)
    padded_full = padded_2(own_full, (("mesh", 1),), rim, wrap)
    proj = jnp.dot(padded_full, w_send, preferred_element_type=jnp.float32).astype(jnp.bfloat16)
    near = jnp.dot(own_full, w_recv, preferred_element_type=jnp.float32) + bias.astype(jnp.float32)
    summed = edge_sums(proj, near, nbr, count)
    partial_prod = jnp.dot(summed, w_out, preferred_element_type=jnp.float32)
    update = lax.psum_scatter(
        partial_prod.astype(jnp.bfloat16), "mp", scatter_dimension=2, tiled=True
    ).astype(jnp.float32)
    return (latent.astype(jnp.float32) + update).astype(jnp.bfloat16)


def by_features(
    g_nodes, r_nodes, g_nbr, g_count, r_nbr, r_count, bnd_src, bnd_part, bnd_node,
    g_ws, g_wd, g_b1, g_w2, r_ws, r_wd, r_b1, r_w2,
):
    batch_rows, reg_rows, feats = r_nodes.shape
    dest = bnd_part[:, 0]
    outgoing = jnp.moveaxis(g_nodes[:, bnd_src], 1, 0)
    init = jnp.zeros((reg_rows + 1, batch_rows, feats), jnp.float32)
    target = dest * reg_rows + bnd_node
    mine = lax.axis_index("mesh")
    piece_rows = lax.all_gather(outgoing, "mesh", axis=0, tiled=True)
    piece_target = lax.all_gather(target, "mesh", axis=0, tiled=True)
    local = jnp.where(piece_target // reg_rows == mine, piece_target % reg_rows + 1, 0)
    landed = init.at[local].add(piece_rows.astype(jnp.float32))
    force = jnp.moveaxis(landed[1:], 1, 0)
    regional = (r_nodes.astype(jnp.float32) + force).astype(jnp.bfloat16)
    planet = g_nodes
    for layer in range(g_ws.shape[0]):
        planet = graph_layer(
            planet, g_nbr, g_count, g_ws[layer], g_wd[layer], g_b1[layer], g_w2[layer], True
        )
    for layer in range(r_ws.shape[0]):
        regional = graph_layer(
            regional, r_nbr, r_count, r_ws[layer], r_wd[layer], r_b1[layer], r_w2[layer], False
        )
    return (planet, regional)


def one_hot(flags):
    return jnp.where(flags, 1.0, 0.0).astype(jnp.bfloat16)


def pick_kernel(parts, cap, me_ref, bnd_ref, g_ref, *out_refs):
    rows = g_ref.shape[0]
    total = bnd_ref.shape[1]
    me = me_ref[0]
    src, part, node = (bnd_ref[i:i + 1, :] for i in range(3))
    lines = -(-parts // 8) * 8
    target = lax.rem(lax.broadcasted_iota(jnp.int32, (lines, total), 0) + me, parts)
    named = part == target
    before = one_hot(
        lax.broadcasted_iota(jnp.int32, (total, total), 0) < lax.broadcasted_iota(jnp.int32, (total, total), 1)
    )
    rank = jnp.dot(one_hot(named), before, preferred_element_type=jnp.float32)
    rank = jnp.where(named, rank, -1.0)
    source = one_hot(lax.broadcasted_iota(jnp.int32, (rows, total), 0) == src)
    line = lax.broadcasted_iota(jnp.int32, (16, total), 0)
    high = lax.shift_right_logical(node, 7)
    facts = jnp.where(line == 0, high, jnp.where(line == 1, node - high * 128, jnp.where(line == 2, 1, 0)))
    facts = facts.astype(jnp.float32).astype(jnp.bfloat16)
    place = lax.broadcasted_iota(jnp.int32, (cap, total), 0).astype(jnp.float32)
    across = (((1,), (1,)), ((), ()))
    for k in range(parts):
        chosen = one_hot(place == rank[k:k + 1, :])
        pick = lax.dot_general(chosen, source, across, preferred_element_type=jnp.float32).astype(jnp.bfloat16)
        out_refs[k][:cap, :] = jnp.dot(pick, g_ref[...], preferred_element_type=jnp.float32).astype(jnp.bfloat16)
        told = lax.dot_general(facts, chosen, across, preferred_element_type=jnp.float32)
        out_refs[k][cap:, :] = told.astype(jnp.bfloat16)


def pick_rows(me, bnd, nodes, parts, cap):
    vmem = pl.BlockSpec(memory_space=pltpu.VMEM)
    rows, feats = nodes.shape
    total = bnd.shape[1]
    piece = jax.ShapeDtypeStruct((cap + 16, feats), jnp.bfloat16)
    return pl.pallas_call(
        functools.partial(pick_kernel, parts, cap),
        out_shape=(piece,) * parts,
        in_specs=[pl.BlockSpec(memory_space=pltpu.SMEM), vmem, vmem],
        out_specs=(vmem,) * parts,
        compiler_params=pltpu.CompilerParams(vmem_limit_bytes=32 << 20),
        cost_estimate=SMALL,
        name="pick_rows",
    )(me, bnd, nodes)


def force_kernel(cap, first_ref, r_ref, *refs):
    pieces, (same_ref, other_ref) = refs[:-2], refs[-2:]
    half = same_ref.shape[0]
    first = first_ref[0]
    for out_ref, start in ((same_ref, first * half), (other_ref, (1 - first) * half)):
        start = pl.multiple_of(start, 16)
        row = (lax.broadcasted_iota(jnp.int32, (half, cap), 0) + start).astype(jnp.float32)
        total = r_ref[pl.ds(start, half), :].astype(jnp.float32)
        for piece in pieces:
            facts = piece[cap:, :].astype(jnp.float32)
            node = jnp.where(facts[2:3, :] > 0.5, facts[0:1, :] * 128.0 + facts[1:2, :], -1.0)
            total += jnp.dot(one_hot(row == node), piece[:cap, :], preferred_element_type=jnp.float32)
        out_ref[...] = total.astype(jnp.bfloat16)


def add_force(first, nodes, pieces, cap):
    vmem = pl.BlockSpec(memory_space=pltpu.VMEM)
    rows, feats = nodes.shape
    block = jax.ShapeDtypeStruct((rows // 2, feats), jnp.bfloat16)
    return pl.pallas_call(
        functools.partial(force_kernel, cap),
        out_shape=(block, block),
        in_specs=[pl.BlockSpec(memory_space=pltpu.SMEM)] + [vmem] * (1 + len(pieces)),
        out_specs=(vmem, vmem),
        compiler_params=pltpu.CompilerParams(vmem_limit_bytes=32 << 20),
        cost_estimate=SMALL,
        name="add_force",
    )(first, nodes, *pieces)


def layer_kernel(
    layer, slots, last, core_ref, idx_ref, own_hbm, sib_hbm, rim_hbm, ws_hbm, wd_hbm, w2_hbm, b_hbm, near_hbm, far_hbm,
    *refs,
):
    outs, refs = (refs[:2], refs[2:]) if last else (refs[:1], refs[1:])
    own, sib, rim, ws, wd, w2, bias, near_w, far_w, ws_x, wd_x, w2_x, proj, near, summed, sems = refs
    rows, width = own.shape
    share = width // 2
    chunks = width // LANES
    core = core_ref[0]
    pairs = (
        (own_hbm, own), (wd_hbm.at[layer], wd), (ws_hbm.at[layer], ws), (b_hbm, bias),
        (near_hbm, near_w), (far_hbm, far_w), (sib_hbm, sib), (rim_hbm, rim), (w2_hbm.at[layer], w2),
    )
    copies = [pltpu.make_async_copy(src, dst, sems.at[i]) for i, (src, dst) in enumerate(pairs)]
    for copy in copies:
        copy.start()
    window = 3 * rows
    proj[0:8, :] = jnp.full((8, LANES), DEAD, jnp.float32)
    proj[4 * window + 4:4 * window + 16, :] = jnp.full((12, LANES), DEAD, jnp.float32)

    def put(dst, base, first, values):
        for c in range(values.shape[1] // LANES):
            dst[pl.ds(base * chunks + first + c, rows, stride=chunks), :] = values[:, c * LANES:(c + 1) * LANES]

    for i in (0, 1, 2, 3):
        copies[i].wait()
    part = share // LANES
    b_own = bias[layer:layer + 1, :].astype(jnp.float32)
    put(near, 0, 0, (jnp.dot(own[...], wd[...], preferred_element_type=jnp.float32) + b_own) * 0.5)
    put(proj, 1, 0, jnp.dot(own[...], ws[...], preferred_element_type=jnp.float32) * 0.5)
    for i in (4, 5):
        copies[i].wait()
    here, there = pl.multiple_of(core * share, 16), pl.multiple_of((1 - core) * share, 16)
    for spot, piece in ((here, near_w), (there, far_w)):
        ws_x[pl.ds(spot, share), :] = piece[0:share, :]
        wd_x[pl.ds(spot, share), :] = piece[share:2 * share, :]

    @pl.when(core == 0)
    def _():
        w2_x[:, :share] = near_w[2 * share:3 * share, :]
        w2_x[:, share:] = far_w[2 * share:3 * share, :]

    @pl.when(core != 0)
    def _():
        w2_x[:, share:] = near_w[2 * share:3 * share, :]
        w2_x[:, :share] = far_w[2 * share:3 * share, :]

    b_other = near_w[3 * share:3 * share + 1, :].astype(jnp.float32)
    put(near, 0, part, (jnp.dot(own[...], wd_x[...], preferred_element_type=jnp.float32) + b_other) * 0.5)
    put(proj, 1, part, jnp.dot(own[...], ws_x[...], preferred_element_type=jnp.float32) * 0.5)
    for i, ref, base in ((6, sib, rows + 1), (7, rim, 2 * rows + 1)):
        copies[i].wait()
        put(proj, base, 0, jnp.dot(ref[...], ws[...], preferred_element_type=jnp.float32) * 0.5)
        put(proj, base, part, jnp.dot(ref[...], ws_x[...], preferred_element_type=jnp.float32) * 0.5)
    low = lax.broadcasted_iota(jnp.int32, (8, LANES), 0) < chunks

    def nodes(q, carry):
        spot = pl.ds(pl.multiple_of(8 * q, 8), 8)
        mine = near[spot, :]
        total = None
        for j in range(slots):
            upper = proj[pl.ds(pl.multiple_of(idx_ref[j * rows + 2 * q], 4), 8), :]
            lower = proj[pl.ds(pl.multiple_of(idx_ref[j * rows + 2 * q + 1], 4), 8), :]
            y = jnp.where(low, upper, lower) + mine
            act = y * jnp.tanh(y) + y
            total = act if total is None else total + act
        summed[spot, :] = total
        return carry

    lax.fori_loop(0, rows // 2, nodes, 0, unroll=8)
    copies[8].wait()
    update = None
    for c in range(chunks):
        values = summed[pl.ds(c, rows, stride=chunks), :].astype(jnp.bfloat16)
        if c < part:
            w_rows = w2[c * LANES:(c + 1) * LANES, :]
        else:
            w_rows = w2_x[(c - part) * LANES:(c - part + 1) * LANES, :]
        term = jnp.dot(values, w_rows, preferred_element_type=jnp.float32)
        update = term if update is None else update + term
    result = (own[...].astype(jnp.float32) + update).astype(jnp.bfloat16)
    if not last:
        outs[0][...] = result
    else:
        @pl.when(core == 0)
        def _():
            outs[0][...] = result[:, :share]
            outs[1][...] = result[:, share:]

        @pl.when(core != 0)
        def _():
            outs[0][...] = result[:, share:]
            outs[1][...] = result[:, :share]


def run_layer(layer, slots, last, core, idx, own, sib, rim, ws, wd, w2, bias, near_w, far_w):
    rows, width = own.shape
    share = width // 2
    chunks = width // LANES
    anywhere = pl.BlockSpec(memory_space=pl.ANY)
    smem = pl.BlockSpec(memory_space=pltpu.SMEM)
    vmem = pl.BlockSpec(memory_space=pltpu.VMEM)
    bf16, f32 = jnp.bfloat16, jnp.float32
    if last:
        out_shape = (jax.ShapeDtypeStruct((rows, share), bf16),) * 2
        out_specs = (vmem, vmem)
    else:
        out_shape, out_specs = jax.ShapeDtypeStruct((rows, width), bf16), vmem
    edges = rows * slots
    return pl.pallas_call(
        functools.partial(layer_kernel, layer, slots, last),
        out_shape=out_shape,
        in_specs=[smem, smem] + [anywhere] * 3 + [pl.BlockSpec(memory_space=pltpu.HBM)] * 3 + [anywhere] * 3,
        out_specs=out_specs,
        scratch_shapes=[
            pltpu.VMEM((rows, width), bf16),
            pltpu.VMEM((rows, width), bf16),
            pltpu.VMEM((rows, width), bf16),
            pltpu.VMEM((width, share), bf16),
            pltpu.VMEM((width, share), bf16),
            pltpu.VMEM((share, width), bf16),
            pltpu.VMEM(bias.shape, bf16),
            pltpu.VMEM(near_w.shape, bf16),
            pltpu.VMEM(far_w.shape, bf16),
            pltpu.VMEM((width, share), bf16),
            pltpu.VMEM((width, share), bf16),
            pltpu.VMEM((share, width), bf16),
            pltpu.VMEM((3 * rows * chunks + 96, LANES), f32),
            pltpu.VMEM((rows * chunks, LANES), f32),
            pltpu.VMEM((rows * chunks, LANES), f32),
            pltpu.SemaphoreType.DMA((9,)),
        ],
        compiler_params=pltpu.CompilerParams(vmem_limit_bytes=32 << 20),
        cost_estimate=pl.CostEstimate(flops=64 * rows * width * width, bytes_accessed=10 * rows * width, transcendentals=0),
        name="graph_layer",
    )(core, idx, own, sib, rim, ws, wd, w2, bias, near_w, far_w)


def edge_offsets(nbrs, counts, core):
    graphs, rows, slots = nbrs.shape
    half = rows // 2
    nbr = lax.dynamic_slice(nbrs.transpose(0, 2, 1), (0, 0, core * half), (graphs, slots, half)) - core * half
    count = lax.dynamic_slice(counts, (0, core * half), (graphs, half))
    low = nbr + jnp.where(core == 0, 2 * half, half)
    high = nbr - jnp.where(core == 0, half, 0)
    place = jnp.where(nbr < half, low, jnp.where(nbr < 2 * half, nbr - half, high))
    live = jnp.arange(slots, dtype=jnp.int32)[None, :, None] < count[:, None, :]
    place = jnp.where(live, place, 3 * half)
    odd = jnp.arange(half, dtype=jnp.int32) % 2
    return (4 * (place + 1 - odd)).reshape(graphs, slots * half)


def spread_rows(same, other):
    a = lax.ppermute(same, ("mp", "batch"), [(0, 0), (1, 2), (2, 1), (3, 3)])
    b = lax.ppermute(other, ("mp", "batch"), [(0, 1), (1, 3), (2, 0), (3, 2)])
    return a, b


def gather_rows(a, b):
    same = lax.ppermute(a, ("mp", "batch"), [(0, 0), (1, 2), (2, 1), (3, 3)])
    other = lax.ppermute(b, ("mp", "batch"), [(0, 2), (1, 0), (2, 3), (3, 1)])
    return same, other


def ordered(which, a, b, axis):
    return jnp.where(which == 0, jnp.concatenate([a, b], axis), jnp.concatenate([b, a], axis))


def swap(values, axis):
    return lax.ppermute(values, axis, [(0, 1), (1, 0)])


def rims(own, wrap):
    size = lax.axis_size("mesh")
    pairs = []
    for m in range(size):
        if wrap or m + 1 < size:
            pairs.append((2 * m + 1, 2 * ((m + 1) % size)))
        if wrap or m > 0:
            pairs.append((2 * m, 2 * ((m - 1) % size) + 1))
    return lax.ppermute(own, ("mesh", "batch"), pairs)


def pack_kernel(order, core_ref, g_bias, r_bias, *refs):
    weights, outs = (refs[:3], refs[3:6]), refs[6:]
    share = g_bias.shape[1]
    here = pl.multiple_of(core_ref[0] * share, share)
    for (graph, layer), out in zip(order, outs):
        ws, wd, w2 = weights[graph]
        bias = (g_bias, r_bias)[graph][layer:layer + 1, :]
        out[0:share, :] = ws[layer, pl.ds(here, share), :]
        out[share:2 * share, :] = wd[layer, pl.ds(here, share), :]
        out[2 * share:3 * share, :] = w2[layer, :, pl.ds(here, share)]
        out[3 * share:, :] = jnp.broadcast_to(bias, (16, share))


def pack_weights(order, core, g_weights, g_bias, r_weights, r_bias):
    share = g_bias.shape[1]
    vmem = pl.BlockSpec(memory_space=pltpu.VMEM)
    return pl.pallas_call(
        functools.partial(pack_kernel, order),
        out_shape=(jax.ShapeDtypeStruct((3 * share + 16, share), jnp.bfloat16),) * len(order),
        in_specs=[pl.BlockSpec(memory_space=pltpu.SMEM)] + [vmem] * 8,
        out_specs=(vmem,) * len(order),
        compiler_params=pltpu.CompilerParams(vmem_limit_bytes=32 << 20),
        cost_estimate=SMALL,
        name="pack_weights",
    )(core, g_bias, r_bias, *g_weights, *r_weights)


def by_rows(
    g_nodes, r_nodes, g_nbr, g_count, r_nbr, r_count, bnd_src, bnd_part, bnd_node,
    g_ws, g_wd, g_b1, g_w2, r_ws, r_wd, r_b1, r_w2,
):
    part = lax.axis_index("mp")
    core = lax.axis_index("batch")
    parts = lax.axis_size("mesh")
    slots = g_nbr.shape[1]
    layers = g_ws.shape[0]
    rows = g_nodes.shape[1]
    half = rows // 2
    cap = 2 * bnd_src.shape[0] // parts
    me = lax.axis_index("mesh").reshape(1)
    core1 = core.reshape(1)
    g_own, r_own = g_nodes[0], r_nodes[0]
    g_weights, r_weights = (g_ws, g_wd, g_w2), (r_ws, r_wd, r_w2)
    after = lax.optimization_barrier

    same = lax.dynamic_slice(g_own, (part * half, 0), (half, g_own.shape[1]))
    other = lax.dynamic_slice(g_own, ((1 - part) * half, 0), (half, g_own.shape[1]))
    same, other, bnd_src = after((same, other, bnd_src))
    g_a, g_b = spread_rows(same, other)
    bnd = jnp.stack([bnd_src, bnd_part[:, 0], bnd_node])
    pieces = pick_rows(me, bnd, g_own, parts, cap)
    landed = [pieces[0]]
    for k in range(1, parts):
        landed.append(lax.ppermute(pieces[k], "mesh", [(i, (i + k) % parts) for i in range(parts)]))
    idx = edge_offsets(jnp.stack([g_nbr, r_nbr]), jnp.stack([g_count, r_count]), core)

    order = [(graph, layer) for layer in range(layers) for graph in (0, 1)]
    packs = pack_weights(order, core1, g_weights, g_b1, r_weights, r_b1)
    g_a, g_b, g_idx, r_idx, core1, landed[0], sent = after((g_a, g_b, idx[0], idx[1], core1, landed[0], packs[0]))
    near_w = [swap(sent, "mp")]
    planet = ordered(core, g_a, g_b, 1)
    g_sib, g_rim = swap(planet, "batch"), rims(planet, True)
    g_sib, r_own = after((g_sib, r_own))
    r_pair = add_force(part.reshape(1), r_own, landed, cap)
    *r_pair, g_idx, near_w[0] = after((*r_pair, g_idx, near_w[0]))
    r_a, r_b = spread_rows(*r_pair)
    regional, g_idx = after((ordered(core, r_a, r_b, 1), g_idx))
    r_sib, r_rim = swap(regional, "batch"), rims(regional, False)
    far_w = []
    for layer in range(layers):
        last = layer == layers - 1
        for graph in (0, 1):
            i = 2 * layer + graph
            far_w.append(swap(near_w[i], "batch"))
            if i + 1 < len(order):
                sent, near_w[i] = after((packs[i + 1], near_w[i]))
                near_w.append(swap(sent, "mp"))
            if graph == 0:
                planet = run_layer(
                    layer, slots, last, core1, g_idx, planet, g_sib, g_rim,
                    g_ws, g_wd, g_w2, g_b1, near_w[i], far_w[i],
                )
                *planet, core1, near_w[i + 1] = after((*(planet if last else (planet,)), core1, near_w[i + 1]))
                if not last:
                    planet = planet[0]
                    g_sib, g_rim = swap(planet, "batch"), rims(planet, True)
                if layer:
                    r_sib, r_rim = swap(regional, "batch"), rims(regional, False)
            else:
                regional = run_layer(
                    layer, slots, last, core1, r_idx, regional, r_sib, r_rim,
                    r_ws, r_wd, r_w2, r_b1, near_w[i], far_w[i],
                )
                if not last:
                    regional, core1, near_w[i + 1] = after((regional, core1, near_w[i + 1]))
    g_out = ordered(part, *gather_rows(*planet), 0)
    r_out = ordered(part, *gather_rows(*regional), 0)
    return g_out[None], r_out[None]


def solution(mesh):
    in_specs = (
        P(("groups", "batch"), "mesh", "mp"),
        P(("groups", "batch"), "mesh", "mp"),
        P("mesh", None),
        P("mesh"),
        P("mesh", None),
        P("mesh"),
        P("mesh"),
        P("mesh", None),
        P("mesh"),
        P(None, None, "mp"),
        P(None, None, "mp"),
        P(None, "mp"),
        P(None, "mp", None),
        P(None, None, "mp"),
        P(None, None, "mp"),
        P(None, "mp"),
        P(None, "mp", None),
    )
    out_specs = (P(("groups", "batch"), "mesh", "mp"), P(("groups", "batch"), "mesh", "mp"))
    square = mesh.shape["mp"] == 2 and mesh.shape["batch"] == 2
    return jax.shard_map(
        by_rows if square else by_features, mesh=mesh, in_specs=in_specs, out_specs=out_specs, check_vma=False
    )
```

```python
import functools

import jax
import jax.numpy as jnp
from jax import lax
from jax.experimental import pallas as pl
from jax.experimental.pallas import tpu as pltpu
from jax.sharding import PartitionSpec as P

LANES = 128
DEAD = -1e30
SMALL = pl.CostEstimate(flops=1, bytes_accessed=1, transcendentals=0)


def padded_2(shard, sides, width, wrap):
    for axis, dim in sides:
        size, length = (lax.axis_size(axis), shard.shape[dim])
        up = [(i, (i + 1) % size) for i in range(size if wrap else size - 1)]
        down = [(j, i) for i, j in up]
        last = lax.slice_in_dim(shard, length - width, length, axis=dim)
        leading = lax.slice_in_dim(shard, 0, width, axis=dim)
        before = lax.ppermute(last, axis, up)
        after = lax.ppermute(leading, axis, down)
        shard = jnp.concatenate([before, shard, after], axis=dim)
    return shard


def edge_sums(proj, near, nbr, count):
    slots = nbr.shape[1]
    live = jnp.arange(slots, dtype=jnp.int32)[None, :] < count[:, None]
    pre = proj[:, nbr].astype(jnp.float32) + near[:, :, None]
    acts = jnp.where(live[None, :, :, None], jax.nn.silu(pre), 0.0)
    return jnp.sum(acts, axis=2).astype(jnp.bfloat16)


def graph_layer(latent, nbr, count, w_send, w_recv, bias, w_out, wrap):
    rim = latent.shape[1] // 2
    own_full = lax.all_gather(latent, "mp", axis=2, tiled=True)
    padded_full = padded_2(own_full, (("mesh", 1),), rim, wrap)
    proj = jnp.dot(padded_full, w_send, preferred_element_type=jnp.float32).astype(jnp.bfloat16)
    near = jnp.dot(own_full, w_recv, preferred_element_type=jnp.float32) + bias.astype(jnp.float32)
    summed = edge_sums(proj, near, nbr, count)
    partial_prod = jnp.dot(summed, w_out, preferred_element_type=jnp.float32)
    update = lax.psum_scatter(
        partial_prod.astype(jnp.bfloat16), "mp", scatter_dimension=2, tiled=True
    ).astype(jnp.float32)
    return (latent.astype(jnp.float32) + update).astype(jnp.bfloat16)


def by_features(
    g_nodes, r_nodes, g_nbr, g_count, r_nbr, r_count, bnd_src, bnd_part, bnd_node,
    g_ws, g_wd, g_b1, g_w2, r_ws, r_wd, r_b1, r_w2,
):
    batch_rows, reg_rows, feats = r_nodes.shape
    dest = bnd_part[:, 0]
    outgoing = jnp.moveaxis(g_nodes[:, bnd_src], 1, 0)
    init = jnp.zeros((reg_rows + 1, batch_rows, feats), jnp.float32)
    target = dest * reg_rows + bnd_node
    mine = lax.axis_index("mesh")
    piece_rows = lax.all_gather(outgoing, "mesh", axis=0, tiled=True)
    piece_target = lax.all_gather(target, "mesh", axis=0, tiled=True)
    local = jnp.where(piece_target // reg_rows == mine, piece_target % reg_rows + 1, 0)
    landed = init.at[local].add(piece_rows.astype(jnp.float32))
    force = jnp.moveaxis(landed[1:], 1, 0)
    regional = (r_nodes.astype(jnp.float32) + force).astype(jnp.bfloat16)
    planet = g_nodes
    for layer in range(g_ws.shape[0]):
        planet = graph_layer(
            planet, g_nbr, g_count, g_ws[layer], g_wd[layer], g_b1[layer], g_w2[layer], True
        )
    for layer in range(r_ws.shape[0]):
        regional = graph_layer(
            regional, r_nbr, r_count, r_ws[layer], r_wd[layer], r_b1[layer], r_w2[layer], False
        )
    return (planet, regional)


def one_hot(flags):
    return jnp.where(flags, 1.0, 0.0).astype(jnp.bfloat16)


def pick_kernel(parts, cap, me_ref, bnd_ref, g_ref, *out_refs):
    rows = g_ref.shape[0]
    total = bnd_ref.shape[1]
    me = me_ref[0]
    src, part, node = (bnd_ref[i:i + 1, :] for i in range(3))
    lines = -(-parts // 8) * 8
    target = lax.rem(lax.broadcasted_iota(jnp.int32, (lines, total), 0) + me, parts)
    named = part == target
    before = one_hot(
        lax.broadcasted_iota(jnp.int32, (total, total), 0) < lax.broadcasted_iota(jnp.int32, (total, total), 1)
    )
    rank = jnp.dot(one_hot(named), before, preferred_element_type=jnp.float32)
    rank = jnp.where(named, rank, -1.0)
    source = one_hot(lax.broadcasted_iota(jnp.int32, (rows, total), 0) == src)
    line = lax.broadcasted_iota(jnp.int32, (16, total), 0)
    high = lax.shift_right_logical(node, 7)
    facts = jnp.where(line == 0, high, jnp.where(line == 1, node - high * 128, jnp.where(line == 2, 1, 0)))
    facts = facts.astype(jnp.float32).astype(jnp.bfloat16)
    place = lax.broadcasted_iota(jnp.int32, (cap, total), 0).astype(jnp.float32)
    across = (((1,), (1,)), ((), ()))
    for k in range(parts):
        chosen = one_hot(place == rank[k:k + 1, :])
        pick = lax.dot_general(chosen, source, across, preferred_element_type=jnp.float32).astype(jnp.bfloat16)
        out_refs[k][:cap, :] = jnp.dot(pick, g_ref[...], preferred_element_type=jnp.float32).astype(jnp.bfloat16)
        told = lax.dot_general(facts, chosen, across, preferred_element_type=jnp.float32)
        out_refs[k][cap:, :] = told.astype(jnp.bfloat16)


def pick_rows(me, bnd, nodes, parts, cap):
    vmem = pl.BlockSpec(memory_space=pltpu.VMEM)
    rows, feats = nodes.shape
    total = bnd.shape[1]
    piece = jax.ShapeDtypeStruct((cap + 16, feats), jnp.bfloat16)
    return pl.pallas_call(
        functools.partial(pick_kernel, parts, cap),
        out_shape=(piece,) * parts,
        in_specs=[pl.BlockSpec(memory_space=pltpu.SMEM), vmem, vmem],
        out_specs=(vmem,) * parts,
        compiler_params=pltpu.CompilerParams(vmem_limit_bytes=32 << 20),
        cost_estimate=SMALL,
        name="pick_rows",
    )(me, bnd, nodes)


def force_kernel(cap, first_ref, r_ref, *refs):
    pieces, (same_ref, other_ref) = refs[:-2], refs[-2:]
    half = same_ref.shape[0]
    first = first_ref[0]
    for out_ref, start in ((same_ref, first * half), (other_ref, (1 - first) * half)):
        start = pl.multiple_of(start, 16)
        row = (lax.broadcasted_iota(jnp.int32, (half, cap), 0) + start).astype(jnp.float32)
        total = r_ref[pl.ds(start, half), :].astype(jnp.float32)
        for piece in pieces:
            facts = piece[cap:, :].astype(jnp.float32)
            node = jnp.where(facts[2:3, :] > 0.5, facts[0:1, :] * 128.0 + facts[1:2, :], -1.0)
            total += jnp.dot(one_hot(row == node), piece[:cap, :], preferred_element_type=jnp.float32)
        out_ref[...] = total.astype(jnp.bfloat16)


def add_force(first, nodes, pieces, cap):
    vmem = pl.BlockSpec(memory_space=pltpu.VMEM)
    rows, feats = nodes.shape
    block = jax.ShapeDtypeStruct((rows // 2, feats), jnp.bfloat16)
    return pl.pallas_call(
        functools.partial(force_kernel, cap),
        out_shape=(block, block),
        in_specs=[pl.BlockSpec(memory_space=pltpu.SMEM)] + [vmem] * (1 + len(pieces)),
        out_specs=(vmem, vmem),
        compiler_params=pltpu.CompilerParams(vmem_limit_bytes=32 << 20),
        cost_estimate=SMALL,
        name="add_force",
    )(first, nodes, *pieces)


def layer_kernel(
    layer, slots, last, core_ref, idx_ref, own_hbm, sib_hbm, rim_hbm, ws_hbm, wd_hbm, w2_hbm, b_hbm, near_hbm, far_hbm,
    *refs,
):
    outs, refs = (refs[:2], refs[2:]) if last else (refs[:1], refs[1:])
    own, sib, rim, ws, wd, w2, bias, near_w, far_w, ws_x, wd_x, w2_x, proj, near, summed, sems = refs
    rows, width = own.shape
    share = width // 2
    chunks = width // LANES
    core = core_ref[0]
    pairs = (
        (own_hbm, own), (wd_hbm.at[layer], wd), (ws_hbm.at[layer], ws), (b_hbm, bias),
        (near_hbm, near_w), (far_hbm, far_w), (sib_hbm, sib), (rim_hbm, rim), (w2_hbm.at[layer], w2),
    )
    copies = [pltpu.make_async_copy(src, dst, sems.at[i]) for i, (src, dst) in enumerate(pairs)]
    for copy in copies:
        copy.start()
    window = 3 * rows
    proj[0:8, :] = jnp.full((8, LANES), DEAD, jnp.float32)
    proj[4 * window + 4:4 * window + 16, :] = jnp.full((12, LANES), DEAD, jnp.float32)

    def put(dst, base, first, values):
        for c in range(values.shape[1] // LANES):
            dst[pl.ds(base * chunks + first + c, rows, stride=chunks), :] = values[:, c * LANES:(c + 1) * LANES]

    for i in (0, 1, 2, 3):
        copies[i].wait()
    part = share // LANES
    b_own = bias[layer:layer + 1, :].astype(jnp.float32)
    put(near, 0, 0, (jnp.dot(own[...], wd[...], preferred_element_type=jnp.float32) + b_own) * 0.5)
    put(proj, 1, 0, jnp.dot(own[...], ws[...], preferred_element_type=jnp.float32) * 0.5)
    for i in (4, 5):
        copies[i].wait()
    here, there = pl.multiple_of(core * share, 16), pl.multiple_of((1 - core) * share, 16)
    for spot, piece in ((here, near_w), (there, far_w)):
        ws_x[pl.ds(spot, share), :] = piece[0:share, :]
        wd_x[pl.ds(spot, share), :] = piece[share:2 * share, :]

    @pl.when(core == 0)
    def _():
        w2_x[:, :share] = near_w[2 * share:3 * share, :]
        w2_x[:, share:] = far_w[2 * share:3 * share, :]

    @pl.when(core != 0)
    def _():
        w2_x[:, share:] = near_w[2 * share:3 * share, :]
        w2_x[:, :share] = far_w[2 * share:3 * share, :]

    b_other = near_w[3 * share:3 * share + 1, :].astype(jnp.float32)
    put(near, 0, part, (jnp.dot(own[...], wd_x[...], preferred_element_type=jnp.float32) + b_other) * 0.5)
    put(proj, 1, part, jnp.dot(own[...], ws_x[...], preferred_element_type=jnp.float32) * 0.5)
    for i, ref, base in ((6, sib, rows + 1), (7, rim, 2 * rows + 1)):
        copies[i].wait()
        put(proj, base, 0, jnp.dot(ref[...], ws[...], preferred_element_type=jnp.float32) * 0.5)
        put(proj, base, part, jnp.dot(ref[...], ws_x[...], preferred_element_type=jnp.float32) * 0.5)
    low = lax.broadcasted_iota(jnp.int32, (8, LANES), 0) < chunks

    def nodes(q, carry):
        spot = pl.ds(pl.multiple_of(8 * q, 8), 8)
        mine = near[spot, :]
        total = None
        for j in range(slots):
            upper = proj[pl.ds(pl.multiple_of(idx_ref[j * rows + 2 * q], 4), 8), :]
            lower = proj[pl.ds(pl.multiple_of(idx_ref[j * rows + 2 * q + 1], 4), 8), :]
            y = jnp.where(low, upper, lower) + mine
            act = y * jnp.tanh(y) + y
            total = act if total is None else total + act
        summed[spot, :] = total
        return carry

    lax.fori_loop(0, rows // 2, nodes, 0, unroll=8)
    copies[8].wait()
    update = None
    for c in range(chunks):
        values = summed[pl.ds(c, rows, stride=chunks), :].astype(jnp.bfloat16)
        if c < part:
            w_rows = w2[c * LANES:(c + 1) * LANES, :]
        else:
            w_rows = w2_x[(c - part) * LANES:(c - part + 1) * LANES, :]
        term = jnp.dot(values, w_rows, preferred_element_type=jnp.float32)
        update = term if update is None else update + term
    result = (own[...].astype(jnp.float32) + update).astype(jnp.bfloat16)
    if not last:
        outs[0][...] = result
    else:
        @pl.when(core == 0)
        def _():
            outs[0][...] = result[:, :share]
            outs[1][...] = result[:, share:]

        @pl.when(core != 0)
        def _():
            outs[0][...] = result[:, share:]
            outs[1][...] = result[:, :share]


def run_layer(layer, slots, last, core, idx, own, sib, rim, ws, wd, w2, bias, near_w, far_w):
    rows, width = own.shape
    share = width // 2
    chunks = width // LANES
    anywhere = pl.BlockSpec(memory_space=pl.ANY)
    smem = pl.BlockSpec(memory_space=pltpu.SMEM)
    vmem = pl.BlockSpec(memory_space=pltpu.VMEM)
    bf16, f32 = jnp.bfloat16, jnp.float32
    if last:
        out_shape = (jax.ShapeDtypeStruct((rows, share), bf16),) * 2
        out_specs = (vmem, vmem)
    else:
        out_shape, out_specs = jax.ShapeDtypeStruct((rows, width), bf16), vmem
    edges = rows * slots
    return pl.pallas_call(
        functools.partial(layer_kernel, layer, slots, last),
        out_shape=out_shape,
        in_specs=[smem, smem] + [anywhere] * 3 + [pl.BlockSpec(memory_space=pltpu.HBM)] * 3 + [anywhere] * 3,
        out_specs=out_specs,
        scratch_shapes=[
            pltpu.VMEM((rows, width), bf16),
            pltpu.VMEM((rows, width), bf16),
            pltpu.VMEM((rows, width), bf16),
            pltpu.VMEM((width, share), bf16),
            pltpu.VMEM((width, share), bf16),
            pltpu.VMEM((share, width), bf16),
            pltpu.VMEM(bias.shape, bf16),
            pltpu.VMEM(near_w.shape, bf16),
            pltpu.VMEM(far_w.shape, bf16),
            pltpu.VMEM((width, share), bf16),
            pltpu.VMEM((width, share), bf16),
            pltpu.VMEM((share, width), bf16),
            pltpu.VMEM((3 * rows * chunks + 96, LANES), f32),
            pltpu.VMEM((rows * chunks, LANES), f32),
            pltpu.VMEM((rows * chunks, LANES), f32),
            pltpu.SemaphoreType.DMA((9,)),
        ],
        compiler_params=pltpu.CompilerParams(vmem_limit_bytes=32 << 20),
        cost_estimate=pl.CostEstimate(flops=64 * rows * width * width, bytes_accessed=10 * rows * width, transcendentals=0),
        name="graph_layer",
    )(core, idx, own, sib, rim, ws, wd, w2, bias, near_w, far_w)


def edge_offsets(nbrs, counts, core):
    graphs, rows, slots = nbrs.shape
    half = rows // 2
    nbr = lax.dynamic_slice(nbrs.transpose(0, 2, 1), (0, 0, core * half), (graphs, slots, half)) - core * half
    count = lax.dynamic_slice(counts, (0, core * half), (graphs, half))
    low = nbr + jnp.where(core == 0, 2 * half, half)
    high = nbr - jnp.where(core == 0, half, 0)
    place = jnp.where(nbr < half, low, jnp.where(nbr < 2 * half, nbr - half, high))
    live = jnp.arange(slots, dtype=jnp.int32)[None, :, None] < count[:, None, :]
    place = jnp.where(live, place, 3 * half)
    odd = jnp.arange(half, dtype=jnp.int32) % 2
    return (4 * (place + 1 - odd)).reshape(graphs, slots * half)


def spread_rows(same, other):
    a = lax.ppermute(same, ("mp", "batch"), [(0, 0), (1, 2), (2, 1), (3, 3)])
    b = lax.ppermute(other, ("mp", "batch"), [(0, 1), (1, 3), (2, 0), (3, 2)])
    return a, b


def gather_rows(a, b):
    same = lax.ppermute(a, ("mp", "batch"), [(0, 0), (1, 2), (2, 1), (3, 3)])
    other = lax.ppermute(b, ("mp", "batch"), [(0, 2), (1, 0), (2, 3), (3, 1)])
    return same, other


def ordered(which, a, b, axis):
    return jnp.where(which == 0, jnp.concatenate([a, b], axis), jnp.concatenate([b, a], axis))


def swap(values, axis):
    return lax.ppermute(values, axis, [(0, 1), (1, 0)])


def rims(own, wrap):
    size = lax.axis_size("mesh")
    pairs = []
    for m in range(size):
        if wrap or m + 1 < size:
            pairs.append((2 * m + 1, 2 * ((m + 1) % size)))
        if wrap or m > 0:
            pairs.append((2 * m, 2 * ((m - 1) % size) + 1))
    return lax.ppermute(own, ("mesh", "batch"), pairs)


def pack_kernel(order, core_ref, g_bias, r_bias, *refs):
    weights, outs, sems = (refs[:3], refs[3:6]), refs[6:-1], refs[-1]
    share = g_bias.shape[1]
    here = pl.multiple_of(core_ref[0] * share, share)
    copies = []
    for (graph, layer), out in zip(order, outs):
        ws, wd, w2 = weights[graph]
        sources = (ws.at[layer, pl.ds(here, share), :], wd.at[layer, pl.ds(here, share), :], w2.at[layer, :, pl.ds(here, share)])
        for i, source in enumerate(sources):
            copies.append(pltpu.make_async_copy(source, out.at[i * share:(i + 1) * share, :], sems.at[len(copies)]))
            copies[-1].start()
    for (graph, layer), out in zip(order, outs):
        bias = (g_bias, r_bias)[graph][layer:layer + 1, :]
        out[3 * share:, :] = jnp.broadcast_to(bias, (16, share))
    for copy in copies:
        copy.wait()


def pack_weights(order, core, g_weights, g_bias, r_weights, r_bias):
    share = g_bias.shape[1]
    vmem = pl.BlockSpec(memory_space=pltpu.VMEM)
    hbm = pl.BlockSpec(memory_space=pltpu.HBM)
    return pl.pallas_call(
        functools.partial(pack_kernel, order),
        out_shape=(jax.ShapeDtypeStruct((3 * share + 16, share), jnp.bfloat16),) * len(order),
        in_specs=[pl.BlockSpec(memory_space=pltpu.SMEM)] + [vmem] * 2 + [hbm] * 6,
        out_specs=(vmem,) * len(order),
        scratch_shapes=[pltpu.SemaphoreType.DMA((3 * len(order),))],
        compiler_params=pltpu.CompilerParams(vmem_limit_bytes=32 << 20),
        cost_estimate=SMALL,
        name="pack_weights",
    )(core, g_bias, r_bias, *g_weights, *r_weights)


def by_rows(
    g_nodes, r_nodes, g_nbr, g_count, r_nbr, r_count, bnd_src, bnd_part, bnd_node,
    g_ws, g_wd, g_b1, g_w2, r_ws, r_wd, r_b1, r_w2,
):
    part = lax.axis_index("mp")
    core = lax.axis_index("batch")
    parts = lax.axis_size("mesh")
    slots = g_nbr.shape[1]
    layers = g_ws.shape[0]
    rows = g_nodes.shape[1]
    half = rows // 2
    cap = 2 * bnd_src.shape[0] // parts
    me = lax.axis_index("mesh").reshape(1)
    core1 = core.reshape(1)
    g_own, r_own = g_nodes[0], r_nodes[0]
    g_weights, r_weights = (g_ws, g_wd, g_w2), (r_ws, r_wd, r_w2)
    after = lax.optimization_barrier

    bnd = jnp.stack([bnd_src, bnd_part[:, 0], bnd_node])
    pieces = pick_rows(me, bnd, g_own, parts, cap)
    landed = [pieces[0]]
    for k in range(1, parts):
        landed.append(lax.ppermute(pieces[k], "mesh", [(i, (i + k) % parts) for i in range(parts)]))
    landed[0], g_late = after((landed[0], g_own))
    same = lax.dynamic_slice(g_late, (part * half, 0), (half, g_own.shape[1]))
    other = lax.dynamic_slice(g_late, ((1 - part) * half, 0), (half, g_own.shape[1]))
    same, other, core1 = after((same, other, core1))
    g_a, g_b = spread_rows(same, other)
    idx = edge_offsets(jnp.stack([g_nbr, r_nbr]), jnp.stack([g_count, r_count]), core)

    order = [(graph, layer) for layer in range(layers) for graph in (0, 1)]
    packs = list(pack_weights(order, core1, g_weights, g_b1, r_weights, r_b1))
    near_w = [swap(packs[0], "mp")]
    g_idx, r_idx = idx[0], idx[1]
    g_a, g_b, g_idx, r_idx, packs[1], *landed = after((g_a, g_b, g_idx, r_idx, packs[1], *landed))
    planet = ordered(core, g_a, g_b, 1)
    g_sib, g_rim = swap(planet, "batch"), rims(planet, True)
    r_a, r_b = spread_rows(*add_force(part.reshape(1), r_own, landed, cap))
    r_a, r_b, g_sib, near_w[0] = after((r_a, r_b, g_sib, near_w[0]))
    regional, g_idx = after((ordered(core, r_a, r_b, 1), g_idx))
    r_sib, r_rim = swap(regional, "batch"), rims(regional, False)
    far_w = []
    for layer in range(layers):
        last = layer == layers - 1
        for graph in (0, 1):
            i = 2 * layer + graph
            far_w.append(swap(near_w[i], "batch"))
            if i + 1 < len(order):
                sent, near_w[i] = after((packs[i + 1], near_w[i]))
                near_w.append(swap(sent, "mp"))
            if graph == 0:
                planet = run_layer(
                    layer, slots, last, core1, g_idx, planet, g_sib, g_rim,
                    g_ws, g_wd, g_w2, g_b1, near_w[i], far_w[i],
                )
                *planet, core1, near_w[i + 1] = after((*(planet if last else (planet,)), core1, near_w[i + 1]))
                if not last:
                    planet = planet[0]
                    g_sib, g_rim = swap(planet, "batch"), rims(planet, True)
                if layer:
                    r_sib, r_rim = swap(regional, "batch"), rims(regional, False)
            else:
                regional = run_layer(
                    layer, slots, last, core1, r_idx, regional, r_sib, r_rim,
                    r_ws, r_wd, r_w2, r_b1, near_w[i], far_w[i],
                )
                if not last:
                    regional, core1, near_w[i + 1] = after((regional, core1, near_w[i + 1]))
    g_out = ordered(part, *gather_rows(*planet), 0)
    r_out = ordered(part, *gather_rows(*regional), 0)
    return g_out[None], r_out[None]


def solution(mesh):
    in_specs = (
        P(("groups", "batch"), "mesh", "mp"),
        P(("groups", "batch"), "mesh", "mp"),
        P("mesh", None),
        P("mesh"),
        P("mesh", None),
        P("mesh"),
        P("mesh"),
        P("mesh", None),
        P("mesh"),
        P(None, None, "mp"),
        P(None, None, "mp"),
        P(None, "mp"),
        P(None, "mp", None),
        P(None, None, "mp"),
        P(None, None, "mp"),
        P(None, "mp"),
        P(None, "mp", None),
    )
    out_specs = (P(("groups", "batch"), "mesh", "mp"), P(("groups", "batch"), "mesh", "mp"))
    square = mesh.shape["mp"] == 2 and mesh.shape["batch"] == 2
    return jax.shard_map(
        by_rows if square else by_features, mesh=mesh, in_specs=in_specs, out_specs=out_specs, check_vma=False
    )
```

```python
import functools

import jax
import jax.numpy as jnp
from jax import lax
from jax.experimental import pallas as pl
from jax.experimental.pallas import tpu as pltpu
from jax.sharding import PartitionSpec as P

LANES = 128
DEAD = -1e30
SMALL = pl.CostEstimate(flops=1, bytes_accessed=1, transcendentals=0)


def padded_2(shard, sides, width, wrap):
    for axis, dim in sides:
        size, length = (lax.axis_size(axis), shard.shape[dim])
        up = [(i, (i + 1) % size) for i in range(size if wrap else size - 1)]
        down = [(j, i) for i, j in up]
        last = lax.slice_in_dim(shard, length - width, length, axis=dim)
        leading = lax.slice_in_dim(shard, 0, width, axis=dim)
        before = lax.ppermute(last, axis, up)
        after = lax.ppermute(leading, axis, down)
        shard = jnp.concatenate([before, shard, after], axis=dim)
    return shard


def edge_sums(proj, near, nbr, count):
    slots = nbr.shape[1]
    live = jnp.arange(slots, dtype=jnp.int32)[None, :] < count[:, None]
    pre = proj[:, nbr].astype(jnp.float32) + near[:, :, None]
    acts = jnp.where(live[None, :, :, None], jax.nn.silu(pre), 0.0)
    return jnp.sum(acts, axis=2).astype(jnp.bfloat16)


def graph_layer(latent, nbr, count, w_send, w_recv, bias, w_out, wrap):
    rim = latent.shape[1] // 2
    own_full = lax.all_gather(latent, "mp", axis=2, tiled=True)
    padded_full = padded_2(own_full, (("mesh", 1),), rim, wrap)
    proj = jnp.dot(padded_full, w_send, preferred_element_type=jnp.float32).astype(jnp.bfloat16)
    near = jnp.dot(own_full, w_recv, preferred_element_type=jnp.float32) + bias.astype(jnp.float32)
    summed = edge_sums(proj, near, nbr, count)
    partial_prod = jnp.dot(summed, w_out, preferred_element_type=jnp.float32)
    update = lax.psum_scatter(
        partial_prod.astype(jnp.bfloat16), "mp", scatter_dimension=2, tiled=True
    ).astype(jnp.float32)
    return (latent.astype(jnp.float32) + update).astype(jnp.bfloat16)


def by_features(
    g_nodes, r_nodes, g_nbr, g_count, r_nbr, r_count, bnd_src, bnd_part, bnd_node,
    g_ws, g_wd, g_b1, g_w2, r_ws, r_wd, r_b1, r_w2,
):
    batch_rows, reg_rows, feats = r_nodes.shape
    dest = bnd_part[:, 0]
    outgoing = jnp.moveaxis(g_nodes[:, bnd_src], 1, 0)
    init = jnp.zeros((reg_rows + 1, batch_rows, feats), jnp.float32)
    target = dest * reg_rows + bnd_node
    mine = lax.axis_index("mesh")
    piece_rows = lax.all_gather(outgoing, "mesh", axis=0, tiled=True)
    piece_target = lax.all_gather(target, "mesh", axis=0, tiled=True)
    local = jnp.where(piece_target // reg_rows == mine, piece_target % reg_rows + 1, 0)
    landed = init.at[local].add(piece_rows.astype(jnp.float32))
    force = jnp.moveaxis(landed[1:], 1, 0)
    regional = (r_nodes.astype(jnp.float32) + force).astype(jnp.bfloat16)
    planet = g_nodes
    for layer in range(g_ws.shape[0]):
        planet = graph_layer(
            planet, g_nbr, g_count, g_ws[layer], g_wd[layer], g_b1[layer], g_w2[layer], True
        )
    for layer in range(r_ws.shape[0]):
        regional = graph_layer(
            regional, r_nbr, r_count, r_ws[layer], r_wd[layer], r_b1[layer], r_w2[layer], False
        )
    return (planet, regional)


def one_hot(flags):
    return jnp.where(flags, 1.0, 0.0).astype(jnp.bfloat16)


def pick_kernel(parts, cap, me_ref, bnd_ref, g_ref, *out_refs):
    rows = g_ref.shape[0]
    total = bnd_ref.shape[1]
    me = me_ref[0]
    src, part, node = (bnd_ref[i:i + 1, :] for i in range(3))
    lines = -(-parts // 8) * 8
    target = lax.rem(lax.broadcasted_iota(jnp.int32, (lines, total), 0) + me, parts)
    named = part == target
    before = one_hot(
        lax.broadcasted_iota(jnp.int32, (total, total), 0) < lax.broadcasted_iota(jnp.int32, (total, total), 1)
    )
    rank = jnp.dot(one_hot(named), before, preferred_element_type=jnp.float32)
    rank = jnp.where(named, rank, -1.0)
    source = one_hot(lax.broadcasted_iota(jnp.int32, (rows, total), 0) == src)
    line = lax.broadcasted_iota(jnp.int32, (16, total), 0)
    high = lax.shift_right_logical(node, 7)
    facts = jnp.where(line == 0, high, jnp.where(line == 1, node - high * 128, jnp.where(line == 2, 1, 0)))
    facts = facts.astype(jnp.float32).astype(jnp.bfloat16)
    place = lax.broadcasted_iota(jnp.int32, (cap, total), 0).astype(jnp.float32)
    across = (((1,), (1,)), ((), ()))
    for k in range(parts):
        chosen = one_hot(place == rank[k:k + 1, :])
        pick = lax.dot_general(chosen, source, across, preferred_element_type=jnp.float32).astype(jnp.bfloat16)
        out_refs[k][:cap, :] = jnp.dot(pick, g_ref[...], preferred_element_type=jnp.float32).astype(jnp.bfloat16)
        told = lax.dot_general(facts, chosen, across, preferred_element_type=jnp.float32)
        out_refs[k][cap:, :] = told.astype(jnp.bfloat16)


def pick_rows(me, bnd, nodes, parts, cap):
    vmem = pl.BlockSpec(memory_space=pltpu.VMEM)
    rows, feats = nodes.shape
    total = bnd.shape[1]
    piece = jax.ShapeDtypeStruct((cap + 16, feats), jnp.bfloat16)
    return pl.pallas_call(
        functools.partial(pick_kernel, parts, cap),
        out_shape=(piece,) * parts,
        in_specs=[pl.BlockSpec(memory_space=pltpu.SMEM), vmem, vmem],
        out_specs=(vmem,) * parts,
        compiler_params=pltpu.CompilerParams(vmem_limit_bytes=32 << 20),
        cost_estimate=SMALL,
        name="pick_rows",
    )(me, bnd, nodes)


def force_kernel(cap, first_ref, r_ref, *refs):
    pieces, (same_ref, other_ref) = refs[:-2], refs[-2:]
    half = same_ref.shape[0]
    first = first_ref[0]
    for out_ref, start in ((same_ref, first * half), (other_ref, (1 - first) * half)):
        start = pl.multiple_of(start, 16)
        row = (lax.broadcasted_iota(jnp.int32, (half, cap), 0) + start).astype(jnp.float32)
        total = r_ref[pl.ds(start, half), :].astype(jnp.float32)
        for piece in pieces:
            facts = piece[cap:, :].astype(jnp.float32)
            node = jnp.where(facts[2:3, :] > 0.5, facts[0:1, :] * 128.0 + facts[1:2, :], -1.0)
            total += jnp.dot(one_hot(row == node), piece[:cap, :], preferred_element_type=jnp.float32)
        out_ref[...] = total.astype(jnp.bfloat16)


def add_force(first, nodes, pieces, cap):
    vmem = pl.BlockSpec(memory_space=pltpu.VMEM)
    rows, feats = nodes.shape
    block = jax.ShapeDtypeStruct((rows // 2, feats), jnp.bfloat16)
    return pl.pallas_call(
        functools.partial(force_kernel, cap),
        out_shape=(block, block),
        in_specs=[pl.BlockSpec(memory_space=pltpu.SMEM)] + [vmem] * (1 + len(pieces)),
        out_specs=(vmem, vmem),
        compiler_params=pltpu.CompilerParams(vmem_limit_bytes=32 << 20),
        cost_estimate=SMALL,
        name="add_force",
    )(first, nodes, *pieces)


def layer_kernel(
    layer, slots, last, core_ref, idx_ref, own, sib, rim, bias, near_w, far_w, ws_hbm, wd_hbm, w2_hbm, *refs
):
    outs, refs = (refs[:2], refs[2:]) if last else (refs[:1], refs[1:])
    ws, wd, w2, ws_x, wd_x, w2_x, proj, near, summed, sems = refs
    rows, width = own.shape
    share = width // 2
    chunks = width // LANES
    part = chunks // 2
    core = core_ref[0]
    pairs = ((wd_hbm, wd), (ws_hbm, ws), (w2_hbm, w2))
    copies = [pltpu.make_async_copy(src.at[layer], dst, sems.at[i]) for i, (src, dst) in enumerate(pairs)]
    for copy in copies:
        copy.start()
    window = 3 * rows
    proj[0:8, :] = jnp.full((8, LANES), DEAD, jnp.float32)
    proj[4 * window + 4:4 * window + 16, :] = jnp.full((12, LANES), DEAD, jnp.float32)
    here, there = pl.multiple_of(core * share, 16), pl.multiple_of((1 - core) * share, 16)
    for spot, piece in ((here, near_w), (there, far_w)):
        ws_x[pl.ds(spot, share), :] = piece[0:share, :]
        wd_x[pl.ds(spot, share), :] = piece[share:2 * share, :]

    @pl.when(core == 0)
    def _():
        w2_x[:, :share] = near_w[2 * share:3 * share, :]
        w2_x[:, share:] = far_w[2 * share:3 * share, :]

    @pl.when(core != 0)
    def _():
        w2_x[:, share:] = near_w[2 * share:3 * share, :]
        w2_x[:, :share] = far_w[2 * share:3 * share, :]

    def put(dst, base, first, values):
        for c in range(values.shape[1] // LANES):
            dst[pl.ds(base * chunks + first + c, rows, stride=chunks), :] = values[:, c * LANES:(c + 1) * LANES] * 0.5

    def product(values, weights):
        return jnp.dot(values[...], weights[...], preferred_element_type=jnp.float32)

    b_own = bias[layer:layer + 1, :].astype(jnp.float32)
    b_other = near_w[3 * share:3 * share + 1, :].astype(jnp.float32)
    put(near, 0, part, product(own, wd_x) + b_other)
    put(proj, 1, part, product(own, ws_x))
    copies[0].wait()
    copies[1].wait()
    put(near, 0, 0, product(own, wd) + b_own)
    put(proj, 1, 0, product(own, ws))
    for ref, base in ((sib, rows + 1), (rim, 2 * rows + 1)):
        put(proj, base, 0, product(ref, ws))
        put(proj, base, part, product(ref, ws_x))
    low = lax.broadcasted_iota(jnp.int32, (8, LANES), 0) < chunks

    def nodes(q, carry):
        spot = pl.ds(pl.multiple_of(8 * q, 8), 8)
        mine = near[spot, :]
        total = None
        for j in range(slots):
            upper = proj[pl.ds(pl.multiple_of(idx_ref[j * rows + 2 * q], 4), 8), :]
            lower = proj[pl.ds(pl.multiple_of(idx_ref[j * rows + 2 * q + 1], 4), 8), :]
            y = jnp.where(low, upper, lower) + mine
            act = y * jnp.tanh(y) + y
            total = act if total is None else total + act
        summed[spot, :] = total
        return carry

    lax.fori_loop(0, rows // 2, nodes, 0, unroll=16)
    copies[2].wait()
    sums = [summed[pl.ds(c, rows, stride=chunks), :].astype(jnp.bfloat16) for c in range(chunks)]
    update = product(jnp.concatenate(sums[:part], 1), w2) + product(jnp.concatenate(sums[part:], 1), w2_x)
    result = (own[...].astype(jnp.float32) + update).astype(jnp.bfloat16)
    if not last:
        outs[0][...] = result
    else:
        @pl.when(core == 0)
        def _():
            outs[0][...] = result[:, :share]
            outs[1][...] = result[:, share:]

        @pl.when(core != 0)
        def _():
            outs[0][...] = result[:, share:]
            outs[1][...] = result[:, :share]


def run_layer(layer, slots, last, core, idx, own, sib, rim, ws, wd, w2, bias, near_w, far_w):
    rows, width = own.shape
    share = width // 2
    chunks = width // LANES
    smem = pl.BlockSpec(memory_space=pltpu.SMEM)
    vmem = pl.BlockSpec(memory_space=pltpu.VMEM)
    bf16, f32 = jnp.bfloat16, jnp.float32
    if last:
        out_shape = (jax.ShapeDtypeStruct((rows, share), bf16),) * 2
        out_specs = (vmem, vmem)
    else:
        out_shape, out_specs = jax.ShapeDtypeStruct((rows, width), bf16), vmem
    return pl.pallas_call(
        functools.partial(layer_kernel, layer, slots, last),
        out_shape=out_shape,
        in_specs=[smem] * 2 + [vmem] * 6 + [pl.BlockSpec(memory_space=pl.ANY)] * 3,
        out_specs=out_specs,
        scratch_shapes=[
            pltpu.VMEM((width, share), bf16),
            pltpu.VMEM((width, share), bf16),
            pltpu.VMEM((share, width), bf16),
            pltpu.VMEM((width, share), bf16),
            pltpu.VMEM((width, share), bf16),
            pltpu.VMEM((share, width), bf16),
            pltpu.VMEM((3 * rows * chunks + 96, LANES), f32),
            pltpu.VMEM((rows * chunks, LANES), f32),
            pltpu.VMEM((rows * chunks, LANES), f32),
            pltpu.SemaphoreType.DMA((3,)),
        ],
        compiler_params=pltpu.CompilerParams(vmem_limit_bytes=32 << 20),
        cost_estimate=pl.CostEstimate(flops=64 * rows * width * width, bytes_accessed=10 * rows * width, transcendentals=0),
        name="graph_layer",
    )(core, idx, own, sib, rim, bias, near_w, far_w, ws, wd, w2)


def edge_offsets(nbrs, counts, core):
    graphs, rows, slots = nbrs.shape
    half = rows // 2
    nbr = lax.dynamic_slice(nbrs.transpose(0, 2, 1), (0, 0, core * half), (graphs, slots, half)) - core * half
    count = lax.dynamic_slice(counts, (0, core * half), (graphs, half))
    low = nbr + jnp.where(core == 0, 2 * half, half)
    high = nbr - jnp.where(core == 0, half, 0)
    place = jnp.where(nbr < half, low, jnp.where(nbr < 2 * half, nbr - half, high))
    live = jnp.arange(slots, dtype=jnp.int32)[None, :, None] < count[:, None, :]
    place = jnp.where(live, place, 3 * half)
    odd = jnp.arange(half, dtype=jnp.int32) % 2
    return (4 * (place + 1 - odd)).reshape(graphs, slots * half)


def spread_rows(same, other):
    a = lax.ppermute(same, ("mp", "batch"), [(0, 0), (1, 2), (2, 1), (3, 3)])
    b = lax.ppermute(other, ("mp", "batch"), [(0, 1), (1, 3), (2, 0), (3, 2)])
    return a, b


def gather_rows(a, b):
    same = lax.ppermute(a, ("mp", "batch"), [(0, 0), (1, 2), (2, 1), (3, 3)])
    other = lax.ppermute(b, ("mp", "batch"), [(0, 2), (1, 0), (2, 3), (3, 1)])
    return same, other


def ordered(which, a, b, axis):
    return jnp.where(which == 0, jnp.concatenate([a, b], axis), jnp.concatenate([b, a], axis))


def swap(values, axis):
    return lax.ppermute(values, axis, [(0, 1), (1, 0)])


def rims(own, wrap):
    size = lax.axis_size("mesh")
    pairs = []
    for m in range(size):
        if wrap or m + 1 < size:
            pairs.append((2 * m + 1, 2 * ((m + 1) % size)))
        if wrap or m > 0:
            pairs.append((2 * m, 2 * ((m - 1) % size) + 1))
    return lax.ppermute(own, ("mesh", "batch"), pairs)


def pack_kernel(order, core_ref, g_bias, r_bias, *refs):
    weights, outs, sems = (refs[:3], refs[3:6]), refs[6:-1], refs[-1]
    share = g_bias.shape[1]
    here = pl.multiple_of(core_ref[0] * share, share)
    copies = []
    for (graph, layer), out in zip(order, outs):
        ws, wd, w2 = weights[graph]
        sources = (ws.at[layer, pl.ds(here, share), :], wd.at[layer, pl.ds(here, share), :], w2.at[layer, :, pl.ds(here, share)])
        for i, source in enumerate(sources):
            copies.append(pltpu.make_async_copy(source, out.at[i * share:(i + 1) * share, :], sems.at[len(copies)]))
            copies[-1].start()
    for (graph, layer), out in zip(order, outs):
        bias = (g_bias, r_bias)[graph][layer:layer + 1, :]
        out[3 * share:, :] = jnp.broadcast_to(bias, (16, share))
    for copy in copies:
        copy.wait()


def pack_weights(order, core, g_weights, g_bias, r_weights, r_bias):
    share = g_bias.shape[1]
    vmem = pl.BlockSpec(memory_space=pltpu.VMEM)
    hbm = pl.BlockSpec(memory_space=pltpu.HBM)
    return pl.pallas_call(
        functools.partial(pack_kernel, order),
        out_shape=(jax.ShapeDtypeStruct((3 * share + 16, share), jnp.bfloat16),) * len(order),
        in_specs=[pl.BlockSpec(memory_space=pltpu.SMEM)] + [vmem] * 2 + [hbm] * 6,
        out_specs=(vmem,) * len(order),
        scratch_shapes=[pltpu.SemaphoreType.DMA((3 * len(order),))],
        compiler_params=pltpu.CompilerParams(vmem_limit_bytes=60 << 20),
        cost_estimate=SMALL,
        name="pack_weights",
    )(core, g_bias, r_bias, *g_weights, *r_weights)


def by_rows(
    g_nodes, r_nodes, g_nbr, g_count, r_nbr, r_count, bnd_src, bnd_part, bnd_node,
    g_ws, g_wd, g_b1, g_w2, r_ws, r_wd, r_b1, r_w2,
):
    part = lax.axis_index("mp")
    core = lax.axis_index("batch")
    parts = lax.axis_size("mesh")
    slots = g_nbr.shape[1]
    layers = g_ws.shape[0]
    rows = g_nodes.shape[1]
    half = rows // 2
    cap = 2 * bnd_src.shape[0] // parts
    me = lax.axis_index("mesh").reshape(1)
    core1 = core.reshape(1)
    g_own, r_own = g_nodes[0], r_nodes[0]
    g_weights, r_weights = (g_ws, g_wd, g_w2), (r_ws, r_wd, r_w2)
    after = lax.optimization_barrier

    bnd = jnp.stack([bnd_src, bnd_part[:, 0], bnd_node])
    pieces = pick_rows(me, bnd, g_own, parts, cap)
    landed = [pieces[0]]
    for k in range(1, parts):
        landed.append(lax.ppermute(pieces[k], "mesh", [(i, (i + k) % parts) for i in range(parts)]))
    landed[0], g_late = after((landed[0], g_own))
    same = lax.dynamic_slice(g_late, (part * half, 0), (half, g_own.shape[1]))
    other = lax.dynamic_slice(g_late, ((1 - part) * half, 0), (half, g_own.shape[1]))
    same, other, core1 = after((same, other, core1))
    g_a, g_b = spread_rows(same, other)
    idx = edge_offsets(jnp.stack([g_nbr, r_nbr]), jnp.stack([g_count, r_count]), core)

    order = [(graph, layer) for layer in range(layers) for graph in (0, 1)]
    packs = list(pack_weights(order, core1, g_weights, g_b1, r_weights, r_b1))
    near_w = [swap(packs[0], "mp")]
    g_idx, r_idx = idx[0], idx[1]
    g_a, g_b, g_idx, r_idx, packs[1], *landed = after((g_a, g_b, g_idx, r_idx, packs[1], *landed))
    planet = ordered(core, g_a, g_b, 1)
    g_sib, g_rim = swap(planet, "batch"), rims(planet, True)
    r_a, r_b = spread_rows(*add_force(part.reshape(1), r_own, landed, cap))
    r_a, r_b, g_sib, near_w[0] = after((r_a, r_b, g_sib, near_w[0]))
    regional, g_idx = after((ordered(core, r_a, r_b, 1), g_idx))
    r_sib, r_rim = swap(regional, "batch"), rims(regional, False)
    far_w = []
    for layer in range(layers):
        last = layer == layers - 1
        for graph in (0, 1):
            i = 2 * layer + graph
            far_w.append(swap(near_w[i], "batch"))
            if i + 1 < len(order):
                sent, near_w[i] = after((packs[i + 1], near_w[i]))
                near_w.append(swap(sent, "mp"))
            if graph == 0:
                planet = run_layer(
                    layer, slots, last, core1, g_idx, planet, g_sib, g_rim,
                    g_ws, g_wd, g_w2, g_b1, near_w[i], far_w[i],
                )
                *planet, core1, near_w[i + 1] = after((*(planet if last else (planet,)), core1, near_w[i + 1]))
                if not last:
                    planet = planet[0]
                    g_sib, g_rim = swap(planet, "batch"), rims(planet, True)
                if layer:
                    r_sib, r_rim = swap(regional, "batch"), rims(regional, False)
            else:
                regional = run_layer(
                    layer, slots, last, core1, r_idx, regional, r_sib, r_rim,
                    r_ws, r_wd, r_w2, r_b1, near_w[i], far_w[i],
                )
                if not last:
                    regional, core1, near_w[i + 1] = after((regional, core1, near_w[i + 1]))
    g_out = ordered(part, *gather_rows(*planet), 0)
    r_out = ordered(part, *gather_rows(*regional), 0)
    return g_out[None], r_out[None]


def solution(mesh):
    in_specs = (
        P(("groups", "batch"), "mesh", "mp"),
        P(("groups", "batch"), "mesh", "mp"),
        P("mesh", None),
        P("mesh"),
        P("mesh", None),
        P("mesh"),
        P("mesh"),
        P("mesh", None),
        P("mesh"),
        P(None, None, "mp"),
        P(None, None, "mp"),
        P(None, "mp"),
        P(None, "mp", None),
        P(None, None, "mp"),
        P(None, None, "mp"),
        P(None, "mp"),
        P(None, "mp", None),
    )
    out_specs = (P(("groups", "batch"), "mesh", "mp"), P(("groups", "batch"), "mesh", "mp"))
    square = mesh.shape["mp"] == 2 and mesh.shape["batch"] == 2
    return jax.shard_map(
        by_rows if square else by_features, mesh=mesh, in_specs=in_specs, out_specs=out_specs, check_vma=False
    )
```

```python
import functools

import jax
import jax.numpy as jnp
from jax import lax
from jax.experimental import pallas as pl
from jax.experimental.pallas import tpu as pltpu
from jax.sharding import PartitionSpec as P

LANES = 128
DEAD = -1e30
SMALL = pl.CostEstimate(flops=1, bytes_accessed=1, transcendentals=0)


def padded_2(shard, sides, width, wrap):
    for axis, dim in sides:
        size, length = (lax.axis_size(axis), shard.shape[dim])
        up = [(i, (i + 1) % size) for i in range(size if wrap else size - 1)]
        down = [(j, i) for i, j in up]
        last = lax.slice_in_dim(shard, length - width, length, axis=dim)
        leading = lax.slice_in_dim(shard, 0, width, axis=dim)
        before = lax.ppermute(last, axis, up)
        after = lax.ppermute(leading, axis, down)
        shard = jnp.concatenate([before, shard, after], axis=dim)
    return shard


def edge_sums(proj, near, nbr, count):
    slots = nbr.shape[1]
    live = jnp.arange(slots, dtype=jnp.int32)[None, :] < count[:, None]
    pre = proj[:, nbr].astype(jnp.float32) + near[:, :, None]
    acts = jnp.where(live[None, :, :, None], jax.nn.silu(pre), 0.0)
    return jnp.sum(acts, axis=2).astype(jnp.bfloat16)


def graph_layer(latent, nbr, count, w_send, w_recv, bias, w_out, wrap):
    rim = latent.shape[1] // 2
    own_full = lax.all_gather(latent, "mp", axis=2, tiled=True)
    padded_full = padded_2(own_full, (("mesh", 1),), rim, wrap)
    proj = jnp.dot(padded_full, w_send, preferred_element_type=jnp.float32).astype(jnp.bfloat16)
    near = jnp.dot(own_full, w_recv, preferred_element_type=jnp.float32) + bias.astype(jnp.float32)
    summed = edge_sums(proj, near, nbr, count)
    partial_prod = jnp.dot(summed, w_out, preferred_element_type=jnp.float32)
    update = lax.psum_scatter(
        partial_prod.astype(jnp.bfloat16), "mp", scatter_dimension=2, tiled=True
    ).astype(jnp.float32)
    return (latent.astype(jnp.float32) + update).astype(jnp.bfloat16)


def by_features(
    g_nodes, r_nodes, g_nbr, g_count, r_nbr, r_count, bnd_src, bnd_part, bnd_node,
    g_ws, g_wd, g_b1, g_w2, r_ws, r_wd, r_b1, r_w2,
):
    batch_rows, reg_rows, feats = r_nodes.shape
    dest = bnd_part[:, 0]
    outgoing = jnp.moveaxis(g_nodes[:, bnd_src], 1, 0)
    init = jnp.zeros((reg_rows + 1, batch_rows, feats), jnp.float32)
    target = dest * reg_rows + bnd_node
    mine = lax.axis_index("mesh")
    piece_rows = lax.all_gather(outgoing, "mesh", axis=0, tiled=True)
    piece_target = lax.all_gather(target, "mesh", axis=0, tiled=True)
    local = jnp.where(piece_target // reg_rows == mine, piece_target % reg_rows + 1, 0)
    landed = init.at[local].add(piece_rows.astype(jnp.float32))
    force = jnp.moveaxis(landed[1:], 1, 0)
    regional = (r_nodes.astype(jnp.float32) + force).astype(jnp.bfloat16)
    planet = g_nodes
    for layer in range(g_ws.shape[0]):
        planet = graph_layer(
            planet, g_nbr, g_count, g_ws[layer], g_wd[layer], g_b1[layer], g_w2[layer], True
        )
    for layer in range(r_ws.shape[0]):
        regional = graph_layer(
            regional, r_nbr, r_count, r_ws[layer], r_wd[layer], r_b1[layer], r_w2[layer], False
        )
    return (planet, regional)


def one_hot(flags):
    return jnp.where(flags, 1.0, 0.0).astype(jnp.bfloat16)


def pick_kernel(parts, cap, me_ref, bnd_ref, g_ref, *out_refs):
    rows = g_ref.shape[0]
    total = bnd_ref.shape[1]
    me = me_ref[0]
    src, part, node = (bnd_ref[i:i + 1, :] for i in range(3))
    lines = -(-parts // 8) * 8
    target = lax.rem(lax.broadcasted_iota(jnp.int32, (lines, total), 0) + me, parts)
    named = part == target
    before = one_hot(
        lax.broadcasted_iota(jnp.int32, (total, total), 0) < lax.broadcasted_iota(jnp.int32, (total, total), 1)
    )
    rank = jnp.dot(one_hot(named), before, preferred_element_type=jnp.float32)
    rank = jnp.where(named, rank, -1.0)
    source = one_hot(lax.broadcasted_iota(jnp.int32, (rows, total), 0) == src)
    line = lax.broadcasted_iota(jnp.int32, (16, total), 0)
    high = lax.shift_right_logical(node, 7)
    facts = jnp.where(line == 0, high, jnp.where(line == 1, node - high * 128, jnp.where(line == 2, 1, 0)))
    facts = facts.astype(jnp.float32).astype(jnp.bfloat16)
    place = lax.broadcasted_iota(jnp.int32, (cap, total), 0).astype(jnp.float32)
    across = (((1,), (1,)), ((), ()))
    for k in range(parts):
        chosen = one_hot(place == rank[k:k + 1, :])
        pick = lax.dot_general(chosen, source, across, preferred_element_type=jnp.float32).astype(jnp.bfloat16)
        out_refs[k][:cap, :] = jnp.dot(pick, g_ref[...], preferred_element_type=jnp.float32).astype(jnp.bfloat16)
        told = lax.dot_general(facts, chosen, across, preferred_element_type=jnp.float32)
        out_refs[k][cap:, :] = told.astype(jnp.bfloat16)


def pick_rows(me, bnd, nodes, parts, cap):
    vmem = pl.BlockSpec(memory_space=pltpu.VMEM)
    rows, feats = nodes.shape
    total = bnd.shape[1]
    piece = jax.ShapeDtypeStruct((cap + 16, feats), jnp.bfloat16)
    return pl.pallas_call(
        functools.partial(pick_kernel, parts, cap),
        out_shape=(piece,) * parts,
        in_specs=[pl.BlockSpec(memory_space=pltpu.SMEM), vmem, vmem],
        out_specs=(vmem,) * parts,
        compiler_params=pltpu.CompilerParams(vmem_limit_bytes=32 << 20),
        cost_estimate=SMALL,
        name="pick_rows",
    )(me, bnd, nodes)


def force_kernel(cap, first_ref, r_ref, *refs):
    pieces, (same_ref, other_ref) = refs[:-2], refs[-2:]
    half = same_ref.shape[0]
    first = first_ref[0]
    for out_ref, start in ((same_ref, first * half), (other_ref, (1 - first) * half)):
        start = pl.multiple_of(start, 16)
        row = (lax.broadcasted_iota(jnp.int32, (half, cap), 0) + start).astype(jnp.float32)
        total = r_ref[pl.ds(start, half), :].astype(jnp.float32)
        for piece in pieces:
            facts = piece[cap:, :].astype(jnp.float32)
            node = jnp.where(facts[2:3, :] > 0.5, facts[0:1, :] * 128.0 + facts[1:2, :], -1.0)
            total += jnp.dot(one_hot(row == node), piece[:cap, :], preferred_element_type=jnp.float32)
        out_ref[...] = total.astype(jnp.bfloat16)


def add_force(first, nodes, pieces, cap):
    vmem = pl.BlockSpec(memory_space=pltpu.VMEM)
    rows, feats = nodes.shape
    block = jax.ShapeDtypeStruct((rows // 2, feats), jnp.bfloat16)
    return pl.pallas_call(
        functools.partial(force_kernel, cap),
        out_shape=(block, block),
        in_specs=[pl.BlockSpec(memory_space=pltpu.SMEM)] + [vmem] * (1 + len(pieces)),
        out_specs=(vmem, vmem),
        compiler_params=pltpu.CompilerParams(vmem_limit_bytes=32 << 20),
        cost_estimate=SMALL,
        name="add_force",
    )(first, nodes, *pieces)


def layer_kernel(
    layer, slots, last, core_ref, idx_ref, own, sib, rim, bias, near_w, far_w, ws_hbm, wd_hbm, w2_hbm, *refs
):
    outs, refs = (refs[:2], refs[2:]) if last else (refs[:1], refs[1:])
    ws, wd, w2, ws_x, wd_x, w2_x, proj, near, summed, sems = refs
    rows, width = own.shape
    share = width // 2
    chunks = width // LANES
    part = chunks // 2
    core = core_ref[0]
    pairs = ((wd_hbm, wd), (ws_hbm, ws), (w2_hbm, w2))
    copies = [pltpu.make_async_copy(src.at[layer], dst, sems.at[i]) for i, (src, dst) in enumerate(pairs)]
    for copy in copies:
        copy.start()
    window = 3 * rows
    proj[0:8, :] = jnp.full((8, LANES), DEAD, jnp.float32)
    proj[4 * window + 4:4 * window + 16, :] = jnp.full((12, LANES), DEAD, jnp.float32)
    here, there = pl.multiple_of(core * share, 16), pl.multiple_of((1 - core) * share, 16)
    for spot, piece in ((here, near_w), (there, far_w)):
        ws_x[pl.ds(spot, share), :] = piece[0:share, :]
        wd_x[pl.ds(spot, share), :] = piece[share:2 * share, :]

    @pl.when(core == 0)
    def _():
        w2_x[:, :share] = near_w[2 * share:3 * share, :]
        w2_x[:, share:] = far_w[2 * share:3 * share, :]

    @pl.when(core != 0)
    def _():
        w2_x[:, share:] = near_w[2 * share:3 * share, :]
        w2_x[:, :share] = far_w[2 * share:3 * share, :]

    def put(dst, base, first, values):
        for c in range(values.shape[1] // LANES):
            dst[pl.ds(base * chunks + first + c, rows, stride=chunks), :] = values[:, c * LANES:(c + 1) * LANES] * 0.5

    def product(values, weights):
        return jnp.dot(values[...], weights[...], preferred_element_type=jnp.float32)

    b_own = bias[layer:layer + 1, :].astype(jnp.float32)
    b_other = near_w[3 * share:3 * share + 1, :].astype(jnp.float32)
    put(near, 0, part, product(own, wd_x) + b_other)
    put(proj, 1, part, product(own, ws_x))
    copies[0].wait()
    copies[1].wait()
    put(near, 0, 0, product(own, wd) + b_own)
    put(proj, 1, 0, product(own, ws))
    for ref, base in ((sib, rows + 1), (rim, 2 * rows + 1)):
        put(proj, base, 0, product(ref, ws))
        put(proj, base, part, product(ref, ws_x))
    low = lax.broadcasted_iota(jnp.int32, (8, LANES), 0) < chunks

    def nodes(q, carry):
        spot = pl.ds(pl.multiple_of(8 * q, 8), 8)
        mine = near[spot, :]
        total = None
        for j in range(slots):
            upper = proj[pl.ds(pl.multiple_of(idx_ref[j * rows + 2 * q], 4), 8), :]
            lower = proj[pl.ds(pl.multiple_of(idx_ref[j * rows + 2 * q + 1], 4), 8), :]
            y = jnp.where(low, upper, lower) + mine
            act = y * jnp.tanh(y) + y
            total = act if total is None else total + act
        summed[spot, :] = total
        return carry

    lax.fori_loop(0, rows // 2, nodes, 0, unroll=16)
    copies[2].wait()
    sums = [summed[pl.ds(c, rows, stride=chunks), :].astype(jnp.bfloat16) for c in range(chunks)]
    update = product(jnp.concatenate(sums[:part], 1), w2) + product(jnp.concatenate(sums[part:], 1), w2_x)
    result = (own[...].astype(jnp.float32) + update).astype(jnp.bfloat16)
    if not last:
        outs[0][...] = result
    else:
        @pl.when(core == 0)
        def _():
            outs[0][...] = result[:, :share]
            outs[1][...] = result[:, share:]

        @pl.when(core != 0)
        def _():
            outs[0][...] = result[:, share:]
            outs[1][...] = result[:, :share]


def run_layer(layer, slots, last, core, idx, own, sib, rim, ws, wd, w2, bias, near_w, far_w):
    rows, width = own.shape
    share = width // 2
    chunks = width // LANES
    smem = pl.BlockSpec(memory_space=pltpu.SMEM)
    vmem = pl.BlockSpec(memory_space=pltpu.VMEM)
    bf16, f32 = jnp.bfloat16, jnp.float32
    if last:
        out_shape = (jax.ShapeDtypeStruct((rows, share), bf16),) * 2
        out_specs = (vmem, vmem)
    else:
        out_shape, out_specs = jax.ShapeDtypeStruct((rows, width), bf16), vmem
    return pl.pallas_call(
        functools.partial(layer_kernel, layer, slots, last),
        out_shape=out_shape,
        in_specs=[smem] * 2 + [vmem] * 6 + [pl.BlockSpec(memory_space=pl.ANY)] * 3,
        out_specs=out_specs,
        scratch_shapes=[
            pltpu.VMEM((width, share), bf16),
            pltpu.VMEM((width, share), bf16),
            pltpu.VMEM((share, width), bf16),
            pltpu.VMEM((width, share), bf16),
            pltpu.VMEM((width, share), bf16),
            pltpu.VMEM((share, width), bf16),
            pltpu.VMEM((3 * rows * chunks + 96, LANES), f32),
            pltpu.VMEM((rows * chunks, LANES), f32),
            pltpu.VMEM((rows * chunks, LANES), f32),
            pltpu.SemaphoreType.DMA((3,)),
        ],
        compiler_params=pltpu.CompilerParams(vmem_limit_bytes=32 << 20),
        cost_estimate=pl.CostEstimate(flops=64 * rows * width * width, bytes_accessed=10 * rows * width, transcendentals=0),
        name="graph_layer",
    )(core, idx, own, sib, rim, bias, near_w, far_w, ws, wd, w2)


def edge_offsets(nbrs, counts, core):
    graphs, rows, slots = nbrs.shape
    half = rows // 2
    nbr = lax.dynamic_slice(nbrs.transpose(0, 2, 1), (0, 0, core * half), (graphs, slots, half)) - core * half
    count = lax.dynamic_slice(counts, (0, core * half), (graphs, half))
    low = nbr + jnp.where(core == 0, 2 * half, half)
    high = nbr - jnp.where(core == 0, half, 0)
    place = jnp.where(nbr < half, low, jnp.where(nbr < 2 * half, nbr - half, high))
    live = jnp.arange(slots, dtype=jnp.int32)[None, :, None] < count[:, None, :]
    place = jnp.where(live, place, 3 * half)
    odd = jnp.arange(half, dtype=jnp.int32) % 2
    return (4 * (place + 1 - odd)).reshape(graphs, slots * half)


def spread_rows(same, other):
    a = lax.ppermute(same, ("mp", "batch"), [(0, 0), (1, 2), (2, 1), (3, 3)])
    b = lax.ppermute(other, ("mp", "batch"), [(0, 1), (1, 3), (2, 0), (3, 2)])
    return a, b


def gather_rows(a, b):
    same = lax.ppermute(a, ("mp", "batch"), [(0, 0), (1, 2), (2, 1), (3, 3)])
    other = lax.ppermute(b, ("mp", "batch"), [(0, 2), (1, 0), (2, 3), (3, 1)])
    return same, other


def ordered(which, a, b, axis):
    return jnp.where(which == 0, jnp.concatenate([a, b], axis), jnp.concatenate([b, a], axis))


def swap(values, axis):
    return lax.ppermute(values, axis, [(0, 1), (1, 0)])


def rims(own, wrap):
    size = lax.axis_size("mesh")
    pairs = []
    for m in range(size):
        if wrap or m + 1 < size:
            pairs.append((2 * m + 1, 2 * ((m + 1) % size)))
        if wrap or m > 0:
            pairs.append((2 * m, 2 * ((m - 1) % size) + 1))
    return lax.ppermute(own, ("mesh", "batch"), pairs)


def pack_kernel(order, core_ref, g_bias, r_bias, *refs):
    weights, outs, sems = (refs[:3], refs[3:6]), refs[6:-1], refs[-1]
    share = g_bias.shape[1]
    here = pl.multiple_of(core_ref[0] * share, share)
    copies = []
    for (graph, layer), out in zip(order, outs):
        ws, wd, w2 = weights[graph]
        sources = (ws.at[layer, pl.ds(here, share), :], wd.at[layer, pl.ds(here, share), :], w2.at[layer, :, pl.ds(here, share)])
        for i, source in enumerate(sources):
            copies.append(pltpu.make_async_copy(source, out.at[i * share:(i + 1) * share, :], sems.at[len(copies)]))
            copies[-1].start()
    for (graph, layer), out in zip(order, outs):
        bias = (g_bias, r_bias)[graph][layer:layer + 1, :]
        out[3 * share:, :] = jnp.broadcast_to(bias, (16, share))
    for copy in copies:
        copy.wait()


def pack_weights(order, core, g_weights, g_bias, r_weights, r_bias):
    share = g_bias.shape[1]
    vmem = pl.BlockSpec(memory_space=pltpu.VMEM)
    hbm = pl.BlockSpec(memory_space=pltpu.HBM)
    return pl.pallas_call(
        functools.partial(pack_kernel, order),
        out_shape=(jax.ShapeDtypeStruct((3 * share + 16, share), jnp.bfloat16),) * len(order),
        in_specs=[pl.BlockSpec(memory_space=pltpu.SMEM)] + [vmem] * 2 + [hbm] * 6,
        out_specs=(vmem,) * len(order),
        scratch_shapes=[pltpu.SemaphoreType.DMA((3 * len(order),))],
        compiler_params=pltpu.CompilerParams(vmem_limit_bytes=60 << 20),
        cost_estimate=pl.CostEstimate(flops=256 * share**3, bytes_accessed=1, transcendentals=0),
        name="pack_weights",
    )(core, g_bias, r_bias, *g_weights, *r_weights)


def by_rows(
    g_nodes, r_nodes, g_nbr, g_count, r_nbr, r_count, bnd_src, bnd_part, bnd_node,
    g_ws, g_wd, g_b1, g_w2, r_ws, r_wd, r_b1, r_w2,
):
    part = lax.axis_index("mp")
    core = lax.axis_index("batch")
    parts = lax.axis_size("mesh")
    slots = g_nbr.shape[1]
    layers = g_ws.shape[0]
    rows = g_nodes.shape[1]
    half = rows // 2
    cap = 2 * bnd_src.shape[0] // parts
    me = lax.axis_index("mesh").reshape(1)
    core1 = core.reshape(1)
    g_own, r_own = g_nodes[0], r_nodes[0]
    g_weights, r_weights = (g_ws, g_wd, g_w2), (r_ws, r_wd, r_w2)
    after = lax.optimization_barrier

    bnd = jnp.stack([bnd_src, bnd_part[:, 0], bnd_node])
    pieces = pick_rows(me, bnd, g_own, parts, cap)
    landed = [pieces[0]]
    for k in range(1, parts):
        landed.append(lax.ppermute(pieces[k], "mesh", [(i, (i + k) % parts) for i in range(parts)]))
    landed[0], g_late = after((landed[0], g_own))
    same = lax.dynamic_slice(g_late, (part * half, 0), (half, g_own.shape[1]))
    other = lax.dynamic_slice(g_late, ((1 - part) * half, 0), (half, g_own.shape[1]))
    same, other, core1 = after((same, other, core1))
    g_a, g_b = spread_rows(same, other)
    idx = edge_offsets(jnp.stack([g_nbr, r_nbr]), jnp.stack([g_count, r_count]), core)

    order = [(graph, layer) for layer in range(layers) for graph in (0, 1)]
    packs = list(pack_weights(order, core1, g_weights, g_b1, r_weights, r_b1))
    landed[1], packs[0] = after((landed[1], packs[0]))
    near_w = [swap(packs[0], "mp")]
    g_idx, r_idx = idx[0], idx[1]
    g_a, g_b, g_idx, r_idx, packs[1], *landed = after((g_a, g_b, g_idx, r_idx, packs[1], *landed))
    planet = ordered(core, g_a, g_b, 1)
    g_sib, g_rim = swap(planet, "batch"), rims(planet, True)
    *r_pair, packs[1] = after((*add_force(part.reshape(1), r_own, landed, cap), packs[1]))
    r_a, r_b = spread_rows(*r_pair)
    near_w.append(swap(packs[1], "mp"))
    r_a, r_b, g_sib, g_rim, near_w[0] = after((r_a, r_b, g_sib, g_rim, near_w[0]))
    regional, g_idx = after((ordered(core, r_a, r_b, 1), g_idx))
    r_sib, r_rim = swap(regional, "batch"), rims(regional, False)
    for i, (graph, layer) in enumerate(order):
        last = layer == layers - 1
        far_w = swap(near_w[i], "batch")
        if i + 1 < len(order):
            near_w[i + 1], core1 = after((near_w[i + 1], core1))
        if i + 2 < len(order):
            packs[i + 2], near_w[i + 1] = after((packs[i + 2], near_w[i + 1]))
            near_w.append(swap(packs[i + 2], "mp"))
        if graph == 0:
            planet = run_layer(
                layer, slots, last, core1, g_idx, planet, g_sib, g_rim, g_ws, g_wd, g_w2, g_b1, near_w[i], far_w
            )
            *planet, core1 = after((*(planet if last else (planet,)), core1))
            if not last:
                planet = planet[0]
                g_sib, g_rim = swap(planet, "batch"), rims(planet, True)
        else:
            regional = run_layer(
                layer, slots, last, core1, r_idx, regional, r_sib, r_rim, r_ws, r_wd, r_w2, r_b1, near_w[i], far_w
            )
            if not last:
                regional, core1 = after((regional, core1))
                r_sib, r_rim = swap(regional, "batch"), rims(regional, False)
    g_out = ordered(part, *gather_rows(*planet), 0)
    r_out = ordered(part, *gather_rows(*regional), 0)
    return g_out[None], r_out[None]


def solution(mesh):
    in_specs = (
        P(("groups", "batch"), "mesh", "mp"),
        P(("groups", "batch"), "mesh", "mp"),
        P("mesh", None),
        P("mesh"),
        P("mesh", None),
        P("mesh"),
        P("mesh"),
        P("mesh", None),
        P("mesh"),
        P(None, None, "mp"),
        P(None, None, "mp"),
        P(None, "mp"),
        P(None, "mp", None),
        P(None, None, "mp"),
        P(None, None, "mp"),
        P(None, "mp"),
        P(None, "mp", None),
    )
    out_specs = (P(("groups", "batch"), "mesh", "mp"), P(("groups", "batch"), "mesh", "mp"))
    square = mesh.shape["mp"] == 2 and mesh.shape["batch"] == 2
    return jax.shard_map(
        by_rows if square else by_features, mesh=mesh, in_specs=in_specs, out_specs=out_specs, check_vma=False
    )
```

```python
import functools

import jax
import jax.numpy as jnp
from jax import lax
from jax.experimental import pallas as pl
from jax.experimental.pallas import tpu as pltpu
from jax.sharding import PartitionSpec as P

LANES = 128
DEAD = -1e30
SMALL = pl.CostEstimate(flops=1, bytes_accessed=1, transcendentals=0)


def padded_2(shard, sides, width, wrap):
    for axis, dim in sides:
        size, length = (lax.axis_size(axis), shard.shape[dim])
        up = [(i, (i + 1) % size) for i in range(size if wrap else size - 1)]
        down = [(j, i) for i, j in up]
        last = lax.slice_in_dim(shard, length - width, length, axis=dim)
        leading = lax.slice_in_dim(shard, 0, width, axis=dim)
        before = lax.ppermute(last, axis, up)
        after = lax.ppermute(leading, axis, down)
        shard = jnp.concatenate([before, shard, after], axis=dim)
    return shard


def edge_sums(proj, near, nbr, count):
    slots = nbr.shape[1]
    live = jnp.arange(slots, dtype=jnp.int32)[None, :] < count[:, None]
    pre = proj[:, nbr].astype(jnp.float32) + near[:, :, None]
    acts = jnp.where(live[None, :, :, None], jax.nn.silu(pre), 0.0)
    return jnp.sum(acts, axis=2).astype(jnp.bfloat16)


def graph_layer(latent, nbr, count, w_send, w_recv, bias, w_out, wrap):
    rim = latent.shape[1] // 2
    own_full = lax.all_gather(latent, "mp", axis=2, tiled=True)
    padded_full = padded_2(own_full, (("mesh", 1),), rim, wrap)
    proj = jnp.dot(padded_full, w_send, preferred_element_type=jnp.float32).astype(jnp.bfloat16)
    near = jnp.dot(own_full, w_recv, preferred_element_type=jnp.float32) + bias.astype(jnp.float32)
    summed = edge_sums(proj, near, nbr, count)
    partial_prod = jnp.dot(summed, w_out, preferred_element_type=jnp.float32)
    update = lax.psum_scatter(
        partial_prod.astype(jnp.bfloat16), "mp", scatter_dimension=2, tiled=True
    ).astype(jnp.float32)
    return (latent.astype(jnp.float32) + update).astype(jnp.bfloat16)


def by_features(
    g_nodes, r_nodes, g_nbr, g_count, r_nbr, r_count, bnd_src, bnd_part, bnd_node,
    g_ws, g_wd, g_b1, g_w2, r_ws, r_wd, r_b1, r_w2,
):
    batch_rows, reg_rows, feats = r_nodes.shape
    dest = bnd_part[:, 0]
    outgoing = jnp.moveaxis(g_nodes[:, bnd_src], 1, 0)
    init = jnp.zeros((reg_rows + 1, batch_rows, feats), jnp.float32)
    target = dest * reg_rows + bnd_node
    mine = lax.axis_index("mesh")
    piece_rows = lax.all_gather(outgoing, "mesh", axis=0, tiled=True)
    piece_target = lax.all_gather(target, "mesh", axis=0, tiled=True)
    local = jnp.where(piece_target // reg_rows == mine, piece_target % reg_rows + 1, 0)
    landed = init.at[local].add(piece_rows.astype(jnp.float32))
    force = jnp.moveaxis(landed[1:], 1, 0)
    regional = (r_nodes.astype(jnp.float32) + force).astype(jnp.bfloat16)
    planet = g_nodes
    for layer in range(g_ws.shape[0]):
        planet = graph_layer(
            planet, g_nbr, g_count, g_ws[layer], g_wd[layer], g_b1[layer], g_w2[layer], True
        )
    for layer in range(r_ws.shape[0]):
        regional = graph_layer(
            regional, r_nbr, r_count, r_ws[layer], r_wd[layer], r_b1[layer], r_w2[layer], False
        )
    return (planet, regional)


def one_hot(flags):
    return jnp.where(flags, 1.0, 0.0).astype(jnp.bfloat16)


def pick_kernel(parts, cap, me_ref, bnd_ref, g_ref, *out_refs):
    rows = g_ref.shape[0]
    total = bnd_ref.shape[1]
    me = me_ref[0]
    src, part, node = (bnd_ref[i:i + 1, :] for i in range(3))
    lines = -(-parts // 8) * 8
    target = lax.rem(lax.broadcasted_iota(jnp.int32, (lines, total), 0) + me, parts)
    named = part == target
    before = one_hot(
        lax.broadcasted_iota(jnp.int32, (total, total), 0) < lax.broadcasted_iota(jnp.int32, (total, total), 1)
    )
    rank = jnp.dot(one_hot(named), before, preferred_element_type=jnp.float32)
    rank = jnp.where(named, rank, -1.0)
    source = one_hot(lax.broadcasted_iota(jnp.int32, (rows, total), 0) == src)
    line = lax.broadcasted_iota(jnp.int32, (16, total), 0)
    high = lax.shift_right_logical(node, 7)
    facts = jnp.where(line == 0, high, jnp.where(line == 1, node - high * 128, jnp.where(line == 2, 1, 0)))
    facts = facts.astype(jnp.float32).astype(jnp.bfloat16)
    place = lax.broadcasted_iota(jnp.int32, (cap, total), 0).astype(jnp.float32)
    across = (((1,), (1,)), ((), ()))
    for k in range(parts):
        chosen = one_hot(place == rank[k:k + 1, :])
        pick = lax.dot_general(chosen, source, across, preferred_element_type=jnp.float32).astype(jnp.bfloat16)
        out_refs[k][:cap, :] = jnp.dot(pick, g_ref[...], preferred_element_type=jnp.float32).astype(jnp.bfloat16)
        told = lax.dot_general(facts, chosen, across, preferred_element_type=jnp.float32)
        out_refs[k][cap:, :] = told.astype(jnp.bfloat16)


def pick_rows(me, bnd, nodes, parts, cap):
    vmem = pl.BlockSpec(memory_space=pltpu.VMEM)
    rows, feats = nodes.shape
    total = bnd.shape[1]
    piece = jax.ShapeDtypeStruct((cap + 16, feats), jnp.bfloat16)
    return pl.pallas_call(
        functools.partial(pick_kernel, parts, cap),
        out_shape=(piece,) * parts,
        in_specs=[pl.BlockSpec(memory_space=pltpu.SMEM), vmem, vmem],
        out_specs=(vmem,) * parts,
        compiler_params=pltpu.CompilerParams(vmem_limit_bytes=32 << 20),
        cost_estimate=SMALL,
        name="pick_rows",
    )(me, bnd, nodes)


def force_kernel(cap, first_ref, r_ref, *refs):
    pieces, (same_ref, other_ref) = refs[:-2], refs[-2:]
    half = same_ref.shape[0]
    first = first_ref[0]
    for out_ref, start in ((same_ref, first * half), (other_ref, (1 - first) * half)):
        start = pl.multiple_of(start, 16)
        row = (lax.broadcasted_iota(jnp.int32, (half, cap), 0) + start).astype(jnp.float32)
        total = r_ref[pl.ds(start, half), :].astype(jnp.float32)
        for piece in pieces:
            facts = piece[cap:, :].astype(jnp.float32)
            node = jnp.where(facts[2:3, :] > 0.5, facts[0:1, :] * 128.0 + facts[1:2, :], -1.0)
            total += jnp.dot(one_hot(row == node), piece[:cap, :], preferred_element_type=jnp.float32)
        out_ref[...] = total.astype(jnp.bfloat16)


def add_force(first, nodes, pieces, cap):
    vmem = pl.BlockSpec(memory_space=pltpu.VMEM)
    rows, feats = nodes.shape
    block = jax.ShapeDtypeStruct((rows // 2, feats), jnp.bfloat16)
    return pl.pallas_call(
        functools.partial(force_kernel, cap),
        out_shape=(block, block),
        in_specs=[pl.BlockSpec(memory_space=pltpu.SMEM)] + [vmem] * (1 + len(pieces)),
        out_specs=(vmem, vmem),
        compiler_params=pltpu.CompilerParams(vmem_limit_bytes=32 << 20),
        cost_estimate=SMALL,
        name="add_force",
    )(first, nodes, *pieces)


def layer_kernel(
    layer, slots, last, core_ref, idx_ref, own, sib, rim, bias, near_w, far_w, ws_hbm, wd_hbm, w2_hbm, *refs
):
    outs, refs = (refs[:2], refs[2:]) if last else (refs[:1], refs[1:])
    ws, wd, w2, ws_x, wd_x, w2_x, proj, near, summed, sems = refs
    rows, width = own.shape
    share = width // 2
    chunks = width // LANES
    part = chunks // 2
    core = core_ref[0]
    pairs = ((wd_hbm, wd), (ws_hbm, ws), (w2_hbm, w2))
    copies = [pltpu.make_async_copy(src.at[layer], dst, sems.at[i]) for i, (src, dst) in enumerate(pairs)]
    for copy in copies:
        copy.start()
    window = 3 * rows
    proj[0:8, :] = jnp.full((8, LANES), DEAD, jnp.float32)
    proj[4 * window + 4:4 * window + 16, :] = jnp.full((12, LANES), DEAD, jnp.float32)
    here, there = pl.multiple_of(core * share, 16), pl.multiple_of((1 - core) * share, 16)
    for spot, piece in ((here, near_w), (there, far_w)):
        ws_x[pl.ds(spot, share), :] = piece[0:share, :]
        wd_x[pl.ds(spot, share), :] = piece[share:2 * share, :]

    @pl.when(core == 0)
    def _():
        w2_x[:, :share] = near_w[2 * share:3 * share, :]
        w2_x[:, share:] = far_w[2 * share:3 * share, :]

    @pl.when(core != 0)
    def _():
        w2_x[:, share:] = near_w[2 * share:3 * share, :]
        w2_x[:, :share] = far_w[2 * share:3 * share, :]

    def put(dst, base, first, values):
        for c in range(values.shape[1] // LANES):
            dst[pl.ds(base * chunks + first + c, rows, stride=chunks), :] = values[:, c * LANES:(c + 1) * LANES] * 0.5

    def product(values, weights):
        return jnp.dot(values[...], weights[...], preferred_element_type=jnp.float32)

    b_own = bias[layer:layer + 1, :].astype(jnp.float32)
    b_other = near_w[3 * share:3 * share + 1, :].astype(jnp.float32)
    put(near, 0, part, product(own, wd_x) + b_other)
    put(proj, 1, part, product(own, ws_x))
    copies[0].wait()
    copies[1].wait()
    put(near, 0, 0, product(own, wd) + b_own)
    put(proj, 1, 0, product(own, ws))
    for ref, base in ((sib, rows + 1), (rim, 2 * rows + 1)):
        put(proj, base, 0, product(ref, ws))
        put(proj, base, part, product(ref, ws_x))
    low = lax.broadcasted_iota(jnp.int32, (8, LANES), 0) < chunks

    def nodes(q, carry):
        spot = pl.ds(pl.multiple_of(8 * q, 8), 8)
        mine = near[spot, :]
        total = None
        for j in range(slots):
            upper = proj[pl.ds(pl.multiple_of(idx_ref[j * rows + 2 * q], 4), 8), :]
            lower = proj[pl.ds(pl.multiple_of(idx_ref[j * rows + 2 * q + 1], 4), 8), :]
            y = jnp.where(low, upper, lower) + mine
            act = y * jnp.tanh(y) + y
            total = act if total is None else total + act
        summed[spot, :] = total
        return carry

    lax.fori_loop(0, rows // 2, nodes, 0, unroll=16)
    copies[2].wait()
    sums = [summed[pl.ds(c, rows, stride=chunks), :].astype(jnp.bfloat16) for c in range(chunks)]
    update = product(jnp.concatenate(sums[:part], 1), w2) + product(jnp.concatenate(sums[part:], 1), w2_x)
    result = (own[...].astype(jnp.float32) + update).astype(jnp.bfloat16)
    if not last:
        outs[0][...] = result
    else:
        @pl.when(core == 0)
        def _():
            outs[0][...] = result[:, :share]
            outs[1][...] = result[:, share:]

        @pl.when(core != 0)
        def _():
            outs[0][...] = result[:, share:]
            outs[1][...] = result[:, :share]


def run_layer(layer, slots, last, core, idx, own, sib, rim, ws, wd, w2, bias, near_w, far_w):
    rows, width = own.shape
    share = width // 2
    chunks = width // LANES
    smem = pl.BlockSpec(memory_space=pltpu.SMEM)
    vmem = pl.BlockSpec(memory_space=pltpu.VMEM)
    bf16, f32 = jnp.bfloat16, jnp.float32
    if last:
        out_shape = (jax.ShapeDtypeStruct((rows, share), bf16),) * 2
        out_specs = (vmem, vmem)
    else:
        out_shape, out_specs = jax.ShapeDtypeStruct((rows, width), bf16), vmem
    return pl.pallas_call(
        functools.partial(layer_kernel, layer, slots, last),
        out_shape=out_shape,
        in_specs=[smem] * 2 + [vmem] * 6 + [pl.BlockSpec(memory_space=pl.ANY)] * 3,
        out_specs=out_specs,
        scratch_shapes=[
            pltpu.VMEM((width, share), bf16),
            pltpu.VMEM((width, share), bf16),
            pltpu.VMEM((share, width), bf16),
            pltpu.VMEM((width, share), bf16),
            pltpu.VMEM((width, share), bf16),
            pltpu.VMEM((share, width), bf16),
            pltpu.VMEM((3 * rows * chunks + 96, LANES), f32),
            pltpu.VMEM((rows * chunks, LANES), f32),
            pltpu.VMEM((rows * chunks, LANES), f32),
            pltpu.SemaphoreType.DMA((3,)),
        ],
        compiler_params=pltpu.CompilerParams(vmem_limit_bytes=32 << 20),
        cost_estimate=pl.CostEstimate(flops=64 * rows * width * width, bytes_accessed=10 * rows * width, transcendentals=0),
        name="graph_layer",
    )(core, idx, own, sib, rim, bias, near_w, far_w, ws, wd, w2)


def edge_offsets(nbrs, counts, core):
    graphs, rows, slots = nbrs.shape
    half = rows // 2
    nbr = lax.dynamic_slice(nbrs.transpose(0, 2, 1), (0, 0, core * half), (graphs, slots, half)) - core * half
    count = lax.dynamic_slice(counts, (0, core * half), (graphs, half))
    low = nbr + jnp.where(core == 0, 2 * half, half)
    high = nbr - jnp.where(core == 0, half, 0)
    place = jnp.where(nbr < half, low, jnp.where(nbr < 2 * half, nbr - half, high))
    live = jnp.arange(slots, dtype=jnp.int32)[None, :, None] < count[:, None, :]
    place = jnp.where(live, place, 3 * half)
    odd = jnp.arange(half, dtype=jnp.int32) % 2
    return (4 * (place + 1 - odd)).reshape(graphs, slots * half)


def spread_rows(same, other):
    a = lax.ppermute(same, ("mp", "batch"), [(0, 0), (1, 2), (2, 1), (3, 3)])
    b = lax.ppermute(other, ("mp", "batch"), [(0, 1), (1, 3), (2, 0), (3, 2)])
    return a, b


def gather_rows(a, b):
    same = lax.ppermute(a, ("mp", "batch"), [(0, 0), (1, 2), (2, 1), (3, 3)])
    other = lax.ppermute(b, ("mp", "batch"), [(0, 2), (1, 0), (2, 3), (3, 1)])
    return same, other


def ordered(which, a, b, axis):
    return jnp.where(which == 0, jnp.concatenate([a, b], axis), jnp.concatenate([b, a], axis))


def swap(values, axis):
    return lax.ppermute(values, axis, [(0, 1), (1, 0)])


def rims(own, wrap):
    size = lax.axis_size("mesh")
    pairs = []
    for m in range(size):
        if wrap or m + 1 < size:
            pairs.append((2 * m + 1, 2 * ((m + 1) % size)))
        if wrap or m > 0:
            pairs.append((2 * m, 2 * ((m - 1) % size) + 1))
    return lax.ppermute(own, ("mesh", "batch"), pairs)


def pack_kernel(order, core_ref, g_bias, r_bias, *refs):
    weights, outs, sems = (refs[:3], refs[3:6]), refs[6:-1], refs[-1]
    share = g_bias.shape[1]
    here = pl.multiple_of(core_ref[0] * share, share)
    copies = []
    for (graph, layer), out in zip(order, outs):
        ws, wd, w2 = weights[graph]
        sources = (ws.at[layer, pl.ds(here, share), :], wd.at[layer, pl.ds(here, share), :], w2.at[layer, :, pl.ds(here, share)])
        for i, source in enumerate(sources):
            copies.append(pltpu.make_async_copy(source, out.at[i * share:(i + 1) * share, :], sems.at[len(copies)]))
            copies[-1].start()
    for (graph, layer), out in zip(order, outs):
        bias = (g_bias, r_bias)[graph][layer:layer + 1, :]
        out[3 * share:, :] = jnp.broadcast_to(bias, (16, share))
    for copy in copies:
        copy.wait()


def pack_weights(order, core, g_weights, g_bias, r_weights, r_bias):
    share = g_bias.shape[1]
    vmem = pl.BlockSpec(memory_space=pltpu.VMEM)
    hbm = pl.BlockSpec(memory_space=pltpu.HBM)
    return pl.pallas_call(
        functools.partial(pack_kernel, order),
        out_shape=(jax.ShapeDtypeStruct((3 * share + 16, share), jnp.bfloat16),) * len(order),
        in_specs=[pl.BlockSpec(memory_space=pltpu.SMEM)] + [vmem] * 2 + [hbm] * 6,
        out_specs=(vmem,) * len(order),
        scratch_shapes=[pltpu.SemaphoreType.DMA((3 * len(order),))],
        compiler_params=pltpu.CompilerParams(vmem_limit_bytes=60 << 20),
        cost_estimate=pl.CostEstimate(flops=256 * share**3, bytes_accessed=1, transcendentals=0),
        name="pack_weights",
    )(core, g_bias, r_bias, *g_weights, *r_weights)


def by_rows(
    g_nodes, r_nodes, g_nbr, g_count, r_nbr, r_count, bnd_src, bnd_part, bnd_node,
    g_ws, g_wd, g_b1, g_w2, r_ws, r_wd, r_b1, r_w2,
):
    part = lax.axis_index("mp")
    core = lax.axis_index("batch")
    parts = lax.axis_size("mesh")
    slots = g_nbr.shape[1]
    layers = g_ws.shape[0]
    rows = g_nodes.shape[1]
    half = rows // 2
    cap = 2 * bnd_src.shape[0] // parts
    me = lax.axis_index("mesh").reshape(1)
    core1 = core.reshape(1)
    g_own, r_own = g_nodes[0], r_nodes[0]
    g_weights, r_weights = (g_ws, g_wd, g_w2), (r_ws, r_wd, r_w2)
    after = lax.optimization_barrier

    bnd = jnp.stack([bnd_src, bnd_part[:, 0], bnd_node])
    pieces = pick_rows(me, bnd, g_own, parts, cap)
    landed = [pieces[0]]
    for k in range(1, parts):
        landed.append(lax.ppermute(pieces[k], "mesh", [(i, (i + k) % parts) for i in range(parts)]))
    landed[0], g_late = after((landed[0], g_own))
    same = lax.dynamic_slice(g_late, (part * half, 0), (half, g_own.shape[1]))
    other = lax.dynamic_slice(g_late, ((1 - part) * half, 0), (half, g_own.shape[1]))
    same, other, core1 = after((same, other, core1))
    g_a, g_b = spread_rows(same, other)
    idx = edge_offsets(jnp.stack([g_nbr, r_nbr]), jnp.stack([g_count, r_count]), core)

    order = [(graph, layer) for layer in range(layers) for graph in (0, 1)]
    g_a, g_b, core1 = after((g_a, g_b, core1))
    packs = list(pack_weights(order, core1, g_weights, g_b1, r_weights, r_b1))
    near_w = [swap(packs[0], "mp")]
    g_idx, r_idx = idx[0], idx[1]
    g_a, g_b, g_idx, r_idx, near_w[0], *landed = after((g_a, g_b, g_idx, r_idx, near_w[0], *landed))
    planet = ordered(core, g_a, g_b, 1)
    g_sib, g_rim = swap(planet, "batch"), rims(planet, True)
    *r_pair, packs[1], g_sib = after((*add_force(part.reshape(1), r_own, landed, cap), packs[1], g_sib))
    r_a, r_b = spread_rows(*r_pair)
    near_w.append(swap(packs[1], "mp"))
    r_a, r_b, g_rim = after((r_a, r_b, g_rim))
    regional, g_idx = after((ordered(core, r_a, r_b, 1), g_idx))
    r_sib, r_rim = swap(regional, "batch"), rims(regional, False)
    for i, (graph, layer) in enumerate(order):
        last = layer == layers - 1
        far_w = swap(near_w[i], "batch")
        if i + 1 < len(order):
            near_w[i + 1], core1 = after((near_w[i + 1], core1))
        if i + 2 < len(order):
            packs[i + 2], near_w[i + 1] = after((packs[i + 2], near_w[i + 1]))
            near_w.append(swap(packs[i + 2], "mp"))
        if graph == 0:
            planet = run_layer(
                layer, slots, last, core1, g_idx, planet, g_sib, g_rim, g_ws, g_wd, g_w2, g_b1, near_w[i], far_w
            )
            *planet, core1 = after((*(planet if last else (planet,)), core1))
            if not last:
                planet = planet[0]
                g_sib, g_rim = swap(planet, "batch"), rims(planet, True)
        else:
            regional = run_layer(
                layer, slots, last, core1, r_idx, regional, r_sib, r_rim, r_ws, r_wd, r_w2, r_b1, near_w[i], far_w
            )
            if not last:
                regional, core1 = after((regional, core1))
                r_sib, r_rim = swap(regional, "batch"), rims(regional, False)
    g_out = ordered(part, *gather_rows(*planet), 0)
    r_out = ordered(part, *gather_rows(*regional), 0)
    return g_out[None], r_out[None]


def solution(mesh):
    in_specs = (
        P(("groups", "batch"), "mesh", "mp"),
        P(("groups", "batch"), "mesh", "mp"),
        P("mesh", None),
        P("mesh"),
        P("mesh", None),
        P("mesh"),
        P("mesh"),
        P("mesh", None),
        P("mesh"),
        P(None, None, "mp"),
        P(None, None, "mp"),
        P(None, "mp"),
        P(None, "mp", None),
        P(None, None, "mp"),
        P(None, None, "mp"),
        P(None, "mp"),
        P(None, "mp", None),
    )
    out_specs = (P(("groups", "batch"), "mesh", "mp"), P(("groups", "batch"), "mesh", "mp"))
    square = mesh.shape["mp"] == 2 and mesh.shape["batch"] == 2
    return jax.shard_map(
        by_rows if square else by_features, mesh=mesh, in_specs=in_specs, out_specs=out_specs, check_vma=False
    )
```

```python
import functools

import jax
import jax.numpy as jnp
from jax import lax
from jax.experimental import pallas as pl
from jax.experimental.pallas import tpu as pltpu
from jax.sharding import PartitionSpec as P

LANES = 128
DEAD = -1e30
SMALL = pl.CostEstimate(flops=1, bytes_accessed=1, transcendentals=0)


def padded_2(shard, sides, width, wrap):
    for axis, dim in sides:
        size, length = (lax.axis_size(axis), shard.shape[dim])
        up = [(i, (i + 1) % size) for i in range(size if wrap else size - 1)]
        down = [(j, i) for i, j in up]
        last = lax.slice_in_dim(shard, length - width, length, axis=dim)
        leading = lax.slice_in_dim(shard, 0, width, axis=dim)
        before = lax.ppermute(last, axis, up)
        after = lax.ppermute(leading, axis, down)
        shard = jnp.concatenate([before, shard, after], axis=dim)
    return shard


def edge_sums(proj, near, nbr, count):
    slots = nbr.shape[1]
    live = jnp.arange(slots, dtype=jnp.int32)[None, :] < count[:, None]
    pre = proj[:, nbr].astype(jnp.float32) + near[:, :, None]
    acts = jnp.where(live[None, :, :, None], jax.nn.silu(pre), 0.0)
    return jnp.sum(acts, axis=2).astype(jnp.bfloat16)


def graph_layer(latent, nbr, count, w_send, w_recv, bias, w_out, wrap):
    rim = latent.shape[1] // 2
    own_full = lax.all_gather(latent, "mp", axis=2, tiled=True)
    padded_full = padded_2(own_full, (("mesh", 1),), rim, wrap)
    proj = jnp.dot(padded_full, w_send, preferred_element_type=jnp.float32).astype(jnp.bfloat16)
    near = jnp.dot(own_full, w_recv, preferred_element_type=jnp.float32) + bias.astype(jnp.float32)
    summed = edge_sums(proj, near, nbr, count)
    partial_prod = jnp.dot(summed, w_out, preferred_element_type=jnp.float32)
    update = lax.psum_scatter(
        partial_prod.astype(jnp.bfloat16), "mp", scatter_dimension=2, tiled=True
    ).astype(jnp.float32)
    return (latent.astype(jnp.float32) + update).astype(jnp.bfloat16)


def by_features(
    g_nodes, r_nodes, g_nbr, g_count, r_nbr, r_count, bnd_src, bnd_part, bnd_node,
    g_ws, g_wd, g_b1, g_w2, r_ws, r_wd, r_b1, r_w2,
):
    batch_rows, reg_rows, feats = r_nodes.shape
    dest = bnd_part[:, 0]
    outgoing = jnp.moveaxis(g_nodes[:, bnd_src], 1, 0)
    init = jnp.zeros((reg_rows + 1, batch_rows, feats), jnp.float32)
    target = dest * reg_rows + bnd_node
    mine = lax.axis_index("mesh")
    piece_rows = lax.all_gather(outgoing, "mesh", axis=0, tiled=True)
    piece_target = lax.all_gather(target, "mesh", axis=0, tiled=True)
    local = jnp.where(piece_target // reg_rows == mine, piece_target % reg_rows + 1, 0)
    landed = init.at[local].add(piece_rows.astype(jnp.float32))
    force = jnp.moveaxis(landed[1:], 1, 0)
    regional = (r_nodes.astype(jnp.float32) + force).astype(jnp.bfloat16)
    planet = g_nodes
    for layer in range(g_ws.shape[0]):
        planet = graph_layer(
            planet, g_nbr, g_count, g_ws[layer], g_wd[layer], g_b1[layer], g_w2[layer], True
        )
    for layer in range(r_ws.shape[0]):
        regional = graph_layer(
            regional, r_nbr, r_count, r_ws[layer], r_wd[layer], r_b1[layer], r_w2[layer], False
        )
    return (planet, regional)


def one_hot(flags):
    return jnp.where(flags, 1.0, 0.0).astype(jnp.bfloat16)


def pick_kernel(parts, cap, me_ref, bnd_ref, g_ref, *out_refs):
    rows = g_ref.shape[0]
    total = bnd_ref.shape[1]
    me = me_ref[0]
    src, part, node = (bnd_ref[i:i + 1, :] for i in range(3))
    lines = -(-parts // 8) * 8
    target = lax.rem(lax.broadcasted_iota(jnp.int32, (lines, total), 0) + me, parts)
    named = part == target
    before = one_hot(
        lax.broadcasted_iota(jnp.int32, (total, total), 0) < lax.broadcasted_iota(jnp.int32, (total, total), 1)
    )
    rank = jnp.dot(one_hot(named), before, preferred_element_type=jnp.float32)
    rank = jnp.where(named, rank, -1.0)
    source = one_hot(lax.broadcasted_iota(jnp.int32, (rows, total), 0) == src)
    line = lax.broadcasted_iota(jnp.int32, (16, total), 0)
    high = lax.shift_right_logical(node, 7)
    facts = jnp.where(line == 0, high, jnp.where(line == 1, node - high * 128, jnp.where(line == 2, 1, 0)))
    facts = facts.astype(jnp.float32).astype(jnp.bfloat16)
    place = lax.broadcasted_iota(jnp.int32, (cap, total), 0).astype(jnp.float32)
    across = (((1,), (1,)), ((), ()))
    for k in range(parts):
        chosen = one_hot(place == rank[k:k + 1, :])
        pick = lax.dot_general(chosen, source, across, preferred_element_type=jnp.float32).astype(jnp.bfloat16)
        out_refs[k][:cap, :] = jnp.dot(pick, g_ref[...], preferred_element_type=jnp.float32).astype(jnp.bfloat16)
        told = lax.dot_general(facts, chosen, across, preferred_element_type=jnp.float32)
        out_refs[k][cap:, :] = told.astype(jnp.bfloat16)


def pick_rows(me, bnd, nodes, parts, cap):
    vmem = pl.BlockSpec(memory_space=pltpu.VMEM)
    rows, feats = nodes.shape
    total = bnd.shape[1]
    piece = jax.ShapeDtypeStruct((cap + 16, feats), jnp.bfloat16)
    return pl.pallas_call(
        functools.partial(pick_kernel, parts, cap),
        out_shape=(piece,) * parts,
        in_specs=[pl.BlockSpec(memory_space=pltpu.SMEM), vmem, vmem],
        out_specs=(vmem,) * parts,
        compiler_params=pltpu.CompilerParams(vmem_limit_bytes=32 << 20),
        cost_estimate=SMALL,
        name="pick_rows",
    )(me, bnd, nodes)


def force_kernel(cap, first_ref, r_ref, *refs):
    pieces, (same_ref, other_ref) = refs[:-2], refs[-2:]
    half = same_ref.shape[0]
    first = first_ref[0]
    for out_ref, start in ((same_ref, first * half), (other_ref, (1 - first) * half)):
        start = pl.multiple_of(start, 16)
        row = (lax.broadcasted_iota(jnp.int32, (half, cap), 0) + start).astype(jnp.float32)
        total = r_ref[pl.ds(start, half), :].astype(jnp.float32)
        for piece in pieces:
            facts = piece[cap:, :].astype(jnp.float32)
            node = jnp.where(facts[2:3, :] > 0.5, facts[0:1, :] * 128.0 + facts[1:2, :], -1.0)
            total += jnp.dot(one_hot(row == node), piece[:cap, :], preferred_element_type=jnp.float32)
        out_ref[...] = total.astype(jnp.bfloat16)


def add_force(first, nodes, pieces, cap):
    vmem = pl.BlockSpec(memory_space=pltpu.VMEM)
    rows, feats = nodes.shape
    block = jax.ShapeDtypeStruct((rows // 2, feats), jnp.bfloat16)
    return pl.pallas_call(
        functools.partial(force_kernel, cap),
        out_shape=(block, block),
        in_specs=[pl.BlockSpec(memory_space=pltpu.SMEM)] + [vmem] * (1 + len(pieces)),
        out_specs=(vmem, vmem),
        compiler_params=pltpu.CompilerParams(vmem_limit_bytes=32 << 20),
        cost_estimate=SMALL,
        name="add_force",
    )(first, nodes, *pieces)


def layer_kernel(
    layer, slots, last, core_ref, idx_ref, own, sib, rim, bias, near_w, far_w, ws_hbm, wd_hbm, w2_hbm, *refs
):
    outs, refs = (refs[:2], refs[2:]) if last else (refs[:1], refs[1:])
    ws, wd, w2, ws_x, wd_x, w2_x, proj, near, summed, sems = refs
    rows, width = own.shape
    share = width // 2
    chunks = width // LANES
    part = chunks // 2
    core = core_ref[0]
    pairs = ((wd_hbm, wd), (ws_hbm, ws), (w2_hbm, w2))
    copies = [pltpu.make_async_copy(src.at[layer], dst, sems.at[i]) for i, (src, dst) in enumerate(pairs)]
    for copy in copies:
        copy.start()
    window = 3 * rows
    proj[0:8, :] = jnp.full((8, LANES), DEAD, jnp.float32)
    proj[4 * window + 4:4 * window + 16, :] = jnp.full((12, LANES), DEAD, jnp.float32)
    here, there = pl.multiple_of(core * share, 16), pl.multiple_of((1 - core) * share, 16)
    for spot, piece in ((here, near_w), (there, far_w)):
        ws_x[pl.ds(spot, share), :] = piece[0:share, :]
        wd_x[pl.ds(spot, share), :] = piece[share:2 * share, :]

    @pl.when(core == 0)
    def _():
        w2_x[:, :share] = near_w[2 * share:3 * share, :]
        w2_x[:, share:] = far_w[2 * share:3 * share, :]

    @pl.when(core != 0)
    def _():
        w2_x[:, share:] = near_w[2 * share:3 * share, :]
        w2_x[:, :share] = far_w[2 * share:3 * share, :]

    def put(dst, base, first, values):
        for c in range(values.shape[1] // LANES):
            dst[pl.ds(base * chunks + first + c, rows, stride=chunks), :] = values[:, c * LANES:(c + 1) * LANES] * 0.5

    def product(values, weights):
        return jnp.dot(values[...], weights[...], preferred_element_type=jnp.float32)

    b_own = bias[layer:layer + 1, :].astype(jnp.float32)
    b_other = near_w[3 * share:3 * share + 1, :].astype(jnp.float32)
    put(near, 0, part, product(own, wd_x) + b_other)
    put(proj, 1, part, product(own, ws_x))
    copies[0].wait()
    copies[1].wait()
    put(near, 0, 0, product(own, wd) + b_own)
    put(proj, 1, 0, product(own, ws))
    for ref, base in ((sib, rows + 1), (rim, 2 * rows + 1)):
        put(proj, base, 0, product(ref, ws))
        put(proj, base, part, product(ref, ws_x))
    low = lax.broadcasted_iota(jnp.int32, (8, LANES), 0) < chunks

    def nodes(q, carry):
        spot = pl.ds(pl.multiple_of(8 * q, 8), 8)
        mine = near[spot, :]
        total = None
        for j in range(slots):
            upper = proj[pl.ds(pl.multiple_of(idx_ref[j * rows + 2 * q], 4), 8), :]
            lower = proj[pl.ds(pl.multiple_of(idx_ref[j * rows + 2 * q + 1], 4), 8), :]
            y = jnp.where(low, upper, lower) + mine
            act = y * jnp.tanh(y) + y
            total = act if total is None else total + act
        summed[spot, :] = total
        return carry

    lax.fori_loop(0, rows // 2, nodes, 0, unroll=16)
    copies[2].wait()
    sums = [summed[pl.ds(c, rows, stride=chunks), :].astype(jnp.bfloat16) for c in range(chunks)]
    update = product(jnp.concatenate(sums[:part], 1), w2) + product(jnp.concatenate(sums[part:], 1), w2_x)
    result = (own[...].astype(jnp.float32) + update).astype(jnp.bfloat16)
    if not last:
        outs[0][...] = result
    else:
        @pl.when(core == 0)
        def _():
            outs[0][...] = result[:, :share]
            outs[1][...] = result[:, share:]

        @pl.when(core != 0)
        def _():
            outs[0][...] = result[:, share:]
            outs[1][...] = result[:, :share]


def run_layer(layer, slots, last, core, idx, own, sib, rim, ws, wd, w2, bias, near_w, far_w):
    rows, width = own.shape
    share = width // 2
    chunks = width // LANES
    smem = pl.BlockSpec(memory_space=pltpu.SMEM)
    vmem = pl.BlockSpec(memory_space=pltpu.VMEM)
    bf16, f32 = jnp.bfloat16, jnp.float32
    if last:
        out_shape = (jax.ShapeDtypeStruct((rows, share), bf16),) * 2
        out_specs = (vmem, vmem)
    else:
        out_shape, out_specs = jax.ShapeDtypeStruct((rows, width), bf16), vmem
    return pl.pallas_call(
        functools.partial(layer_kernel, layer, slots, last),
        out_shape=out_shape,
        in_specs=[smem] * 2 + [vmem] * 6 + [pl.BlockSpec(memory_space=pl.ANY)] * 3,
        out_specs=out_specs,
        scratch_shapes=[
            pltpu.VMEM((width, share), bf16),
            pltpu.VMEM((width, share), bf16),
            pltpu.VMEM((share, width), bf16),
            pltpu.VMEM((width, share), bf16),
            pltpu.VMEM((width, share), bf16),
            pltpu.VMEM((share, width), bf16),
            pltpu.VMEM((3 * rows * chunks + 96, LANES), f32),
            pltpu.VMEM((rows * chunks, LANES), f32),
            pltpu.VMEM((rows * chunks, LANES), f32),
            pltpu.SemaphoreType.DMA((3,)),
        ],
        compiler_params=pltpu.CompilerParams(vmem_limit_bytes=32 << 20),
        cost_estimate=pl.CostEstimate(flops=64 * rows * width * width, bytes_accessed=10 * rows * width, transcendentals=0),
        name="graph_layer",
    )(core, idx, own, sib, rim, bias, near_w, far_w, ws, wd, w2)


def edge_offsets(nbrs, counts, core):
    graphs, rows, slots = nbrs.shape
    half = rows // 2
    nbr = lax.dynamic_slice(nbrs.transpose(0, 2, 1), (0, 0, core * half), (graphs, slots, half)) - core * half
    count = lax.dynamic_slice(counts, (0, core * half), (graphs, half))
    low = nbr + jnp.where(core == 0, 2 * half, half)
    high = nbr - jnp.where(core == 0, half, 0)
    place = jnp.where(nbr < half, low, jnp.where(nbr < 2 * half, nbr - half, high))
    live = jnp.arange(slots, dtype=jnp.int32)[None, :, None] < count[:, None, :]
    place = jnp.where(live, place, 3 * half)
    odd = jnp.arange(half, dtype=jnp.int32) % 2
    return (4 * (place + 1 - odd)).reshape(graphs, slots * half)


def spread_rows(same, other):
    a = lax.ppermute(same, ("mp", "batch"), [(0, 0), (1, 2), (2, 1), (3, 3)])
    b = lax.ppermute(other, ("mp", "batch"), [(0, 1), (1, 3), (2, 0), (3, 2)])
    return a, b


def gather_rows(a, b):
    same = lax.ppermute(a, ("mp", "batch"), [(0, 0), (1, 2), (2, 1), (3, 3)])
    other = lax.ppermute(b, ("mp", "batch"), [(0, 2), (1, 0), (2, 3), (3, 1)])
    return same, other


def ordered(which, a, b, axis):
    return jnp.where(which == 0, jnp.concatenate([a, b], axis), jnp.concatenate([b, a], axis))


def swap(values, axis):
    return lax.ppermute(values, axis, [(0, 1), (1, 0)])


def rims(own, wrap):
    size = lax.axis_size("mesh")
    pairs = []
    for m in range(size):
        if wrap or m + 1 < size:
            pairs.append((2 * m + 1, 2 * ((m + 1) % size)))
        if wrap or m > 0:
            pairs.append((2 * m, 2 * ((m - 1) % size) + 1))
    return lax.ppermute(own, ("mesh", "batch"), pairs)


def pack_kernel(order, core_ref, g_bias, r_bias, *refs):
    weights, outs, sems = (refs[:3], refs[3:6]), refs[6:-1], refs[-1]
    share = g_bias.shape[1]
    here = pl.multiple_of(core_ref[0] * share, share)
    copies = []
    for (graph, layer), out in zip(order, outs):
        ws, wd, w2 = weights[graph]
        sources = (ws.at[layer, pl.ds(here, share), :], wd.at[layer, pl.ds(here, share), :], w2.at[layer, :, pl.ds(here, share)])
        for i, source in enumerate(sources):
            copies.append(pltpu.make_async_copy(source, out.at[i * share:(i + 1) * share, :], sems.at[len(copies)]))
            copies[-1].start()
    for (graph, layer), out in zip(order, outs):
        bias = (g_bias, r_bias)[graph][layer:layer + 1, :]
        out[3 * share:, :] = jnp.broadcast_to(bias, (16, share))
    for copy in copies:
        copy.wait()


def pack_weights(order, core, g_weights, g_bias, r_weights, r_bias):
    share = g_bias.shape[1]
    vmem = pl.BlockSpec(memory_space=pltpu.VMEM)
    hbm = pl.BlockSpec(memory_space=pltpu.HBM)
    return pl.pallas_call(
        functools.partial(pack_kernel, order),
        out_shape=(jax.ShapeDtypeStruct((3 * share + 16, share), jnp.bfloat16),) * len(order),
        in_specs=[pl.BlockSpec(memory_space=pltpu.SMEM)] + [vmem] * 2 + [hbm] * 6,
        out_specs=(vmem,) * len(order),
        scratch_shapes=[pltpu.SemaphoreType.DMA((3 * len(order),))],
        compiler_params=pltpu.CompilerParams(vmem_limit_bytes=60 << 20),
        cost_estimate=pl.CostEstimate(flops=256 * share**3, bytes_accessed=1, transcendentals=0),
        name="pack_weights",
    )(core, g_bias, r_bias, *g_weights, *r_weights)


def by_rows(
    g_nodes, r_nodes, g_nbr, g_count, r_nbr, r_count, bnd_src, bnd_part, bnd_node,
    g_ws, g_wd, g_b1, g_w2, r_ws, r_wd, r_b1, r_w2,
):
    part = lax.axis_index("mp")
    core = lax.axis_index("batch")
    parts = lax.axis_size("mesh")
    slots = g_nbr.shape[1]
    layers = g_ws.shape[0]
    rows = g_nodes.shape[1]
    half = rows // 2
    cap = 2 * bnd_src.shape[0] // parts
    me = lax.axis_index("mesh").reshape(1)
    core1 = core.reshape(1)
    g_own, r_own = g_nodes[0], r_nodes[0]
    g_weights, r_weights = (g_ws, g_wd, g_w2), (r_ws, r_wd, r_w2)
    after = lax.optimization_barrier

    bnd = jnp.stack([bnd_src, bnd_part[:, 0], bnd_node])
    pieces = pick_rows(me, bnd, g_own, parts, cap)
    landed = [pieces[0]]
    for k in range(1, parts):
        landed.append(lax.ppermute(pieces[k], "mesh", [(i, (i + k) % parts) for i in range(parts)]))
    landed[0], g_late = after((landed[0], g_own))
    same = lax.dynamic_slice(g_late, (part * half, 0), (half, g_own.shape[1]))
    other = lax.dynamic_slice(g_late, ((1 - part) * half, 0), (half, g_own.shape[1]))
    same, other, core1 = after((same, other, core1))
    g_a, g_b = spread_rows(same, other)
    idx = edge_offsets(jnp.stack([g_nbr, r_nbr]), jnp.stack([g_count, r_count]), core)

    order = [(graph, layer) for layer in range(layers) for graph in (0, 1)]
    packs = list(pack_weights(order, core1, g_weights, g_b1, r_weights, r_b1))
    landed[1], packs[0] = after((landed[1], packs[0]))
    near_w = [swap(packs[0], "mp")]
    g_idx, r_idx = idx[0], idx[1]
    g_a, g_b, g_idx, r_idx, packs[1], *landed = after((g_a, g_b, g_idx, r_idx, packs[1], *landed))
    planet = ordered(core, g_a, g_b, 1)
    g_sib, g_rim = swap(planet, "batch"), rims(planet, True)
    *r_pair, packs[1] = after((*add_force(part.reshape(1), r_own, landed, cap), packs[1]))
    r_a, r_b = spread_rows(*r_pair)
    near_w.append(swap(packs[1], "mp"))
    r_a, r_b, g_sib, g_rim, near_w[0] = after((r_a, r_b, g_sib, g_rim, near_w[0]))
    regional, g_idx = after((ordered(core, r_a, r_b, 1), g_idx))
    r_sib, r_rim = swap(regional, "batch"), rims(regional, False)
    for i, (graph, layer) in enumerate(order):
        last = layer == layers - 1
        far_w = swap(near_w[i], "batch")
        if graph == 0:
            planet = run_layer(
                layer, slots, last, core1, g_idx, planet, g_sib, g_rim, g_ws, g_wd, g_w2, g_b1, near_w[i], far_w
            )
            *planet, core1, near_w[i + 1] = after((*(planet if last else (planet,)), core1, near_w[i + 1]))
            if not last:
                planet = planet[0]
                g_sib, g_rim = swap(planet, "batch"), rims(planet, True)
        else:
            regional = run_layer(
                layer, slots, last, core1, r_idx, regional, r_sib, r_rim, r_ws, r_wd, r_w2, r_b1, near_w[i], far_w
            )
            if not last:
                regional, core1, near_w[i + 1] = after((regional, core1, near_w[i + 1]))
                r_sib, r_rim = swap(regional, "batch"), rims(regional, False)
        if i + 2 < len(order):
            packs[i + 2], near_w[i + 1] = after((packs[i + 2], near_w[i + 1]))
            near_w.append(swap(packs[i + 2], "mp"))
    g_out = ordered(part, *gather_rows(*planet), 0)
    r_out = ordered(part, *gather_rows(*regional), 0)
    return g_out[None], r_out[None]


def solution(mesh):
    in_specs = (
        P(("groups", "batch"), "mesh", "mp"),
        P(("groups", "batch"), "mesh", "mp"),
        P("mesh", None),
        P("mesh"),
        P("mesh", None),
        P("mesh"),
        P("mesh"),
        P("mesh", None),
        P("mesh"),
        P(None, None, "mp"),
        P(None, None, "mp"),
        P(None, "mp"),
        P(None, "mp", None),
        P(None, None, "mp"),
        P(None, None, "mp"),
        P(None, "mp"),
        P(None, "mp", None),
    )
    out_specs = (P(("groups", "batch"), "mesh", "mp"), P(("groups", "batch"), "mesh", "mp"))
    square = mesh.shape["mp"] == 2 and mesh.shape["batch"] == 2
    return jax.shard_map(
        by_rows if square else by_features, mesh=mesh, in_specs=in_specs, out_specs=out_specs, check_vma=False
    )
```

```python
import functools

import jax
import jax.numpy as jnp
from jax import lax
from jax.experimental import pallas as pl
from jax.experimental.pallas import tpu as pltpu
from jax.sharding import PartitionSpec as P

LANES = 128
DEAD = -1e30
SMALL = pl.CostEstimate(flops=1, bytes_accessed=1, transcendentals=0)


def padded_2(shard, sides, width, wrap):
    for axis, dim in sides:
        size, length = (lax.axis_size(axis), shard.shape[dim])
        up = [(i, (i + 1) % size) for i in range(size if wrap else size - 1)]
        down = [(j, i) for i, j in up]
        last = lax.slice_in_dim(shard, length - width, length, axis=dim)
        leading = lax.slice_in_dim(shard, 0, width, axis=dim)
        before = lax.ppermute(last, axis, up)
        after = lax.ppermute(leading, axis, down)
        shard = jnp.concatenate([before, shard, after], axis=dim)
    return shard


def edge_sums(proj, near, nbr, count):
    slots = nbr.shape[1]
    live = jnp.arange(slots, dtype=jnp.int32)[None, :] < count[:, None]
    pre = proj[:, nbr].astype(jnp.float32) + near[:, :, None]
    acts = jnp.where(live[None, :, :, None], jax.nn.silu(pre), 0.0)
    return jnp.sum(acts, axis=2).astype(jnp.bfloat16)


def graph_layer(latent, nbr, count, w_send, w_recv, bias, w_out, wrap):
    rim = latent.shape[1] // 2
    own_full = lax.all_gather(latent, "mp", axis=2, tiled=True)
    padded_full = padded_2(own_full, (("mesh", 1),), rim, wrap)
    proj = jnp.dot(padded_full, w_send, preferred_element_type=jnp.float32).astype(jnp.bfloat16)
    near = jnp.dot(own_full, w_recv, preferred_element_type=jnp.float32) + bias.astype(jnp.float32)
    summed = edge_sums(proj, near, nbr, count)
    partial_prod = jnp.dot(summed, w_out, preferred_element_type=jnp.float32)
    update = lax.psum_scatter(
        partial_prod.astype(jnp.bfloat16), "mp", scatter_dimension=2, tiled=True
    ).astype(jnp.float32)
    return (latent.astype(jnp.float32) + update).astype(jnp.bfloat16)


def by_features(
    g_nodes, r_nodes, g_nbr, g_count, r_nbr, r_count, bnd_src, bnd_part, bnd_node,
    g_ws, g_wd, g_b1, g_w2, r_ws, r_wd, r_b1, r_w2,
):
    batch_rows, reg_rows, feats = r_nodes.shape
    dest = bnd_part[:, 0]
    outgoing = jnp.moveaxis(g_nodes[:, bnd_src], 1, 0)
    init = jnp.zeros((reg_rows + 1, batch_rows, feats), jnp.float32)
    target = dest * reg_rows + bnd_node
    mine = lax.axis_index("mesh")
    piece_rows = lax.all_gather(outgoing, "mesh", axis=0, tiled=True)
    piece_target = lax.all_gather(target, "mesh", axis=0, tiled=True)
    local = jnp.where(piece_target // reg_rows == mine, piece_target % reg_rows + 1, 0)
    landed = init.at[local].add(piece_rows.astype(jnp.float32))
    force = jnp.moveaxis(landed[1:], 1, 0)
    regional = (r_nodes.astype(jnp.float32) + force).astype(jnp.bfloat16)
    planet = g_nodes
    for layer in range(g_ws.shape[0]):
        planet = graph_layer(
            planet, g_nbr, g_count, g_ws[layer], g_wd[layer], g_b1[layer], g_w2[layer], True
        )
    for layer in range(r_ws.shape[0]):
        regional = graph_layer(
            regional, r_nbr, r_count, r_ws[layer], r_wd[layer], r_b1[layer], r_w2[layer], False
        )
    return (planet, regional)


def one_hot(flags):
    return jnp.where(flags, 1.0, 0.0).astype(jnp.bfloat16)


def pick_kernel(parts, cap, me_ref, bnd_ref, g_ref, *out_refs):
    rows = g_ref.shape[0]
    total = bnd_ref.shape[1]
    me = me_ref[0]
    src, part, node = (bnd_ref[i:i + 1, :] for i in range(3))
    lines = -(-parts // 8) * 8
    target = lax.rem(lax.broadcasted_iota(jnp.int32, (lines, total), 0) + me, parts)
    named = part == target
    before = one_hot(
        lax.broadcasted_iota(jnp.int32, (total, total), 0) < lax.broadcasted_iota(jnp.int32, (total, total), 1)
    )
    rank = jnp.dot(one_hot(named), before, preferred_element_type=jnp.float32)
    rank = jnp.where(named, rank, -1.0)
    source = one_hot(lax.broadcasted_iota(jnp.int32, (rows, total), 0) == src)
    line = lax.broadcasted_iota(jnp.int32, (16, total), 0)
    high = lax.shift_right_logical(node, 7)
    facts = jnp.where(line == 0, high, jnp.where(line == 1, node - high * 128, jnp.where(line == 2, 1, 0)))
    facts = facts.astype(jnp.float32).astype(jnp.bfloat16)
    place = lax.broadcasted_iota(jnp.int32, (cap, total), 0).astype(jnp.float32)
    across = (((1,), (1,)), ((), ()))
    for k in range(parts):
        chosen = one_hot(place == rank[k:k + 1, :])
        pick = lax.dot_general(chosen, source, across, preferred_element_type=jnp.float32).astype(jnp.bfloat16)
        out_refs[k][:cap, :] = jnp.dot(pick, g_ref[...], preferred_element_type=jnp.float32).astype(jnp.bfloat16)
        told = lax.dot_general(facts, chosen, across, preferred_element_type=jnp.float32)
        out_refs[k][cap:, :] = told.astype(jnp.bfloat16)


def pick_rows(me, bnd, nodes, parts, cap):
    vmem = pl.BlockSpec(memory_space=pltpu.VMEM)
    rows, feats = nodes.shape
    total = bnd.shape[1]
    piece = jax.ShapeDtypeStruct((cap + 16, feats), jnp.bfloat16)
    return pl.pallas_call(
        functools.partial(pick_kernel, parts, cap),
        out_shape=(piece,) * parts,
        in_specs=[pl.BlockSpec(memory_space=pltpu.SMEM), vmem, vmem],
        out_specs=(vmem,) * parts,
        compiler_params=pltpu.CompilerParams(vmem_limit_bytes=32 << 20),
        cost_estimate=SMALL,
        name="pick_rows",
    )(me, bnd, nodes)


def force_kernel(cap, first_ref, r_ref, *refs):
    pieces, (same_ref, other_ref) = refs[:-2], refs[-2:]
    half = same_ref.shape[0]
    first = first_ref[0]
    for out_ref, start in ((same_ref, first * half), (other_ref, (1 - first) * half)):
        start = pl.multiple_of(start, 16)
        row = (lax.broadcasted_iota(jnp.int32, (half, cap), 0) + start).astype(jnp.float32)
        total = r_ref[pl.ds(start, half), :].astype(jnp.float32)
        for piece in pieces:
            facts = piece[cap:, :].astype(jnp.float32)
            node = jnp.where(facts[2:3, :] > 0.5, facts[0:1, :] * 128.0 + facts[1:2, :], -1.0)
            total += jnp.dot(one_hot(row == node), piece[:cap, :], preferred_element_type=jnp.float32)
        out_ref[...] = total.astype(jnp.bfloat16)


def add_force(first, nodes, pieces, cap):
    vmem = pl.BlockSpec(memory_space=pltpu.VMEM)
    rows, feats = nodes.shape
    block = jax.ShapeDtypeStruct((rows // 2, feats), jnp.bfloat16)
    return pl.pallas_call(
        functools.partial(force_kernel, cap),
        out_shape=(block, block),
        in_specs=[pl.BlockSpec(memory_space=pltpu.SMEM)] + [vmem] * (1 + len(pieces)),
        out_specs=(vmem, vmem),
        compiler_params=pltpu.CompilerParams(vmem_limit_bytes=32 << 20),
        cost_estimate=SMALL,
        name="add_force",
    )(first, nodes, *pieces)


def layer_kernel(
    layer, graph, slots, last, spot_ref, idx_ref, own, sib, rim, bias, w_a, w_b, w_c, w_d, ws_hbm, wd_hbm, w2_hbm, *refs
):
    outs, refs = (refs[:2], refs[2:]) if last else (refs[:1], refs[1:])
    ws, wd, w2, ws_x, wd_x, w2_x, proj, near, summed, sems = refs
    rows, width = own.shape
    share = width // 2
    chunks = width // LANES
    part = chunks // 2
    group, core = spot_ref[0], spot_ref[1]
    pairs = ((wd_hbm, wd), (ws_hbm, ws), (w2_hbm, w2))
    copies = [pltpu.make_async_copy(src.at[layer], dst, sems.at[i]) for i, (src, dst) in enumerate(pairs)]
    for copy in copies:
        copy.start()
    window = 3 * rows
    proj[0:8, :] = jnp.full((8, LANES), DEAD, jnp.float32)
    proj[4 * window + 4:4 * window + 16, :] = jnp.full((12, LANES), DEAD, jnp.float32)
    half = share // 2
    base = graph * (3 * half + 16)
    pieces = ((group, core, w_a), (1 - group, core, w_b), (group, 1 - core, w_c), (1 - group, 1 - core, w_d))
    for y, c, piece in pieces:
        spot = pl.ds(pl.multiple_of((2 * c + y) * half, half), half)
        ws_x[spot, :] = piece[base:base + half, :]
        wd_x[spot, :] = piece[base + half:base + 2 * half, :]

    def place(left, right):
        for here, there, y in ((left[0], right[0], group), (left[1], right[1], 1 - group)):
            spot = pl.ds(pl.multiple_of(y * half, half), half)
            w2_x[spot, :share] = here[base + 2 * half:base + 3 * half, :]
            w2_x[spot, share:] = there[base + 2 * half:base + 3 * half, :]

    @pl.when(core == 0)
    def _():
        place((w_a, w_b), (w_c, w_d))

    @pl.when(core != 0)
    def _():
        place((w_c, w_d), (w_a, w_b))

    def put(dst, base, first, values):
        for c in range(values.shape[1] // LANES):
            dst[pl.ds(base * chunks + first + c, rows, stride=chunks), :] = values[:, c * LANES:(c + 1) * LANES] * 0.5

    def product(values, weights):
        return jnp.dot(values[...], weights[...], preferred_element_type=jnp.float32)

    b_own = bias[layer:layer + 1, :].astype(jnp.float32)
    b_other = w_a[base + 3 * half:base + 3 * half + 1, :].astype(jnp.float32)
    put(near, 0, part, product(own, wd_x) + b_other)
    put(proj, 1, part, product(own, ws_x))
    copies[0].wait()
    copies[1].wait()
    put(near, 0, 0, product(own, wd) + b_own)
    put(proj, 1, 0, product(own, ws))
    for ref, base in ((sib, rows + 1), (rim, 2 * rows + 1)):
        put(proj, base, 0, product(ref, ws))
        put(proj, base, part, product(ref, ws_x))
    low = lax.broadcasted_iota(jnp.int32, (8, LANES), 0) < chunks

    def nodes(q, carry):
        spot = pl.ds(pl.multiple_of(8 * q, 8), 8)
        mine = near[spot, :]
        total = None
        for j in range(slots):
            upper = proj[pl.ds(pl.multiple_of(idx_ref[j * rows + 2 * q], 4), 8), :]
            lower = proj[pl.ds(pl.multiple_of(idx_ref[j * rows + 2 * q + 1], 4), 8), :]
            y = jnp.where(low, upper, lower) + mine
            act = y * jnp.tanh(y) + y
            total = act if total is None else total + act
        summed[spot, :] = total
        return carry

    lax.fori_loop(0, rows // 2, nodes, 0, unroll=16)
    copies[2].wait()
    sums = [summed[pl.ds(c, rows, stride=chunks), :].astype(jnp.bfloat16) for c in range(chunks)]
    update = product(jnp.concatenate(sums[:part], 1), w2) + product(jnp.concatenate(sums[part:], 1), w2_x)
    result = (own[...].astype(jnp.float32) + update).astype(jnp.bfloat16)
    if not last:
        outs[0][...] = result
    else:
        @pl.when(core == 0)
        def _():
            outs[0][...] = result[:, :share]
            outs[1][...] = result[:, share:]

        @pl.when(core != 0)
        def _():
            outs[0][...] = result[:, share:]
            outs[1][...] = result[:, :share]


def run_layer(layer, graph, slots, last, spot, idx, own, sib, rim, ws, wd, w2, bias, pieces):
    rows, width = own.shape
    share = width // 2
    chunks = width // LANES
    smem = pl.BlockSpec(memory_space=pltpu.SMEM)
    vmem = pl.BlockSpec(memory_space=pltpu.VMEM)
    bf16, f32 = jnp.bfloat16, jnp.float32
    if last:
        out_shape = (jax.ShapeDtypeStruct((rows, share), bf16),) * 2
        out_specs = (vmem, vmem)
    else:
        out_shape, out_specs = jax.ShapeDtypeStruct((rows, width), bf16), vmem
    return pl.pallas_call(
        functools.partial(layer_kernel, layer, graph, slots, last),
        out_shape=out_shape,
        in_specs=[smem] * 2 + [vmem] * 8 + [pl.BlockSpec(memory_space=pl.ANY)] * 3,
        out_specs=out_specs,
        scratch_shapes=[
            pltpu.VMEM((width, share), bf16),
            pltpu.VMEM((width, share), bf16),
            pltpu.VMEM((share, width), bf16),
            pltpu.VMEM((width, share), bf16),
            pltpu.VMEM((width, share), bf16),
            pltpu.VMEM((share, width), bf16),
            pltpu.VMEM((3 * rows * chunks + 96, LANES), f32),
            pltpu.VMEM((rows * chunks, LANES), f32),
            pltpu.VMEM((rows * chunks, LANES), f32),
            pltpu.SemaphoreType.DMA((3,)),
        ],
        compiler_params=pltpu.CompilerParams(vmem_limit_bytes=32 << 20),
        cost_estimate=pl.CostEstimate(flops=64 * rows * width * width, bytes_accessed=10 * rows * width, transcendentals=0),
        name="graph_layer",
    )(spot, idx, own, sib, rim, bias, *pieces, ws, wd, w2)


def edge_offsets(nbrs, counts, core):
    graphs, rows, slots = nbrs.shape
    half = rows // 2
    nbr = lax.dynamic_slice(nbrs.transpose(0, 2, 1), (0, 0, core * half), (graphs, slots, half)) - core * half
    count = lax.dynamic_slice(counts, (0, core * half), (graphs, half))
    low = nbr + jnp.where(core == 0, 2 * half, half)
    high = nbr - jnp.where(core == 0, half, 0)
    place = jnp.where(nbr < half, low, jnp.where(nbr < 2 * half, nbr - half, high))
    live = jnp.arange(slots, dtype=jnp.int32)[None, :, None] < count[:, None, :]
    place = jnp.where(live, place, 3 * half)
    odd = jnp.arange(half, dtype=jnp.int32) % 2
    return (4 * (place + 1 - odd)).reshape(graphs, slots * half)


def spread_rows(same, other):
    a = lax.ppermute(same, ("mp", "batch"), [(0, 0), (1, 2), (2, 1), (3, 3)])
    b = lax.ppermute(other, ("mp", "batch"), [(0, 1), (1, 3), (2, 0), (3, 2)])
    return a, b


def gather_rows(a, b):
    same = lax.ppermute(a, ("mp", "batch"), [(0, 0), (1, 2), (2, 1), (3, 3)])
    other = lax.ppermute(b, ("mp", "batch"), [(0, 2), (1, 0), (2, 3), (3, 1)])
    return same, other


def ordered(which, a, b, axis):
    return jnp.where(which == 0, jnp.concatenate([a, b], axis), jnp.concatenate([b, a], axis))


def swap(values, axis):
    return lax.ppermute(values, axis, [(0, 1), (1, 0)])


def rims(own, wrap):
    size = lax.axis_size("mesh")
    pairs = []
    for m in range(size):
        if wrap or m + 1 < size:
            pairs.append((2 * m + 1, 2 * ((m + 1) % size)))
        if wrap or m > 0:
            pairs.append((2 * m, 2 * ((m - 1) % size) + 1))
    return lax.ppermute(own, ("mesh", "batch"), pairs)


def all_pieces(near_w, across):
    return near_w, across, swap(near_w, "batch"), swap(across, "batch")


def pack_kernel(graphs, spot_ref, g_bias, r_bias, *refs):
    weights, outs, sems = (refs[:3], refs[3:6]), refs[6:-1], refs[-1]
    share = g_bias.shape[1]
    half = share // 2
    group, core = spot_ref[0], spot_ref[1]
    rows = pl.ds(pl.multiple_of((2 * core + group) * half, half), half)
    columns = pl.ds(pl.multiple_of(core * share, share), share)
    copies = []
    for layer, out in enumerate(outs):
        for graph in range(graphs):
            ws, wd, w2 = weights[graph]
            base = graph * (3 * half + 16)
            sources = (
                ws.at[layer, rows, :], wd.at[layer, rows, :],
                w2.at[layer, pl.ds(pl.multiple_of(group * half, half), half), columns],
            )
            for i, source in enumerate(sources):
                spot = base + i * half
                copies.append(pltpu.make_async_copy(source, out.at[spot:spot + half, :], sems.at[len(copies)]))
                copies[-1].start()
    for layer, out in enumerate(outs):
        for graph in range(graphs):
            base = graph * (3 * half + 16) + 3 * half
            bias = (g_bias, r_bias)[graph][layer:layer + 1, :]
            out[base:base + 16, :] = jnp.broadcast_to(bias, (16, share))
    for copy in copies:
        copy.wait()


def pack_weights(spot, g_weights, g_bias, r_weights, r_bias):
    layers, share = g_bias.shape
    graphs = 2
    vmem = pl.BlockSpec(memory_space=pltpu.VMEM)
    hbm = pl.BlockSpec(memory_space=pltpu.HBM)
    size = graphs * (3 * share // 2 + 16)
    return pl.pallas_call(
        functools.partial(pack_kernel, graphs),
        out_shape=(jax.ShapeDtypeStruct((size, share), jnp.bfloat16),) * layers,
        in_specs=[pl.BlockSpec(memory_space=pltpu.SMEM)] + [vmem] * 2 + [hbm] * 6,
        out_specs=(vmem,) * layers,
        scratch_shapes=[pltpu.SemaphoreType.DMA((3 * graphs * layers,))],
        compiler_params=pltpu.CompilerParams(vmem_limit_bytes=60 << 20),
        cost_estimate=pl.CostEstimate(flops=256 * share**3, bytes_accessed=1, transcendentals=0),
        name="pack_weights",
    )(spot, g_bias, r_bias, *g_weights, *r_weights)


def by_rows(
    g_nodes, r_nodes, g_nbr, g_count, r_nbr, r_count, bnd_src, bnd_part, bnd_node,
    g_ws, g_wd, g_b1, g_w2, r_ws, r_wd, r_b1, r_w2,
):
    part = lax.axis_index("mp")
    core = lax.axis_index("batch")
    parts = lax.axis_size("mesh")
    slots = g_nbr.shape[1]
    layers = g_ws.shape[0]
    rows = g_nodes.shape[1]
    half = rows // 2
    cap = 2 * bnd_src.shape[0] // parts
    me = lax.axis_index("mesh").reshape(1)
    spot = jnp.stack([lax.axis_index("groups"), core])
    g_own, r_own = g_nodes[0], r_nodes[0]
    g_weights, r_weights = (g_ws, g_wd, g_w2), (r_ws, r_wd, r_w2)
    after = lax.optimization_barrier

    bnd = jnp.stack([bnd_src, bnd_part[:, 0], bnd_node])
    pieces = pick_rows(me, bnd, g_own, parts, cap)
    landed = [pieces[0]]
    for k in range(1, parts):
        landed.append(lax.ppermute(pieces[k], "mesh", [(i, (i + k) % parts) for i in range(parts)]))
    landed[0], g_late = after((landed[0], g_own))
    same = lax.dynamic_slice(g_late, (part * half, 0), (half, g_own.shape[1]))
    other = lax.dynamic_slice(g_late, ((1 - part) * half, 0), (half, g_own.shape[1]))
    same, other, spot = after((same, other, spot))
    g_a, g_b = spread_rows(same, other)
    idx = edge_offsets(jnp.stack([g_nbr, r_nbr]), jnp.stack([g_count, r_count]), core)

    g_a, g_b, spot = after((g_a, g_b, spot))
    packs = list(pack_weights(spot, g_weights, g_b1, r_weights, r_b1))
    near_w = swap(packs[0], "mp")
    g_idx, r_idx = idx[0], idx[1]
    g_a, g_b, g_idx, r_idx, *landed = after((g_a, g_b, g_idx, r_idx, *landed))
    planet = ordered(core, g_a, g_b, 1)
    g_sib, g_rim = swap(planet, "batch"), rims(planet, True)
    *r_pair, near_w, packs[1:] = after((*add_force(part.reshape(1), r_own, landed, cap), near_w, packs[1:]))
    across = swap(near_w, "groups")
    r_a, r_b = spread_rows(*r_pair)
    r_a, r_b, g_sib, g_rim, across = after((r_a, r_b, g_sib, g_rim, across))
    pieces = all_pieces(near_w, across)
    later = [swap(pack, "mp") for pack in packs[1:]]
    regional, g_idx, later = after((ordered(core, r_a, r_b, 1), g_idx, later))
    r_sib, r_rim = swap(regional, "batch"), rims(regional, False)
    for layer in range(layers):
        last = layer == layers - 1
        planet = run_layer(
            layer, 0, slots, last, spot, g_idx, planet, g_sib, g_rim, g_ws, g_wd, g_w2, g_b1, pieces
        )
        *planet, spot = after((*(planet if last else (planet,)), spot))
        if not last:
            planet = planet[0]
            g_sib, g_rim = swap(planet, "batch"), rims(planet, True)
            across = swap(later[layer], "groups")
        regional = run_layer(
            layer, 1, slots, last, spot, r_idx, regional, r_sib, r_rim, r_ws, r_wd, r_w2, r_b1, pieces
        )
        if not last:
            regional, spot = after((regional, spot))
            r_sib, r_rim = swap(regional, "batch"), rims(regional, False)
            pieces = all_pieces(later[layer], across)
    g_out = ordered(part, *gather_rows(*planet), 0)
    g_out, *regional_rows = after((g_out, *gather_rows(*regional)))
    r_out = ordered(part, *regional_rows, 0)
    return g_out[None], r_out[None]


def solution(mesh):
    in_specs = (
        P(("groups", "batch"), "mesh", "mp"),
        P(("groups", "batch"), "mesh", "mp"),
        P("mesh", None),
        P("mesh"),
        P("mesh", None),
        P("mesh"),
        P("mesh"),
        P("mesh", None),
        P("mesh"),
        P(None, None, "mp"),
        P(None, None, "mp"),
        P(None, "mp"),
        P(None, "mp", None),
        P(None, None, "mp"),
        P(None, None, "mp"),
        P(None, "mp"),
        P(None, "mp", None),
    )
    out_specs = (P(("groups", "batch"), "mesh", "mp"), P(("groups", "batch"), "mesh", "mp"))
    square = mesh.shape["mp"] == 2 and mesh.shape["batch"] == 2 and mesh.shape["groups"] == 2
    return jax.shard_map(
        by_rows if square else by_features, mesh=mesh, in_specs=in_specs, out_specs=out_specs, check_vma=False
    )
```

```python
import functools

import jax
import jax.numpy as jnp
from jax import lax
from jax.experimental import pallas as pl
from jax.experimental.pallas import tpu as pltpu
from jax.sharding import PartitionSpec as P

LANES = 128
DEAD = -1e30
SMALL = pl.CostEstimate(flops=1, bytes_accessed=1, transcendentals=0)


def padded_2(shard, sides, width, wrap):
    for axis, dim in sides:
        size, length = (lax.axis_size(axis), shard.shape[dim])
        up = [(i, (i + 1) % size) for i in range(size if wrap else size - 1)]
        down = [(j, i) for i, j in up]
        last = lax.slice_in_dim(shard, length - width, length, axis=dim)
        leading = lax.slice_in_dim(shard, 0, width, axis=dim)
        before = lax.ppermute(last, axis, up)
        after = lax.ppermute(leading, axis, down)
        shard = jnp.concatenate([before, shard, after], axis=dim)
    return shard


def edge_sums(proj, near, nbr, count):
    slots = nbr.shape[1]
    live = jnp.arange(slots, dtype=jnp.int32)[None, :] < count[:, None]
    pre = proj[:, nbr].astype(jnp.float32) + near[:, :, None]
    acts = jnp.where(live[None, :, :, None], jax.nn.silu(pre), 0.0)
    return jnp.sum(acts, axis=2).astype(jnp.bfloat16)


def graph_layer(latent, nbr, count, w_send, w_recv, bias, w_out, wrap):
    rim = latent.shape[1] // 2
    own_full = lax.all_gather(latent, "mp", axis=2, tiled=True)
    padded_full = padded_2(own_full, (("mesh", 1),), rim, wrap)
    proj = jnp.dot(padded_full, w_send, preferred_element_type=jnp.float32).astype(jnp.bfloat16)
    near = jnp.dot(own_full, w_recv, preferred_element_type=jnp.float32) + bias.astype(jnp.float32)
    summed = edge_sums(proj, near, nbr, count)
    partial_prod = jnp.dot(summed, w_out, preferred_element_type=jnp.float32)
    update = lax.psum_scatter(
        partial_prod.astype(jnp.bfloat16), "mp", scatter_dimension=2, tiled=True
    ).astype(jnp.float32)
    return (latent.astype(jnp.float32) + update).astype(jnp.bfloat16)


def by_features(
    g_nodes, r_nodes, g_nbr, g_count, r_nbr, r_count, bnd_src, bnd_part, bnd_node,
    g_ws, g_wd, g_b1, g_w2, r_ws, r_wd, r_b1, r_w2,
):
    batch_rows, reg_rows, feats = r_nodes.shape
    dest = bnd_part[:, 0]
    outgoing = jnp.moveaxis(g_nodes[:, bnd_src], 1, 0)
    init = jnp.zeros((reg_rows + 1, batch_rows, feats), jnp.float32)
    target = dest * reg_rows + bnd_node
    mine = lax.axis_index("mesh")
    piece_rows = lax.all_gather(outgoing, "mesh", axis=0, tiled=True)
    piece_target = lax.all_gather(target, "mesh", axis=0, tiled=True)
    local = jnp.where(piece_target // reg_rows == mine, piece_target % reg_rows + 1, 0)
    landed = init.at[local].add(piece_rows.astype(jnp.float32))
    force = jnp.moveaxis(landed[1:], 1, 0)
    regional = (r_nodes.astype(jnp.float32) + force).astype(jnp.bfloat16)
    planet = g_nodes
    for layer in range(g_ws.shape[0]):
        planet = graph_layer(
            planet, g_nbr, g_count, g_ws[layer], g_wd[layer], g_b1[layer], g_w2[layer], True
        )
    for layer in range(r_ws.shape[0]):
        regional = graph_layer(
            regional, r_nbr, r_count, r_ws[layer], r_wd[layer], r_b1[layer], r_w2[layer], False
        )
    return (planet, regional)


def one_hot(flags):
    return jnp.where(flags, 1.0, 0.0).astype(jnp.bfloat16)


def pick_kernel(parts, cap, me_ref, bnd_ref, g_ref, *out_refs):
    rows = g_ref.shape[0]
    total = bnd_ref.shape[1]
    me = me_ref[0]
    src, part, node = (bnd_ref[i:i + 1, :] for i in range(3))
    lines = -(-parts // 8) * 8
    target = lax.rem(lax.broadcasted_iota(jnp.int32, (lines, total), 0) + me, parts)
    named = part == target
    before = one_hot(
        lax.broadcasted_iota(jnp.int32, (total, total), 0) < lax.broadcasted_iota(jnp.int32, (total, total), 1)
    )
    rank = jnp.dot(one_hot(named), before, preferred_element_type=jnp.float32)
    rank = jnp.where(named, rank, -1.0)
    source = one_hot(lax.broadcasted_iota(jnp.int32, (rows, total), 0) == src)
    line = lax.broadcasted_iota(jnp.int32, (16, total), 0)
    high = lax.shift_right_logical(node, 7)
    facts = jnp.where(line == 0, high, jnp.where(line == 1, node - high * 128, jnp.where(line == 2, 1, 0)))
    facts = facts.astype(jnp.float32).astype(jnp.bfloat16)
    place = lax.broadcasted_iota(jnp.int32, (cap, total), 0).astype(jnp.float32)
    across = (((1,), (1,)), ((), ()))
    for k in range(parts):
        chosen = one_hot(place == rank[k:k + 1, :])
        pick = lax.dot_general(chosen, source, across, preferred_element_type=jnp.float32).astype(jnp.bfloat16)
        out_refs[k][:cap, :] = jnp.dot(pick, g_ref[...], preferred_element_type=jnp.float32).astype(jnp.bfloat16)
        told = lax.dot_general(facts, chosen, across, preferred_element_type=jnp.float32)
        out_refs[k][cap:, :] = told.astype(jnp.bfloat16)


def pick_rows(me, bnd, nodes, parts, cap):
    vmem = pl.BlockSpec(memory_space=pltpu.VMEM)
    rows, feats = nodes.shape
    total = bnd.shape[1]
    piece = jax.ShapeDtypeStruct((cap + 16, feats), jnp.bfloat16)
    return pl.pallas_call(
        functools.partial(pick_kernel, parts, cap),
        out_shape=(piece,) * parts,
        in_specs=[pl.BlockSpec(memory_space=pltpu.SMEM), vmem, vmem],
        out_specs=(vmem,) * parts,
        compiler_params=pltpu.CompilerParams(vmem_limit_bytes=32 << 20),
        cost_estimate=pl.CostEstimate(flops=32 * rows**2 * feats, bytes_accessed=1, transcendentals=0),
        name="pick_rows",
    )(me, bnd, nodes)


def force_kernel(cap, first_ref, r_ref, *refs):
    pieces, (same_ref, other_ref) = refs[:-2], refs[-2:]
    half = same_ref.shape[0]
    first = first_ref[0]
    for out_ref, start in ((same_ref, first * half), (other_ref, (1 - first) * half)):
        start = pl.multiple_of(start, 16)
        row = (lax.broadcasted_iota(jnp.int32, (half, cap), 0) + start).astype(jnp.float32)
        total = r_ref[pl.ds(start, half), :].astype(jnp.float32)
        for piece in pieces:
            facts = piece[cap:, :].astype(jnp.float32)
            node = jnp.where(facts[2:3, :] > 0.5, facts[0:1, :] * 128.0 + facts[1:2, :], -1.0)
            total += jnp.dot(one_hot(row == node), piece[:cap, :], preferred_element_type=jnp.float32)
        out_ref[...] = total.astype(jnp.bfloat16)


def add_force(first, nodes, pieces, cap):
    vmem = pl.BlockSpec(memory_space=pltpu.VMEM)
    rows, feats = nodes.shape
    block = jax.ShapeDtypeStruct((rows // 2, feats), jnp.bfloat16)
    return pl.pallas_call(
        functools.partial(force_kernel, cap),
        out_shape=(block, block),
        in_specs=[pl.BlockSpec(memory_space=pltpu.SMEM)] + [vmem] * (1 + len(pieces)),
        out_specs=(vmem, vmem),
        compiler_params=pltpu.CompilerParams(vmem_limit_bytes=32 << 20),
        cost_estimate=SMALL,
        name="add_force",
    )(first, nodes, *pieces)


def layer_kernel(
    layer, slots, last, core_ref, idx_ref, own, sib, rim, bias, near_w, far_w, ws_hbm, wd_hbm, w2_hbm, *refs
):
    outs, refs = (refs[:2], refs[2:]) if last else (refs[:1], refs[1:])
    ws, wd, w2, ws_x, wd_x, w2_x, proj, near, summed, sems = refs
    rows, width = own.shape
    share = width // 2
    chunks = width // LANES
    part = chunks // 2
    core = core_ref[0]
    pairs = ((wd_hbm, wd), (ws_hbm, ws), (w2_hbm, w2))
    copies = [pltpu.make_async_copy(src.at[layer], dst, sems.at[i]) for i, (src, dst) in enumerate(pairs)]
    for copy in copies:
        copy.start()
    window = 3 * rows
    proj[0:8, :] = jnp.full((8, LANES), DEAD, jnp.float32)
    proj[4 * window + 4:4 * window + 16, :] = jnp.full((12, LANES), DEAD, jnp.float32)
    here, there = pl.multiple_of(core * share, 16), pl.multiple_of((1 - core) * share, 16)
    for spot, piece in ((here, near_w), (there, far_w)):
        ws_x[pl.ds(spot, share), :] = piece[0:share, :]
        wd_x[pl.ds(spot, share), :] = piece[share:2 * share, :]

    @pl.when(core == 0)
    def _():
        w2_x[:, :share] = near_w[2 * share:3 * share, :]
        w2_x[:, share:] = far_w[2 * share:3 * share, :]

    @pl.when(core != 0)
    def _():
        w2_x[:, share:] = near_w[2 * share:3 * share, :]
        w2_x[:, :share] = far_w[2 * share:3 * share, :]

    def put(dst, base, first, values):
        for c in range(values.shape[1] // LANES):
            dst[pl.ds(base * chunks + first + c, rows, stride=chunks), :] = values[:, c * LANES:(c + 1) * LANES] * 0.5

    def product(values, weights):
        return jnp.dot(values[...], weights[...], preferred_element_type=jnp.float32)

    b_own = bias[layer:layer + 1, :].astype(jnp.float32)
    b_other = near_w[3 * share:3 * share + 1, :].astype(jnp.float32)
    put(near, 0, part, product(own, wd_x) + b_other)
    put(proj, 1, part, product(own, ws_x))
    copies[0].wait()
    copies[1].wait()
    put(near, 0, 0, product(own, wd) + b_own)
    put(proj, 1, 0, product(own, ws))
    for ref, base in ((sib, rows + 1), (rim, 2 * rows + 1)):
        put(proj, base, 0, product(ref, ws))
        put(proj, base, part, product(ref, ws_x))
    low = lax.broadcasted_iota(jnp.int32, (8, LANES), 0) < chunks

    def nodes(q, carry):
        spot = pl.ds(pl.multiple_of(8 * q, 8), 8)
        mine = near[spot, :]
        total = None
        for j in range(slots):
            upper = proj[pl.ds(pl.multiple_of(idx_ref[j * rows + 2 * q], 4), 8), :]
            lower = proj[pl.ds(pl.multiple_of(idx_ref[j * rows + 2 * q + 1], 4), 8), :]
            y = jnp.where(low, upper, lower) + mine
            act = y * jnp.tanh(y) + y
            total = act if total is None else total + act
        summed[spot, :] = total
        return carry

    lax.fori_loop(0, rows // 2, nodes, 0, unroll=16)
    copies[2].wait()
    sums = [summed[pl.ds(c, rows, stride=chunks), :].astype(jnp.bfloat16) for c in range(chunks)]
    update = product(jnp.concatenate(sums[:part], 1), w2) + product(jnp.concatenate(sums[part:], 1), w2_x)
    result = (own[...].astype(jnp.float32) + update).astype(jnp.bfloat16)
    if not last:
        outs[0][...] = result
    else:
        @pl.when(core == 0)
        def _():
            outs[0][...] = result[:, :share]
            outs[1][...] = result[:, share:]

        @pl.when(core != 0)
        def _():
            outs[0][...] = result[:, share:]
            outs[1][...] = result[:, :share]


def run_layer(layer, slots, last, core, idx, own, sib, rim, ws, wd, w2, bias, near_w, far_w):
    rows, width = own.shape
    share = width // 2
    chunks = width // LANES
    smem = pl.BlockSpec(memory_space=pltpu.SMEM)
    vmem = pl.BlockSpec(memory_space=pltpu.VMEM)
    bf16, f32 = jnp.bfloat16, jnp.float32
    if last:
        out_shape = (jax.ShapeDtypeStruct((rows, share), bf16),) * 2
        out_specs = (vmem, vmem)
    else:
        out_shape, out_specs = jax.ShapeDtypeStruct((rows, width), bf16), vmem
    return pl.pallas_call(
        functools.partial(layer_kernel, layer, slots, last),
        out_shape=out_shape,
        in_specs=[smem] * 2 + [vmem] * 6 + [pl.BlockSpec(memory_space=pl.ANY)] * 3,
        out_specs=out_specs,
        scratch_shapes=[
            pltpu.VMEM((width, share), bf16),
            pltpu.VMEM((width, share), bf16),
            pltpu.VMEM((share, width), bf16),
            pltpu.VMEM((width, share), bf16),
            pltpu.VMEM((width, share), bf16),
            pltpu.VMEM((share, width), bf16),
            pltpu.VMEM((3 * rows * chunks + 96, LANES), f32),
            pltpu.VMEM((rows * chunks, LANES), f32),
            pltpu.VMEM((rows * chunks, LANES), f32),
            pltpu.SemaphoreType.DMA((3,)),
        ],
        compiler_params=pltpu.CompilerParams(vmem_limit_bytes=32 << 20),
        cost_estimate=pl.CostEstimate(flops=64 * rows * width * width, bytes_accessed=10 * rows * width, transcendentals=0),
        name="graph_layer",
    )(core, idx, own, sib, rim, bias, near_w, far_w, ws, wd, w2)


def edge_offsets(nbrs, counts, core):
    graphs, rows, slots = nbrs.shape
    half = rows // 2
    nbr = lax.dynamic_slice(nbrs.transpose(0, 2, 1), (0, 0, core * half), (graphs, slots, half)) - core * half
    count = lax.dynamic_slice(counts, (0, core * half), (graphs, half))
    low = nbr + jnp.where(core == 0, 2 * half, half)
    high = nbr - jnp.where(core == 0, half, 0)
    place = jnp.where(nbr < half, low, jnp.where(nbr < 2 * half, nbr - half, high))
    live = jnp.arange(slots, dtype=jnp.int32)[None, :, None] < count[:, None, :]
    place = jnp.where(live, place, 3 * half)
    odd = jnp.arange(half, dtype=jnp.int32) % 2
    return (4 * (place + 1 - odd)).reshape(graphs, slots * half)


def spread_rows(same, other):
    a = lax.ppermute(same, ("mp", "batch"), [(0, 0), (1, 2), (2, 1), (3, 3)])
    b = lax.ppermute(other, ("mp", "batch"), [(0, 1), (1, 3), (2, 0), (3, 2)])
    return a, b


def gather_rows(a, b):
    same = lax.ppermute(a, ("mp", "batch"), [(0, 0), (1, 2), (2, 1), (3, 3)])
    other = lax.ppermute(b, ("mp", "batch"), [(0, 2), (1, 0), (2, 3), (3, 1)])
    return same, other


def ordered(which, a, b, axis):
    return jnp.where(which == 0, jnp.concatenate([a, b], axis), jnp.concatenate([b, a], axis))


def swap(values, axis):
    return lax.ppermute(values, axis, [(0, 1), (1, 0)])


def rims(own, wrap):
    size = lax.axis_size("mesh")
    pairs = []
    for m in range(size):
        if wrap or m + 1 < size:
            pairs.append((2 * m + 1, 2 * ((m + 1) % size)))
        if wrap or m > 0:
            pairs.append((2 * m, 2 * ((m - 1) % size) + 1))
    return lax.ppermute(own, ("mesh", "batch"), pairs)


def pack_kernel(order, core_ref, g_bias, r_bias, *refs):
    weights, outs, sems = (refs[:3], refs[3:6]), refs[6:-1], refs[-1]
    share = g_bias.shape[1]
    here = pl.multiple_of(core_ref[0] * share, share)
    copies = []
    for (graph, layer), out in zip(order, outs):
        ws, wd, w2 = weights[graph]
        sources = (ws.at[layer, pl.ds(here, share), :], wd.at[layer, pl.ds(here, share), :], w2.at[layer, :, pl.ds(here, share)])
        for i, source in enumerate(sources):
            copies.append(pltpu.make_async_copy(source, out.at[i * share:(i + 1) * share, :], sems.at[len(copies)]))
            copies[-1].start()
    for (graph, layer), out in zip(order, outs):
        bias = (g_bias, r_bias)[graph][layer:layer + 1, :]
        out[3 * share:, :] = jnp.broadcast_to(bias, (16, share))
    for copy in copies:
        copy.wait()


def pack_weights(order, core, g_weights, g_bias, r_weights, r_bias):
    share = g_bias.shape[1]
    vmem = pl.BlockSpec(memory_space=pltpu.VMEM)
    hbm = pl.BlockSpec(memory_space=pltpu.HBM)
    return pl.pallas_call(
        functools.partial(pack_kernel, order),
        out_shape=(jax.ShapeDtypeStruct((3 * share + 16, share), jnp.bfloat16),) * len(order),
        in_specs=[pl.BlockSpec(memory_space=pltpu.SMEM)] + [vmem] * 2 + [hbm] * 6,
        out_specs=(vmem,) * len(order),
        scratch_shapes=[pltpu.SemaphoreType.DMA((3 * len(order),))],
        compiler_params=pltpu.CompilerParams(vmem_limit_bytes=60 << 20),
        cost_estimate=pl.CostEstimate(flops=256 * share**3, bytes_accessed=1, transcendentals=0),
        name="pack_weights",
    )(core, g_bias, r_bias, *g_weights, *r_weights)


def by_rows(
    g_nodes, r_nodes, g_nbr, g_count, r_nbr, r_count, bnd_src, bnd_part, bnd_node,
    g_ws, g_wd, g_b1, g_w2, r_ws, r_wd, r_b1, r_w2,
):
    part = lax.axis_index("mp")
    core = lax.axis_index("batch")
    parts = lax.axis_size("mesh")
    slots = g_nbr.shape[1]
    layers = g_ws.shape[0]
    rows = g_nodes.shape[1]
    half = rows // 2
    cap = 2 * bnd_src.shape[0] // parts
    me = lax.axis_index("mesh").reshape(1)
    core1 = core.reshape(1)
    g_own, r_own = g_nodes[0], r_nodes[0]
    g_weights, r_weights = (g_ws, g_wd, g_w2), (r_ws, r_wd, r_w2)
    after = lax.optimization_barrier

    same = lax.dynamic_slice(g_own, (part * half, 0), (half, g_own.shape[1]))
    other = lax.dynamic_slice(g_own, ((1 - part) * half, 0), (half, g_own.shape[1]))
    g_a, g_b = spread_rows(same, other)
    order = [(graph, layer) for layer in range(layers) for graph in (0, 1)]
    packs = list(pack_weights(order[:1], core1, g_weights, g_b1, r_weights, r_b1))
    near_w = [swap(packs[0], "mp")]
    bnd = jnp.stack([bnd_src, bnd_part[:, 0], bnd_node])
    bnd, packs[0], same, other = after((bnd, packs[0], same, other))
    pieces = pick_rows(me, bnd, g_own, parts, cap)
    landed = [pieces[0]]
    for k in range(1, parts):
        landed.append(lax.ppermute(pieces[k], "mesh", [(i, (i + k) % parts) for i in range(parts)]))
    landed[0], core1, g_a, g_b = after((landed[0], core1, g_a, g_b))
    idx = edge_offsets(jnp.stack([g_nbr, r_nbr]), jnp.stack([g_count, r_count]), core)
    packs += pack_weights(order[1:], core1, g_weights, g_b1, r_weights, r_b1)
    g_idx, r_idx = idx[0], idx[1]
    g_a, g_b, g_idx, r_idx, packs[1], near_w[0], *landed = after(
        (g_a, g_b, g_idx, r_idx, packs[1], near_w[0], *landed)
    )
    planet = ordered(core, g_a, g_b, 1)
    g_sib, g_rim = swap(planet, "batch"), rims(planet, True)
    r_a, r_b = spread_rows(*add_force(part.reshape(1), r_own, landed, cap))
    r_a, r_b, packs[1] = after((r_a, r_b, packs[1]))
    near_w.append(swap(packs[1], "mp"))
    r_a, r_b, g_sib, g_rim, near_w[0] = after((r_a, r_b, g_sib, g_rim, near_w[0]))
    regional, g_idx = after((ordered(core, r_a, r_b, 1), g_idx))
    r_sib, r_rim = swap(regional, "batch"), rims(regional, False)
    for i, (graph, layer) in enumerate(order):
        last = layer == layers - 1
        far_w = swap(near_w[i], "batch")
        if i + 1 < len(order):
            near_w[i + 1], core1 = after((near_w[i + 1], core1))
        if i + 2 < len(order):
            packs[i + 2], near_w[i + 1] = after((packs[i + 2], near_w[i + 1]))
            near_w.append(swap(packs[i + 2], "mp"))
        if graph == 0:
            planet = run_layer(
                layer, slots, last, core1, g_idx, planet, g_sib, g_rim, g_ws, g_wd, g_w2, g_b1, near_w[i], far_w
            )
            *planet, core1 = after((*(planet if last else (planet,)), core1))
            if not last:
                planet = planet[0]
                g_sib, g_rim = swap(planet, "batch"), rims(planet, True)
        else:
            regional = run_layer(
                layer, slots, last, core1, r_idx, regional, r_sib, r_rim, r_ws, r_wd, r_w2, r_b1, near_w[i], far_w
            )
            if not last:
                regional, core1 = after((regional, core1))
                r_sib, r_rim = swap(regional, "batch"), rims(regional, False)
    g_out = ordered(part, *gather_rows(*planet), 0)
    g_out, *regional_rows = after((g_out, *gather_rows(*regional)))
    r_out = ordered(part, *regional_rows, 0)
    return g_out[None], r_out[None]


def solution(mesh):
    in_specs = (
        P(("groups", "batch"), "mesh", "mp"),
        P(("groups", "batch"), "mesh", "mp"),
        P("mesh", None),
        P("mesh"),
        P("mesh", None),
        P("mesh"),
        P("mesh"),
        P("mesh", None),
        P("mesh"),
        P(None, None, "mp"),
        P(None, None, "mp"),
        P(None, "mp"),
        P(None, "mp", None),
        P(None, None, "mp"),
        P(None, None, "mp"),
        P(None, "mp"),
        P(None, "mp", None),
    )
    out_specs = (P(("groups", "batch"), "mesh", "mp"), P(("groups", "batch"), "mesh", "mp"))
    square = mesh.shape["mp"] == 2 and mesh.shape["batch"] == 2
    return jax.shard_map(
        by_rows if square else by_features, mesh=mesh, in_specs=in_specs, out_specs=out_specs, check_vma=False
    )
```

```python
import functools

import jax
import jax.numpy as jnp
from jax import lax
from jax.experimental import pallas as pl
from jax.experimental.pallas import tpu as pltpu
from jax.sharding import PartitionSpec as P

LANES = 128
DEAD = -1e30
SMALL = pl.CostEstimate(flops=1, bytes_accessed=1, transcendentals=0)


def padded_2(shard, sides, width, wrap):
    for axis, dim in sides:
        size, length = (lax.axis_size(axis), shard.shape[dim])
        up = [(i, (i + 1) % size) for i in range(size if wrap else size - 1)]
        down = [(j, i) for i, j in up]
        last = lax.slice_in_dim(shard, length - width, length, axis=dim)
        leading = lax.slice_in_dim(shard, 0, width, axis=dim)
        before = lax.ppermute(last, axis, up)
        after = lax.ppermute(leading, axis, down)
        shard = jnp.concatenate([before, shard, after], axis=dim)
    return shard


def edge_sums(proj, near, nbr, count):
    slots = nbr.shape[1]
    live = jnp.arange(slots, dtype=jnp.int32)[None, :] < count[:, None]
    pre = proj[:, nbr].astype(jnp.float32) + near[:, :, None]
    acts = jnp.where(live[None, :, :, None], jax.nn.silu(pre), 0.0)
    return jnp.sum(acts, axis=2).astype(jnp.bfloat16)


def graph_layer(latent, nbr, count, w_send, w_recv, bias, w_out, wrap):
    rim = latent.shape[1] // 2
    own_full = lax.all_gather(latent, "mp", axis=2, tiled=True)
    padded_full = padded_2(own_full, (("mesh", 1),), rim, wrap)
    proj = jnp.dot(padded_full, w_send, preferred_element_type=jnp.float32).astype(jnp.bfloat16)
    near = jnp.dot(own_full, w_recv, preferred_element_type=jnp.float32) + bias.astype(jnp.float32)
    summed = edge_sums(proj, near, nbr, count)
    partial_prod = jnp.dot(summed, w_out, preferred_element_type=jnp.float32)
    update = lax.psum_scatter(
        partial_prod.astype(jnp.bfloat16), "mp", scatter_dimension=2, tiled=True
    ).astype(jnp.float32)
    return (latent.astype(jnp.float32) + update).astype(jnp.bfloat16)


def by_features(
    g_nodes, r_nodes, g_nbr, g_count, r_nbr, r_count, bnd_src, bnd_part, bnd_node,
    g_ws, g_wd, g_b1, g_w2, r_ws, r_wd, r_b1, r_w2,
):
    batch_rows, reg_rows, feats = r_nodes.shape
    dest = bnd_part[:, 0]
    outgoing = jnp.moveaxis(g_nodes[:, bnd_src], 1, 0)
    init = jnp.zeros((reg_rows + 1, batch_rows, feats), jnp.float32)
    target = dest * reg_rows + bnd_node
    mine = lax.axis_index("mesh")
    piece_rows = lax.all_gather(outgoing, "mesh", axis=0, tiled=True)
    piece_target = lax.all_gather(target, "mesh", axis=0, tiled=True)
    local = jnp.where(piece_target // reg_rows == mine, piece_target % reg_rows + 1, 0)
    landed = init.at[local].add(piece_rows.astype(jnp.float32))
    force = jnp.moveaxis(landed[1:], 1, 0)
    regional = (r_nodes.astype(jnp.float32) + force).astype(jnp.bfloat16)
    planet = g_nodes
    for layer in range(g_ws.shape[0]):
        planet = graph_layer(
            planet, g_nbr, g_count, g_ws[layer], g_wd[layer], g_b1[layer], g_w2[layer], True
        )
    for layer in range(r_ws.shape[0]):
        regional = graph_layer(
            regional, r_nbr, r_count, r_ws[layer], r_wd[layer], r_b1[layer], r_w2[layer], False
        )
    return (planet, regional)


def one_hot(flags):
    return jnp.where(flags, 1.0, 0.0).astype(jnp.bfloat16)


def pick_kernel(parts, cap, me_ref, bnd_ref, g_ref, *out_refs):
    rows = g_ref.shape[0]
    total = bnd_ref.shape[1]
    me = me_ref[0]
    src, part, node = (bnd_ref[i:i + 1, :] for i in range(3))
    lines = -(-parts // 8) * 8
    target = lax.rem(lax.broadcasted_iota(jnp.int32, (lines, total), 0) + me, parts)
    named = part == target
    before = one_hot(
        lax.broadcasted_iota(jnp.int32, (total, total), 0) < lax.broadcasted_iota(jnp.int32, (total, total), 1)
    )
    rank = jnp.dot(one_hot(named), before, preferred_element_type=jnp.float32)
    rank = jnp.where(named, rank, -1.0)
    source = one_hot(lax.broadcasted_iota(jnp.int32, (rows, total), 0) == src)
    line = lax.broadcasted_iota(jnp.int32, (16, total), 0)
    high = lax.shift_right_logical(node, 7)
    facts = jnp.where(line == 0, high, jnp.where(line == 1, node - high * 128, jnp.where(line == 2, 1, 0)))
    facts = facts.astype(jnp.float32).astype(jnp.bfloat16)
    place = lax.broadcasted_iota(jnp.int32, (cap, total), 0).astype(jnp.float32)
    across = (((1,), (1,)), ((), ()))
    for k in range(parts):
        chosen = one_hot(place == rank[k:k + 1, :])
        pick = lax.dot_general(chosen, source, across, preferred_element_type=jnp.float32).astype(jnp.bfloat16)
        out_refs[k][:cap, :] = jnp.dot(pick, g_ref[...], preferred_element_type=jnp.float32).astype(jnp.bfloat16)
        told = lax.dot_general(facts, chosen, across, preferred_element_type=jnp.float32)
        out_refs[k][cap:, :] = told.astype(jnp.bfloat16)


def pick_rows(me, bnd, nodes, parts, cap):
    vmem = pl.BlockSpec(memory_space=pltpu.VMEM)
    rows, feats = nodes.shape
    total = bnd.shape[1]
    piece = jax.ShapeDtypeStruct((cap + 16, feats), jnp.bfloat16)
    return pl.pallas_call(
        functools.partial(pick_kernel, parts, cap),
        out_shape=(piece,) * parts,
        in_specs=[pl.BlockSpec(memory_space=pltpu.SMEM), vmem, vmem],
        out_specs=(vmem,) * parts,
        compiler_params=pltpu.CompilerParams(vmem_limit_bytes=32 << 20),
        cost_estimate=pl.CostEstimate(flops=32 * rows**2 * feats, bytes_accessed=1, transcendentals=0),
        name="pick_rows",
    )(me, bnd, nodes)


def force_kernel(cap, first_ref, r_ref, *refs):
    pieces, (same_ref, other_ref) = refs[:-2], refs[-2:]
    half = same_ref.shape[0]
    first = first_ref[0]
    for out_ref, start in ((same_ref, first * half), (other_ref, (1 - first) * half)):
        start = pl.multiple_of(start, 16)
        row = (lax.broadcasted_iota(jnp.int32, (half, cap), 0) + start).astype(jnp.float32)
        total = r_ref[pl.ds(start, half), :].astype(jnp.float32)
        for piece in pieces:
            facts = piece[cap:, :].astype(jnp.float32)
            node = jnp.where(facts[2:3, :] > 0.5, facts[0:1, :] * 128.0 + facts[1:2, :], -1.0)
            total += jnp.dot(one_hot(row == node), piece[:cap, :], preferred_element_type=jnp.float32)
        out_ref[...] = total.astype(jnp.bfloat16)


def add_force(first, nodes, pieces, cap):
    vmem = pl.BlockSpec(memory_space=pltpu.VMEM)
    rows, feats = nodes.shape
    block = jax.ShapeDtypeStruct((rows // 2, feats), jnp.bfloat16)
    return pl.pallas_call(
        functools.partial(force_kernel, cap),
        out_shape=(block, block),
        in_specs=[pl.BlockSpec(memory_space=pltpu.SMEM)] + [vmem] * (1 + len(pieces)),
        out_specs=(vmem, vmem),
        compiler_params=pltpu.CompilerParams(vmem_limit_bytes=32 << 20),
        cost_estimate=SMALL,
        name="add_force",
    )(first, nodes, *pieces)


def layer_kernel(
    layer, slots, last, core_ref, idx_ref, own, sib, rim, bias, near_w, far_w, ws_hbm, wd_hbm, w2_hbm, *refs
):
    outs, refs = (refs[:2], refs[2:]) if last else (refs[:1], refs[1:])
    ws, wd, w2, ws_x, wd_x, w2_x, proj, near, summed, sems = refs
    rows, width = own.shape
    share = width // 2
    chunks = width // LANES
    part = chunks // 2
    core = core_ref[0]
    pairs = ((wd_hbm, wd), (ws_hbm, ws), (w2_hbm, w2))
    copies = [pltpu.make_async_copy(src.at[layer], dst, sems.at[i]) for i, (src, dst) in enumerate(pairs)]
    for copy in copies:
        copy.start()
    window = 3 * rows
    proj[0:8, :] = jnp.full((8, LANES), DEAD, jnp.float32)
    proj[4 * window + 4:4 * window + 16, :] = jnp.full((12, LANES), DEAD, jnp.float32)
    here, there = pl.multiple_of(core * share, 16), pl.multiple_of((1 - core) * share, 16)
    for spot, piece in ((here, near_w), (there, far_w)):
        ws_x[pl.ds(spot, share), :] = piece[0:share, :]
        wd_x[pl.ds(spot, share), :] = piece[share:2 * share, :]

    @pl.when(core == 0)
    def _():
        w2_x[:, :share] = near_w[2 * share:3 * share, :]
        w2_x[:, share:] = far_w[2 * share:3 * share, :]

    @pl.when(core != 0)
    def _():
        w2_x[:, share:] = near_w[2 * share:3 * share, :]
        w2_x[:, :share] = far_w[2 * share:3 * share, :]

    def put(dst, base, first, values):
        for c in range(values.shape[1] // LANES):
            dst[pl.ds(base * chunks + first + c, rows, stride=chunks), :] = values[:, c * LANES:(c + 1) * LANES] * 0.5

    def product(values, weights):
        return jnp.dot(values[...], weights[...], preferred_element_type=jnp.float32)

    b_own = bias[layer:layer + 1, :].astype(jnp.float32)
    b_other = near_w[3 * share:3 * share + 1, :].astype(jnp.float32)
    put(near, 0, part, product(own, wd_x) + b_other)
    put(proj, 1, part, product(own, ws_x))
    copies[0].wait()
    copies[1].wait()
    put(near, 0, 0, product(own, wd) + b_own)
    put(proj, 1, 0, product(own, ws))
    for ref, base in ((sib, rows + 1), (rim, 2 * rows + 1)):
        put(proj, base, 0, product(ref, ws))
        put(proj, base, part, product(ref, ws_x))
    low = lax.broadcasted_iota(jnp.int32, (8, LANES), 0) < chunks

    def nodes(q, carry):
        spot = pl.ds(pl.multiple_of(8 * q, 8), 8)
        mine = near[spot, :]
        total = None
        for j in range(slots):
            upper = proj[pl.ds(pl.multiple_of(idx_ref[j * rows + 2 * q], 4), 8), :]
            lower = proj[pl.ds(pl.multiple_of(idx_ref[j * rows + 2 * q + 1], 4), 8), :]
            y = jnp.where(low, upper, lower) + mine
            act = y * jnp.tanh(y) + y
            total = act if total is None else total + act
        summed[spot, :] = total
        return carry

    lax.fori_loop(0, rows // 2, nodes, 0, unroll=16)
    copies[2].wait()
    sums = [summed[pl.ds(c, rows, stride=chunks), :].astype(jnp.bfloat16) for c in range(chunks)]
    update = product(jnp.concatenate(sums[:part], 1), w2) + product(jnp.concatenate(sums[part:], 1), w2_x)
    result = (own[...].astype(jnp.float32) + update).astype(jnp.bfloat16)
    if not last:
        outs[0][...] = result
    else:
        @pl.when(core == 0)
        def _():
            outs[0][...] = result[:, :share]
            outs[1][...] = result[:, share:]

        @pl.when(core != 0)
        def _():
            outs[0][...] = result[:, share:]
            outs[1][...] = result[:, :share]


def run_layer(layer, slots, last, core, idx, own, sib, rim, ws, wd, w2, bias, near_w, far_w):
    rows, width = own.shape
    share = width // 2
    chunks = width // LANES
    smem = pl.BlockSpec(memory_space=pltpu.SMEM)
    vmem = pl.BlockSpec(memory_space=pltpu.VMEM)
    bf16, f32 = jnp.bfloat16, jnp.float32
    if last:
        out_shape = (jax.ShapeDtypeStruct((rows, share), bf16),) * 2
        out_specs = (vmem, vmem)
    else:
        out_shape, out_specs = jax.ShapeDtypeStruct((rows, width), bf16), vmem
    return pl.pallas_call(
        functools.partial(layer_kernel, layer, slots, last),
        out_shape=out_shape,
        in_specs=[smem] * 2 + [vmem] * 6 + [pl.BlockSpec(memory_space=pl.ANY)] * 3,
        out_specs=out_specs,
        scratch_shapes=[
            pltpu.VMEM((width, share), bf16),
            pltpu.VMEM((width, share), bf16),
            pltpu.VMEM((share, width), bf16),
            pltpu.VMEM((width, share), bf16),
            pltpu.VMEM((width, share), bf16),
            pltpu.VMEM((share, width), bf16),
            pltpu.VMEM((3 * rows * chunks + 96, LANES), f32),
            pltpu.VMEM((rows * chunks, LANES), f32),
            pltpu.VMEM((rows * chunks, LANES), f32),
            pltpu.SemaphoreType.DMA((3,)),
        ],
        compiler_params=pltpu.CompilerParams(vmem_limit_bytes=32 << 20),
        cost_estimate=pl.CostEstimate(flops=64 * rows * width * width, bytes_accessed=10 * rows * width, transcendentals=0),
        name="graph_layer",
    )(core, idx, own, sib, rim, bias, near_w, far_w, ws, wd, w2)


def edge_offsets(nbrs, counts, core):
    graphs, rows, slots = nbrs.shape
    half = rows // 2
    nbr = lax.dynamic_slice(nbrs.transpose(0, 2, 1), (0, 0, core * half), (graphs, slots, half)) - core * half
    count = lax.dynamic_slice(counts, (0, core * half), (graphs, half))
    low = nbr + jnp.where(core == 0, 2 * half, half)
    high = nbr - jnp.where(core == 0, half, 0)
    place = jnp.where(nbr < half, low, jnp.where(nbr < 2 * half, nbr - half, high))
    live = jnp.arange(slots, dtype=jnp.int32)[None, :, None] < count[:, None, :]
    place = jnp.where(live, place, 3 * half)
    odd = jnp.arange(half, dtype=jnp.int32) % 2
    return (4 * (place + 1 - odd)).reshape(graphs, slots * half)


def spread_rows(same, other):
    a = lax.ppermute(same, ("mp", "batch"), [(0, 0), (1, 2), (2, 1), (3, 3)])
    b = lax.ppermute(other, ("mp", "batch"), [(0, 1), (1, 3), (2, 0), (3, 2)])
    return a, b


def gather_rows(a, b):
    same = lax.ppermute(a, ("mp", "batch"), [(0, 0), (1, 2), (2, 1), (3, 3)])
    other = lax.ppermute(b, ("mp", "batch"), [(0, 2), (1, 0), (2, 3), (3, 1)])
    return same, other


def ordered(which, a, b, axis):
    return jnp.where(which == 0, jnp.concatenate([a, b], axis), jnp.concatenate([b, a], axis))


def swap(values, axis):
    return lax.ppermute(values, axis, [(0, 1), (1, 0)])


def rims(own, wrap):
    size = lax.axis_size("mesh")
    pairs = []
    for m in range(size):
        if wrap or m + 1 < size:
            pairs.append((2 * m + 1, 2 * ((m + 1) % size)))
        if wrap or m > 0:
            pairs.append((2 * m, 2 * ((m - 1) % size) + 1))
    return lax.ppermute(own, ("mesh", "batch"), pairs)


def pack_kernel(order, core_ref, g_bias, r_bias, *refs):
    weights, outs, sems = (refs[:3], refs[3:6]), refs[6:-1], refs[-1]
    share = g_bias.shape[1]
    here = pl.multiple_of(core_ref[0] * share, share)
    copies = []
    for (graph, layer), out in zip(order, outs):
        ws, wd, w2 = weights[graph]
        sources = (ws.at[layer, pl.ds(here, share), :], wd.at[layer, pl.ds(here, share), :], w2.at[layer, :, pl.ds(here, share)])
        for i, source in enumerate(sources):
            copies.append(pltpu.make_async_copy(source, out.at[i * share:(i + 1) * share, :], sems.at[len(copies)]))
            copies[-1].start()
    for (graph, layer), out in zip(order, outs):
        bias = (g_bias, r_bias)[graph][layer:layer + 1, :]
        out[3 * share:, :] = jnp.broadcast_to(bias, (16, share))
    for copy in copies:
        copy.wait()


def pack_weights(order, core, g_weights, g_bias, r_weights, r_bias):
    share = g_bias.shape[1]
    vmem = pl.BlockSpec(memory_space=pltpu.VMEM)
    hbm = pl.BlockSpec(memory_space=pltpu.HBM)
    return pl.pallas_call(
        functools.partial(pack_kernel, order),
        out_shape=(jax.ShapeDtypeStruct((3 * share + 16, share), jnp.bfloat16),) * len(order),
        in_specs=[pl.BlockSpec(memory_space=pltpu.SMEM)] + [vmem] * 2 + [hbm] * 6,
        out_specs=(vmem,) * len(order),
        scratch_shapes=[pltpu.SemaphoreType.DMA((3 * len(order),))],
        compiler_params=pltpu.CompilerParams(vmem_limit_bytes=60 << 20),
        cost_estimate=pl.CostEstimate(flops=256 * share**3, bytes_accessed=1, transcendentals=0),
        name="pack_weights",
    )(core, g_bias, r_bias, *g_weights, *r_weights)


def by_rows(
    g_nodes, r_nodes, g_nbr, g_count, r_nbr, r_count, bnd_src, bnd_part, bnd_node,
    g_ws, g_wd, g_b1, g_w2, r_ws, r_wd, r_b1, r_w2,
):
    part = lax.axis_index("mp")
    core = lax.axis_index("batch")
    parts = lax.axis_size("mesh")
    slots = g_nbr.shape[1]
    layers = g_ws.shape[0]
    rows = g_nodes.shape[1]
    half = rows // 2
    cap = 2 * bnd_src.shape[0] // parts
    me = lax.axis_index("mesh").reshape(1)
    core1 = core.reshape(1)
    g_own, r_own = g_nodes[0], r_nodes[0]
    g_weights, r_weights = (g_ws, g_wd, g_w2), (r_ws, r_wd, r_w2)
    after = lax.optimization_barrier

    same = lax.dynamic_slice(g_own, (part * half, 0), (half, g_own.shape[1]))
    other = lax.dynamic_slice(g_own, ((1 - part) * half, 0), (half, g_own.shape[1]))
    g_a, g_b = spread_rows(same, other)
    order = [(graph, layer) for layer in range(layers) for graph in (0, 1)]
    packs = list(pack_weights(order[:1], core1, g_weights, g_b1, r_weights, r_b1))
    near_w = [swap(packs[0], "mp")]
    bnd = jnp.stack([bnd_src, bnd_part[:, 0], bnd_node])
    bnd, packs[0], same, other = after((bnd, packs[0], same, other))
    pieces = pick_rows(me, bnd, g_own, parts, cap)
    landed = [pieces[0]]
    for k in range(1, parts):
        landed.append(lax.ppermute(pieces[k], "mesh", [(i, (i + k) % parts) for i in range(parts)]))
    landed[0], core1, g_a, g_b = after((landed[0], core1, g_a, g_b))
    idx = edge_offsets(jnp.stack([g_nbr, r_nbr]), jnp.stack([g_count, r_count]), core)
    packs += pack_weights(order[1:], core1, g_weights, g_b1, r_weights, r_b1)
    g_idx, r_idx = idx[0], idx[1]
    g_a, g_b, g_idx, r_idx, packs[1], near_w[0], *landed = after(
        (g_a, g_b, g_idx, r_idx, packs[1], near_w[0], *landed)
    )
    planet = ordered(core, g_a, g_b, 1)
    g_sib, g_rim = swap(planet, "batch"), rims(planet, True)
    *r_pair, packs[1] = after((*add_force(part.reshape(1), r_own, landed, cap), packs[1]))
    r_a, r_b = spread_rows(*r_pair)
    near_w.append(swap(packs[1], "mp"))
    r_a, r_b, g_sib, g_rim, near_w[0] = after((r_a, r_b, g_sib, g_rim, near_w[0]))
    regional, g_idx = after((ordered(core, r_a, r_b, 1), g_idx))
    r_sib, r_rim = swap(regional, "batch"), rims(regional, False)
    r_sib, near_w[1] = after((r_sib, near_w[1]))
    for i, (graph, layer) in enumerate(order):
        last = layer == layers - 1
        far_w = swap(near_w[i], "batch")
        if i + 1 < len(order):
            near_w[i + 1], core1 = after((near_w[i + 1], core1))
        if i + 2 < len(order):
            packs[i + 2], near_w[i + 1] = after((packs[i + 2], near_w[i + 1]))
            near_w.append(swap(packs[i + 2], "mp"))
        if graph == 0:
            planet = run_layer(
                layer, slots, last, core1, g_idx, planet, g_sib, g_rim, g_ws, g_wd, g_w2, g_b1, near_w[i], far_w
            )
            *planet, core1 = after((*(planet if last else (planet,)), core1))
            if not last:
                planet = planet[0]
                g_sib, g_rim = swap(planet, "batch"), rims(planet, True)
        else:
            regional = run_layer(
                layer, slots, last, core1, r_idx, regional, r_sib, r_rim, r_ws, r_wd, r_w2, r_b1, near_w[i], far_w
            )
            if not last:
                regional, core1 = after((regional, core1))
                r_sib, r_rim = swap(regional, "batch"), rims(regional, False)
    g_out = ordered(part, *gather_rows(*planet), 0)
    g_out, *regional_rows = after((g_out, *gather_rows(*regional)))
    r_out = ordered(part, *regional_rows, 0)
    return g_out[None], r_out[None]


def solution(mesh):
    in_specs = (
        P(("groups", "batch"), "mesh", "mp"),
        P(("groups", "batch"), "mesh", "mp"),
        P("mesh", None),
        P("mesh"),
        P("mesh", None),
        P("mesh"),
        P("mesh"),
        P("mesh", None),
        P("mesh"),
        P(None, None, "mp"),
        P(None, None, "mp"),
        P(None, "mp"),
        P(None, "mp", None),
        P(None, None, "mp"),
        P(None, None, "mp"),
        P(None, "mp"),
        P(None, "mp", None),
    )
    out_specs = (P(("groups", "batch"), "mesh", "mp"), P(("groups", "batch"), "mesh", "mp"))
    square = mesh.shape["mp"] == 2 and mesh.shape["batch"] == 2
    return jax.shard_map(
        by_rows if square else by_features, mesh=mesh, in_specs=in_specs, out_specs=out_specs, check_vma=False
    )
```

```python
import functools

import jax
import jax.numpy as jnp
from jax import lax
from jax.experimental import pallas as pl
from jax.experimental.pallas import tpu as pltpu
from jax.sharding import PartitionSpec as P

LANES = 128
DEAD = -1e30
SMALL = pl.CostEstimate(flops=1, bytes_accessed=1, transcendentals=0)


def padded_2(shard, sides, width, wrap):
    for axis, dim in sides:
        size, length = (lax.axis_size(axis), shard.shape[dim])
        up = [(i, (i + 1) % size) for i in range(size if wrap else size - 1)]
        down = [(j, i) for i, j in up]
        last = lax.slice_in_dim(shard, length - width, length, axis=dim)
        leading = lax.slice_in_dim(shard, 0, width, axis=dim)
        before = lax.ppermute(last, axis, up)
        after = lax.ppermute(leading, axis, down)
        shard = jnp.concatenate([before, shard, after], axis=dim)
    return shard


def edge_sums(proj, near, nbr, count):
    slots = nbr.shape[1]
    live = jnp.arange(slots, dtype=jnp.int32)[None, :] < count[:, None]
    pre = proj[:, nbr].astype(jnp.float32) + near[:, :, None]
    acts = jnp.where(live[None, :, :, None], jax.nn.silu(pre), 0.0)
    return jnp.sum(acts, axis=2).astype(jnp.bfloat16)


def graph_layer(latent, nbr, count, w_send, w_recv, bias, w_out, wrap):
    rim = latent.shape[1] // 2
    own_full = lax.all_gather(latent, "mp", axis=2, tiled=True)
    padded_full = padded_2(own_full, (("mesh", 1),), rim, wrap)
    proj = jnp.dot(padded_full, w_send, preferred_element_type=jnp.float32).astype(jnp.bfloat16)
    near = jnp.dot(own_full, w_recv, preferred_element_type=jnp.float32) + bias.astype(jnp.float32)
    summed = edge_sums(proj, near, nbr, count)
    partial_prod = jnp.dot(summed, w_out, preferred_element_type=jnp.float32)
    update = lax.psum_scatter(
        partial_prod.astype(jnp.bfloat16), "mp", scatter_dimension=2, tiled=True
    ).astype(jnp.float32)
    return (latent.astype(jnp.float32) + update).astype(jnp.bfloat16)


def by_features(
    g_nodes, r_nodes, g_nbr, g_count, r_nbr, r_count, bnd_src, bnd_part, bnd_node,
    g_ws, g_wd, g_b1, g_w2, r_ws, r_wd, r_b1, r_w2,
):
    batch_rows, reg_rows, feats = r_nodes.shape
    dest = bnd_part[:, 0]
    outgoing = jnp.moveaxis(g_nodes[:, bnd_src], 1, 0)
    init = jnp.zeros((reg_rows + 1, batch_rows, feats), jnp.float32)
    target = dest * reg_rows + bnd_node
    mine = lax.axis_index("mesh")
    piece_rows = lax.all_gather(outgoing, "mesh", axis=0, tiled=True)
    piece_target = lax.all_gather(target, "mesh", axis=0, tiled=True)
    local = jnp.where(piece_target // reg_rows == mine, piece_target % reg_rows + 1, 0)
    landed = init.at[local].add(piece_rows.astype(jnp.float32))
    force = jnp.moveaxis(landed[1:], 1, 0)
    regional = (r_nodes.astype(jnp.float32) + force).astype(jnp.bfloat16)
    planet = g_nodes
    for layer in range(g_ws.shape[0]):
        planet = graph_layer(
            planet, g_nbr, g_count, g_ws[layer], g_wd[layer], g_b1[layer], g_w2[layer], True
        )
    for layer in range(r_ws.shape[0]):
        regional = graph_layer(
            regional, r_nbr, r_count, r_ws[layer], r_wd[layer], r_b1[layer], r_w2[layer], False
        )
    return (planet, regional)


def one_hot(flags):
    return jnp.where(flags, 1.0, 0.0).astype(jnp.bfloat16)


def pick_kernel(parts, cap, me_ref, bnd_ref, g_ref, *out_refs):
    rows = g_ref.shape[0]
    total = bnd_ref.shape[1]
    me = me_ref[0]
    src, part, node = (bnd_ref[i:i + 1, :] for i in range(3))
    lines = -(-parts // 8) * 8
    target = lax.rem(lax.broadcasted_iota(jnp.int32, (lines, total), 0) + me, parts)
    named = part == target
    before = one_hot(
        lax.broadcasted_iota(jnp.int32, (total, total), 0) < lax.broadcasted_iota(jnp.int32, (total, total), 1)
    )
    rank = jnp.dot(one_hot(named), before, preferred_element_type=jnp.float32)
    rank = jnp.where(named, rank, -1.0)
    source = one_hot(lax.broadcasted_iota(jnp.int32, (rows, total), 0) == src)
    line = lax.broadcasted_iota(jnp.int32, (16, total), 0)
    high = lax.shift_right_logical(node, 7)
    facts = jnp.where(line == 0, high, jnp.where(line == 1, node - high * 128, jnp.where(line == 2, 1, 0)))
    facts = facts.astype(jnp.float32).astype(jnp.bfloat16)
    place = lax.broadcasted_iota(jnp.int32, (cap, total), 0).astype(jnp.float32)
    across = (((1,), (1,)), ((), ()))
    for k in range(parts):
        chosen = one_hot(place == rank[k:k + 1, :])
        pick = lax.dot_general(chosen, source, across, preferred_element_type=jnp.float32).astype(jnp.bfloat16)
        out_refs[k][:cap, :] = jnp.dot(pick, g_ref[...], preferred_element_type=jnp.float32).astype(jnp.bfloat16)
        told = lax.dot_general(facts, chosen, across, preferred_element_type=jnp.float32)
        out_refs[k][cap:, :] = told.astype(jnp.bfloat16)


def pick_rows(me, bnd, nodes, parts, cap):
    vmem = pl.BlockSpec(memory_space=pltpu.VMEM)
    rows, feats = nodes.shape
    total = bnd.shape[1]
    piece = jax.ShapeDtypeStruct((cap + 16, feats), jnp.bfloat16)
    return pl.pallas_call(
        functools.partial(pick_kernel, parts, cap),
        out_shape=(piece,) * parts,
        in_specs=[pl.BlockSpec(memory_space=pltpu.SMEM), vmem, vmem],
        out_specs=(vmem,) * parts,
        compiler_params=pltpu.CompilerParams(vmem_limit_bytes=32 << 20),
        cost_estimate=pl.CostEstimate(flops=32 * rows**2 * feats, bytes_accessed=1, transcendentals=0),
        name="pick_rows",
    )(me, bnd, nodes)


def force_kernel(cap, first_ref, r_ref, *refs):
    pieces, (same_ref, other_ref) = refs[:-2], refs[-2:]
    half = same_ref.shape[0]
    first = first_ref[0]
    for out_ref, start in ((same_ref, first * half), (other_ref, (1 - first) * half)):
        start = pl.multiple_of(start, 16)
        row = (lax.broadcasted_iota(jnp.int32, (half, cap), 0) + start).astype(jnp.float32)
        total = r_ref[pl.ds(start, half), :].astype(jnp.float32)
        for piece in pieces:
            facts = piece[cap:, :].astype(jnp.float32)
            node = jnp.where(facts[2:3, :] > 0.5, facts[0:1, :] * 128.0 + facts[1:2, :], -1.0)
            total += jnp.dot(one_hot(row == node), piece[:cap, :], preferred_element_type=jnp.float32)
        out_ref[...] = total.astype(jnp.bfloat16)


def add_force(first, nodes, pieces, cap):
    vmem = pl.BlockSpec(memory_space=pltpu.VMEM)
    rows, feats = nodes.shape
    block = jax.ShapeDtypeStruct((rows // 2, feats), jnp.bfloat16)
    return pl.pallas_call(
        functools.partial(force_kernel, cap),
        out_shape=(block, block),
        in_specs=[pl.BlockSpec(memory_space=pltpu.SMEM)] + [vmem] * (1 + len(pieces)),
        out_specs=(vmem, vmem),
        compiler_params=pltpu.CompilerParams(vmem_limit_bytes=32 << 20),
        cost_estimate=SMALL,
        name="add_force",
    )(first, nodes, *pieces)


def layer_kernel(
    layer, graph, slots, last, core_ref, idx_ref, own, sib, rim, bias, near_w, far_w, ws_hbm, wd_hbm, w2_hbm, *refs
):
    outs, refs = (refs[:2], refs[2:]) if last else (refs[:1], refs[1:])
    ws, wd, w2, ws_x, wd_x, w2_x, proj, near, summed, sems = refs
    rows, width = own.shape
    share = width // 2
    chunks = width // LANES
    part = chunks // 2
    core = core_ref[0]
    pairs = ((wd_hbm, wd), (ws_hbm, ws), (w2_hbm, w2))
    copies = [pltpu.make_async_copy(src.at[layer], dst, sems.at[i]) for i, (src, dst) in enumerate(pairs)]
    for copy in copies:
        copy.start()
    window = 3 * rows
    proj[0:8, :] = jnp.full((8, LANES), DEAD, jnp.float32)
    proj[4 * window + 4:4 * window + 16, :] = jnp.full((12, LANES), DEAD, jnp.float32)
    pack = graph * (3 * share + 16)
    here, there = pl.multiple_of(core * share, 16), pl.multiple_of((1 - core) * share, 16)
    for spot, piece in ((here, near_w), (there, far_w)):
        ws_x[pl.ds(spot, share), :] = piece[pack:pack + share, :]
        wd_x[pl.ds(spot, share), :] = piece[pack + share:pack + 2 * share, :]
    third = slice(pack + 2 * share, pack + 3 * share)

    @pl.when(core == 0)
    def _():
        w2_x[:, :share] = near_w[third, :]
        w2_x[:, share:] = far_w[third, :]

    @pl.when(core != 0)
    def _():
        w2_x[:, share:] = near_w[third, :]
        w2_x[:, :share] = far_w[third, :]

    def put(dst, base, first, values):
        for c in range(values.shape[1] // LANES):
            dst[pl.ds(base * chunks + first + c, rows, stride=chunks), :] = values[:, c * LANES:(c + 1) * LANES] * 0.5

    def product(values, weights):
        return jnp.dot(values[...], weights[...], preferred_element_type=jnp.float32)

    b_own = bias[layer:layer + 1, :].astype(jnp.float32)
    b_other = near_w[pack + 3 * share:pack + 3 * share + 1, :].astype(jnp.float32)
    put(near, 0, part, product(own, wd_x) + b_other)
    put(proj, 1, part, product(own, ws_x))
    copies[0].wait()
    copies[1].wait()
    put(near, 0, 0, product(own, wd) + b_own)
    put(proj, 1, 0, product(own, ws))
    for ref, base in ((sib, rows + 1), (rim, 2 * rows + 1)):
        put(proj, base, 0, product(ref, ws))
        put(proj, base, part, product(ref, ws_x))
    low = lax.broadcasted_iota(jnp.int32, (8, LANES), 0) < chunks

    def nodes(q, carry):
        spot = pl.ds(pl.multiple_of(8 * q, 8), 8)
        mine = near[spot, :]
        total = None
        for j in range(slots):
            upper = proj[pl.ds(pl.multiple_of(idx_ref[j * rows + 2 * q], 4), 8), :]
            lower = proj[pl.ds(pl.multiple_of(idx_ref[j * rows + 2 * q + 1], 4), 8), :]
            y = jnp.where(low, upper, lower) + mine
            act = y * jnp.tanh(y) + y
            total = act if total is None else total + act
        summed[spot, :] = total
        return carry

    lax.fori_loop(0, rows // 2, nodes, 0, unroll=16)
    copies[2].wait()
    sums = [summed[pl.ds(c, rows, stride=chunks), :].astype(jnp.bfloat16) for c in range(chunks)]
    update = product(jnp.concatenate(sums[:part], 1), w2) + product(jnp.concatenate(sums[part:], 1), w2_x)
    result = (own[...].astype(jnp.float32) + update).astype(jnp.bfloat16)
    if not last:
        outs[0][...] = result
    else:
        @pl.when(core == 0)
        def _():
            outs[0][...] = result[:, :share]
            outs[1][...] = result[:, share:]

        @pl.when(core != 0)
        def _():
            outs[0][...] = result[:, share:]
            outs[1][...] = result[:, :share]


def run_layer(layer, graph, slots, last, core, idx, own, sib, rim, ws, wd, w2, bias, near_w, far_w):
    rows, width = own.shape
    share = width // 2
    chunks = width // LANES
    smem = pl.BlockSpec(memory_space=pltpu.SMEM)
    vmem = pl.BlockSpec(memory_space=pltpu.VMEM)
    bf16, f32 = jnp.bfloat16, jnp.float32
    if last:
        out_shape = (jax.ShapeDtypeStruct((rows, share), bf16),) * 2
        out_specs = (vmem, vmem)
    else:
        out_shape, out_specs = jax.ShapeDtypeStruct((rows, width), bf16), vmem
    return pl.pallas_call(
        functools.partial(layer_kernel, layer, graph, slots, last),
        out_shape=out_shape,
        in_specs=[smem] * 2 + [vmem] * 6 + [pl.BlockSpec(memory_space=pl.ANY)] * 3,
        out_specs=out_specs,
        scratch_shapes=[
            pltpu.VMEM((width, share), bf16),
            pltpu.VMEM((width, share), bf16),
            pltpu.VMEM((share, width), bf16),
            pltpu.VMEM((width, share), bf16),
            pltpu.VMEM((width, share), bf16),
            pltpu.VMEM((share, width), bf16),
            pltpu.VMEM((3 * rows * chunks + 96, LANES), f32),
            pltpu.VMEM((rows * chunks, LANES), f32),
            pltpu.VMEM((rows * chunks, LANES), f32),
            pltpu.SemaphoreType.DMA((3,)),
        ],
        compiler_params=pltpu.CompilerParams(vmem_limit_bytes=32 << 20),
        cost_estimate=pl.CostEstimate(flops=64 * rows * width * width, bytes_accessed=10 * rows * width, transcendentals=0),
        name="graph_layer",
    )(core, idx, own, sib, rim, bias, near_w, far_w, ws, wd, w2)


def edge_offsets(nbrs, counts, core):
    graphs, rows, slots = nbrs.shape
    half = rows // 2
    nbr = lax.dynamic_slice(nbrs.transpose(0, 2, 1), (0, 0, core * half), (graphs, slots, half)) - core * half
    count = lax.dynamic_slice(counts, (0, core * half), (graphs, half))
    low = nbr + jnp.where(core == 0, 2 * half, half)
    high = nbr - jnp.where(core == 0, half, 0)
    place = jnp.where(nbr < half, low, jnp.where(nbr < 2 * half, nbr - half, high))
    live = jnp.arange(slots, dtype=jnp.int32)[None, :, None] < count[:, None, :]
    place = jnp.where(live, place, 3 * half)
    odd = jnp.arange(half, dtype=jnp.int32) % 2
    return (4 * (place + 1 - odd)).reshape(graphs, slots * half)


def spread_rows(same, other):
    a = lax.ppermute(same, ("mp", "batch"), [(0, 0), (1, 2), (2, 1), (3, 3)])
    b = lax.ppermute(other, ("mp", "batch"), [(0, 1), (1, 3), (2, 0), (3, 2)])
    return a, b


def gather_rows(a, b):
    same = lax.ppermute(a, ("mp", "batch"), [(0, 0), (1, 2), (2, 1), (3, 3)])
    other = lax.ppermute(b, ("mp", "batch"), [(0, 2), (1, 0), (2, 3), (3, 1)])
    return same, other


def ordered(which, a, b, axis):
    return jnp.where(which == 0, jnp.concatenate([a, b], axis), jnp.concatenate([b, a], axis))


def swap(values, axis):
    return lax.ppermute(values, axis, [(0, 1), (1, 0)])


def rims(own, wrap):
    size = lax.axis_size("mesh")
    pairs = []
    for m in range(size):
        if wrap or m + 1 < size:
            pairs.append((2 * m + 1, 2 * ((m + 1) % size)))
        if wrap or m > 0:
            pairs.append((2 * m, 2 * ((m - 1) % size) + 1))
    return lax.ppermute(own, ("mesh", "batch"), pairs)


def pack_kernel(layers, core_ref, g_bias, r_bias, *refs):
    weights, outs, sems = (refs[:3], refs[3:6]), refs[6:-1], refs[-1]
    share = g_bias.shape[1]
    here = pl.multiple_of(core_ref[0] * share, share)
    copies = []
    for layer, out in zip(layers, outs):
        for graph, (ws, wd, w2) in enumerate(weights):
            base = graph * (3 * share + 16)
            sources = (
                ws.at[layer, pl.ds(here, share), :], wd.at[layer, pl.ds(here, share), :], w2.at[layer, :, pl.ds(here, share)]
            )
            for i, source in enumerate(sources):
                spot = base + i * share
                copies.append(pltpu.make_async_copy(source, out.at[spot:spot + share, :], sems.at[len(copies)]))
                copies[-1].start()
    for layer, out in zip(layers, outs):
        for graph, bias in enumerate((g_bias, r_bias)):
            base = graph * (3 * share + 16) + 3 * share
            out[base:base + 16, :] = jnp.broadcast_to(bias[layer:layer + 1, :], (16, share))
    for copy in copies:
        copy.wait()


def pack_weights(layers, core, g_weights, g_bias, r_weights, r_bias):
    share = g_bias.shape[1]
    vmem = pl.BlockSpec(memory_space=pltpu.VMEM)
    hbm = pl.BlockSpec(memory_space=pltpu.HBM)
    return pl.pallas_call(
        functools.partial(pack_kernel, layers),
        out_shape=(jax.ShapeDtypeStruct((2 * (3 * share + 16), share), jnp.bfloat16),) * len(layers),
        in_specs=[pl.BlockSpec(memory_space=pltpu.SMEM)] + [vmem] * 2 + [hbm] * 6,
        out_specs=(vmem,) * len(layers),
        scratch_shapes=[pltpu.SemaphoreType.DMA((6 * len(layers),))],
        compiler_params=pltpu.CompilerParams(vmem_limit_bytes=60 << 20),
        cost_estimate=pl.CostEstimate(flops=256 * share**3, bytes_accessed=1, transcendentals=0),
        name="pack_weights",
    )(core, g_bias, r_bias, *g_weights, *r_weights)


def by_rows(
    g_nodes, r_nodes, g_nbr, g_count, r_nbr, r_count, bnd_src, bnd_part, bnd_node,
    g_ws, g_wd, g_b1, g_w2, r_ws, r_wd, r_b1, r_w2,
):
    part = lax.axis_index("mp")
    core = lax.axis_index("batch")
    parts = lax.axis_size("mesh")
    slots = g_nbr.shape[1]
    layers = g_ws.shape[0]
    rows = g_nodes.shape[1]
    half = rows // 2
    cap = 2 * bnd_src.shape[0] // parts
    me = lax.axis_index("mesh").reshape(1)
    core1 = core.reshape(1)
    g_own, r_own = g_nodes[0], r_nodes[0]
    g_weights, r_weights = (g_ws, g_wd, g_w2), (r_ws, r_wd, r_w2)
    after = lax.optimization_barrier

    same = lax.dynamic_slice(g_own, (part * half, 0), (half, g_own.shape[1]))
    other = lax.dynamic_slice(g_own, ((1 - part) * half, 0), (half, g_own.shape[1]))
    g_a, g_b = spread_rows(same, other)
    packs = list(pack_weights((0,), core1, g_weights, g_b1, r_weights, r_b1))
    near_w = [swap(packs[0], "mp")]
    bnd = jnp.stack([bnd_src, bnd_part[:, 0], bnd_node])
    bnd, packs[0], same, other = after((bnd, packs[0], same, other))
    pieces = pick_rows(me, bnd, g_own, parts, cap)
    landed = [pieces[0]]
    for k in range(1, parts):
        landed.append(lax.ppermute(pieces[k], "mesh", [(i, (i + k) % parts) for i in range(parts)]))
    landed[0], core1, g_a, g_b = after((landed[0], core1, g_a, g_b))
    idx = edge_offsets(jnp.stack([g_nbr, r_nbr]), jnp.stack([g_count, r_count]), core)
    packs += pack_weights(tuple(range(1, layers)), core1, g_weights, g_b1, r_weights, r_b1)
    g_idx, r_idx = idx[0], idx[1]
    g_a, g_b, g_idx, r_idx, packs[1:], near_w[0], *landed = after(
        (g_a, g_b, g_idx, r_idx, packs[1:], near_w[0], *landed)
    )
    planet = ordered(core, g_a, g_b, 1)
    g_sib, g_rim = swap(planet, "batch"), rims(planet, True)
    *r_pair, packs[1:] = after((*add_force(part.reshape(1), r_own, landed, cap), packs[1:]))
    r_a, r_b = spread_rows(*r_pair)
    near_w += [swap(pack, "mp") for pack in packs[1:]]
    r_a, r_b, g_sib, g_rim = after((r_a, r_b, g_sib, g_rim))
    regional, g_idx = after((ordered(core, r_a, r_b, 1), g_idx))
    r_sib, r_rim = swap(regional, "batch"), rims(regional, False)
    for layer in range(layers):
        last = layer == layers - 1
        far_w = swap(near_w[layer], "batch")
        planet = run_layer(
            layer, 0, slots, last, core1, g_idx, planet, g_sib, g_rim, g_ws, g_wd, g_w2, g_b1, near_w[layer], far_w
        )
        *planet, core1 = after((*(planet if last else (planet,)), core1))
        if not last:
            planet = planet[0]
            g_sib, g_rim = swap(planet, "batch"), rims(planet, True)
            core1, near_w[layer + 1] = after((core1, near_w[layer + 1]))
        regional = run_layer(
            layer, 1, slots, last, core1, r_idx, regional, r_sib, r_rim, r_ws, r_wd, r_w2, r_b1, near_w[layer], far_w
        )
        if not last:
            regional, core1 = after((regional, core1))
            r_sib, r_rim = swap(regional, "batch"), rims(regional, False)
    g_out = ordered(part, *gather_rows(*planet), 0)
    g_out, *regional_rows = after((g_out, *gather_rows(*regional)))
    r_out = ordered(part, *regional_rows, 0)
    return g_out[None], r_out[None]


def solution(mesh):
    in_specs = (
        P(("groups", "batch"), "mesh", "mp"),
        P(("groups", "batch"), "mesh", "mp"),
        P("mesh", None),
        P("mesh"),
        P("mesh", None),
        P("mesh"),
        P("mesh"),
        P("mesh", None),
        P("mesh"),
        P(None, None, "mp"),
        P(None, None, "mp"),
        P(None, "mp"),
        P(None, "mp", None),
        P(None, None, "mp"),
        P(None, None, "mp"),
        P(None, "mp"),
        P(None, "mp", None),
    )
    out_specs = (P(("groups", "batch"), "mesh", "mp"), P(("groups", "batch"), "mesh", "mp"))
    square = mesh.shape["mp"] == 2 and mesh.shape["batch"] == 2
    return jax.shard_map(
        by_rows if square else by_features, mesh=mesh, in_specs=in_specs, out_specs=out_specs, check_vma=False
    )
```

```python
import functools

import jax
import jax.numpy as jnp
from jax import lax
from jax.experimental import pallas as pl
from jax.experimental.pallas import tpu as pltpu
from jax.sharding import PartitionSpec as P

LANES = 128
DEAD = -1e30
SMALL = pl.CostEstimate(flops=1, bytes_accessed=1, transcendentals=0)


def padded_2(shard, sides, width, wrap):
    for axis, dim in sides:
        size, length = (lax.axis_size(axis), shard.shape[dim])
        up = [(i, (i + 1) % size) for i in range(size if wrap else size - 1)]
        down = [(j, i) for i, j in up]
        last = lax.slice_in_dim(shard, length - width, length, axis=dim)
        leading = lax.slice_in_dim(shard, 0, width, axis=dim)
        before = lax.ppermute(last, axis, up)
        after = lax.ppermute(leading, axis, down)
        shard = jnp.concatenate([before, shard, after], axis=dim)
    return shard


def edge_sums(proj, near, nbr, count):
    slots = nbr.shape[1]
    live = jnp.arange(slots, dtype=jnp.int32)[None, :] < count[:, None]
    pre = proj[:, nbr].astype(jnp.float32) + near[:, :, None]
    acts = jnp.where(live[None, :, :, None], jax.nn.silu(pre), 0.0)
    return jnp.sum(acts, axis=2).astype(jnp.bfloat16)


def graph_layer(latent, nbr, count, w_send, w_recv, bias, w_out, wrap):
    rim = latent.shape[1] // 2
    own_full = lax.all_gather(latent, "mp", axis=2, tiled=True)
    padded_full = padded_2(own_full, (("mesh", 1),), rim, wrap)
    proj = jnp.dot(padded_full, w_send, preferred_element_type=jnp.float32).astype(jnp.bfloat16)
    near = jnp.dot(own_full, w_recv, preferred_element_type=jnp.float32) + bias.astype(jnp.float32)
    summed = edge_sums(proj, near, nbr, count)
    partial_prod = jnp.dot(summed, w_out, preferred_element_type=jnp.float32)
    update = lax.psum_scatter(
        partial_prod.astype(jnp.bfloat16), "mp", scatter_dimension=2, tiled=True
    ).astype(jnp.float32)
    return (latent.astype(jnp.float32) + update).astype(jnp.bfloat16)


def by_features(
    g_nodes, r_nodes, g_nbr, g_count, r_nbr, r_count, bnd_src, bnd_part, bnd_node,
    g_ws, g_wd, g_b1, g_w2, r_ws, r_wd, r_b1, r_w2,
):
    batch_rows, reg_rows, feats = r_nodes.shape
    dest = bnd_part[:, 0]
    outgoing = jnp.moveaxis(g_nodes[:, bnd_src], 1, 0)
    init = jnp.zeros((reg_rows + 1, batch_rows, feats), jnp.float32)
    target = dest * reg_rows + bnd_node
    mine = lax.axis_index("mesh")
    piece_rows = lax.all_gather(outgoing, "mesh", axis=0, tiled=True)
    piece_target = lax.all_gather(target, "mesh", axis=0, tiled=True)
    local = jnp.where(piece_target // reg_rows == mine, piece_target % reg_rows + 1, 0)
    landed = init.at[local].add(piece_rows.astype(jnp.float32))
    force = jnp.moveaxis(landed[1:], 1, 0)
    regional = (r_nodes.astype(jnp.float32) + force).astype(jnp.bfloat16)
    planet = g_nodes
    for layer in range(g_ws.shape[0]):
        planet = graph_layer(
            planet, g_nbr, g_count, g_ws[layer], g_wd[layer], g_b1[layer], g_w2[layer], True
        )
    for layer in range(r_ws.shape[0]):
        regional = graph_layer(
            regional, r_nbr, r_count, r_ws[layer], r_wd[layer], r_b1[layer], r_w2[layer], False
        )
    return (planet, regional)


def one_hot(flags):
    return jnp.where(flags, 1.0, 0.0).astype(jnp.bfloat16)


def pick_kernel(parts, cap, me_ref, bnd_ref, g_ref, *out_refs):
    rows = g_ref.shape[0]
    total = bnd_ref.shape[1]
    me = me_ref[0]
    src, part, node = (bnd_ref[i:i + 1, :] for i in range(3))
    lines = -(-parts // 8) * 8
    target = lax.rem(lax.broadcasted_iota(jnp.int32, (lines, total), 0) + me, parts)
    named = part == target
    before = one_hot(
        lax.broadcasted_iota(jnp.int32, (total, total), 0) < lax.broadcasted_iota(jnp.int32, (total, total), 1)
    )
    rank = jnp.dot(one_hot(named), before, preferred_element_type=jnp.float32)
    rank = jnp.where(named, rank, -1.0)
    source = one_hot(lax.broadcasted_iota(jnp.int32, (rows, total), 0) == src)
    line = lax.broadcasted_iota(jnp.int32, (16, total), 0)
    high = lax.shift_right_logical(node, 7)
    facts = jnp.where(line == 0, high, jnp.where(line == 1, node - high * 128, jnp.where(line == 2, 1, 0)))
    facts = facts.astype(jnp.float32).astype(jnp.bfloat16)
    place = lax.broadcasted_iota(jnp.int32, (cap, total), 0).astype(jnp.float32)
    across = (((1,), (1,)), ((), ()))
    for k in range(parts):
        chosen = one_hot(place == rank[k:k + 1, :])
        pick = lax.dot_general(chosen, source, across, preferred_element_type=jnp.float32).astype(jnp.bfloat16)
        out_refs[k][:cap, :] = jnp.dot(pick, g_ref[...], preferred_element_type=jnp.float32).astype(jnp.bfloat16)
        told = lax.dot_general(facts, chosen, across, preferred_element_type=jnp.float32)
        out_refs[k][cap:, :] = told.astype(jnp.bfloat16)


def pick_rows(me, bnd, nodes, parts, cap):
    vmem = pl.BlockSpec(memory_space=pltpu.VMEM)
    rows, feats = nodes.shape
    total = bnd.shape[1]
    piece = jax.ShapeDtypeStruct((cap + 16, feats), jnp.bfloat16)
    return pl.pallas_call(
        functools.partial(pick_kernel, parts, cap),
        out_shape=(piece,) * parts,
        in_specs=[pl.BlockSpec(memory_space=pltpu.SMEM), vmem, vmem],
        out_specs=(vmem,) * parts,
        compiler_params=pltpu.CompilerParams(vmem_limit_bytes=32 << 20),
        cost_estimate=pl.CostEstimate(flops=32 * rows**2 * feats, bytes_accessed=1, transcendentals=0),
        name="pick_rows",
    )(me, bnd, nodes)


def force_kernel(cap, first_ref, r_ref, *refs):
    pieces, (same_ref, other_ref) = refs[:-2], refs[-2:]
    half = same_ref.shape[0]
    first = first_ref[0]
    for out_ref, start in ((same_ref, first * half), (other_ref, (1 - first) * half)):
        start = pl.multiple_of(start, 16)
        row = (lax.broadcasted_iota(jnp.int32, (half, cap), 0) + start).astype(jnp.float32)
        total = r_ref[pl.ds(start, half), :].astype(jnp.float32)
        for piece in pieces:
            facts = piece[cap:, :].astype(jnp.float32)
            node = jnp.where(facts[2:3, :] > 0.5, facts[0:1, :] * 128.0 + facts[1:2, :], -1.0)
            total += jnp.dot(one_hot(row == node), piece[:cap, :], preferred_element_type=jnp.float32)
        out_ref[...] = total.astype(jnp.bfloat16)


def add_force(first, nodes, pieces, cap):
    vmem = pl.BlockSpec(memory_space=pltpu.VMEM)
    rows, feats = nodes.shape
    block = jax.ShapeDtypeStruct((rows // 2, feats), jnp.bfloat16)
    return pl.pallas_call(
        functools.partial(force_kernel, cap),
        out_shape=(block, block),
        in_specs=[pl.BlockSpec(memory_space=pltpu.SMEM)] + [vmem] * (1 + len(pieces)),
        out_specs=(vmem, vmem),
        compiler_params=pltpu.CompilerParams(vmem_limit_bytes=32 << 20),
        cost_estimate=SMALL,
        name="add_force",
    )(first, nodes, *pieces)


def layer_kernel(
    layer, place, slots, last, core_ref, idx_ref, own, sib, rim, bias, near_w, far_w, ws_hbm, wd_hbm, w2_hbm, *refs
):
    outs, refs = (refs[:2], refs[2:]) if last else (refs[:1], refs[1:])
    ws, wd, w2, ws_x, wd_x, w2_x, proj, near, summed, sems = refs
    rows, width = own.shape
    share = width // 2
    chunks = width // LANES
    part = chunks // 2
    core = core_ref[0]
    pairs = ((wd_hbm, wd), (ws_hbm, ws), (w2_hbm, w2))
    copies = [pltpu.make_async_copy(src.at[layer], dst, sems.at[i]) for i, (src, dst) in enumerate(pairs)]
    for copy in copies:
        copy.start()
    window = 3 * rows
    proj[0:8, :] = jnp.full((8, LANES), DEAD, jnp.float32)
    proj[4 * window + 4:4 * window + 16, :] = jnp.full((12, LANES), DEAD, jnp.float32)
    pack = place * (3 * share + 16)
    here, there = pl.multiple_of(core * share, 16), pl.multiple_of((1 - core) * share, 16)
    for spot, piece in ((here, near_w), (there, far_w)):
        ws_x[pl.ds(spot, share), :] = piece[pack:pack + share, :]
        wd_x[pl.ds(spot, share), :] = piece[pack + share:pack + 2 * share, :]
    third = slice(pack + 2 * share, pack + 3 * share)

    @pl.when(core == 0)
    def _():
        w2_x[:, :share] = near_w[third, :]
        w2_x[:, share:] = far_w[third, :]

    @pl.when(core != 0)
    def _():
        w2_x[:, share:] = near_w[third, :]
        w2_x[:, :share] = far_w[third, :]

    def put(dst, base, first, values):
        for c in range(values.shape[1] // LANES):
            dst[pl.ds(base * chunks + first + c, rows, stride=chunks), :] = values[:, c * LANES:(c + 1) * LANES] * 0.5

    def product(values, weights):
        return jnp.dot(values[...], weights[...], preferred_element_type=jnp.float32)

    b_own = bias[layer:layer + 1, :].astype(jnp.float32)
    b_other = near_w[pack + 3 * share:pack + 3 * share + 1, :].astype(jnp.float32)
    put(near, 0, part, product(own, wd_x) + b_other)
    put(proj, 1, part, product(own, ws_x))
    copies[0].wait()
    copies[1].wait()
    put(near, 0, 0, product(own, wd) + b_own)
    put(proj, 1, 0, product(own, ws))
    for ref, base in ((sib, rows + 1), (rim, 2 * rows + 1)):
        put(proj, base, 0, product(ref, ws))
        put(proj, base, part, product(ref, ws_x))
    low = lax.broadcasted_iota(jnp.int32, (8, LANES), 0) < chunks

    def nodes(q, carry):
        spot = pl.ds(pl.multiple_of(8 * q, 8), 8)
        mine = near[spot, :]
        total = None
        for j in range(slots):
            upper = proj[pl.ds(pl.multiple_of(idx_ref[j * rows + 2 * q], 4), 8), :]
            lower = proj[pl.ds(pl.multiple_of(idx_ref[j * rows + 2 * q + 1], 4), 8), :]
            y = jnp.where(low, upper, lower) + mine
            act = y * jnp.tanh(y) + y
            total = act if total is None else total + act
        summed[spot, :] = total
        return carry

    lax.fori_loop(0, rows // 2, nodes, 0, unroll=16)
    copies[2].wait()
    sums = [summed[pl.ds(c, rows, stride=chunks), :].astype(jnp.bfloat16) for c in range(chunks)]
    update = product(jnp.concatenate(sums[:part], 1), w2) + product(jnp.concatenate(sums[part:], 1), w2_x)
    result = (own[...].astype(jnp.float32) + update).astype(jnp.bfloat16)
    if not last:
        outs[0][...] = result
    else:
        @pl.when(core == 0)
        def _():
            outs[0][...] = result[:, :share]
            outs[1][...] = result[:, share:]

        @pl.when(core != 0)
        def _():
            outs[0][...] = result[:, share:]
            outs[1][...] = result[:, :share]


def run_layer(layer, place, slots, last, core, idx, own, sib, rim, ws, wd, w2, bias, near_w, far_w):
    rows, width = own.shape
    share = width // 2
    chunks = width // LANES
    smem = pl.BlockSpec(memory_space=pltpu.SMEM)
    vmem = pl.BlockSpec(memory_space=pltpu.VMEM)
    bf16, f32 = jnp.bfloat16, jnp.float32
    if last:
        out_shape = (jax.ShapeDtypeStruct((rows, share), bf16),) * 2
        out_specs = (vmem, vmem)
    else:
        out_shape, out_specs = jax.ShapeDtypeStruct((rows, width), bf16), vmem
    return pl.pallas_call(
        functools.partial(layer_kernel, layer, place, slots, last),
        out_shape=out_shape,
        in_specs=[smem] * 2 + [vmem] * 6 + [pl.BlockSpec(memory_space=pl.ANY)] * 3,
        out_specs=out_specs,
        scratch_shapes=[
            pltpu.VMEM((width, share), bf16),
            pltpu.VMEM((width, share), bf16),
            pltpu.VMEM((share, width), bf16),
            pltpu.VMEM((width, share), bf16),
            pltpu.VMEM((width, share), bf16),
            pltpu.VMEM((share, width), bf16),
            pltpu.VMEM((3 * rows * chunks + 96, LANES), f32),
            pltpu.VMEM((rows * chunks, LANES), f32),
            pltpu.VMEM((rows * chunks, LANES), f32),
            pltpu.SemaphoreType.DMA((3,)),
        ],
        compiler_params=pltpu.CompilerParams(vmem_limit_bytes=32 << 20),
        cost_estimate=pl.CostEstimate(flops=64 * rows * width * width, bytes_accessed=10 * rows * width, transcendentals=0),
        name="graph_layer",
    )(core, idx, own, sib, rim, bias, near_w, far_w, ws, wd, w2)


def edge_offsets(nbrs, counts, core):
    graphs, rows, slots = nbrs.shape
    half = rows // 2
    nbr = lax.dynamic_slice(nbrs.transpose(0, 2, 1), (0, 0, core * half), (graphs, slots, half)) - core * half
    count = lax.dynamic_slice(counts, (0, core * half), (graphs, half))
    low = nbr + jnp.where(core == 0, 2 * half, half)
    high = nbr - jnp.where(core == 0, half, 0)
    place = jnp.where(nbr < half, low, jnp.where(nbr < 2 * half, nbr - half, high))
    live = jnp.arange(slots, dtype=jnp.int32)[None, :, None] < count[:, None, :]
    place = jnp.where(live, place, 3 * half)
    odd = jnp.arange(half, dtype=jnp.int32) % 2
    return (4 * (place + 1 - odd)).reshape(graphs, slots * half)


def spread_rows(same, other):
    a = lax.ppermute(same, ("mp", "batch"), [(0, 0), (1, 2), (2, 1), (3, 3)])
    b = lax.ppermute(other, ("mp", "batch"), [(0, 1), (1, 3), (2, 0), (3, 2)])
    return a, b


def gather_rows(a, b):
    same = lax.ppermute(a, ("mp", "batch"), [(0, 0), (1, 2), (2, 1), (3, 3)])
    other = lax.ppermute(b, ("mp", "batch"), [(0, 2), (1, 0), (2, 3), (3, 1)])
    return same, other


def ordered(which, a, b, axis):
    return jnp.where(which == 0, jnp.concatenate([a, b], axis), jnp.concatenate([b, a], axis))


def swap(values, axis):
    return lax.ppermute(values, axis, [(0, 1), (1, 0)])


def rims(own, wrap):
    size = lax.axis_size("mesh")
    pairs = []
    for m in range(size):
        if wrap or m + 1 < size:
            pairs.append((2 * m + 1, 2 * ((m + 1) % size)))
        if wrap or m > 0:
            pairs.append((2 * m, 2 * ((m - 1) % size) + 1))
    return lax.ppermute(own, ("mesh", "batch"), pairs)


def pack_kernel(plan, core_ref, g_bias, r_bias, *refs):
    weights, outs, sems = (refs[:3], refs[3:6]), refs[6:-1], refs[-1]
    share = g_bias.shape[1]
    here = pl.multiple_of(core_ref[0] * share, share)
    copies = []
    for members, out in zip(plan, outs):
        for place, (graph, layer) in enumerate(members):
            ws, wd, w2 = weights[graph]
            base = place * (3 * share + 16)
            sources = (
                ws.at[layer, pl.ds(here, share), :], wd.at[layer, pl.ds(here, share), :], w2.at[layer, :, pl.ds(here, share)]
            )
            for i, source in enumerate(sources):
                spot = base + i * share
                copies.append(pltpu.make_async_copy(source, out.at[spot:spot + share, :], sems.at[len(copies)]))
                copies[-1].start()
    for members, out in zip(plan, outs):
        for place, (graph, layer) in enumerate(members):
            base = place * (3 * share + 16) + 3 * share
            bias = (g_bias, r_bias)[graph][layer:layer + 1, :]
            out[base:base + 16, :] = jnp.broadcast_to(bias, (16, share))
    for copy in copies:
        copy.wait()


def pack_weights(plan, core, g_weights, g_bias, r_weights, r_bias):
    share = g_bias.shape[1]
    vmem = pl.BlockSpec(memory_space=pltpu.VMEM)
    hbm = pl.BlockSpec(memory_space=pltpu.HBM)
    sizes = [len(members) for members in plan]
    return pl.pallas_call(
        functools.partial(pack_kernel, plan),
        out_shape=tuple(jax.ShapeDtypeStruct((n * (3 * share + 16), share), jnp.bfloat16) for n in sizes),
        in_specs=[pl.BlockSpec(memory_space=pltpu.SMEM)] + [vmem] * 2 + [hbm] * 6,
        out_specs=(vmem,) * len(sizes),
        scratch_shapes=[pltpu.SemaphoreType.DMA((3 * sum(sizes),))],
        compiler_params=pltpu.CompilerParams(vmem_limit_bytes=60 << 20),
        cost_estimate=pl.CostEstimate(flops=256 * share**3, bytes_accessed=1, transcendentals=0),
        name="pack_weights",
    )(core, g_bias, r_bias, *g_weights, *r_weights)


def by_rows(
    g_nodes, r_nodes, g_nbr, g_count, r_nbr, r_count, bnd_src, bnd_part, bnd_node,
    g_ws, g_wd, g_b1, g_w2, r_ws, r_wd, r_b1, r_w2,
):
    part = lax.axis_index("mp")
    core = lax.axis_index("batch")
    parts = lax.axis_size("mesh")
    slots = g_nbr.shape[1]
    layers = g_ws.shape[0]
    rows = g_nodes.shape[1]
    half = rows // 2
    cap = 2 * bnd_src.shape[0] // parts
    me = lax.axis_index("mesh").reshape(1)
    core1 = core.reshape(1)
    g_own, r_own = g_nodes[0], r_nodes[0]
    g_weights, r_weights = (g_ws, g_wd, g_w2), (r_ws, r_wd, r_w2)
    after = lax.optimization_barrier

    same = lax.dynamic_slice(g_own, (part * half, 0), (half, g_own.shape[1]))
    other = lax.dynamic_slice(g_own, ((1 - part) * half, 0), (half, g_own.shape[1]))
    g_a, g_b = spread_rows(same, other)
    packs = list(pack_weights((((0, 0), (1, 0)),), core1, g_weights, g_b1, r_weights, r_b1))
    near_w = [swap(packs[0], "mp")]
    bnd = jnp.stack([bnd_src, bnd_part[:, 0], bnd_node])
    bnd, packs[0], same, other = after((bnd, packs[0], same, other))
    pieces = pick_rows(me, bnd, g_own, parts, cap)
    landed = [pieces[0]]
    for k in range(1, parts):
        landed.append(lax.ppermute(pieces[k], "mesh", [(i, (i + k) % parts) for i in range(parts)]))
    landed[0], core1, g_a, g_b = after((landed[0], core1, g_a, g_b))
    idx = edge_offsets(jnp.stack([g_nbr, r_nbr]), jnp.stack([g_count, r_count]), core)
    rest = tuple(((graph, layer),) for layer in range(1, layers) for graph in (0, 1))
    packs += pack_weights(rest, core1, g_weights, g_b1, r_weights, r_b1)
    g_idx, r_idx = idx[0], idx[1]
    g_a, g_b, g_idx, r_idx, packs[1:], near_w[0], *landed = after(
        (g_a, g_b, g_idx, r_idx, packs[1:], near_w[0], *landed)
    )
    planet = ordered(core, g_a, g_b, 1)
    g_sib, g_rim = swap(planet, "batch"), rims(planet, True)
    *r_pair, packs[1:] = after((*add_force(part.reshape(1), r_own, landed, cap), packs[1:]))
    r_a, r_b = spread_rows(*r_pair)
    near_w.append(swap(packs[1], "mp"))
    r_a, r_b, g_sib, g_rim = after((r_a, r_b, g_sib, g_rim))
    regional, g_idx = after((ordered(core, r_a, r_b, 1), g_idx))
    r_sib, r_rim = swap(regional, "batch"), rims(regional, False)
    far_w = [swap(near_w[0], "batch")]
    for layer in range(layers):
        last = layer == layers - 1
        i = max(0, 2 * layer - 1)
        if layer:
            far_w.append(swap(near_w[i], "batch"))
        planet = run_layer(
            layer, 0, slots, last, core1, g_idx, planet, g_sib, g_rim, g_ws, g_wd, g_w2, g_b1, near_w[i], far_w[i]
        )
        *planet, core1 = after((*(planet if last else (planet,)), core1))
        if not last:
            planet = planet[0]
            g_sib, g_rim = swap(planet, "batch"), rims(planet, True)
        if layer:
            i += 1
            near_w[i], core1 = after((near_w[i], core1))
            far_w.append(swap(near_w[i], "batch"))
        for j in range(i + 1, min(i + 3, len(packs))):
            if j == len(near_w):
                packs[j], near_w[j - 1] = after((packs[j], near_w[j - 1]))
                near_w.append(swap(packs[j], "mp"))
            if j == i + 1:
                core1, near_w[j] = after((core1, near_w[j]))
        regional = run_layer(
            layer, 1 - min(layer, 1), slots, last, core1, r_idx, regional, r_sib, r_rim, r_ws, r_wd, r_w2, r_b1,
            near_w[i], far_w[i],
        )
        if not last:
            regional, core1 = after((regional, core1))
            r_sib, r_rim = swap(regional, "batch"), rims(regional, False)
    g_out = ordered(part, *gather_rows(*planet), 0)
    g_out, *regional_rows = after((g_out, *gather_rows(*regional)))
    r_out = ordered(part, *regional_rows, 0)
    return g_out[None], r_out[None]


def solution(mesh):
    in_specs = (
        P(("groups", "batch"), "mesh", "mp"),
        P(("groups", "batch"), "mesh", "mp"),
        P("mesh", None),
        P("mesh"),
        P("mesh", None),
        P("mesh"),
        P("mesh"),
        P("mesh", None),
        P("mesh"),
        P(None, None, "mp"),
        P(None, None, "mp"),
        P(None, "mp"),
        P(None, "mp", None),
        P(None, None, "mp"),
        P(None, None, "mp"),
        P(None, "mp"),
        P(None, "mp", None),
    )
    out_specs = (P(("groups", "batch"), "mesh", "mp"), P(("groups", "batch"), "mesh", "mp"))
    square = mesh.shape["mp"] == 2 and mesh.shape["batch"] == 2
    return jax.shard_map(
        by_rows if square else by_features, mesh=mesh, in_specs=in_specs, out_specs=out_specs, check_vma=False
    )
```

```python
import functools

import jax
import jax.numpy as jnp
from jax import lax
from jax.experimental import pallas as pl
from jax.experimental.pallas import tpu as pltpu
from jax.sharding import PartitionSpec as P

LANES = 128
DEAD = -1e30
SMALL = pl.CostEstimate(flops=1, bytes_accessed=1, transcendentals=0)


def padded_2(shard, sides, width, wrap):
    for axis, dim in sides:
        size, length = (lax.axis_size(axis), shard.shape[dim])
        up = [(i, (i + 1) % size) for i in range(size if wrap else size - 1)]
        down = [(j, i) for i, j in up]
        last = lax.slice_in_dim(shard, length - width, length, axis=dim)
        leading = lax.slice_in_dim(shard, 0, width, axis=dim)
        before = lax.ppermute(last, axis, up)
        after = lax.ppermute(leading, axis, down)
        shard = jnp.concatenate([before, shard, after], axis=dim)
    return shard


def edge_sums(proj, near, nbr, count):
    slots = nbr.shape[1]
    live = jnp.arange(slots, dtype=jnp.int32)[None, :] < count[:, None]
    pre = proj[:, nbr].astype(jnp.float32) + near[:, :, None]
    acts = jnp.where(live[None, :, :, None], jax.nn.silu(pre), 0.0)
    return jnp.sum(acts, axis=2).astype(jnp.bfloat16)


def graph_layer(latent, nbr, count, w_send, w_recv, bias, w_out, wrap):
    rim = latent.shape[1] // 2
    own_full = lax.all_gather(latent, "mp", axis=2, tiled=True)
    padded_full = padded_2(own_full, (("mesh", 1),), rim, wrap)
    proj = jnp.dot(padded_full, w_send, preferred_element_type=jnp.float32).astype(jnp.bfloat16)
    near = jnp.dot(own_full, w_recv, preferred_element_type=jnp.float32) + bias.astype(jnp.float32)
    summed = edge_sums(proj, near, nbr, count)
    partial_prod = jnp.dot(summed, w_out, preferred_element_type=jnp.float32)
    update = lax.psum_scatter(
        partial_prod.astype(jnp.bfloat16), "mp", scatter_dimension=2, tiled=True
    ).astype(jnp.float32)
    return (latent.astype(jnp.float32) + update).astype(jnp.bfloat16)


def by_features(
    g_nodes, r_nodes, g_nbr, g_count, r_nbr, r_count, bnd_src, bnd_part, bnd_node,
    g_ws, g_wd, g_b1, g_w2, r_ws, r_wd, r_b1, r_w2,
):
    batch_rows, reg_rows, feats = r_nodes.shape
    dest = bnd_part[:, 0]
    outgoing = jnp.moveaxis(g_nodes[:, bnd_src], 1, 0)
    init = jnp.zeros((reg_rows + 1, batch_rows, feats), jnp.float32)
    target = dest * reg_rows + bnd_node
    mine = lax.axis_index("mesh")
    piece_rows = lax.all_gather(outgoing, "mesh", axis=0, tiled=True)
    piece_target = lax.all_gather(target, "mesh", axis=0, tiled=True)
    local = jnp.where(piece_target // reg_rows == mine, piece_target % reg_rows + 1, 0)
    landed = init.at[local].add(piece_rows.astype(jnp.float32))
    force = jnp.moveaxis(landed[1:], 1, 0)
    regional = (r_nodes.astype(jnp.float32) + force).astype(jnp.bfloat16)
    planet = g_nodes
    for layer in range(g_ws.shape[0]):
        planet = graph_layer(
            planet, g_nbr, g_count, g_ws[layer], g_wd[layer], g_b1[layer], g_w2[layer], True
        )
    for layer in range(r_ws.shape[0]):
        regional = graph_layer(
            regional, r_nbr, r_count, r_ws[layer], r_wd[layer], r_b1[layer], r_w2[layer], False
        )
    return (planet, regional)


def one_hot(flags):
    return jnp.where(flags, 1.0, 0.0).astype(jnp.bfloat16)


def pick_kernel(parts, cap, me_ref, bnd_ref, g_ref, *out_refs):
    rows = g_ref.shape[0]
    total = bnd_ref.shape[1]
    me = me_ref[0]
    src, part, node = (bnd_ref[i:i + 1, :] for i in range(3))
    lines = -(-parts // 8) * 8
    target = lax.rem(lax.broadcasted_iota(jnp.int32, (lines, total), 0) + me, parts)
    named = part == target
    before = one_hot(
        lax.broadcasted_iota(jnp.int32, (total, total), 0) < lax.broadcasted_iota(jnp.int32, (total, total), 1)
    )
    rank = jnp.dot(one_hot(named), before, preferred_element_type=jnp.float32)
    rank = jnp.where(named, rank, -1.0)
    source = one_hot(lax.broadcasted_iota(jnp.int32, (rows, total), 0) == src)
    line = lax.broadcasted_iota(jnp.int32, (16, total), 0)
    high = lax.shift_right_logical(node, 7)
    facts = jnp.where(line == 0, high, jnp.where(line == 1, node - high * 128, jnp.where(line == 2, 1, 0)))
    facts = facts.astype(jnp.float32).astype(jnp.bfloat16)
    place = lax.broadcasted_iota(jnp.int32, (cap, total), 0).astype(jnp.float32)
    across = (((1,), (1,)), ((), ()))
    for k in range(parts):
        chosen = one_hot(place == rank[k:k + 1, :])
        pick = lax.dot_general(chosen, source, across, preferred_element_type=jnp.float32).astype(jnp.bfloat16)
        out_refs[k][:cap, :] = jnp.dot(pick, g_ref[...], preferred_element_type=jnp.float32).astype(jnp.bfloat16)
        told = lax.dot_general(facts, chosen, across, preferred_element_type=jnp.float32)
        out_refs[k][cap:, :] = told.astype(jnp.bfloat16)


def pick_rows(me, bnd, nodes, parts, cap):
    vmem = pl.BlockSpec(memory_space=pltpu.VMEM)
    rows, feats = nodes.shape
    total = bnd.shape[1]
    piece = jax.ShapeDtypeStruct((cap + 16, feats), jnp.bfloat16)
    return pl.pallas_call(
        functools.partial(pick_kernel, parts, cap),
        out_shape=(piece,) * parts,
        in_specs=[pl.BlockSpec(memory_space=pltpu.SMEM), vmem, vmem],
        out_specs=(vmem,) * parts,
        compiler_params=pltpu.CompilerParams(vmem_limit_bytes=32 << 20),
        cost_estimate=pl.CostEstimate(flops=32 * rows**2 * feats, bytes_accessed=1, transcendentals=0),
        name="pick_rows",
    )(me, bnd, nodes)


def force_kernel(cap, first_ref, r_ref, *refs):
    pieces, (same_ref, other_ref) = refs[:-2], refs[-2:]
    half = same_ref.shape[0]
    first = first_ref[0]
    for out_ref, start in ((same_ref, first * half), (other_ref, (1 - first) * half)):
        start = pl.multiple_of(start, 16)
        row = (lax.broadcasted_iota(jnp.int32, (half, cap), 0) + start).astype(jnp.float32)
        total = r_ref[pl.ds(start, half), :].astype(jnp.float32)
        for piece in pieces:
            facts = piece[cap:, :].astype(jnp.float32)
            node = jnp.where(facts[2:3, :] > 0.5, facts[0:1, :] * 128.0 + facts[1:2, :], -1.0)
            total += jnp.dot(one_hot(row == node), piece[:cap, :], preferred_element_type=jnp.float32)
        out_ref[...] = total.astype(jnp.bfloat16)


def add_force(first, nodes, pieces, cap):
    vmem = pl.BlockSpec(memory_space=pltpu.VMEM)
    rows, feats = nodes.shape
    block = jax.ShapeDtypeStruct((rows // 2, feats), jnp.bfloat16)
    return pl.pallas_call(
        functools.partial(force_kernel, cap),
        out_shape=(block, block),
        in_specs=[pl.BlockSpec(memory_space=pltpu.SMEM)] + [vmem] * (1 + len(pieces)),
        out_specs=(vmem, vmem),
        compiler_params=pltpu.CompilerParams(vmem_limit_bytes=32 << 20),
        cost_estimate=SMALL,
        name="add_force",
    )(first, nodes, *pieces)


def layer_kernel(
    layer, slots, last, core_ref, idx_ref, own, sib, rim, bias, near_w, far_w, ws_hbm, wd_hbm, w2_hbm, *refs
):
    outs, refs = (refs[:2], refs[2:]) if last else (refs[:1], refs[1:])
    ws, wd, w2, ws_x, wd_x, w2_x, proj, near, summed, sems = refs
    rows, width = own.shape
    share = width // 2
    chunks = width // LANES
    part = chunks // 2
    core = core_ref[0]
    pairs = ((wd_hbm, wd), (ws_hbm, ws), (w2_hbm, w2))
    copies = [pltpu.make_async_copy(src.at[layer], dst, sems.at[i]) for i, (src, dst) in enumerate(pairs)]
    for copy in copies:
        copy.start()
    window = 3 * rows
    proj[0:8, :] = jnp.full((8, LANES), DEAD, jnp.float32)
    proj[4 * window + 4:4 * window + 16, :] = jnp.full((12, LANES), DEAD, jnp.float32)
    here, there = pl.multiple_of(core * share, 16), pl.multiple_of((1 - core) * share, 16)
    for spot, piece in ((here, near_w), (there, far_w)):
        ws_x[pl.ds(spot, share), :] = piece[0:share, :]
        wd_x[pl.ds(spot, share), :] = piece[share:2 * share, :]

    @pl.when(core == 0)
    def _():
        w2_x[:, :share] = near_w[2 * share:3 * share, :]
        w2_x[:, share:] = far_w[2 * share:3 * share, :]

    @pl.when(core != 0)
    def _():
        w2_x[:, share:] = near_w[2 * share:3 * share, :]
        w2_x[:, :share] = far_w[2 * share:3 * share, :]

    def put(dst, base, first, values):
        for c in range(values.shape[1] // LANES):
            dst[pl.ds(base * chunks + first + c, rows, stride=chunks), :] = values[:, c * LANES:(c + 1) * LANES] * 0.5

    def product(values, weights):
        return jnp.dot(values[...], weights[...], preferred_element_type=jnp.float32)

    b_own = bias[layer:layer + 1, :].astype(jnp.float32)
    b_other = near_w[3 * share:3 * share + 1, :].astype(jnp.float32)
    put(near, 0, part, product(own, wd_x) + b_other)
    put(proj, 1, part, product(own, ws_x))
    copies[0].wait()
    copies[1].wait()
    put(near, 0, 0, product(own, wd) + b_own)
    put(proj, 1, 0, product(own, ws))
    for ref, base in ((sib, rows + 1), (rim, 2 * rows + 1)):
        put(proj, base, 0, product(ref, ws))
        put(proj, base, part, product(ref, ws_x))
    low = lax.broadcasted_iota(jnp.int32, (8, LANES), 0) < chunks

    def nodes(q, carry):
        spot = pl.ds(pl.multiple_of(8 * q, 8), 8)
        mine = near[spot, :]
        total = None
        for j in range(slots):
            upper = proj[pl.ds(pl.multiple_of(idx_ref[j * rows + 2 * q], 4), 8), :]
            lower = proj[pl.ds(pl.multiple_of(idx_ref[j * rows + 2 * q + 1], 4), 8), :]
            y = jnp.where(low, upper, lower) + mine
            act = y * jnp.tanh(y) + y
            total = act if total is None else total + act
        summed[spot, :] = total
        return carry

    lax.fori_loop(0, rows // 2, nodes, 0, unroll=16)
    copies[2].wait()
    sums = [summed[pl.ds(c, rows, stride=chunks), :].astype(jnp.bfloat16) for c in range(chunks)]
    update = product(jnp.concatenate(sums[:part], 1), w2) + product(jnp.concatenate(sums[part:], 1), w2_x)
    result = (own[...].astype(jnp.float32) + update).astype(jnp.bfloat16)
    if not last:
        outs[0][...] = result
    else:
        @pl.when(core == 0)
        def _():
            outs[0][...] = result[:, :share]
            outs[1][...] = result[:, share:]

        @pl.when(core != 0)
        def _():
            outs[0][...] = result[:, share:]
            outs[1][...] = result[:, :share]


def run_layer(layer, slots, last, core, idx, own, sib, rim, ws, wd, w2, bias, near_w, far_w):
    rows, width = own.shape
    share = width // 2
    chunks = width // LANES
    smem = pl.BlockSpec(memory_space=pltpu.SMEM)
    vmem = pl.BlockSpec(memory_space=pltpu.VMEM)
    bf16, f32 = jnp.bfloat16, jnp.float32
    if last:
        out_shape = (jax.ShapeDtypeStruct((rows, share), bf16),) * 2
        out_specs = (vmem, vmem)
    else:
        out_shape, out_specs = jax.ShapeDtypeStruct((rows, width), bf16), vmem
    return pl.pallas_call(
        functools.partial(layer_kernel, layer, slots, last),
        out_shape=out_shape,
        in_specs=[smem] * 2 + [vmem] * 6 + [pl.BlockSpec(memory_space=pl.ANY)] * 3,
        out_specs=out_specs,
        scratch_shapes=[
            pltpu.VMEM((width, share), bf16),
            pltpu.VMEM((width, share), bf16),
            pltpu.VMEM((share, width), bf16),
            pltpu.VMEM((width, share), bf16),
            pltpu.VMEM((width, share), bf16),
            pltpu.VMEM((share, width), bf16),
            pltpu.VMEM((3 * rows * chunks + 96, LANES), f32),
            pltpu.VMEM((rows * chunks, LANES), f32),
            pltpu.VMEM((rows * chunks, LANES), f32),
            pltpu.SemaphoreType.DMA((3,)),
        ],
        compiler_params=pltpu.CompilerParams(vmem_limit_bytes=32 << 20),
        cost_estimate=pl.CostEstimate(flops=64 * rows * width * width, bytes_accessed=10 * rows * width, transcendentals=0),
        name="graph_layer",
    )(core, idx, own, sib, rim, bias, near_w, far_w, ws, wd, w2)


def edge_offsets(nbrs, counts, core):
    graphs, rows, slots = nbrs.shape
    half = rows // 2
    nbr = lax.dynamic_slice(nbrs.transpose(0, 2, 1), (0, 0, core * half), (graphs, slots, half)) - core * half
    count = lax.dynamic_slice(counts, (0, core * half), (graphs, half))
    low = nbr + jnp.where(core == 0, 2 * half, half)
    high = nbr - jnp.where(core == 0, half, 0)
    place = jnp.where(nbr < half, low, jnp.where(nbr < 2 * half, nbr - half, high))
    live = jnp.arange(slots, dtype=jnp.int32)[None, :, None] < count[:, None, :]
    place = jnp.where(live, place, 3 * half)
    odd = jnp.arange(half, dtype=jnp.int32) % 2
    return (4 * (place + 1 - odd)).reshape(graphs, slots * half)


def spread_rows(same, other):
    a = lax.ppermute(same, ("mp", "batch"), [(0, 0), (1, 2), (2, 1), (3, 3)])
    b = lax.ppermute(other, ("mp", "batch"), [(0, 1), (1, 3), (2, 0), (3, 2)])
    return a, b


def gather_rows(a, b):
    same = lax.ppermute(a, ("mp", "batch"), [(0, 0), (1, 2), (2, 1), (3, 3)])
    other = lax.ppermute(b, ("mp", "batch"), [(0, 2), (1, 0), (2, 3), (3, 1)])
    return same, other


def ordered(which, a, b, axis):
    return jnp.where(which == 0, jnp.concatenate([a, b], axis), jnp.concatenate([b, a], axis))


def swap(values, axis):
    return lax.ppermute(values, axis, [(0, 1), (1, 0)])


def rims(own, wrap):
    size = lax.axis_size("mesh")
    pairs = []
    for m in range(size):
        if wrap or m + 1 < size:
            pairs.append((2 * m + 1, 2 * ((m + 1) % size)))
        if wrap or m > 0:
            pairs.append((2 * m, 2 * ((m - 1) % size) + 1))
    return lax.ppermute(own, ("mesh", "batch"), pairs)


def pack_kernel(order, core_ref, g_bias, r_bias, *refs):
    weights, outs, sems = (refs[:3], refs[3:6]), refs[6:-1], refs[-1]
    share = g_bias.shape[1]
    here = pl.multiple_of(core_ref[0] * share, share)
    copies = []
    for (graph, layer), out in zip(order, outs):
        ws, wd, w2 = weights[graph]
        sources = (ws.at[layer, pl.ds(here, share), :], wd.at[layer, pl.ds(here, share), :], w2.at[layer, :, pl.ds(here, share)])
        for i, source in enumerate(sources):
            copies.append(pltpu.make_async_copy(source, out.at[i * share:(i + 1) * share, :], sems.at[len(copies)]))
            copies[-1].start()
    for (graph, layer), out in zip(order, outs):
        bias = (g_bias, r_bias)[graph][layer:layer + 1, :]
        out[3 * share:, :] = jnp.broadcast_to(bias, (16, share))
    for copy in copies:
        copy.wait()


def pack_weights(order, core, g_weights, g_bias, r_weights, r_bias):
    share = g_bias.shape[1]
    vmem = pl.BlockSpec(memory_space=pltpu.VMEM)
    hbm = pl.BlockSpec(memory_space=pltpu.HBM)
    return pl.pallas_call(
        functools.partial(pack_kernel, order),
        out_shape=(jax.ShapeDtypeStruct((3 * share + 16, share), jnp.bfloat16),) * len(order),
        in_specs=[pl.BlockSpec(memory_space=pltpu.SMEM)] + [vmem] * 2 + [hbm] * 6,
        out_specs=(vmem,) * len(order),
        scratch_shapes=[pltpu.SemaphoreType.DMA((3 * len(order),))],
        compiler_params=pltpu.CompilerParams(vmem_limit_bytes=60 << 20),
        cost_estimate=pl.CostEstimate(flops=256 * share**3, bytes_accessed=1, transcendentals=0),
        name="pack_weights",
    )(core, g_bias, r_bias, *g_weights, *r_weights)


def by_rows(
    g_nodes, r_nodes, g_nbr, g_count, r_nbr, r_count, bnd_src, bnd_part, bnd_node,
    g_ws, g_wd, g_b1, g_w2, r_ws, r_wd, r_b1, r_w2,
):
    part = lax.axis_index("mp")
    core = lax.axis_index("batch")
    parts = lax.axis_size("mesh")
    slots = g_nbr.shape[1]
    layers = g_ws.shape[0]
    rows = g_nodes.shape[1]
    half = rows // 2
    cap = 2 * bnd_src.shape[0] // parts
    me = lax.axis_index("mesh").reshape(1)
    core1 = core.reshape(1)
    g_own, r_own = g_nodes[0], r_nodes[0]
    g_weights, r_weights = (g_ws, g_wd, g_w2), (r_ws, r_wd, r_w2)
    after = lax.optimization_barrier

    same = lax.dynamic_slice(g_own, (part * half, 0), (half, g_own.shape[1]))
    other = lax.dynamic_slice(g_own, ((1 - part) * half, 0), (half, g_own.shape[1]))
    g_a, g_b = spread_rows(same, other)
    order = [(graph, layer) for layer in range(layers) for graph in (0, 1)]
    packs = list(pack_weights(order[:1], core1, g_weights, g_b1, r_weights, r_b1))
    near_w = [swap(packs[0], "mp")]
    bnd = jnp.stack([bnd_src, bnd_part[:, 0], bnd_node])
    bnd, packs[0], same, other = after((bnd, packs[0], same, other))
    pieces = pick_rows(me, bnd, g_own, parts, cap)
    landed = [pieces[0]]
    for k in range(1, parts):
        landed.append(lax.ppermute(pieces[k], "mesh", [(i, (i + k) % parts) for i in range(parts)]))
    landed[0], core1, g_a, g_b = after((landed[0], core1, g_a, g_b))
    idx = edge_offsets(jnp.stack([g_nbr, r_nbr]), jnp.stack([g_count, r_count]), core)
    packs += pack_weights(order[1:], core1, g_weights, g_b1, r_weights, r_b1)
    g_idx, r_idx = idx[0], idx[1]
    g_a, g_b, g_idx, r_idx, packs[1], near_w[0], *landed = after(
        (g_a, g_b, g_idx, r_idx, packs[1], near_w[0], *landed)
    )
    planet = ordered(core, g_a, g_b, 1)
    g_sib, g_rim = swap(planet, "batch"), rims(planet, True)
    r_a, r_b = spread_rows(*add_force(part.reshape(1), r_own, landed, cap))
    r_a, r_b, packs[1] = after((r_a, r_b, packs[1]))
    near_w.append(swap(packs[1], "mp"))
    r_a, r_b, g_sib, g_rim, near_w[0] = after((r_a, r_b, g_sib, g_rim, near_w[0]))
    regional, g_idx = after((ordered(core, r_a, r_b, 1), g_idx))
    r_sib, r_rim = swap(regional, "batch"), rims(regional, False)
    for i, (graph, layer) in enumerate(order):
        last = layer == layers - 1
        far_w = swap(near_w[i], "batch")
        if graph == 0:
            planet = run_layer(
                layer, slots, last, core1, g_idx, planet, g_sib, g_rim, g_ws, g_wd, g_w2, g_b1, near_w[i], far_w
            )
            *planet, core1, near_w[i + 1] = after((*(planet if last else (planet,)), core1, near_w[i + 1]))
            if not last:
                planet = planet[0]
                g_sib, g_rim = swap(planet, "batch"), rims(planet, True)
        else:
            regional = run_layer(
                layer, slots, last, core1, r_idx, regional, r_sib, r_rim, r_ws, r_wd, r_w2, r_b1, near_w[i], far_w
            )
            if not last:
                regional, core1, near_w[i + 1] = after((regional, core1, near_w[i + 1]))
                r_sib, r_rim = swap(regional, "batch"), rims(regional, False)
        if i + 2 < len(order):
            packs[i + 2], near_w[i + 1] = after((packs[i + 2], near_w[i + 1]))
            near_w.append(swap(packs[i + 2], "mp"))
    g_out = ordered(part, *gather_rows(*planet), 0)
    g_out, *regional_rows = after((g_out, *gather_rows(*regional)))
    r_out = ordered(part, *regional_rows, 0)
    return g_out[None], r_out[None]


def solution(mesh):
    in_specs = (
        P(("groups", "batch"), "mesh", "mp"),
        P(("groups", "batch"), "mesh", "mp"),
        P("mesh", None),
        P("mesh"),
        P("mesh", None),
        P("mesh"),
        P("mesh"),
        P("mesh", None),
        P("mesh"),
        P(None, None, "mp"),
        P(None, None, "mp"),
        P(None, "mp"),
        P(None, "mp", None),
        P(None, None, "mp"),
        P(None, None, "mp"),
        P(None, "mp"),
        P(None, "mp", None),
    )
    out_specs = (P(("groups", "batch"), "mesh", "mp"), P(("groups", "batch"), "mesh", "mp"))
    square = mesh.shape["mp"] == 2 and mesh.shape["batch"] == 2
    return jax.shard_map(
        by_rows if square else by_features, mesh=mesh, in_specs=in_specs, out_specs=out_specs, check_vma=False
    )
```

```python
import functools

import jax
import jax.numpy as jnp
from jax import lax
from jax.experimental import pallas as pl
from jax.experimental.pallas import tpu as pltpu
from jax.sharding import PartitionSpec as P

LANES = 128
DEAD = -1e30
SMALL = pl.CostEstimate(flops=1, bytes_accessed=1, transcendentals=0)


def padded_2(shard, sides, width, wrap):
    for axis, dim in sides:
        size, length = (lax.axis_size(axis), shard.shape[dim])
        up = [(i, (i + 1) % size) for i in range(size if wrap else size - 1)]
        down = [(j, i) for i, j in up]
        last = lax.slice_in_dim(shard, length - width, length, axis=dim)
        leading = lax.slice_in_dim(shard, 0, width, axis=dim)
        before = lax.ppermute(last, axis, up)
        after = lax.ppermute(leading, axis, down)
        shard = jnp.concatenate([before, shard, after], axis=dim)
    return shard


def edge_sums(proj, near, nbr, count):
    slots = nbr.shape[1]
    live = jnp.arange(slots, dtype=jnp.int32)[None, :] < count[:, None]
    pre = proj[:, nbr].astype(jnp.float32) + near[:, :, None]
    acts = jnp.where(live[None, :, :, None], jax.nn.silu(pre), 0.0)
    return jnp.sum(acts, axis=2).astype(jnp.bfloat16)


def graph_layer(latent, nbr, count, w_send, w_recv, bias, w_out, wrap):
    rim = latent.shape[1] // 2
    own_full = lax.all_gather(latent, "mp", axis=2, tiled=True)
    padded_full = padded_2(own_full, (("mesh", 1),), rim, wrap)
    proj = jnp.dot(padded_full, w_send, preferred_element_type=jnp.float32).astype(jnp.bfloat16)
    near = jnp.dot(own_full, w_recv, preferred_element_type=jnp.float32) + bias.astype(jnp.float32)
    summed = edge_sums(proj, near, nbr, count)
    partial_prod = jnp.dot(summed, w_out, preferred_element_type=jnp.float32)
    update = lax.psum_scatter(
        partial_prod.astype(jnp.bfloat16), "mp", scatter_dimension=2, tiled=True
    ).astype(jnp.float32)
    return (latent.astype(jnp.float32) + update).astype(jnp.bfloat16)


def by_features(
    g_nodes, r_nodes, g_nbr, g_count, r_nbr, r_count, bnd_src, bnd_part, bnd_node,
    g_ws, g_wd, g_b1, g_w2, r_ws, r_wd, r_b1, r_w2,
):
    batch_rows, reg_rows, feats = r_nodes.shape
    dest = bnd_part[:, 0]
    outgoing = jnp.moveaxis(g_nodes[:, bnd_src], 1, 0)
    init = jnp.zeros((reg_rows + 1, batch_rows, feats), jnp.float32)
    target = dest * reg_rows + bnd_node
    mine = lax.axis_index("mesh")
    piece_rows = lax.all_gather(outgoing, "mesh", axis=0, tiled=True)
    piece_target = lax.all_gather(target, "mesh", axis=0, tiled=True)
    local = jnp.where(piece_target // reg_rows == mine, piece_target % reg_rows + 1, 0)
    landed = init.at[local].add(piece_rows.astype(jnp.float32))
    force = jnp.moveaxis(landed[1:], 1, 0)
    regional = (r_nodes.astype(jnp.float32) + force).astype(jnp.bfloat16)
    planet = g_nodes
    for layer in range(g_ws.shape[0]):
        planet = graph_layer(
            planet, g_nbr, g_count, g_ws[layer], g_wd[layer], g_b1[layer], g_w2[layer], True
        )
    for layer in range(r_ws.shape[0]):
        regional = graph_layer(
            regional, r_nbr, r_count, r_ws[layer], r_wd[layer], r_b1[layer], r_w2[layer], False
        )
    return (planet, regional)


def one_hot(flags):
    return jnp.where(flags, 1.0, 0.0).astype(jnp.bfloat16)


def pick_kernel(parts, cap, me_ref, bnd_ref, g_ref, *out_refs):
    rows = g_ref.shape[0]
    total = bnd_ref.shape[1]
    me = me_ref[0]
    src, part, node = (bnd_ref[i:i + 1, :] for i in range(3))
    lines = -(-parts // 8) * 8
    target = lax.rem(lax.broadcasted_iota(jnp.int32, (lines, total), 0) + me, parts)
    named = part == target
    before = one_hot(
        lax.broadcasted_iota(jnp.int32, (total, total), 0) < lax.broadcasted_iota(jnp.int32, (total, total), 1)
    )
    rank = jnp.dot(one_hot(named), before, preferred_element_type=jnp.float32)
    rank = jnp.where(named, rank, -1.0)
    source = one_hot(lax.broadcasted_iota(jnp.int32, (rows, total), 0) == src)
    line = lax.broadcasted_iota(jnp.int32, (16, total), 0)
    high = lax.shift_right_logical(node, 7)
    facts = jnp.where(line == 0, high, jnp.where(line == 1, node - high * 128, jnp.where(line == 2, 1, 0)))
    facts = facts.astype(jnp.float32).astype(jnp.bfloat16)
    place = lax.broadcasted_iota(jnp.int32, (cap, total), 0).astype(jnp.float32)
    across = (((1,), (1,)), ((), ()))
    for k in range(parts):
        chosen = one_hot(place == rank[k:k + 1, :])
        pick = lax.dot_general(chosen, source, across, preferred_element_type=jnp.float32).astype(jnp.bfloat16)
        out_refs[k][:cap, :] = jnp.dot(pick, g_ref[...], preferred_element_type=jnp.float32).astype(jnp.bfloat16)
        told = lax.dot_general(facts, chosen, across, preferred_element_type=jnp.float32)
        out_refs[k][cap:, :] = told.astype(jnp.bfloat16)


def pick_rows(me, bnd, nodes, parts, cap):
    vmem = pl.BlockSpec(memory_space=pltpu.VMEM)
    rows, feats = nodes.shape
    total = bnd.shape[1]
    piece = jax.ShapeDtypeStruct((cap + 16, feats), jnp.bfloat16)
    return pl.pallas_call(
        functools.partial(pick_kernel, parts, cap),
        out_shape=(piece,) * parts,
        in_specs=[pl.BlockSpec(memory_space=pltpu.SMEM), vmem, vmem],
        out_specs=(vmem,) * parts,
        compiler_params=pltpu.CompilerParams(vmem_limit_bytes=32 << 20),
        cost_estimate=pl.CostEstimate(flops=32 * rows**2 * feats, bytes_accessed=1, transcendentals=0),
        name="pick_rows",
    )(me, bnd, nodes)


def force_kernel(cap, first_ref, r_ref, *refs):
    pieces, (same_ref, other_ref) = refs[:-2], refs[-2:]
    half = same_ref.shape[0]
    first = first_ref[0]
    for out_ref, start in ((same_ref, first * half), (other_ref, (1 - first) * half)):
        start = pl.multiple_of(start, 16)
        row = (lax.broadcasted_iota(jnp.int32, (half, cap), 0) + start).astype(jnp.float32)
        total = r_ref[pl.ds(start, half), :].astype(jnp.float32)
        for piece in pieces:
            facts = piece[cap:, :].astype(jnp.float32)
            node = jnp.where(facts[2:3, :] > 0.5, facts[0:1, :] * 128.0 + facts[1:2, :], -1.0)
            total += jnp.dot(one_hot(row == node), piece[:cap, :], preferred_element_type=jnp.float32)
        out_ref[...] = total.astype(jnp.bfloat16)


def add_force(first, nodes, pieces, cap):
    vmem = pl.BlockSpec(memory_space=pltpu.VMEM)
    rows, feats = nodes.shape
    block = jax.ShapeDtypeStruct((rows // 2, feats), jnp.bfloat16)
    return pl.pallas_call(
        functools.partial(force_kernel, cap),
        out_shape=(block, block),
        in_specs=[pl.BlockSpec(memory_space=pltpu.SMEM)] + [vmem] * (1 + len(pieces)),
        out_specs=(vmem, vmem),
        compiler_params=pltpu.CompilerParams(vmem_limit_bytes=32 << 20),
        cost_estimate=SMALL,
        name="add_force",
    )(first, nodes, *pieces)


def layer_kernel(
    layer, place, slots, last, core_ref, idx_ref, own, sib, rim, bias, near_w, far_w, ws_hbm, wd_hbm, w2_hbm, *refs
):
    outs, refs = (refs[:2], refs[2:]) if last else (refs[:1], refs[1:])
    ws, wd, w2, ws_x, wd_x, w2_x, proj, near, summed, sems = refs
    rows, width = own.shape
    share = width // 2
    chunks = width // LANES
    part = chunks // 2
    core = core_ref[0]
    pairs = ((wd_hbm, wd), (ws_hbm, ws), (w2_hbm, w2))
    copies = [pltpu.make_async_copy(src.at[layer], dst, sems.at[i]) for i, (src, dst) in enumerate(pairs)]
    for copy in copies:
        copy.start()
    window = 3 * rows
    proj[0:8, :] = jnp.full((8, LANES), DEAD, jnp.float32)
    proj[4 * window + 4:4 * window + 16, :] = jnp.full((12, LANES), DEAD, jnp.float32)
    pack = place * (3 * share + 16)
    here, there = pl.multiple_of(core * share, 16), pl.multiple_of((1 - core) * share, 16)
    for spot, piece in ((here, near_w), (there, far_w)):
        ws_x[pl.ds(spot, share), :] = piece[pack:pack + share, :]
        wd_x[pl.ds(spot, share), :] = piece[pack + share:pack + 2 * share, :]
    third = slice(pack + 2 * share, pack + 3 * share)

    @pl.when(core == 0)
    def _():
        w2_x[:, :share] = near_w[third, :]
        w2_x[:, share:] = far_w[third, :]

    @pl.when(core != 0)
    def _():
        w2_x[:, share:] = near_w[third, :]
        w2_x[:, :share] = far_w[third, :]

    def put(dst, base, first, values):
        for c in range(values.shape[1] // LANES):
            dst[pl.ds(base * chunks + first + c, rows, stride=chunks), :] = values[:, c * LANES:(c + 1) * LANES] * 0.5

    def product(values, weights):
        return jnp.dot(values[...], weights[...], preferred_element_type=jnp.float32)

    b_own = bias[layer:layer + 1, :].astype(jnp.float32)
    b_other = near_w[pack + 3 * share:pack + 3 * share + 1, :].astype(jnp.float32)
    put(near, 0, part, product(own, wd_x) + b_other)
    put(proj, 1, part, product(own, ws_x))
    copies[0].wait()
    copies[1].wait()
    put(near, 0, 0, product(own, wd) + b_own)
    put(proj, 1, 0, product(own, ws))
    for ref, base in ((sib, rows + 1), (rim, 2 * rows + 1)):
        put(proj, base, 0, product(ref, ws))
        put(proj, base, part, product(ref, ws_x))
    low = lax.broadcasted_iota(jnp.int32, (8, LANES), 0) < chunks

    def nodes(q, carry):
        spot = pl.ds(pl.multiple_of(8 * q, 8), 8)
        mine = near[spot, :]
        total = None
        for j in range(slots):
            upper = proj[pl.ds(pl.multiple_of(idx_ref[j * rows + 2 * q], 4), 8), :]
            lower = proj[pl.ds(pl.multiple_of(idx_ref[j * rows + 2 * q + 1], 4), 8), :]
            y = jnp.where(low, upper, lower) + mine
            act = y * jnp.tanh(y) + y
            total = act if total is None else total + act
        summed[spot, :] = total
        return carry

    lax.fori_loop(0, rows // 2, nodes, 0, unroll=16)
    copies[2].wait()
    sums = [summed[pl.ds(c, rows, stride=chunks), :].astype(jnp.bfloat16) for c in range(chunks)]
    update = product(jnp.concatenate(sums[:part], 1), w2) + product(jnp.concatenate(sums[part:], 1), w2_x)
    result = (own[...].astype(jnp.float32) + update).astype(jnp.bfloat16)
    if not last:
        outs[0][...] = result
    else:
        @pl.when(core == 0)
        def _():
            outs[0][...] = result[:, :share]
            outs[1][...] = result[:, share:]

        @pl.when(core != 0)
        def _():
            outs[0][...] = result[:, share:]
            outs[1][...] = result[:, :share]


def run_layer(layer, place, slots, last, core, idx, own, sib, rim, ws, wd, w2, bias, near_w, far_w):
    rows, width = own.shape
    share = width // 2
    chunks = width // LANES
    smem = pl.BlockSpec(memory_space=pltpu.SMEM)
    vmem = pl.BlockSpec(memory_space=pltpu.VMEM)
    bf16, f32 = jnp.bfloat16, jnp.float32
    if last:
        out_shape = (jax.ShapeDtypeStruct((rows, share), bf16),) * 2
        out_specs = (vmem, vmem)
    else:
        out_shape, out_specs = jax.ShapeDtypeStruct((rows, width), bf16), vmem
    return pl.pallas_call(
        functools.partial(layer_kernel, layer, place, slots, last),
        out_shape=out_shape,
        in_specs=[smem] * 2 + [vmem] * 6 + [pl.BlockSpec(memory_space=pl.ANY)] * 3,
        out_specs=out_specs,
        scratch_shapes=[
            pltpu.VMEM((width, share), bf16),
            pltpu.VMEM((width, share), bf16),
            pltpu.VMEM((share, width), bf16),
            pltpu.VMEM((width, share), bf16),
            pltpu.VMEM((width, share), bf16),
            pltpu.VMEM((share, width), bf16),
            pltpu.VMEM((3 * rows * chunks + 96, LANES), f32),
            pltpu.VMEM((rows * chunks, LANES), f32),
            pltpu.VMEM((rows * chunks, LANES), f32),
            pltpu.SemaphoreType.DMA((3,)),
        ],
        compiler_params=pltpu.CompilerParams(vmem_limit_bytes=32 << 20),
        cost_estimate=pl.CostEstimate(flops=64 * rows * width * width, bytes_accessed=10 * rows * width, transcendentals=0),
        name="graph_layer",
    )(core, idx, own, sib, rim, bias, near_w, far_w, ws, wd, w2)


def edge_offsets(nbrs, counts, core):
    graphs, rows, slots = nbrs.shape
    half = rows // 2
    nbr = lax.dynamic_slice(nbrs.transpose(0, 2, 1), (0, 0, core * half), (graphs, slots, half)) - core * half
    count = lax.dynamic_slice(counts, (0, core * half), (graphs, half))
    low = nbr + jnp.where(core == 0, 2 * half, half)
    high = nbr - jnp.where(core == 0, half, 0)
    place = jnp.where(nbr < half, low, jnp.where(nbr < 2 * half, nbr - half, high))
    live = jnp.arange(slots, dtype=jnp.int32)[None, :, None] < count[:, None, :]
    place = jnp.where(live, place, 3 * half)
    odd = jnp.arange(half, dtype=jnp.int32) % 2
    return (4 * (place + 1 - odd)).reshape(graphs, slots * half)


def spread_rows(same, other):
    a = lax.ppermute(same, ("mp", "batch"), [(0, 0), (1, 2), (2, 1), (3, 3)])
    b = lax.ppermute(other, ("mp", "batch"), [(0, 1), (1, 3), (2, 0), (3, 2)])
    return a, b


def gather_rows(a, b):
    same = lax.ppermute(a, ("mp", "batch"), [(0, 0), (1, 2), (2, 1), (3, 3)])
    other = lax.ppermute(b, ("mp", "batch"), [(0, 2), (1, 0), (2, 3), (3, 1)])
    return same, other


def ordered(which, a, b, axis):
    return jnp.where(which == 0, jnp.concatenate([a, b], axis), jnp.concatenate([b, a], axis))


def swap(values, axis):
    return lax.ppermute(values, axis, [(0, 1), (1, 0)])


def rims(own, wrap):
    size = lax.axis_size("mesh")
    pairs = []
    for m in range(size):
        if wrap or m + 1 < size:
            pairs.append((2 * m + 1, 2 * ((m + 1) % size)))
        if wrap or m > 0:
            pairs.append((2 * m, 2 * ((m - 1) % size) + 1))
    return lax.ppermute(own, ("mesh", "batch"), pairs)


def pack_kernel(plan, core_ref, g_bias, r_bias, *refs):
    weights, outs, sems = (refs[:3], refs[3:6]), refs[6:-1], refs[-1]
    share = g_bias.shape[1]
    here = pl.multiple_of(core_ref[0] * share, share)
    copies = []
    for members, out in zip(plan, outs):
        for place, (graph, layer) in enumerate(members):
            ws, wd, w2 = weights[graph]
            base = place * (3 * share + 16)
            sources = (
                ws.at[layer, pl.ds(here, share), :], wd.at[layer, pl.ds(here, share), :], w2.at[layer, :, pl.ds(here, share)]
            )
            for i, source in enumerate(sources):
                spot = base + i * share
                copies.append(pltpu.make_async_copy(source, out.at[spot:spot + share, :], sems.at[len(copies)]))
                copies[-1].start()
    for members, out in zip(plan, outs):
        for place, (graph, layer) in enumerate(members):
            base = place * (3 * share + 16) + 3 * share
            bias = (g_bias, r_bias)[graph][layer:layer + 1, :]
            out[base:base + 16, :] = jnp.broadcast_to(bias, (16, share))
    for copy in copies:
        copy.wait()


def pack_weights(plan, core, g_weights, g_bias, r_weights, r_bias):
    share = g_bias.shape[1]
    vmem = pl.BlockSpec(memory_space=pltpu.VMEM)
    hbm = pl.BlockSpec(memory_space=pltpu.HBM)
    sizes = [len(members) for members in plan]
    return pl.pallas_call(
        functools.partial(pack_kernel, plan),
        out_shape=tuple(jax.ShapeDtypeStruct((n * (3 * share + 16), share), jnp.bfloat16) for n in sizes),
        in_specs=[pl.BlockSpec(memory_space=pltpu.SMEM)] + [vmem] * 2 + [hbm] * 6,
        out_specs=(vmem,) * len(sizes),
        scratch_shapes=[pltpu.SemaphoreType.DMA((3 * sum(sizes),))],
        compiler_params=pltpu.CompilerParams(vmem_limit_bytes=60 << 20),
        cost_estimate=pl.CostEstimate(flops=256 * share**3, bytes_accessed=1, transcendentals=0),
        name="pack_weights",
    )(core, g_bias, r_bias, *g_weights, *r_weights)


def by_rows(
    g_nodes, r_nodes, g_nbr, g_count, r_nbr, r_count, bnd_src, bnd_part, bnd_node,
    g_ws, g_wd, g_b1, g_w2, r_ws, r_wd, r_b1, r_w2,
):
    part = lax.axis_index("mp")
    core = lax.axis_index("batch")
    parts = lax.axis_size("mesh")
    slots = g_nbr.shape[1]
    layers = g_ws.shape[0]
    rows = g_nodes.shape[1]
    half = rows // 2
    cap = 2 * bnd_src.shape[0] // parts
    me = lax.axis_index("mesh").reshape(1)
    core1 = core.reshape(1)
    g_own, r_own = g_nodes[0], r_nodes[0]
    g_weights, r_weights = (g_ws, g_wd, g_w2), (r_ws, r_wd, r_w2)
    after = lax.optimization_barrier

    packs = list(pack_weights((((0, 0), (1, 0)),), core1, g_weights, g_b1, r_weights, r_b1))
    near_w = [swap(packs[0], "mp")]
    packs[0], g_own = after((packs[0], g_own))
    same = lax.dynamic_slice(g_own, (part * half, 0), (half, g_own.shape[1]))
    other = lax.dynamic_slice(g_own, ((1 - part) * half, 0), (half, g_own.shape[1]))
    g_a, g_b = spread_rows(same, other)
    bnd = jnp.stack([bnd_src, bnd_part[:, 0], bnd_node])
    bnd, packs[0], same, other = after((bnd, packs[0], same, other))
    pieces = pick_rows(me, bnd, g_own, parts, cap)
    landed = [pieces[0]]
    for k in range(1, parts):
        landed.append(lax.ppermute(pieces[k], "mesh", [(i, (i + k) % parts) for i in range(parts)]))
    landed[0], core1, g_a, g_b = after((landed[0], core1, g_a, g_b))
    idx = edge_offsets(jnp.stack([g_nbr, r_nbr]), jnp.stack([g_count, r_count]), core)
    rest = tuple(((graph, layer),) for layer in range(1, layers) for graph in (0, 1))
    packs += pack_weights(rest, core1, g_weights, g_b1, r_weights, r_b1)
    g_idx, r_idx = idx[0], idx[1]
    g_a, g_b, g_idx, r_idx, packs[1:], near_w[0], *landed = after(
        (g_a, g_b, g_idx, r_idx, packs[1:], near_w[0], *landed)
    )
    planet = ordered(core, g_a, g_b, 1)
    g_sib, g_rim = swap(planet, "batch"), rims(planet, True)
    *r_pair, packs[1:] = after((*add_force(part.reshape(1), r_own, landed, cap), packs[1:]))
    r_a, r_b = spread_rows(*r_pair)
    near_w.append(swap(packs[1], "mp"))
    r_a, r_b, g_sib, g_rim = after((r_a, r_b, g_sib, g_rim))
    regional, g_idx = after((ordered(core, r_a, r_b, 1), g_idx))
    r_sib, r_rim = swap(regional, "batch"), rims(regional, False)
    far_w = [swap(near_w[0], "batch")]
    for layer in range(layers):
        last = layer == layers - 1
        i = max(0, 2 * layer - 1)
        if layer:
            far_w.append(swap(near_w[i], "batch"))
        planet = run_layer(
            layer, 0, slots, last, core1, g_idx, planet, g_sib, g_rim, g_ws, g_wd, g_w2, g_b1, near_w[i], far_w[i]
        )
        *planet, core1 = after((*(planet if last else (planet,)), core1))
        if not last:
            planet = planet[0]
            g_sib, g_rim = swap(planet, "batch"), rims(planet, True)
        if layer:
            i += 1
            near_w[i], core1 = after((near_w[i], core1))
            far_w.append(swap(near_w[i], "batch"))
        for j in range(i + 1, min(i + 3, len(packs))):
            if j == len(near_w):
                packs[j], near_w[j - 1] = after((packs[j], near_w[j - 1]))
                near_w.append(swap(packs[j], "mp"))
            if j == i + 1:
                core1, near_w[j] = after((core1, near_w[j]))
        regional = run_layer(
            layer, 1 - min(layer, 1), slots, last, core1, r_idx, regional, r_sib, r_rim, r_ws, r_wd, r_w2, r_b1,
            near_w[i], far_w[i],
        )
        if not last:
            regional, core1 = after((regional, core1))
            r_sib, r_rim = swap(regional, "batch"), rims(regional, False)
    g_out = ordered(part, *gather_rows(*planet), 0)
    g_out, *regional_rows = after((g_out, *gather_rows(*regional)))
    r_out = ordered(part, *regional_rows, 0)
    return g_out[None], r_out[None]


def solution(mesh):
    in_specs = (
        P(("groups", "batch"), "mesh", "mp"),
        P(("groups", "batch"), "mesh", "mp"),
        P("mesh", None),
        P("mesh"),
        P("mesh", None),
        P("mesh"),
        P("mesh"),
        P("mesh", None),
        P("mesh"),
        P(None, None, "mp"),
        P(None, None, "mp"),
        P(None, "mp"),
        P(None, "mp", None),
        P(None, None, "mp"),
        P(None, None, "mp"),
        P(None, "mp"),
        P(None, "mp", None),
    )
    out_specs = (P(("groups", "batch"), "mesh", "mp"), P(("groups", "batch"), "mesh", "mp"))
    square = mesh.shape["mp"] == 2 and mesh.shape["batch"] == 2
    return jax.shard_map(
        by_rows if square else by_features, mesh=mesh, in_specs=in_specs, out_specs=out_specs, check_vma=False
    )
```

```python
import functools

import jax
import jax.numpy as jnp
from jax import lax
from jax.experimental import pallas as pl
from jax.experimental.pallas import tpu as pltpu
from jax.sharding import PartitionSpec as P

LANES = 128
DEAD = -1e30
SMALL = pl.CostEstimate(flops=1, bytes_accessed=1, transcendentals=0)


def padded_2(shard, sides, width, wrap):
    for axis, dim in sides:
        size, length = (lax.axis_size(axis), shard.shape[dim])
        up = [(i, (i + 1) % size) for i in range(size if wrap else size - 1)]
        down = [(j, i) for i, j in up]
        last = lax.slice_in_dim(shard, length - width, length, axis=dim)
        leading = lax.slice_in_dim(shard, 0, width, axis=dim)
        before = lax.ppermute(last, axis, up)
        after = lax.ppermute(leading, axis, down)
        shard = jnp.concatenate([before, shard, after], axis=dim)
    return shard


def edge_sums(proj, near, nbr, count):
    slots = nbr.shape[1]
    live = jnp.arange(slots, dtype=jnp.int32)[None, :] < count[:, None]
    pre = proj[:, nbr].astype(jnp.float32) + near[:, :, None]
    acts = jnp.where(live[None, :, :, None], jax.nn.silu(pre), 0.0)
    return jnp.sum(acts, axis=2).astype(jnp.bfloat16)


def graph_layer(latent, nbr, count, w_send, w_recv, bias, w_out, wrap):
    rim = latent.shape[1] // 2
    own_full = lax.all_gather(latent, "mp", axis=2, tiled=True)
    padded_full = padded_2(own_full, (("mesh", 1),), rim, wrap)
    proj = jnp.dot(padded_full, w_send, preferred_element_type=jnp.float32).astype(jnp.bfloat16)
    near = jnp.dot(own_full, w_recv, preferred_element_type=jnp.float32) + bias.astype(jnp.float32)
    summed = edge_sums(proj, near, nbr, count)
    partial_prod = jnp.dot(summed, w_out, preferred_element_type=jnp.float32)
    update = lax.psum_scatter(
        partial_prod.astype(jnp.bfloat16), "mp", scatter_dimension=2, tiled=True
    ).astype(jnp.float32)
    return (latent.astype(jnp.float32) + update).astype(jnp.bfloat16)


def by_features(
    g_nodes, r_nodes, g_nbr, g_count, r_nbr, r_count, bnd_src, bnd_part, bnd_node,
    g_ws, g_wd, g_b1, g_w2, r_ws, r_wd, r_b1, r_w2,
):
    batch_rows, reg_rows, feats = r_nodes.shape
    dest = bnd_part[:, 0]
    outgoing = jnp.moveaxis(g_nodes[:, bnd_src], 1, 0)
    init = jnp.zeros((reg_rows + 1, batch_rows, feats), jnp.float32)
    target = dest * reg_rows + bnd_node
    mine = lax.axis_index("mesh")
    piece_rows = lax.all_gather(outgoing, "mesh", axis=0, tiled=True)
    piece_target = lax.all_gather(target, "mesh", axis=0, tiled=True)
    local = jnp.where(piece_target // reg_rows == mine, piece_target % reg_rows + 1, 0)
    landed = init.at[local].add(piece_rows.astype(jnp.float32))
    force = jnp.moveaxis(landed[1:], 1, 0)
    regional = (r_nodes.astype(jnp.float32) + force).astype(jnp.bfloat16)
    planet = g_nodes
    for layer in range(g_ws.shape[0]):
        planet = graph_layer(
            planet, g_nbr, g_count, g_ws[layer], g_wd[layer], g_b1[layer], g_w2[layer], True
        )
    for layer in range(r_ws.shape[0]):
        regional = graph_layer(
            regional, r_nbr, r_count, r_ws[layer], r_wd[layer], r_b1[layer], r_w2[layer], False
        )
    return (planet, regional)


def one_hot(flags):
    return jnp.where(flags, 1.0, 0.0).astype(jnp.bfloat16)


def pick_kernel(parts, cap, me_ref, bnd_ref, g_ref, *out_refs):
    rows = g_ref.shape[0]
    total = bnd_ref.shape[1]
    me = me_ref[0]
    src, part, node = (bnd_ref[i:i + 1, :] for i in range(3))
    lines = -(-parts // 8) * 8
    target = lax.rem(lax.broadcasted_iota(jnp.int32, (lines, total), 0) + me, parts)
    named = part == target
    before = one_hot(
        lax.broadcasted_iota(jnp.int32, (total, total), 0) < lax.broadcasted_iota(jnp.int32, (total, total), 1)
    )
    rank = jnp.dot(one_hot(named), before, preferred_element_type=jnp.float32)
    rank = jnp.where(named, rank, -1.0)
    source = one_hot(lax.broadcasted_iota(jnp.int32, (rows, total), 0) == src)
    line = lax.broadcasted_iota(jnp.int32, (16, total), 0)
    high = lax.shift_right_logical(node, 7)
    facts = jnp.where(line == 0, high, jnp.where(line == 1, node - high * 128, jnp.where(line == 2, 1, 0)))
    facts = facts.astype(jnp.float32).astype(jnp.bfloat16)
    place = lax.broadcasted_iota(jnp.int32, (cap, total), 0).astype(jnp.float32)
    across = (((1,), (1,)), ((), ()))
    for k in range(parts):
        chosen = one_hot(place == rank[k:k + 1, :])
        pick = lax.dot_general(chosen, source, across, preferred_element_type=jnp.float32).astype(jnp.bfloat16)
        out_refs[k][:cap, :] = jnp.dot(pick, g_ref[...], preferred_element_type=jnp.float32).astype(jnp.bfloat16)
        told = lax.dot_general(facts, chosen, across, preferred_element_type=jnp.float32)
        out_refs[k][cap:, :] = told.astype(jnp.bfloat16)


def pick_rows(me, bnd, nodes, parts, cap):
    vmem = pl.BlockSpec(memory_space=pltpu.VMEM)
    rows, feats = nodes.shape
    total = bnd.shape[1]
    piece = jax.ShapeDtypeStruct((cap + 16, feats), jnp.bfloat16)
    return pl.pallas_call(
        functools.partial(pick_kernel, parts, cap),
        out_shape=(piece,) * parts,
        in_specs=[pl.BlockSpec(memory_space=pltpu.SMEM), vmem, vmem],
        out_specs=(vmem,) * parts,
        compiler_params=pltpu.CompilerParams(vmem_limit_bytes=32 << 20),
        cost_estimate=pl.CostEstimate(flops=32 * rows**2 * feats, bytes_accessed=1, transcendentals=0),
        name="pick_rows",
    )(me, bnd, nodes)


def force_kernel(cap, first_ref, r_ref, *refs):
    pieces, (same_ref, other_ref) = refs[:-2], refs[-2:]
    half = same_ref.shape[0]
    first = first_ref[0]
    for out_ref, start in ((same_ref, first * half), (other_ref, (1 - first) * half)):
        start = pl.multiple_of(start, 16)
        row = (lax.broadcasted_iota(jnp.int32, (half, cap), 0) + start).astype(jnp.float32)
        total = r_ref[pl.ds(start, half), :].astype(jnp.float32)
        for piece in pieces:
            facts = piece[cap:, :].astype(jnp.float32)
            node = jnp.where(facts[2:3, :] > 0.5, facts[0:1, :] * 128.0 + facts[1:2, :], -1.0)
            total += jnp.dot(one_hot(row == node), piece[:cap, :], preferred_element_type=jnp.float32)
        out_ref[...] = total.astype(jnp.bfloat16)


def add_force(first, nodes, pieces, cap):
    vmem = pl.BlockSpec(memory_space=pltpu.VMEM)
    rows, feats = nodes.shape
    block = jax.ShapeDtypeStruct((rows // 2, feats), jnp.bfloat16)
    return pl.pallas_call(
        functools.partial(force_kernel, cap),
        out_shape=(block, block),
        in_specs=[pl.BlockSpec(memory_space=pltpu.SMEM)] + [vmem] * (1 + len(pieces)),
        out_specs=(vmem, vmem),
        compiler_params=pltpu.CompilerParams(vmem_limit_bytes=32 << 20),
        cost_estimate=SMALL,
        name="add_force",
    )(first, nodes, *pieces)


def layer_kernel(
    layer, place, slots, last, core_ref, idx_ref, own, sib, rim, bias, near_w, far_w, ws_hbm, wd_hbm, w2_hbm, *refs
):
    outs, refs = (refs[:2], refs[2:]) if last else (refs[:1], refs[1:])
    ws, wd, w2, ws_x, wd_x, w2_x, proj, near, summed, sems = refs
    rows, width = own.shape
    share = width // 2
    chunks = width // LANES
    part = chunks // 2
    core = core_ref[0]
    pairs = ((wd_hbm, wd), (ws_hbm, ws), (w2_hbm, w2))
    copies = [pltpu.make_async_copy(src.at[layer], dst, sems.at[i]) for i, (src, dst) in enumerate(pairs)]
    for copy in copies:
        copy.start()
    window = 3 * rows
    proj[0:8, :] = jnp.full((8, LANES), DEAD, jnp.float32)
    proj[4 * window + 4:4 * window + 16, :] = jnp.full((12, LANES), DEAD, jnp.float32)
    pack = place * (3 * share + 16)
    here, there = pl.multiple_of(core * share, 16), pl.multiple_of((1 - core) * share, 16)
    for spot, piece in ((here, near_w), (there, far_w)):
        ws_x[pl.ds(spot, share), :] = piece[pack:pack + share, :]
        wd_x[pl.ds(spot, share), :] = piece[pack + share:pack + 2 * share, :]
    third = slice(pack + 2 * share, pack + 3 * share)

    @pl.when(core == 0)
    def _():
        w2_x[:, :share] = near_w[third, :]
        w2_x[:, share:] = far_w[third, :]

    @pl.when(core != 0)
    def _():
        w2_x[:, share:] = near_w[third, :]
        w2_x[:, :share] = far_w[third, :]

    def put(dst, base, first, values):
        for c in range(values.shape[1] // LANES):
            dst[pl.ds(base * chunks + first + c, rows, stride=chunks), :] = values[:, c * LANES:(c + 1) * LANES] * 0.5

    def product(values, weights):
        return jnp.dot(values[...], weights[...], preferred_element_type=jnp.float32)

    b_own = bias[layer:layer + 1, :].astype(jnp.float32)
    b_other = near_w[pack + 3 * share:pack + 3 * share + 1, :].astype(jnp.float32)
    put(near, 0, part, product(own, wd_x) + b_other)
    put(proj, 1, part, product(own, ws_x))
    copies[0].wait()
    copies[1].wait()
    put(near, 0, 0, product(own, wd) + b_own)
    put(proj, 1, 0, product(own, ws))
    for ref, base in ((sib, rows + 1), (rim, 2 * rows + 1)):
        put(proj, base, 0, product(ref, ws))
        put(proj, base, part, product(ref, ws_x))
    low = lax.broadcasted_iota(jnp.int32, (8, LANES), 0) < chunks

    def nodes(q, carry):
        spot = pl.ds(pl.multiple_of(8 * q, 8), 8)
        mine = near[spot, :]
        total = None
        for j in range(slots):
            upper = proj[pl.ds(pl.multiple_of(idx_ref[j * rows + 2 * q], 4), 8), :]
            lower = proj[pl.ds(pl.multiple_of(idx_ref[j * rows + 2 * q + 1], 4), 8), :]
            y = jnp.where(low, upper, lower) + mine
            act = y * jnp.tanh(y) + y
            total = act if total is None else total + act
        summed[spot, :] = total
        return carry

    lax.fori_loop(0, rows // 2, nodes, 0, unroll=16)
    copies[2].wait()
    sums = [summed[pl.ds(c, rows, stride=chunks), :].astype(jnp.bfloat16) for c in range(chunks)]
    update = product(jnp.concatenate(sums[:part], 1), w2) + product(jnp.concatenate(sums[part:], 1), w2_x)
    result = (own[...].astype(jnp.float32) + update).astype(jnp.bfloat16)
    if not last:
        outs[0][...] = result
    else:
        @pl.when(core == 0)
        def _():
            outs[0][...] = result[:, :share]
            outs[1][...] = result[:, share:]

        @pl.when(core != 0)
        def _():
            outs[0][...] = result[:, share:]
            outs[1][...] = result[:, :share]


def run_layer(layer, place, slots, last, core, idx, own, sib, rim, ws, wd, w2, bias, near_w, far_w, cost=64):
    rows, width = own.shape
    share = width // 2
    chunks = width // LANES
    smem = pl.BlockSpec(memory_space=pltpu.SMEM)
    vmem = pl.BlockSpec(memory_space=pltpu.VMEM)
    bf16, f32 = jnp.bfloat16, jnp.float32
    if last:
        out_shape = (jax.ShapeDtypeStruct((rows, share), bf16),) * 2
        out_specs = (vmem, vmem)
    else:
        out_shape, out_specs = jax.ShapeDtypeStruct((rows, width), bf16), vmem
    return pl.pallas_call(
        functools.partial(layer_kernel, layer, place, slots, last),
        out_shape=out_shape,
        in_specs=[smem] * 2 + [vmem] * 6 + [pl.BlockSpec(memory_space=pl.ANY)] * 3,
        out_specs=out_specs,
        scratch_shapes=[
            pltpu.VMEM((width, share), bf16),
            pltpu.VMEM((width, share), bf16),
            pltpu.VMEM((share, width), bf16),
            pltpu.VMEM((width, share), bf16),
            pltpu.VMEM((width, share), bf16),
            pltpu.VMEM((share, width), bf16),
            pltpu.VMEM((3 * rows * chunks + 96, LANES), f32),
            pltpu.VMEM((rows * chunks, LANES), f32),
            pltpu.VMEM((rows * chunks, LANES), f32),
            pltpu.SemaphoreType.DMA((3,)),
        ],
        compiler_params=pltpu.CompilerParams(vmem_limit_bytes=32 << 20),
        cost_estimate=pl.CostEstimate(flops=cost * rows * width * width, bytes_accessed=10 * rows * width, transcendentals=0),
        name="graph_layer",
    )(core, idx, own, sib, rim, bias, near_w, far_w, ws, wd, w2)


def edge_offsets(nbrs, counts, core):
    graphs, rows, slots = nbrs.shape
    half = rows // 2
    nbr = lax.dynamic_slice(nbrs.transpose(0, 2, 1), (0, 0, core * half), (graphs, slots, half)) - core * half
    count = lax.dynamic_slice(counts, (0, core * half), (graphs, half))
    low = nbr + jnp.where(core == 0, 2 * half, half)
    high = nbr - jnp.where(core == 0, half, 0)
    place = jnp.where(nbr < half, low, jnp.where(nbr < 2 * half, nbr - half, high))
    live = jnp.arange(slots, dtype=jnp.int32)[None, :, None] < count[:, None, :]
    place = jnp.where(live, place, 3 * half)
    odd = jnp.arange(half, dtype=jnp.int32) % 2
    return (4 * (place + 1 - odd)).reshape(graphs, slots * half)


def spread_rows(same, other):
    a = lax.ppermute(same, ("mp", "batch"), [(0, 0), (1, 2), (2, 1), (3, 3)])
    b = lax.ppermute(other, ("mp", "batch"), [(0, 1), (1, 3), (2, 0), (3, 2)])
    return a, b


def gather_rows(a, b):
    same = lax.ppermute(a, ("mp", "batch"), [(0, 0), (1, 2), (2, 1), (3, 3)])
    other = lax.ppermute(b, ("mp", "batch"), [(0, 2), (1, 0), (2, 3), (3, 1)])
    return same, other


def ordered(which, a, b, axis):
    return jnp.where(which == 0, jnp.concatenate([a, b], axis), jnp.concatenate([b, a], axis))


def swap(values, axis):
    return lax.ppermute(values, axis, [(0, 1), (1, 0)])


def rims(own, wrap):
    size = lax.axis_size("mesh")
    pairs = []
    for m in range(size):
        if wrap or m + 1 < size:
            pairs.append((2 * m + 1, 2 * ((m + 1) % size)))
        if wrap or m > 0:
            pairs.append((2 * m, 2 * ((m - 1) % size) + 1))
    return lax.ppermute(own, ("mesh", "batch"), pairs)


def pack_kernel(plan, core_ref, g_bias, r_bias, *refs):
    weights, outs, sems = (refs[:3], refs[3:6]), refs[6:-1], refs[-1]
    share = g_bias.shape[1]
    here = pl.multiple_of(core_ref[0] * share, share)
    copies = []
    for members, out in zip(plan, outs):
        for place, (graph, layer) in enumerate(members):
            ws, wd, w2 = weights[graph]
            base = place * (3 * share + 16)
            sources = (
                ws.at[layer, pl.ds(here, share), :], wd.at[layer, pl.ds(here, share), :], w2.at[layer, :, pl.ds(here, share)]
            )
            for i, source in enumerate(sources):
                spot = base + i * share
                copies.append(pltpu.make_async_copy(source, out.at[spot:spot + share, :], sems.at[len(copies)]))
                copies[-1].start()
    for members, out in zip(plan, outs):
        for place, (graph, layer) in enumerate(members):
            base = place * (3 * share + 16) + 3 * share
            bias = (g_bias, r_bias)[graph][layer:layer + 1, :]
            out[base:base + 16, :] = jnp.broadcast_to(bias, (16, share))
    for copy in copies:
        copy.wait()


def pack_weights(plan, core, g_weights, g_bias, r_weights, r_bias):
    share = g_bias.shape[1]
    vmem = pl.BlockSpec(memory_space=pltpu.VMEM)
    hbm = pl.BlockSpec(memory_space=pltpu.HBM)
    sizes = [len(members) for members in plan]
    return pl.pallas_call(
        functools.partial(pack_kernel, plan),
        out_shape=tuple(jax.ShapeDtypeStruct((n * (3 * share + 16), share), jnp.bfloat16) for n in sizes),
        in_specs=[pl.BlockSpec(memory_space=pltpu.SMEM)] + [vmem] * 2 + [hbm] * 6,
        out_specs=(vmem,) * len(sizes),
        scratch_shapes=[pltpu.SemaphoreType.DMA((3 * sum(sizes),))],
        compiler_params=pltpu.CompilerParams(vmem_limit_bytes=60 << 20),
        cost_estimate=pl.CostEstimate(flops=256 * share**3, bytes_accessed=1, transcendentals=0),
        name="pack_weights",
    )(core, g_bias, r_bias, *g_weights, *r_weights)


def by_rows(
    g_nodes, r_nodes, g_nbr, g_count, r_nbr, r_count, bnd_src, bnd_part, bnd_node,
    g_ws, g_wd, g_b1, g_w2, r_ws, r_wd, r_b1, r_w2,
):
    part = lax.axis_index("mp")
    core = lax.axis_index("batch")
    parts = lax.axis_size("mesh")
    slots = g_nbr.shape[1]
    layers = g_ws.shape[0]
    rows = g_nodes.shape[1]
    half = rows // 2
    cap = 2 * bnd_src.shape[0] // parts
    me = lax.axis_index("mesh").reshape(1)
    core1 = core.reshape(1)
    g_own, r_own = g_nodes[0], r_nodes[0]
    g_weights, r_weights = (g_ws, g_wd, g_w2), (r_ws, r_wd, r_w2)
    after = lax.optimization_barrier

    same = lax.dynamic_slice(g_own, (part * half, 0), (half, g_own.shape[1]))
    other = lax.dynamic_slice(g_own, ((1 - part) * half, 0), (half, g_own.shape[1]))
    g_a, g_b = spread_rows(same, other)
    packs = list(pack_weights((((0, 0), (1, 0)),), core1, g_weights, g_b1, r_weights, r_b1))
    near_w = [swap(packs[0], "mp")]
    bnd = jnp.stack([bnd_src, bnd_part[:, 0], bnd_node])
    bnd, packs[0], same, other = after((bnd, packs[0], same, other))
    pieces = pick_rows(me, bnd, g_own, parts, cap)
    landed = [pieces[0]]
    for k in range(1, parts):
        landed.append(lax.ppermute(pieces[k], "mesh", [(i, (i + k) % parts) for i in range(parts)]))
    landed[0], core1, g_a, g_b = after((landed[0], core1, g_a, g_b))
    idx = edge_offsets(jnp.stack([g_nbr, r_nbr]), jnp.stack([g_count, r_count]), core)
    rest = tuple(((graph, layer),) for layer in range(1, layers) for graph in (0, 1))
    packs += pack_weights(rest, core1, g_weights, g_b1, r_weights, r_b1)
    g_idx, r_idx = idx[0], idx[1]
    g_a, g_b, g_idx, r_idx, packs[1:], *landed = after((g_a, g_b, g_idx, r_idx, packs[1:], *landed))
    planet = ordered(core, g_a, g_b, 1)
    g_sib, g_rim = swap(planet, "batch"), rims(planet, True)
    *r_pair, packs[1:] = after((*add_force(part.reshape(1), r_own, landed, cap), packs[1:]))
    r_a, r_b = spread_rows(*r_pair)
    near_w.append(swap(packs[1], "mp"))
    r_a, r_b, g_sib, g_rim, near_w[0] = after((r_a, r_b, g_sib, g_rim, near_w[0]))
    regional, g_idx = after((ordered(core, r_a, r_b, 1), g_idx))
    r_sib, r_rim = swap(regional, "batch"), rims(regional, False)
    far_w = [swap(near_w[0], "batch")]
    for layer in range(layers):
        last = layer == layers - 1
        i = max(0, 2 * layer - 1)
        if layer:
            far_w.append(swap(near_w[i], "batch"))
        planet = run_layer(
            layer, 0, slots, last, core1, g_idx, planet, g_sib, g_rim, g_ws, g_wd, g_w2, g_b1, near_w[i], far_w[i],
            8 if layer else 64,
        )
        *planet, core1 = after((*(planet if last else (planet,)), core1))
        if not last:
            planet = planet[0]
            g_sib, g_rim = swap(planet, "batch"), rims(planet, True)
        if layer:
            i += 1
            near_w[i], core1 = after((near_w[i], core1))
            far_w.append(swap(near_w[i], "batch"))
        for j in range(i + 1, min(i + 3, len(packs))):
            if j == len(near_w):
                packs[j], near_w[j - 1] = after((packs[j], near_w[j - 1]))
                near_w.append(swap(packs[j], "mp"))
            if j == i + 1:
                core1, near_w[j] = after((core1, near_w[j]))
        regional = run_layer(
            layer, 1 - min(layer, 1), slots, last, core1, r_idx, regional, r_sib, r_rim, r_ws, r_wd, r_w2, r_b1,
            near_w[i], far_w[i],
        )
        if not last:
            regional, core1 = after((regional, core1))
            r_sib, r_rim = swap(regional, "batch"), rims(regional, False)
    g_out = ordered(part, *gather_rows(*planet), 0)
    g_out, *regional_rows = after((g_out, *gather_rows(*regional)))
    r_out = ordered(part, *regional_rows, 0)
    return g_out[None], r_out[None]


def solution(mesh):
    in_specs = (
        P(("groups", "batch"), "mesh", "mp"),
        P(("groups", "batch"), "mesh", "mp"),
        P("mesh", None),
        P("mesh"),
        P("mesh", None),
        P("mesh"),
        P("mesh"),
        P("mesh", None),
        P("mesh"),
        P(None, None, "mp"),
        P(None, None, "mp"),
        P(None, "mp"),
        P(None, "mp", None),
        P(None, None, "mp"),
        P(None, None, "mp"),
        P(None, "mp"),
        P(None, "mp", None),
    )
    out_specs = (P(("groups", "batch"), "mesh", "mp"), P(("groups", "batch"), "mesh", "mp"))
    square = mesh.shape["mp"] == 2 and mesh.shape["batch"] == 2
    return jax.shard_map(
        by_rows if square else by_features, mesh=mesh, in_specs=in_specs, out_specs=out_specs, check_vma=False
    )
```

```python
import functools

import jax
import jax.numpy as jnp
from jax import lax
from jax.experimental import pallas as pl
from jax.experimental.pallas import tpu as pltpu
from jax.sharding import PartitionSpec as P

LANES = 128
DEAD = -1e30
SMALL = pl.CostEstimate(flops=1, bytes_accessed=1, transcendentals=0)


def padded_2(shard, sides, width, wrap):
    for axis, dim in sides:
        size, length = (lax.axis_size(axis), shard.shape[dim])
        up = [(i, (i + 1) % size) for i in range(size if wrap else size - 1)]
        down = [(j, i) for i, j in up]
        last = lax.slice_in_dim(shard, length - width, length, axis=dim)
        leading = lax.slice_in_dim(shard, 0, width, axis=dim)
        before = lax.ppermute(last, axis, up)
        after = lax.ppermute(leading, axis, down)
        shard = jnp.concatenate([before, shard, after], axis=dim)
    return shard


def edge_sums(proj, near, nbr, count):
    slots = nbr.shape[1]
    live = jnp.arange(slots, dtype=jnp.int32)[None, :] < count[:, None]
    pre = proj[:, nbr].astype(jnp.float32) + near[:, :, None]
    acts = jnp.where(live[None, :, :, None], jax.nn.silu(pre), 0.0)
    return jnp.sum(acts, axis=2).astype(jnp.bfloat16)


def graph_layer(latent, nbr, count, w_send, w_recv, bias, w_out, wrap):
    rim = latent.shape[1] // 2
    own_full = lax.all_gather(latent, "mp", axis=2, tiled=True)
    padded_full = padded_2(own_full, (("mesh", 1),), rim, wrap)
    proj = jnp.dot(padded_full, w_send, preferred_element_type=jnp.float32).astype(jnp.bfloat16)
    near = jnp.dot(own_full, w_recv, preferred_element_type=jnp.float32) + bias.astype(jnp.float32)
    summed = edge_sums(proj, near, nbr, count)
    partial_prod = jnp.dot(summed, w_out, preferred_element_type=jnp.float32)
    update = lax.psum_scatter(
        partial_prod.astype(jnp.bfloat16), "mp", scatter_dimension=2, tiled=True
    ).astype(jnp.float32)
    return (latent.astype(jnp.float32) + update).astype(jnp.bfloat16)


def by_features(
    g_nodes, r_nodes, g_nbr, g_count, r_nbr, r_count, bnd_src, bnd_part, bnd_node,
    g_ws, g_wd, g_b1, g_w2, r_ws, r_wd, r_b1, r_w2,
):
    batch_rows, reg_rows, feats = r_nodes.shape
    dest = bnd_part[:, 0]
    outgoing = jnp.moveaxis(g_nodes[:, bnd_src], 1, 0)
    init = jnp.zeros((reg_rows + 1, batch_rows, feats), jnp.float32)
    target = dest * reg_rows + bnd_node
    mine = lax.axis_index("mesh")
    piece_rows = lax.all_gather(outgoing, "mesh", axis=0, tiled=True)
    piece_target = lax.all_gather(target, "mesh", axis=0, tiled=True)
    local = jnp.where(piece_target // reg_rows == mine, piece_target % reg_rows + 1, 0)
    landed = init.at[local].add(piece_rows.astype(jnp.float32))
    force = jnp.moveaxis(landed[1:], 1, 0)
    regional = (r_nodes.astype(jnp.float32) + force).astype(jnp.bfloat16)
    planet = g_nodes
    for layer in range(g_ws.shape[0]):
        planet = graph_layer(
            planet, g_nbr, g_count, g_ws[layer], g_wd[layer], g_b1[layer], g_w2[layer], True
        )
    for layer in range(r_ws.shape[0]):
        regional = graph_layer(
            regional, r_nbr, r_count, r_ws[layer], r_wd[layer], r_b1[layer], r_w2[layer], False
        )
    return (planet, regional)


def one_hot(flags):
    return jnp.where(flags, 1.0, 0.0).astype(jnp.bfloat16)


def pick_kernel(parts, cap, me_ref, bnd_ref, g_ref, *out_refs):
    rows = g_ref.shape[0]
    total = bnd_ref.shape[1]
    me = me_ref[0]
    src, part, node = (bnd_ref[i:i + 1, :] for i in range(3))
    lines = -(-parts // 8) * 8
    target = lax.rem(lax.broadcasted_iota(jnp.int32, (lines, total), 0) + me, parts)
    named = part == target
    before = one_hot(
        lax.broadcasted_iota(jnp.int32, (total, total), 0) < lax.broadcasted_iota(jnp.int32, (total, total), 1)
    )
    rank = jnp.dot(one_hot(named), before, preferred_element_type=jnp.float32)
    rank = jnp.where(named, rank, -1.0)
    source = one_hot(lax.broadcasted_iota(jnp.int32, (rows, total), 0) == src)
    line = lax.broadcasted_iota(jnp.int32, (16, total), 0)
    high = lax.shift_right_logical(node, 7)
    facts = jnp.where(line == 0, high, jnp.where(line == 1, node - high * 128, jnp.where(line == 2, 1, 0)))
    facts = facts.astype(jnp.float32).astype(jnp.bfloat16)
    place = lax.broadcasted_iota(jnp.int32, (cap, total), 0).astype(jnp.float32)
    across = (((1,), (1,)), ((), ()))
    for k in range(parts):
        chosen = one_hot(place == rank[k:k + 1, :])
        pick = lax.dot_general(chosen, source, across, preferred_element_type=jnp.float32).astype(jnp.bfloat16)
        out_refs[k][:cap, :] = jnp.dot(pick, g_ref[...], preferred_element_type=jnp.float32).astype(jnp.bfloat16)
        told = lax.dot_general(facts, chosen, across, preferred_element_type=jnp.float32)
        out_refs[k][cap:, :] = told.astype(jnp.bfloat16)


def pick_rows(me, bnd, nodes, parts, cap):
    vmem = pl.BlockSpec(memory_space=pltpu.VMEM)
    rows, feats = nodes.shape
    total = bnd.shape[1]
    piece = jax.ShapeDtypeStruct((cap + 16, feats), jnp.bfloat16)
    return pl.pallas_call(
        functools.partial(pick_kernel, parts, cap),
        out_shape=(piece,) * parts,
        in_specs=[pl.BlockSpec(memory_space=pltpu.SMEM), vmem, vmem],
        out_specs=(vmem,) * parts,
        compiler_params=pltpu.CompilerParams(vmem_limit_bytes=32 << 20),
        cost_estimate=pl.CostEstimate(flops=32 * rows**2 * feats, bytes_accessed=1, transcendentals=0),
        name="pick_rows",
    )(me, bnd, nodes)


def force_kernel(cap, first_ref, r_ref, *refs):
    pieces, (same_ref, other_ref) = refs[:-2], refs[-2:]
    half = same_ref.shape[0]
    first = first_ref[0]
    for out_ref, start in ((same_ref, first * half), (other_ref, (1 - first) * half)):
        start = pl.multiple_of(start, 16)
        row = (lax.broadcasted_iota(jnp.int32, (half, cap), 0) + start).astype(jnp.float32)
        total = r_ref[pl.ds(start, half), :].astype(jnp.float32)
        for piece in pieces:
            facts = piece[cap:, :].astype(jnp.float32)
            node = jnp.where(facts[2:3, :] > 0.5, facts[0:1, :] * 128.0 + facts[1:2, :], -1.0)
            total += jnp.dot(one_hot(row == node), piece[:cap, :], preferred_element_type=jnp.float32)
        out_ref[...] = total.astype(jnp.bfloat16)


def add_force(first, nodes, pieces, cap):
    vmem = pl.BlockSpec(memory_space=pltpu.VMEM)
    rows, feats = nodes.shape
    block = jax.ShapeDtypeStruct((rows // 2, feats), jnp.bfloat16)
    return pl.pallas_call(
        functools.partial(force_kernel, cap),
        out_shape=(block, block),
        in_specs=[pl.BlockSpec(memory_space=pltpu.SMEM)] + [vmem] * (1 + len(pieces)),
        out_specs=(vmem, vmem),
        compiler_params=pltpu.CompilerParams(vmem_limit_bytes=32 << 20),
        cost_estimate=SMALL,
        name="add_force",
    )(first, nodes, *pieces)


def layer_kernel(
    layer, place, slots, last, core_ref, idx_ref, own, sib, rim, bias, near_w, far_w, ws_hbm, wd_hbm, w2_hbm, *refs
):
    outs, refs = (refs[:2], refs[2:]) if last else (refs[:1], refs[1:])
    ws, wd, w2, ws_x, wd_x, w2_x, proj, near, summed, sems = refs
    rows, width = own.shape
    share = width // 2
    chunks = width // LANES
    part = chunks // 2
    core = core_ref[0]
    pairs = ((wd_hbm, wd), (ws_hbm, ws), (w2_hbm, w2))
    copies = [pltpu.make_async_copy(src.at[layer], dst, sems.at[i]) for i, (src, dst) in enumerate(pairs)]
    for copy in copies:
        copy.start()
    window = 3 * rows
    proj[0:8, :] = jnp.full((8, LANES), DEAD, jnp.float32)
    proj[4 * window + 4:4 * window + 16, :] = jnp.full((12, LANES), DEAD, jnp.float32)
    pack = place * (3 * share + 16)
    here, there = pl.multiple_of(core * share, 16), pl.multiple_of((1 - core) * share, 16)
    for spot, piece in ((here, near_w), (there, far_w)):
        ws_x[pl.ds(spot, share), :] = piece[pack:pack + share, :]
        wd_x[pl.ds(spot, share), :] = piece[pack + share:pack + 2 * share, :]
    third = slice(pack + 2 * share, pack + 3 * share)

    @pl.when(core == 0)
    def _():
        w2_x[:, :share] = near_w[third, :]
        w2_x[:, share:] = far_w[third, :]

    @pl.when(core != 0)
    def _():
        w2_x[:, share:] = near_w[third, :]
        w2_x[:, :share] = far_w[third, :]

    def put(dst, base, first, values):
        for c in range(values.shape[1] // LANES):
            dst[pl.ds(base * chunks + first + c, rows, stride=chunks), :] = values[:, c * LANES:(c + 1) * LANES] * 0.5

    def product(values, weights):
        return jnp.dot(values[...], weights[...], preferred_element_type=jnp.float32)

    b_own = bias[layer:layer + 1, :].astype(jnp.float32)
    b_other = near_w[pack + 3 * share:pack + 3 * share + 1, :].astype(jnp.float32)
    put(near, 0, part, product(own, wd_x) + b_other)
    put(proj, 1, part, product(own, ws_x))
    copies[0].wait()
    copies[1].wait()
    put(near, 0, 0, product(own, wd) + b_own)
    put(proj, 1, 0, product(own, ws))
    for ref, base in ((sib, rows + 1), (rim, 2 * rows + 1)):
        put(proj, base, 0, product(ref, ws))
        put(proj, base, part, product(ref, ws_x))
    low = lax.broadcasted_iota(jnp.int32, (8, LANES), 0) < chunks

    def nodes(q, carry):
        spot = pl.ds(pl.multiple_of(8 * q, 8), 8)
        mine = near[spot, :]
        total = None
        for j in range(slots):
            upper = proj[pl.ds(pl.multiple_of(idx_ref[j * rows + 2 * q], 4), 8), :]
            lower = proj[pl.ds(pl.multiple_of(idx_ref[j * rows + 2 * q + 1], 4), 8), :]
            y = jnp.where(low, upper, lower) + mine
            act = y * jnp.tanh(y) + y
            total = act if total is None else total + act
        summed[spot, :] = total
        return carry

    lax.fori_loop(0, rows // 2, nodes, 0, unroll=16)
    copies[2].wait()
    sums = [summed[pl.ds(c, rows, stride=chunks), :].astype(jnp.bfloat16) for c in range(chunks)]
    update = product(jnp.concatenate(sums[:part], 1), w2) + product(jnp.concatenate(sums[part:], 1), w2_x)
    result = (own[...].astype(jnp.float32) + update).astype(jnp.bfloat16)
    if not last:
        outs[0][...] = result
    else:
        @pl.when(core == 0)
        def _():
            outs[0][...] = result[:, :share]
            outs[1][...] = result[:, share:]

        @pl.when(core != 0)
        def _():
            outs[0][...] = result[:, share:]
            outs[1][...] = result[:, :share]


def run_layer(layer, place, slots, last, core, idx, own, sib, rim, ws, wd, w2, bias, near_w, far_w, cost=64):
    rows, width = own.shape
    share = width // 2
    chunks = width // LANES
    smem = pl.BlockSpec(memory_space=pltpu.SMEM)
    vmem = pl.BlockSpec(memory_space=pltpu.VMEM)
    bf16, f32 = jnp.bfloat16, jnp.float32
    if last:
        out_shape = (jax.ShapeDtypeStruct((rows, share), bf16),) * 2
        out_specs = (vmem, vmem)
    else:
        out_shape, out_specs = jax.ShapeDtypeStruct((rows, width), bf16), vmem
    return pl.pallas_call(
        functools.partial(layer_kernel, layer, place, slots, last),
        out_shape=out_shape,
        in_specs=[smem] * 2 + [vmem] * 6 + [pl.BlockSpec(memory_space=pl.ANY)] * 3,
        out_specs=out_specs,
        scratch_shapes=[
            pltpu.VMEM((width, share), bf16),
            pltpu.VMEM((width, share), bf16),
            pltpu.VMEM((share, width), bf16),
            pltpu.VMEM((width, share), bf16),
            pltpu.VMEM((width, share), bf16),
            pltpu.VMEM((share, width), bf16),
            pltpu.VMEM((3 * rows * chunks + 96, LANES), f32),
            pltpu.VMEM((rows * chunks, LANES), f32),
            pltpu.VMEM((rows * chunks, LANES), f32),
            pltpu.SemaphoreType.DMA((3,)),
        ],
        compiler_params=pltpu.CompilerParams(vmem_limit_bytes=32 << 20),
        cost_estimate=pl.CostEstimate(flops=cost * rows * width * width, bytes_accessed=10 * rows * width, transcendentals=0),
        name="graph_layer",
    )(core, idx, own, sib, rim, bias, near_w, far_w, ws, wd, w2)


def edge_offsets(nbrs, counts, core):
    graphs, rows, slots = nbrs.shape
    half = rows // 2
    nbr = lax.dynamic_slice(nbrs.transpose(0, 2, 1), (0, 0, core * half), (graphs, slots, half)) - core * half
    count = lax.dynamic_slice(counts, (0, core * half), (graphs, half))
    low = nbr + jnp.where(core == 0, 2 * half, half)
    high = nbr - jnp.where(core == 0, half, 0)
    place = jnp.where(nbr < half, low, jnp.where(nbr < 2 * half, nbr - half, high))
    live = jnp.arange(slots, dtype=jnp.int32)[None, :, None] < count[:, None, :]
    place = jnp.where(live, place, 3 * half)
    odd = jnp.arange(half, dtype=jnp.int32) % 2
    return (4 * (place + 1 - odd)).reshape(graphs, slots * half)


def spread_rows(same, other):
    a = lax.ppermute(same, ("mp", "batch"), [(0, 0), (1, 2), (2, 1), (3, 3)])
    b = lax.ppermute(other, ("mp", "batch"), [(0, 1), (1, 3), (2, 0), (3, 2)])
    return a, b


def gather_rows(a, b):
    same = lax.ppermute(a, ("mp", "batch"), [(0, 0), (1, 2), (2, 1), (3, 3)])
    other = lax.ppermute(b, ("mp", "batch"), [(0, 2), (1, 0), (2, 3), (3, 1)])
    return same, other


def ordered(which, a, b, axis):
    return jnp.where(which == 0, jnp.concatenate([a, b], axis), jnp.concatenate([b, a], axis))


def swap(values, axis):
    return lax.ppermute(values, axis, [(0, 1), (1, 0)])


def rims(own, wrap):
    size = lax.axis_size("mesh")
    pairs = []
    for m in range(size):
        if wrap or m + 1 < size:
            pairs.append((2 * m + 1, 2 * ((m + 1) % size)))
        if wrap or m > 0:
            pairs.append((2 * m, 2 * ((m - 1) % size) + 1))
    return lax.ppermute(own, ("mesh", "batch"), pairs)


def pack_kernel(plan, core_ref, g_bias, r_bias, *refs):
    weights, outs, sems = (refs[:3], refs[3:6]), refs[6:-1], refs[-1]
    share = g_bias.shape[1]
    here = pl.multiple_of(core_ref[0] * share, share)
    copies = []
    for members, out in zip(plan, outs):
        for place, (graph, layer) in enumerate(members):
            ws, wd, w2 = weights[graph]
            base = place * (3 * share + 16)
            sources = (
                ws.at[layer, pl.ds(here, share), :], wd.at[layer, pl.ds(here, share), :], w2.at[layer, :, pl.ds(here, share)]
            )
            for i, source in enumerate(sources):
                spot = base + i * share
                copies.append(pltpu.make_async_copy(source, out.at[spot:spot + share, :], sems.at[len(copies)]))
                copies[-1].start()
    for members, out in zip(plan, outs):
        for place, (graph, layer) in enumerate(members):
            base = place * (3 * share + 16) + 3 * share
            bias = (g_bias, r_bias)[graph][layer:layer + 1, :]
            out[base:base + 16, :] = jnp.broadcast_to(bias, (16, share))
    for copy in copies:
        copy.wait()


def pack_weights(plan, core, g_weights, g_bias, r_weights, r_bias):
    share = g_bias.shape[1]
    vmem = pl.BlockSpec(memory_space=pltpu.VMEM)
    hbm = pl.BlockSpec(memory_space=pltpu.HBM)
    sizes = [len(members) for members in plan]
    return pl.pallas_call(
        functools.partial(pack_kernel, plan),
        out_shape=tuple(jax.ShapeDtypeStruct((n * (3 * share + 16), share), jnp.bfloat16) for n in sizes),
        in_specs=[pl.BlockSpec(memory_space=pltpu.SMEM)] + [vmem] * 2 + [hbm] * 6,
        out_specs=(vmem,) * len(sizes),
        scratch_shapes=[pltpu.SemaphoreType.DMA((3 * sum(sizes),))],
        compiler_params=pltpu.CompilerParams(vmem_limit_bytes=60 << 20),
        cost_estimate=pl.CostEstimate(flops=256 * share**3, bytes_accessed=1, transcendentals=0),
        name="pack_weights",
    )(core, g_bias, r_bias, *g_weights, *r_weights)


def by_rows(
    g_nodes, r_nodes, g_nbr, g_count, r_nbr, r_count, bnd_src, bnd_part, bnd_node,
    g_ws, g_wd, g_b1, g_w2, r_ws, r_wd, r_b1, r_w2,
):
    part = lax.axis_index("mp")
    core = lax.axis_index("batch")
    parts = lax.axis_size("mesh")
    slots = g_nbr.shape[1]
    layers = g_ws.shape[0]
    rows = g_nodes.shape[1]
    half = rows // 2
    cap = 2 * bnd_src.shape[0] // parts
    me = lax.axis_index("mesh").reshape(1)
    core1 = core.reshape(1)
    g_own, r_own = g_nodes[0], r_nodes[0]
    g_weights, r_weights = (g_ws, g_wd, g_w2), (r_ws, r_wd, r_w2)
    after = lax.optimization_barrier

    same = lax.dynamic_slice(g_own, (part * half, 0), (half, g_own.shape[1]))
    other = lax.dynamic_slice(g_own, ((1 - part) * half, 0), (half, g_own.shape[1]))
    g_a, g_b = spread_rows(same, other)
    bnd = jnp.stack([bnd_src, bnd_part[:, 0], bnd_node])
    bnd, same, other = after((bnd, same, other))
    pieces = list(pick_rows(me, bnd, g_own, parts, cap))
    pieces[0], core1 = after((pieces[0], core1))
    packs = list(pack_weights((((0, 0), (1, 0)),), core1, g_weights, g_b1, r_weights, r_b1))
    near_w = [swap(packs[0], "mp")]
    landed = [pieces[0]]
    for k in range(1, parts):
        landed.append(lax.ppermute(pieces[k], "mesh", [(i, (i + k) % parts) for i in range(parts)]))
    landed[0], core1, packs[0], g_a, g_b = after((landed[0], core1, packs[0], g_a, g_b))
    idx = edge_offsets(jnp.stack([g_nbr, r_nbr]), jnp.stack([g_count, r_count]), core)
    rest = tuple(((graph, layer),) for layer in range(1, layers) for graph in (0, 1))
    packs += pack_weights(rest, core1, g_weights, g_b1, r_weights, r_b1)
    g_idx, r_idx = idx[0], idx[1]
    g_a, g_b, g_idx, r_idx, packs[1:], *landed = after((g_a, g_b, g_idx, r_idx, packs[1:], *landed))
    planet = ordered(core, g_a, g_b, 1)
    g_sib, g_rim = swap(planet, "batch"), rims(planet, True)
    *r_pair, packs[1:] = after((*add_force(part.reshape(1), r_own, landed, cap), packs[1:]))
    r_a, r_b = spread_rows(*r_pair)
    near_w.append(swap(packs[1], "mp"))
    r_a, r_b, g_sib, g_rim, near_w[0] = after((r_a, r_b, g_sib, g_rim, near_w[0]))
    regional, g_idx = after((ordered(core, r_a, r_b, 1), g_idx))
    r_sib, r_rim = swap(regional, "batch"), rims(regional, False)
    far_w = [swap(near_w[0], "batch")]
    for layer in range(layers):
        last = layer == layers - 1
        i = max(0, 2 * layer - 1)
        if layer:
            far_w.append(swap(near_w[i], "batch"))
        planet = run_layer(
            layer, 0, slots, last, core1, g_idx, planet, g_sib, g_rim, g_ws, g_wd, g_w2, g_b1, near_w[i], far_w[i],
            8 if layer else 64,
        )
        *planet, core1 = after((*(planet if last else (planet,)), core1))
        if not last:
            planet = planet[0]
            g_sib, g_rim = swap(planet, "batch"), rims(planet, True)
        if layer:
            i += 1
            near_w[i], core1 = after((near_w[i], core1))
            far_w.append(swap(near_w[i], "batch"))
        for j in range(i + 1, min(i + 3, len(packs))):
            if j == len(near_w):
                packs[j], near_w[j - 1] = after((packs[j], near_w[j - 1]))
                near_w.append(swap(packs[j], "mp"))
            if j == i + 1:
                core1, near_w[j] = after((core1, near_w[j]))
        regional = run_layer(
            layer, 1 - min(layer, 1), slots, last, core1, r_idx, regional, r_sib, r_rim, r_ws, r_wd, r_w2, r_b1,
            near_w[i], far_w[i],
        )
        if not last:
            regional, core1 = after((regional, core1))
            r_sib, r_rim = swap(regional, "batch"), rims(regional, False)
    g_out = ordered(part, *gather_rows(*planet), 0)
    g_out, *regional_rows = after((g_out, *gather_rows(*regional)))
    r_out = ordered(part, *regional_rows, 0)
    return g_out[None], r_out[None]


def solution(mesh):
    in_specs = (
        P(("groups", "batch"), "mesh", "mp"),
        P(("groups", "batch"), "mesh", "mp"),
        P("mesh", None),
        P("mesh"),
        P("mesh", None),
        P("mesh"),
        P("mesh"),
        P("mesh", None),
        P("mesh"),
        P(None, None, "mp"),
        P(None, None, "mp"),
        P(None, "mp"),
        P(None, "mp", None),
        P(None, None, "mp"),
        P(None, None, "mp"),
        P(None, "mp"),
        P(None, "mp", None),
    )
    out_specs = (P(("groups", "batch"), "mesh", "mp"), P(("groups", "batch"), "mesh", "mp"))
    square = mesh.shape["mp"] == 2 and mesh.shape["batch"] == 2
    return jax.shard_map(
        by_rows if square else by_features, mesh=mesh, in_specs=in_specs, out_specs=out_specs, check_vma=False
    )
```

```python
import functools

import jax
import jax.numpy as jnp
from jax import lax
from jax.experimental import pallas as pl
from jax.experimental.pallas import tpu as pltpu
from jax.sharding import PartitionSpec as P

LANES = 128
DEAD = -1e30
SMALL = pl.CostEstimate(flops=1, bytes_accessed=1, transcendentals=0)


def padded_2(shard, sides, width, wrap):
    for axis, dim in sides:
        size, length = (lax.axis_size(axis), shard.shape[dim])
        up = [(i, (i + 1) % size) for i in range(size if wrap else size - 1)]
        down = [(j, i) for i, j in up]
        last = lax.slice_in_dim(shard, length - width, length, axis=dim)
        leading = lax.slice_in_dim(shard, 0, width, axis=dim)
        before = lax.ppermute(last, axis, up)
        after = lax.ppermute(leading, axis, down)
        shard = jnp.concatenate([before, shard, after], axis=dim)
    return shard


def edge_sums(proj, near, nbr, count):
    slots = nbr.shape[1]
    live = jnp.arange(slots, dtype=jnp.int32)[None, :] < count[:, None]
    pre = proj[:, nbr].astype(jnp.float32) + near[:, :, None]
    acts = jnp.where(live[None, :, :, None], jax.nn.silu(pre), 0.0)
    return jnp.sum(acts, axis=2).astype(jnp.bfloat16)


def graph_layer(latent, nbr, count, w_send, w_recv, bias, w_out, wrap):
    rim = latent.shape[1] // 2
    own_full = lax.all_gather(latent, "mp", axis=2, tiled=True)
    padded_full = padded_2(own_full, (("mesh", 1),), rim, wrap)
    proj = jnp.dot(padded_full, w_send, preferred_element_type=jnp.float32).astype(jnp.bfloat16)
    near = jnp.dot(own_full, w_recv, preferred_element_type=jnp.float32) + bias.astype(jnp.float32)
    summed = edge_sums(proj, near, nbr, count)
    partial_prod = jnp.dot(summed, w_out, preferred_element_type=jnp.float32)
    update = lax.psum_scatter(
        partial_prod.astype(jnp.bfloat16), "mp", scatter_dimension=2, tiled=True
    ).astype(jnp.float32)
    return (latent.astype(jnp.float32) + update).astype(jnp.bfloat16)


def by_features(
    g_nodes, r_nodes, g_nbr, g_count, r_nbr, r_count, bnd_src, bnd_part, bnd_node,
    g_ws, g_wd, g_b1, g_w2, r_ws, r_wd, r_b1, r_w2,
):
    batch_rows, reg_rows, feats = r_nodes.shape
    dest = bnd_part[:, 0]
    outgoing = jnp.moveaxis(g_nodes[:, bnd_src], 1, 0)
    init = jnp.zeros((reg_rows + 1, batch_rows, feats), jnp.float32)
    target = dest * reg_rows + bnd_node
    mine = lax.axis_index("mesh")
    piece_rows = lax.all_gather(outgoing, "mesh", axis=0, tiled=True)
    piece_target = lax.all_gather(target, "mesh", axis=0, tiled=True)
    local = jnp.where(piece_target // reg_rows == mine, piece_target % reg_rows + 1, 0)
    landed = init.at[local].add(piece_rows.astype(jnp.float32))
    force = jnp.moveaxis(landed[1:], 1, 0)
    regional = (r_nodes.astype(jnp.float32) + force).astype(jnp.bfloat16)
    planet = g_nodes
    for layer in range(g_ws.shape[0]):
        planet = graph_layer(
            planet, g_nbr, g_count, g_ws[layer], g_wd[layer], g_b1[layer], g_w2[layer], True
        )
    for layer in range(r_ws.shape[0]):
        regional = graph_layer(
            regional, r_nbr, r_count, r_ws[layer], r_wd[layer], r_b1[layer], r_w2[layer], False
        )
    return (planet, regional)


def one_hot(flags):
    return jnp.where(flags, 1.0, 0.0).astype(jnp.bfloat16)


def pick_kernel(parts, cap, me_ref, bnd_ref, g_ref, *out_refs):
    rows = g_ref.shape[0]
    total = bnd_ref.shape[1]
    me = me_ref[0]
    src, part, node = (bnd_ref[i:i + 1, :] for i in range(3))
    lines = -(-parts // 8) * 8
    target = lax.rem(lax.broadcasted_iota(jnp.int32, (lines, total), 0) + me, parts)
    named = part == target
    before = one_hot(
        lax.broadcasted_iota(jnp.int32, (total, total), 0) < lax.broadcasted_iota(jnp.int32, (total, total), 1)
    )
    rank = jnp.dot(one_hot(named), before, preferred_element_type=jnp.float32)
    rank = jnp.where(named, rank, -1.0)
    source = one_hot(lax.broadcasted_iota(jnp.int32, (rows, total), 0) == src)
    line = lax.broadcasted_iota(jnp.int32, (16, total), 0)
    high = lax.shift_right_logical(node, 7)
    facts = jnp.where(line == 0, high, jnp.where(line == 1, node - high * 128, jnp.where(line == 2, 1, 0)))
    facts = facts.astype(jnp.float32).astype(jnp.bfloat16)
    place = lax.broadcasted_iota(jnp.int32, (cap, total), 0).astype(jnp.float32)
    across = (((1,), (1,)), ((), ()))
    for k in range(parts):
        chosen = one_hot(place == rank[k:k + 1, :])
        pick = lax.dot_general(chosen, source, across, preferred_element_type=jnp.float32).astype(jnp.bfloat16)
        out_refs[k][:cap, :] = jnp.dot(pick, g_ref[...], preferred_element_type=jnp.float32).astype(jnp.bfloat16)
        told = lax.dot_general(facts, chosen, across, preferred_element_type=jnp.float32)
        out_refs[k][cap:, :] = told.astype(jnp.bfloat16)


def pick_rows(me, bnd, nodes, parts, cap):
    vmem = pl.BlockSpec(memory_space=pltpu.VMEM)
    rows, feats = nodes.shape
    total = bnd.shape[1]
    piece = jax.ShapeDtypeStruct((cap + 16, feats), jnp.bfloat16)
    return pl.pallas_call(
        functools.partial(pick_kernel, parts, cap),
        out_shape=(piece,) * parts,
        in_specs=[pl.BlockSpec(memory_space=pltpu.SMEM), vmem, vmem],
        out_specs=(vmem,) * parts,
        compiler_params=pltpu.CompilerParams(vmem_limit_bytes=32 << 20),
        cost_estimate=pl.CostEstimate(flops=32 * rows**2 * feats, bytes_accessed=1, transcendentals=0),
        name="pick_rows",
    )(me, bnd, nodes)


def force_kernel(cap, first_ref, r_ref, *refs):
    pieces, (same_ref, other_ref) = refs[:-2], refs[-2:]
    half = same_ref.shape[0]
    first = first_ref[0]
    for out_ref, start in ((same_ref, first * half), (other_ref, (1 - first) * half)):
        start = pl.multiple_of(start, 16)
        row = (lax.broadcasted_iota(jnp.int32, (half, cap), 0) + start).astype(jnp.float32)
        total = r_ref[pl.ds(start, half), :].astype(jnp.float32)
        for piece in pieces:
            facts = piece[cap:, :].astype(jnp.float32)
            node = jnp.where(facts[2:3, :] > 0.5, facts[0:1, :] * 128.0 + facts[1:2, :], -1.0)
            total += jnp.dot(one_hot(row == node), piece[:cap, :], preferred_element_type=jnp.float32)
        out_ref[...] = total.astype(jnp.bfloat16)


def add_force(first, nodes, pieces, cap):
    vmem = pl.BlockSpec(memory_space=pltpu.VMEM)
    rows, feats = nodes.shape
    block = jax.ShapeDtypeStruct((rows // 2, feats), jnp.bfloat16)
    return pl.pallas_call(
        functools.partial(force_kernel, cap),
        out_shape=(block, block),
        in_specs=[pl.BlockSpec(memory_space=pltpu.SMEM)] + [vmem] * (1 + len(pieces)),
        out_specs=(vmem, vmem),
        compiler_params=pltpu.CompilerParams(vmem_limit_bytes=32 << 20),
        cost_estimate=SMALL,
        name="add_force",
    )(first, nodes, *pieces)


def layer_kernel(
    layer, place, slots, last, core_ref, idx_ref, own, sib, rim, bias, near_w, far_w, ws_hbm, wd_hbm, w2_hbm, *refs
):
    outs, refs = (refs[:2], refs[2:]) if last else (refs[:1], refs[1:])
    ws, wd, w2, ws_x, wd_x, w2_x, proj, near, summed, sems = refs
    rows, width = own.shape
    share = width // 2
    chunks = width // LANES
    part = chunks // 2
    core = core_ref[0]
    pairs = ((wd_hbm, wd), (ws_hbm, ws), (w2_hbm, w2))
    copies = [pltpu.make_async_copy(src.at[layer], dst, sems.at[i]) for i, (src, dst) in enumerate(pairs)]
    for copy in copies:
        copy.start()
    window = 3 * rows
    proj[0:8, :] = jnp.full((8, LANES), DEAD, jnp.float32)
    proj[4 * window + 4:4 * window + 16, :] = jnp.full((12, LANES), DEAD, jnp.float32)
    pack = place * (3 * share + 16)
    here, there = pl.multiple_of(core * share, 16), pl.multiple_of((1 - core) * share, 16)
    for spot, piece in ((here, near_w), (there, far_w)):
        ws_x[pl.ds(spot, share), :] = piece[pack:pack + share, :]
        wd_x[pl.ds(spot, share), :] = piece[pack + share:pack + 2 * share, :]
    third = slice(pack + 2 * share, pack + 3 * share)

    @pl.when(core == 0)
    def _():
        w2_x[:, :share] = near_w[third, :]
        w2_x[:, share:] = far_w[third, :]

    @pl.when(core != 0)
    def _():
        w2_x[:, share:] = near_w[third, :]
        w2_x[:, :share] = far_w[third, :]

    def put(dst, base, first, values):
        for c in range(values.shape[1] // LANES):
            dst[pl.ds(base * chunks + first + c, rows, stride=chunks), :] = values[:, c * LANES:(c + 1) * LANES] * 0.5

    def product(values, weights):
        return jnp.dot(values[...], weights[...], preferred_element_type=jnp.float32)

    b_own = bias[layer:layer + 1, :].astype(jnp.float32)
    b_other = near_w[pack + 3 * share:pack + 3 * share + 1, :].astype(jnp.float32)
    put(near, 0, part, product(own, wd_x) + b_other)
    put(proj, 1, part, product(own, ws_x))
    copies[0].wait()
    copies[1].wait()
    put(near, 0, 0, product(own, wd) + b_own)
    put(proj, 1, 0, product(own, ws))
    for ref, base in ((sib, rows + 1), (rim, 2 * rows + 1)):
        put(proj, base, 0, product(ref, ws))
        put(proj, base, part, product(ref, ws_x))
    low = lax.broadcasted_iota(jnp.int32, (8, LANES), 0) < chunks

    def nodes(q, carry):
        spot = pl.ds(pl.multiple_of(8 * q, 8), 8)
        mine = near[spot, :]
        total = None
        for j in range(slots):
            upper = proj[pl.ds(pl.multiple_of(idx_ref[j * rows + 2 * q], 4), 8), :]
            lower = proj[pl.ds(pl.multiple_of(idx_ref[j * rows + 2 * q + 1], 4), 8), :]
            y = jnp.where(low, upper, lower) + mine
            act = y * jnp.tanh(y) + y
            total = act if total is None else total + act
        summed[spot, :] = total
        return carry

    lax.fori_loop(0, rows // 2, nodes, 0, unroll=16)
    copies[2].wait()
    sums = [summed[pl.ds(c, rows, stride=chunks), :].astype(jnp.bfloat16) for c in range(chunks)]
    update = product(jnp.concatenate(sums[:part], 1), w2) + product(jnp.concatenate(sums[part:], 1), w2_x)
    result = (own[...].astype(jnp.float32) + update).astype(jnp.bfloat16)
    if not last:
        outs[0][...] = result
    else:
        @pl.when(core == 0)
        def _():
            outs[0][...] = result[:, :share]
            outs[1][...] = result[:, share:]

        @pl.when(core != 0)
        def _():
            outs[0][...] = result[:, share:]
            outs[1][...] = result[:, :share]


def run_layer(layer, place, slots, last, core, idx, own, sib, rim, ws, wd, w2, bias, near_w, far_w, cost=64):
    rows, width = own.shape
    share = width // 2
    chunks = width // LANES
    smem = pl.BlockSpec(memory_space=pltpu.SMEM)
    vmem = pl.BlockSpec(memory_space=pltpu.VMEM)
    bf16, f32 = jnp.bfloat16, jnp.float32
    if last:
        out_shape = (jax.ShapeDtypeStruct((rows, share), bf16),) * 2
        out_specs = (vmem, vmem)
    else:
        out_shape, out_specs = jax.ShapeDtypeStruct((rows, width), bf16), vmem
    return pl.pallas_call(
        functools.partial(layer_kernel, layer, place, slots, last),
        out_shape=out_shape,
        in_specs=[smem] * 2 + [vmem] * 6 + [pl.BlockSpec(memory_space=pl.ANY)] * 3,
        out_specs=out_specs,
        scratch_shapes=[
            pltpu.VMEM((width, share), bf16),
            pltpu.VMEM((width, share), bf16),
            pltpu.VMEM((share, width), bf16),
            pltpu.VMEM((width, share), bf16),
            pltpu.VMEM((width, share), bf16),
            pltpu.VMEM((share, width), bf16),
            pltpu.VMEM((3 * rows * chunks + 96, LANES), f32),
            pltpu.VMEM((rows * chunks, LANES), f32),
            pltpu.VMEM((rows * chunks, LANES), f32),
            pltpu.SemaphoreType.DMA((3,)),
        ],
        compiler_params=pltpu.CompilerParams(vmem_limit_bytes=32 << 20),
        cost_estimate=pl.CostEstimate(flops=cost * rows * width * width, bytes_accessed=10 * rows * width, transcendentals=0),
        name="graph_layer",
    )(core, idx, own, sib, rim, bias, near_w, far_w, ws, wd, w2)


def edge_offsets(nbrs, counts, core):
    graphs, rows, slots = nbrs.shape
    half = rows // 2
    nbr = lax.dynamic_slice(nbrs.transpose(0, 2, 1), (0, 0, core * half), (graphs, slots, half)) - core * half
    count = lax.dynamic_slice(counts, (0, core * half), (graphs, half))
    low = nbr + jnp.where(core == 0, 2 * half, half)
    high = nbr - jnp.where(core == 0, half, 0)
    place = jnp.where(nbr < half, low, jnp.where(nbr < 2 * half, nbr - half, high))
    live = jnp.arange(slots, dtype=jnp.int32)[None, :, None] < count[:, None, :]
    place = jnp.where(live, place, 3 * half)
    odd = jnp.arange(half, dtype=jnp.int32) % 2
    return (4 * (place + 1 - odd)).reshape(graphs, slots * half)


def spread_rows(same, other):
    a = lax.ppermute(same, ("mp", "batch"), [(0, 0), (1, 2), (2, 1), (3, 3)])
    b = lax.ppermute(other, ("mp", "batch"), [(0, 1), (1, 3), (2, 0), (3, 2)])
    return a, b


def gather_rows(a, b):
    same = lax.ppermute(a, ("mp", "batch"), [(0, 0), (1, 2), (2, 1), (3, 3)])
    other = lax.ppermute(b, ("mp", "batch"), [(0, 2), (1, 0), (2, 3), (3, 1)])
    return same, other


def ordered(which, a, b, axis):
    return jnp.where(which == 0, jnp.concatenate([a, b], axis), jnp.concatenate([b, a], axis))


def swap(values, axis):
    return lax.ppermute(values, axis, [(0, 1), (1, 0)])


def rims(own, wrap):
    size = lax.axis_size("mesh")
    pairs = []
    for m in range(size):
        if wrap or m + 1 < size:
            pairs.append((2 * m + 1, 2 * ((m + 1) % size)))
        if wrap or m > 0:
            pairs.append((2 * m, 2 * ((m - 1) % size) + 1))
    return lax.ppermute(own, ("mesh", "batch"), pairs)


def pack_kernel(plan, core_ref, g_bias, r_bias, *refs):
    weights, outs, sems = (refs[:3], refs[3:6]), refs[6:-1], refs[-1]
    share = g_bias.shape[1]
    here = pl.multiple_of(core_ref[0] * share, share)
    copies = []
    for members, out in zip(plan, outs):
        for place, (graph, layer) in enumerate(members):
            ws, wd, w2 = weights[graph]
            base = place * (3 * share + 16)
            sources = (
                ws.at[layer, pl.ds(here, share), :], wd.at[layer, pl.ds(here, share), :], w2.at[layer, :, pl.ds(here, share)]
            )
            for i, source in enumerate(sources):
                spot = base + i * share
                copies.append(pltpu.make_async_copy(source, out.at[spot:spot + share, :], sems.at[len(copies)]))
                copies[-1].start()
    for members, out in zip(plan, outs):
        for place, (graph, layer) in enumerate(members):
            base = place * (3 * share + 16) + 3 * share
            bias = (g_bias, r_bias)[graph][layer:layer + 1, :]
            out[base:base + 16, :] = jnp.broadcast_to(bias, (16, share))
    for copy in copies:
        copy.wait()


def pack_weights(plan, core, g_weights, g_bias, r_weights, r_bias):
    share = g_bias.shape[1]
    vmem = pl.BlockSpec(memory_space=pltpu.VMEM)
    hbm = pl.BlockSpec(memory_space=pltpu.HBM)
    sizes = [len(members) for members in plan]
    return pl.pallas_call(
        functools.partial(pack_kernel, plan),
        out_shape=tuple(jax.ShapeDtypeStruct((n * (3 * share + 16), share), jnp.bfloat16) for n in sizes),
        in_specs=[pl.BlockSpec(memory_space=pltpu.SMEM)] + [vmem] * 2 + [hbm] * 6,
        out_specs=(vmem,) * len(sizes),
        scratch_shapes=[pltpu.SemaphoreType.DMA((3 * sum(sizes),))],
        compiler_params=pltpu.CompilerParams(vmem_limit_bytes=60 << 20),
        cost_estimate=pl.CostEstimate(flops=256 * share**3, bytes_accessed=1, transcendentals=0),
        name="pack_weights",
    )(core, g_bias, r_bias, *g_weights, *r_weights)


def by_rows(
    g_nodes, r_nodes, g_nbr, g_count, r_nbr, r_count, bnd_src, bnd_part, bnd_node,
    g_ws, g_wd, g_b1, g_w2, r_ws, r_wd, r_b1, r_w2,
):
    part = lax.axis_index("mp")
    core = lax.axis_index("batch")
    parts = lax.axis_size("mesh")
    slots = g_nbr.shape[1]
    layers = g_ws.shape[0]
    rows = g_nodes.shape[1]
    half = rows // 2
    cap = 2 * bnd_src.shape[0] // parts
    me = lax.axis_index("mesh").reshape(1)
    core1 = core.reshape(1)
    g_own, r_own = g_nodes[0], r_nodes[0]
    g_weights, r_weights = (g_ws, g_wd, g_w2), (r_ws, r_wd, r_w2)
    after = lax.optimization_barrier

    same = lax.dynamic_slice(g_own, (part * half, 0), (half, g_own.shape[1]))
    other = lax.dynamic_slice(g_own, ((1 - part) * half, 0), (half, g_own.shape[1]))
    g_a, g_b = spread_rows(same, other)
    bnd = jnp.stack([bnd_src, bnd_part[:, 0], bnd_node])
    bnd, same, other = after((bnd, same, other))
    pieces = list(pick_rows(me, bnd, g_own, parts, cap))
    pieces[0], core1 = after((pieces[0], core1))
    packs = list(pack_weights((((0, 0), (1, 0)),), core1, g_weights, g_b1, r_weights, r_b1))
    near_w = [swap(packs[0], "mp")]
    landed = [pieces[0]]
    for k in range(1, parts):
        landed.append(lax.ppermute(pieces[k], "mesh", [(i, (i + k) % parts) for i in range(parts)]))
    landed[0], core1, packs[0], g_a, g_b = after((landed[0], core1, packs[0], g_a, g_b))
    g_nbr, g_count, r_nbr, r_count, landed[1] = after((g_nbr, g_count, r_nbr, r_count, landed[1]))
    idx = edge_offsets(jnp.stack([g_nbr, r_nbr]), jnp.stack([g_count, r_count]), core)
    rest = tuple(((graph, layer),) for layer in range(1, layers) for graph in (0, 1))
    packs += pack_weights(rest, core1, g_weights, g_b1, r_weights, r_b1)
    g_idx, r_idx = idx[0], idx[1]
    g_a, g_b, g_idx, r_idx, packs[1:], *landed = after((g_a, g_b, g_idx, r_idx, packs[1:], *landed))
    planet = ordered(core, g_a, g_b, 1)
    g_sib, g_rim = swap(planet, "batch"), rims(planet, True)
    *r_pair, packs[1:] = after((*add_force(part.reshape(1), r_own, landed, cap), packs[1:]))
    r_a, r_b = spread_rows(*r_pair)
    near_w.append(swap(packs[1], "mp"))
    r_a, r_b, g_sib, g_rim, near_w[0] = after((r_a, r_b, g_sib, g_rim, near_w[0]))
    regional, g_idx = after((ordered(core, r_a, r_b, 1), g_idx))
    r_sib, r_rim = swap(regional, "batch"), rims(regional, False)
    far_w = [swap(near_w[0], "batch")]
    for layer in range(layers):
        last = layer == layers - 1
        i = max(0, 2 * layer - 1)
        if layer:
            far_w.append(swap(near_w[i], "batch"))
        planet = run_layer(
            layer, 0, slots, last, core1, g_idx, planet, g_sib, g_rim, g_ws, g_wd, g_w2, g_b1, near_w[i], far_w[i],
            8 if layer else 64,
        )
        *planet, core1 = after((*(planet if last else (planet,)), core1))
        if not last:
            planet = planet[0]
            g_sib, g_rim = swap(planet, "batch"), rims(planet, True)
        if layer:
            i += 1
            near_w[i], core1 = after((near_w[i], core1))
            far_w.append(swap(near_w[i], "batch"))
        for j in range(i + 1, min(i + 3, len(packs))):
            if j == len(near_w):
                packs[j], near_w[j - 1] = after((packs[j], near_w[j - 1]))
                near_w.append(swap(packs[j], "mp"))
            if j == i + 1:
                core1, near_w[j] = after((core1, near_w[j]))
        regional = run_layer(
            layer, 1 - min(layer, 1), slots, last, core1, r_idx, regional, r_sib, r_rim, r_ws, r_wd, r_w2, r_b1,
            near_w[i], far_w[i],
        )
        if not last:
            regional, core1 = after((regional, core1))
            r_sib, r_rim = swap(regional, "batch"), rims(regional, False)
    g_out = ordered(part, *gather_rows(*planet), 0)
    g_out, *regional_rows = after((g_out, *gather_rows(*regional)))
    r_out = ordered(part, *regional_rows, 0)
    return g_out[None], r_out[None]


def solution(mesh):
    in_specs = (
        P(("groups", "batch"), "mesh", "mp"),
        P(("groups", "batch"), "mesh", "mp"),
        P("mesh", None),
        P("mesh"),
        P("mesh", None),
        P("mesh"),
        P("mesh"),
        P("mesh", None),
        P("mesh"),
        P(None, None, "mp"),
        P(None, None, "mp"),
        P(None, "mp"),
        P(None, "mp", None),
        P(None, None, "mp"),
        P(None, None, "mp"),
        P(None, "mp"),
        P(None, "mp", None),
    )
    out_specs = (P(("groups", "batch"), "mesh", "mp"), P(("groups", "batch"), "mesh", "mp"))
    square = mesh.shape["mp"] == 2 and mesh.shape["batch"] == 2
    return jax.shard_map(
        by_rows if square else by_features, mesh=mesh, in_specs=in_specs, out_specs=out_specs, check_vma=False
    )
```
